32 devices in a mesh: grp: 4 (over y, x), seq: 8 (over z, core).
Axes of the slice: x: 2, y: 2, z: 4, core: 2. Of those that a mesh axis runs over, the one named last changes fastest.
Arguments:
- inputs: bfloat16 [8192, 2560], P(('grp', 'seq')), may hold values from -0.078125 to 0.078125
- out_grad: bfloat16 [8192, 2560], P(('grp', 'seq')), may hold values from -6 to 6
- input_map: bfloat16 [8192, 128], P(('grp', 'seq')), may hold values from -0.09375 to 0.09375
- output_map: bfloat16 [8192, 128], P(('grp', 'seq')), may hold values from -0.09375 to 0.09375
- log_decay: float32 [40, 8192], P(None, ('grp', 'seq')), may hold values from -1 to 0, as said below
Outputs:
- grad_inputs: bfloat16 [8192, 2560], P(('grp', 'seq'))
- grad_input_map: bfloat16 [8192, 128], P(('grp', 'seq'))
- grad_output_map: bfloat16 [8192, 128], P(('grp', 'seq'))
- grad_decay: float32 [40, 8192], P(None, ('grp', 'seq'))
The draws below stay inside these ranges and needn't reach their ends.
Inputs may be any that keep to these rules, and one draw needn't show every extreme that they name: log_decay is negative everywhere.
All inputs are finite; a program needn't handle non-finite values.
Results may differ from the reference program's by a relative error of at most 0.0081.
Values sent between devices are 32-bit elements; how exact they have to be, the bound alone decides.
No kernel may reach another device: no remote copies, remote signals or barrier semaphores. Data moves between devices by JAX's collectives and lax.ppermute only.
A program may use at most 192 MiB of HBM per device.

```python
import math
import jax
import jax.numpy as jnp
from jax import lax

HEADS = 40
HEADDIM = 64
STATE = 128
STRETCH = 256
TOKENS = 8192


def draw_log_decay(key, part):
    keys = jax.random.split(jax.random.fold_in(key, 11), 6)
    fast_share = 0.5
    picked = jax.random.uniform(keys[0], (HEADS, 1), jnp.float32) < fast_share
    fast_rate = jnp.minimum(jnp.exp(jax.random.uniform(keys[1], (HEADS, 1), jnp.float32, math.log(5.0), math.log(8.0))) / STRETCH, 0.15)
    slow_rate = jnp.exp(jax.random.uniform(keys[2], (HEADS, 1), jnp.float32, math.log(0.05), math.log(0.5))) * 2.3 / TOKENS
    baseline_decay_rate = jnp.where(picked, fast_rate, slow_rate)
    coarse_estimate = jnp.exp(jax.random.uniform(keys[3], (HEADS, TOKENS), jnp.float32, -math.log(2.0), math.log(2.0)))
    marked_positions = jax.random.randint(keys[4], (HEADS, 3), 0, TOKENS)
    position_slots = jnp.arange(TOKENS, dtype=jnp.int32)
    sudden_jump = jnp.any(position_slots[None, None, :] == marked_positions[:, :, None], axis=1)
    layer_depth_count = jax.random.uniform(keys[5], (HEADS, TOKENS), jnp.float32, 0.22, 0.69)
    return -(baseline_decay_rate * coarse_estimate) - jnp.where(sudden_jump, layer_depth_count, 0.0)


def levels(rng, extent, cuts, low, high):
    gain = 1.0
    for axis_at, shards_of in cuts:
        heights = jax.random.uniform(jax.random.fold_in(jax.random.fold_in(rng, 6), axis_at), (shards_of,), jnp.float32, low / len(cuts), high / len(cuts))
        gain = gain * jnp.repeat(jnp.exp(heights), extent[axis_at] // shards_of).reshape((-1,) + (1,) * (len(extent) - 1 - axis_at))
    return gain


def bell_draw(own_key, shape, width, reach, shards=(), kind=jnp.bfloat16):
    array = jax.random.normal(own_key, shape, jnp.float32) * width
    if len(shards) > 0:
        array = levels(own_key, shape, shards, -0.22, 0.18) * array
    return jnp.clip(array, min=-reach, max=reach).astype(kind)


def setup_inputs(seed: int = 0) -> dict:
    streams_of = jax.random.split(jax.random.key(seed), 6)
    return {
        "inputs": bell_draw(streams_of[0], (TOKENS, HEADS * HEADDIM), (TOKENS * HEADS * HEADDIM // (32 * STATE)) ** -0.5, 0.078125, ((0, 32),)),
        "out_grad": bell_draw(streams_of[1], (TOKENS, HEADS * HEADDIM), 1.0, 6.0, ((0, 32),)),
        "input_map": bell_draw(streams_of[2], (TOKENS, STATE), (32 * STATE) ** -0.5, 0.09375, ((0, 32),)),
        "output_map": bell_draw(streams_of[3], (TOKENS, STATE), (32 * STATE) ** -0.5, 0.09375, ((0, 32),)),
        "log_decay": draw_log_decay(jax.random.fold_in(streams_of[5], 71), 0),
    }


def mult(form, left, right):
    return jnp.einsum(form, left.astype(jnp.float32), right.astype(jnp.float32), precision=lax.Precision.HIGHEST)


def weigh(values, grads, rates):
    cumulative = jnp.cumsum(rates, axis=1)
    block_decay = cumulative[:, -1]
    decay_tail = jnp.exp(block_decay[:, None] - cumulative)
    decay_lead = jnp.exp(cumulative)
    inputs_tail = (values.astype(jnp.float32) * decay_tail.T[:, :, None]).astype(jnp.bfloat16)
    grads_lead = (grads.astype(jnp.float32) * decay_lead.T[:, :, None]).astype(jnp.bfloat16)
    return cumulative, block_decay, decay_tail, decay_lead, inputs_tail, grads_lead


def block_summary(values, grads, write_map, read_map, rates):
    cumulative, block_decay, decay_tail, decay_lead, inputs_tail, grads_lead = weigh(values, grads, rates)
    own_state = mult('khp,kn->hpn', inputs_tail, write_map)
    own_back = mult('khp,kn->hpn', grads_lead, read_map)
    return block_decay, own_state, own_back


def block_intra(values, grads, write_map, read_map, rates):
    cumulative = jnp.cumsum(rates, axis=1)
    length = rates.shape[1]
    row_ids = lax.broadcasted_iota(jnp.int32, (length, length), 0)
    col_ids = lax.broadcasted_iota(jnp.int32, (length, length), 1)
    causal = (row_ids >= col_ids)[None]
    log_gap = cumulative[:, :, None] - cumulative[:, None, :]
    decay = jnp.where(causal, jnp.exp(jnp.where(causal, log_gap, 0.0)), 0.0)
    scores = jnp.dot(read_map, write_map.T, preferred_element_type=jnp.float32)
    mixing = (scores[None] * decay).astype(jnp.bfloat16)
    y_intra = mult('hij,jhp->ihp', mixing, values)
    dx_intra = mult('hij,ihp->jhp', mixing, grads)
    pair_dots = mult('ihp,jhp->hij', values, grads)
    head_sum = jnp.sum(pair_dots * jnp.swapaxes(decay, 1, 2), axis=0).astype(jnp.bfloat16)
    db_intra = jnp.dot(head_sum, read_map, preferred_element_type=jnp.float32)
    dc_intra = jnp.dot(head_sum.T, write_map, preferred_element_type=jnp.float32)
    return y_intra, dx_intra, db_intra, dc_intra


def block_final(values, grads, write_map, read_map, rates, y_intra, dx_intra, db_intra, dc_intra, state_in, back_in):
    cumulative, block_decay, decay_tail, decay_lead, inputs_tail, grads_lead = weigh(values, grads, rates)
    state_half = state_in.astype(jnp.bfloat16)
    back_half = back_in.astype(jnp.bfloat16)
    outputs_full = y_intra + mult('kn,hpn->khp', read_map, state_half) * decay_lead.T[:, :, None]
    grad_full = dx_intra + mult('kn,hpn->khp', write_map, back_half) * decay_tail.T[:, :, None]
    grad_write = db_intra + mult('khp,hpn->kn', inputs_tail, back_half)
    grad_read = dc_intra + mult('khp,hpn->kn', grads_lead, state_half)
    change = jnp.sum(grads.astype(jnp.float32) * outputs_full - values.astype(jnp.float32) * grad_full, axis=2).T
    return grad_full.astype(jnp.bfloat16), grad_write.astype(jnp.bfloat16), grad_read.astype(jnp.bfloat16), change


def reference(inputs, out_grad, input_map, output_map, log_decay):
    head_count = log_decay.shape[0]
    tokens = inputs.shape[0]
    head_size = inputs.shape[1] // head_count
    blocks = tokens // STRETCH
    parts = (inputs.reshape(blocks, STRETCH, head_count, head_size),
             out_grad.reshape(blocks, STRETCH, head_count, head_size),
             input_map.reshape(blocks, STRETCH, STATE),
             output_map.reshape(blocks, STRETCH, STATE),
             log_decay.reshape(head_count, blocks, STRETCH).transpose(1, 0, 2))
    empty_state = jnp.zeros((head_count, head_size, STATE), jnp.float32)

    def forward(running, pieces):
        block_decay, own_state, own_back = block_summary(*pieces)
        return jnp.exp(block_decay)[:, None, None] * running + own_state, running

    def backward(running, pieces):
        block_decay, own_state, own_back = block_summary(*pieces)
        return jnp.exp(block_decay)[:, None, None] * running + own_back, running

    _, state_stack = lax.scan(forward, empty_state, parts)
    _, back_stack = lax.scan(backward, empty_state, parts, reverse=True)

    def finish(item):
        pieces, state_in, back_in = item
        intra = block_intra(*pieces)
        return block_final(*pieces, *intra, state_in, back_in)

    grad_values, grad_write, grad_read, change = lax.map(finish, (parts, state_stack, back_stack))
    change = change.transpose(1, 0, 2).reshape(head_count, tokens)
    grad_decay = jnp.cumsum(change[:, ::-1], axis=1)[:, ::-1]
    return (grad_values.reshape(tokens, head_count * head_size),
            grad_write.reshape(tokens, STATE),
            grad_read.reshape(tokens, STATE),
            grad_decay)
```

```python
import jax
import jax.numpy as jnp
from jax import lax
from jax.experimental import pallas as pl
from jax.experimental.pallas import tpu as pltpu
from jax.sharding import PartitionSpec as P

STATE = 128
STRETCH = 256
LANES = 512
F32 = jnp.float32
BF16 = jnp.bfloat16
HIGHEST = lax.Precision.HIGHEST


def dot(left, right, left_dim, right_dim, precision=None):
    return lax.dot_general(
        left,
        right,
        (((left_dim,), (right_dim,)), ((), ())),
        precision=precision,
        preferred_element_type=F32,
    )


def iota(shape, dim):
    return lax.broadcasted_iota(jnp.int32, shape, dim)


def lower(length):
    return (iota((length, length), 0) >= iota((length, length), 1)).astype(F32)


def thrice(rates):
    heads, length = rates.shape
    spare = jnp.zeros((STATE - 3 * heads, length), F32)
    return jnp.concatenate([rates, rates, rates, spare], axis=0)


def three_terms(value, heads):
    lane = iota(value.shape, 1)
    first = value.astype(BF16)
    rest = value - first.astype(F32)
    second = rest.astype(BF16)
    third = (rest - second.astype(F32)).astype(BF16)
    return jnp.where(lane < heads, first, jnp.where(lane < 2 * heads, second, third))


def spreader(chunk, heads, head_size, lanes):
    row = iota((STATE, lanes), 0)
    head = (iota((STATE, lanes), 1) + chunk * lanes) // head_size
    hit = (row == head) | (row == head + heads) | (row == head + 2 * heads)
    return hit.astype(F32).astype(BF16)


def head_adder(chunk, head_size, lanes):
    head = (iota((lanes, STATE), 0) + chunk * lanes) // head_size
    return (iota((lanes, STATE), 1) == head).astype(F32).astype(BF16)


def head_sums(value, adder):
    first = value.astype(BF16)
    second = (value - first.astype(F32)).astype(BF16)
    return dot(first, adder, 1, 0) + dot(second, adder, 1, 0)


def decay_terms(rates, heads):
    length = rates.shape[1]
    running = dot(lower(length), thrice(rates), 1, 1, HIGHEST)
    last = running[length - 1 : length, :]
    return (
        running,
        three_terms(jnp.exp(last - running), heads),
        three_terms(jnp.exp(running), heads),
    )


def summary_kernel(
    heads, place, x_ref, g_ref, write_ref, read_ref, rates_ref,
    send_ref, keep_ref, decay_ref, total_ref, tail_ref, lead_ref, write_t, read_t,
):
    chunk = pl.program_id(0)
    head_size = x_ref.shape[1] * pl.num_programs(0) // heads

    @pl.when(chunk == 0)
    def _():
        running, tail, lead = decay_terms(rates_ref[...], heads)
        tail_ref[...] = tail
        lead_ref[...] = lead
        total_ref[...] = running[STRETCH - 8 :, :]
        write_t[...] = write_ref[...].astype(F32).T.astype(BF16)
        read_t[...] = read_ref[...].astype(F32).T.astype(BF16)

    spread = spreader(chunk, heads, head_size, x_ref.shape[1])
    tail = dot(tail_ref[...], spread, 1, 0)
    lead = dot(lead_ref[...], spread, 1, 0)
    inputs_tail = (x_ref[...].astype(F32) * tail).astype(BF16)
    grads_lead = (g_ref[...].astype(F32) * lead).astype(BF16)
    state = dot(write_t[...], inputs_tail, 1, 0)
    back = dot(read_t[...], grads_lead, 1, 0)
    decay_ref[...] = lead[STRETCH - 8 :, :]
    first = place[0] == 0
    send_ref[...] = jnp.where(first, state, back)
    keep_ref[...] = jnp.where(first, back, state)


def summary(place, x, g, write_map, read_map, rates):
    tokens, wide = x.shape
    heads = rates.shape[0]
    whole = lambda shape: pl.BlockSpec(shape, lambda c: (0, 0))
    strip = lambda rows: pl.BlockSpec((rows, LANES), lambda c: (0, c))
    return pl.pallas_call(
        lambda *refs: summary_kernel(heads, *refs),
        grid=(wide // LANES,),
        in_specs=[
            pl.BlockSpec(memory_space=pltpu.SMEM),
            strip(tokens),
            strip(tokens),
            whole((tokens, STATE)),
            whole((tokens, STATE)),
            whole((heads, tokens)),
        ],
        out_specs=[strip(STATE), strip(STATE), strip(8), whole((8, STATE))],
        out_shape=[
            jax.ShapeDtypeStruct((STATE, wide), F32),
            jax.ShapeDtypeStruct((STATE, wide), F32),
            jax.ShapeDtypeStruct((8, wide), F32),
            jax.ShapeDtypeStruct((8, STATE), F32),
        ],
        scratch_shapes=[
            pltpu.VMEM((tokens, STATE), BF16),
            pltpu.VMEM((tokens, STATE), BF16),
            pltpu.VMEM((STATE, tokens), BF16),
            pltpu.VMEM((STATE, tokens), BF16),
        ],
        compiler_params=pltpu.CompilerParams(vmem_limit_bytes=32 << 20),
        name="summary",
    )(place, x, g, write_map, read_map, rates)


def intra_kernel(
    heads, x_ref, g_ref, write_ref, read_ref, rates_ref,
    dx_ref, db_ref, dc_ref, change_ref, column_ref, row_ref, scores_ref, mask_ref, pairs_ref,
):
    chunk = pl.program_id(0)
    lanes = x_ref.shape[1]
    head_size = lanes * pl.num_programs(0) // heads
    per_chunk = lanes // head_size

    @pl.when(chunk == 0)
    def _():
        rates = rates_ref[...]
        triangle = lower(STRETCH)
        column_ref[...] = dot(triangle, thrice(rates), 1, 1, HIGHEST)
        row_ref[...] = dot(rates, triangle, 1, 1, HIGHEST)
        mask_ref[...] = triangle
        scores_ref[...] = dot(read_ref[...], write_ref[...], 1, 1)
        pairs_ref[...] = jnp.zeros_like(pairs_ref)
        change_ref[...] = jnp.zeros_like(change_ref)

    columns = pltpu.roll(column_ref[...], STATE - chunk * per_chunk, 1)
    rows = row_ref[pl.ds(pl.multiple_of(chunk * per_chunk, per_chunk), per_chunk), :]
    causal = mask_ref[...] > 0.5
    scores = scores_ref[...]
    pairs = pairs_ref[...]
    low_half = iota((STRETCH, 2 * head_size), 1) < head_size
    adder = head_adder(chunk, head_size, lanes)
    for pair in range(per_chunk // 2):
        strip = slice(pair * 2 * head_size, (pair + 1) * 2 * head_size)
        x = x_ref[:, strip]
        g = g_ref[:, strip]
        ys, dxs = [], []
        for half in range(2):
            head = 2 * pair + half
            gap = columns[:, head : head + 1] - rows[head : head + 1, :]
            decay = jnp.where(causal, jnp.exp(gap), 0.0)
            mixing = (scores * decay).astype(BF16)
            ys.append(dot(mixing, x, 1, 0))
            dxs.append(dot(mixing, g, 0, 0))
            mine = low_half if half == 0 else jnp.logical_not(low_half)
            pairs = pairs + dot(jnp.where(mine, g, jnp.zeros_like(g)), x, 1, 1) * decay
        y = jnp.where(low_half, ys[0], ys[1])
        dx = jnp.where(low_half, dxs[0], dxs[1])
        dx_ref[:, strip] = dx
        change_ref[...] += head_sums(
            g.astype(F32) * y - x.astype(F32) * dx, adder[strip, :]
        )
    pairs_ref[...] = pairs

    @pl.when(chunk == pl.num_programs(0) - 1)
    def _():
        summed = pairs_ref[...].astype(BF16)
        db_ref[...] = dot(summed, read_ref[...], 0, 0)
        dc_ref[...] = dot(summed, write_ref[...], 1, 0)


def intra(x, g, write_map, read_map, rates):
    tokens, wide = x.shape
    heads = rates.shape[0]
    whole = lambda shape: pl.BlockSpec(shape, lambda c: (0, 0))
    strip = lambda rows: pl.BlockSpec((rows, LANES), lambda c: (0, c))
    return pl.pallas_call(
        lambda *refs: intra_kernel(heads, *refs),
        grid=(wide // LANES,),
        in_specs=[
            strip(tokens),
            strip(tokens),
            whole((tokens, STATE)),
            whole((tokens, STATE)),
            whole((heads, tokens)),
        ],
        out_specs=[strip(tokens)] + [whole((tokens, STATE))] * 3,
        out_shape=[
            jax.ShapeDtypeStruct((tokens, wide), F32),
            jax.ShapeDtypeStruct((tokens, STATE), F32),
            jax.ShapeDtypeStruct((tokens, STATE), F32),
            jax.ShapeDtypeStruct((tokens, STATE), F32),
        ],
        scratch_shapes=[
            pltpu.VMEM((tokens, STATE), F32),
            pltpu.VMEM((heads, tokens), F32),
            pltpu.VMEM((tokens, tokens), F32),
            pltpu.VMEM((tokens, tokens), F32),
            pltpu.VMEM((tokens, tokens), F32),
        ],
        compiler_params=pltpu.CompilerParams(vmem_limit_bytes=32 << 20),
        cost_estimate=pl.CostEstimate(
            flops=30_000_000_000, bytes_accessed=6_000_000, transcendentals=heads * tokens * tokens
        ),
        name="intra",
    )(x, g, write_map, read_map, rates)


def finish_kernel(
    heads, pieces, place, x_ref, g_ref, write_ref, read_ref, rates_ref,
    dx_ref, db_ref, dc_ref, change_ref, first_ref, other_decay_ref, *rest,
):
    own_pieces = rest[:pieces]
    far_pieces = rest[pieces : 2 * pieces]
    (grad_ref, write_out, read_out, suffix_ref, tail_ref, lead_ref, own_ref, far_ref, sum_ref,
     db_sum, dc_sum) = rest[2 * pieces :]
    chunk = pl.program_id(0)
    lanes = x_ref.shape[1]
    head_size = lanes * pl.num_programs(0) // heads
    part = STATE // pieces

    @pl.when(chunk == 0)
    def _():
        _, tail, lead = decay_terms(rates_ref[...], heads)
        tail_ref[...] = tail
        lead_ref[...] = lead
        sum_ref[...] = change_ref[...]
        db_sum[...] = db_ref[...]
        dc_sum[...] = dc_ref[...]

    for step in range(pieces):
        rows = pl.ds(pl.multiple_of((place[1] ^ step) * part, part), part)
        own_ref[rows, :] = own_pieces[step][...]
        far_ref[rows, :] = far_pieces[step][...]
    own = own_ref[...] * other_decay_ref[0:1, :] + first_ref[...]
    far = far_ref[...]
    is_first = place[0] == 0
    state = jnp.where(is_first, far, own).astype(BF16)
    back = jnp.where(is_first, own, far).astype(BF16)
    spread = spreader(chunk, heads, head_size, lanes)
    tail = dot(tail_ref[...], spread, 1, 0)
    lead = dot(lead_ref[...], spread, 1, 0)
    x = x_ref[...].astype(F32)
    g = g_ref[...].astype(F32)
    y = dot(read_ref[...], state, 1, 0) * lead
    dx = dot(write_ref[...], back, 1, 0) * tail
    grad_ref[...] = (dx_ref[...] + dx).astype(BF16)
    sum_ref[...] += head_sums(g * y - x * dx, head_adder(chunk, head_size, lanes))
    db_sum[...] += dot((x * tail).astype(BF16), back, 1, 1)
    dc_sum[...] += dot((g * lead).astype(BF16), state, 1, 1)

    @pl.when(chunk == pl.num_programs(0) - 1)
    def _():
        write_out[...] = db_sum[...].astype(BF16)
        read_out[...] = dc_sum[...].astype(BF16)
        suffix_ref[...] = dot(sum_ref[...], lower(STRETCH), 0, 0, HIGHEST)[:heads, :]


def finish(place, x, g, write_map, read_map, rates, parts, first, other_decay, own, far):
    tokens, wide = x.shape
    heads = rates.shape[0]
    pieces = len(own)
    whole = lambda shape: pl.BlockSpec(shape, lambda c: (0, 0))
    strip = lambda rows: pl.BlockSpec((rows, LANES), lambda c: (0, c))
    return pl.pallas_call(
        lambda *refs: finish_kernel(heads, pieces, *refs),
        grid=(wide // LANES,),
        in_specs=[
            pl.BlockSpec(memory_space=pltpu.SMEM),
            strip(tokens),
            strip(tokens),
            whole((tokens, STATE)),
            whole((tokens, STATE)),
            whole((heads, tokens)),
            strip(tokens),
            whole((tokens, STATE)),
            whole((tokens, STATE)),
            whole((tokens, STATE)),
            strip(STATE),
            strip(1),
        ]
        + [strip(STATE // pieces)] * (2 * pieces),
        out_specs=[
            strip(tokens),
            whole((tokens, STATE)),
            whole((tokens, STATE)),
            whole((heads, tokens)),
        ],
        out_shape=[
            jax.ShapeDtypeStruct((tokens, wide), BF16),
            jax.ShapeDtypeStruct((tokens, STATE), BF16),
            jax.ShapeDtypeStruct((tokens, STATE), BF16),
            jax.ShapeDtypeStruct((heads, tokens), F32),
        ],
        scratch_shapes=[
            pltpu.VMEM((tokens, STATE), BF16),
            pltpu.VMEM((tokens, STATE), BF16),
            pltpu.VMEM((STATE, LANES), F32),
            pltpu.VMEM((STATE, LANES), F32),
            pltpu.VMEM((tokens, STATE), F32),
            pltpu.VMEM((tokens, STATE), F32),
            pltpu.VMEM((tokens, STATE), F32),
        ],
        compiler_params=pltpu.CompilerParams(vmem_limit_bytes=32 << 20),
        name="finish",
    )(place, x, g, write_map, read_map, rates, *parts, first, other_decay, *own, *far)


def chain_weights(logs, order, target):
    rank = order * jnp.arange(logs.shape[0])
    goal = order * target
    between = (rank[None, :] > rank[:, None]) & (rank[None, :] < goal)
    passed = jnp.sum(jnp.where(between[:, :, None], logs[None], 0.0), axis=1)
    return jnp.where((rank < goal)[:, None], jnp.exp(passed), 0.0)


def per_device(inputs, out_grad, input_map, output_map, log_decay):
    heads = log_decay.shape[0]
    head_size = inputs.shape[1] // heads
    groups, shards = lax.axis_size("grp"), lax.axis_size("seq")
    chips = shards // 2
    part = STATE // chips
    group, shard = lax.axis_index("grp"), lax.axis_index("seq")
    chip, core = shard // 2, shard % 2
    order = 2 * core - 1
    place = jnp.stack([core, chip]).astype(jnp.int32)
    everyone = [(a, z, c) for a in range(groups) for z in range(chips) for c in range(2)]

    def move(value, target):
        pairs = []
        for a, z, c in everyone:
            to = target(a, z, c)
            if to is not None:
                pairs.append((a * shards + 2 * z + c, to[0] * shards + 2 * to[1] + to[2]))
        return lax.ppermute(value, ("grp", "seq"), pairs)

    def widen(value):
        return jnp.repeat(value, head_size, axis=-1)

    send, keep, own_decay, totals = summary(place, inputs, out_grad, input_map, output_map, log_decay)
    every_log = lax.all_gather(totals[7:8, :heads], ("grp", "seq"), axis=0, tiled=True)
    parts = intra(inputs, out_grad, input_map, output_map, log_decay)

    first = move(send, lambda a, z, c: (a, z, 1 - c))
    chip_total = own_decay[7:8] * first + keep

    logs = every_log.reshape(groups, chips, 2, heads)
    chip_logs = jnp.sum(logs, axis=2)
    my_logs = lax.dynamic_index_in_dim(chip_logs, group, 0, keepdims=False)
    group_logs = jnp.sum(chip_logs, axis=1)

    def piece(index):
        return lax.dynamic_slice_in_dim(chip_total, index * part, part, 0)

    at = [piece(chip)] + [
        move(piece(chip ^ step), lambda a, z, c: (a, z ^ step, c)) for step in range(1, chips)
    ]

    def weighted(weights, values):
        total = None
        for step, value in enumerate(values):
            row = lax.dynamic_index_in_dim(weights, chip ^ step, 0, keepdims=True)
            total = value * row if total is None else total + value * row
        return total

    end = jnp.where(core == 1, chips, -1)
    group_total = weighted(widen(chain_weights(my_logs, order, end)), at)
    group_weights = widen(chain_weights(group_logs, order, group))
    incoming = jnp.zeros_like(group_total)
    for step in range(1, groups):

        def later(a, z, c):
            to = a + step if c == 1 else a - step
            return (to, z, c) if 0 <= to < groups else None

        got = move(group_total, later)
        source = jnp.clip(group - order * step, 0, groups - 1)
        valid = (group - order * step == source).astype(F32)
        row = lax.dynamic_index_in_dim(group_weights, source, 0, keepdims=True)
        incoming = incoming + got * (row * valid)

    def entering(step):
        target = chip ^ step
        rank = order * jnp.arange(chips)
        ahead = jnp.exp(
            jnp.sum(jnp.where((rank < order * target)[:, None], my_logs, 0.0), axis=0)
        )
        return widen(ahead)[None] * incoming + weighted(
            widen(chain_weights(my_logs, order, target)), at
        )

    own = [
        entering(step) if step == 0 else move(entering(step), lambda a, z, c: (a, z ^ step, c))
        for step in range(chips)
    ]
    far = [move(value, lambda a, z, c: (a, z, 1 - c)) for value in own]
    other_log = lax.dynamic_index_in_dim(
        every_log, group * shards + (shard ^ 1), 0, keepdims=True
    )
    grad_inputs, grad_write, grad_read, suffix = finish(
        place,
        inputs,
        out_grad,
        input_map,
        output_map,
        log_decay,
        parts,
        first,
        widen(jnp.exp(other_log)),
        own,
        far,
    )
    every_total = lax.all_gather(suffix[:, :1].T, ("grp", "seq"), axis=0, tiled=True)
    ranks = lax.broadcasted_iota(jnp.int32, every_total.shape, 0)
    later_sum = jnp.sum(jnp.where(ranks > group * shards + shard, every_total, 0.0), axis=0)
    return (grad_inputs, grad_write, grad_read, suffix + later_sum[:, None])


def solution(mesh):
    tokens = P(("grp", "seq"), None)
    in_specs = (tokens, tokens, tokens, tokens, P(None, ("grp", "seq")))
    out_specs = (tokens, tokens, tokens, P(None, ("grp", "seq")))
    return jax.shard_map(
        per_device, mesh=mesh, in_specs=in_specs, out_specs=out_specs, check_vma=False
    )
```

```python
import jax
import jax.numpy as jnp
from jax import lax
from jax.experimental import pallas as pl
from jax.experimental.pallas import tpu as pltpu
from jax.sharding import PartitionSpec as P

STATE = 128
STRETCH = 256
LANES = 512
STRIP = 128
META = 8
BIG_VMEM = 56 << 20
SMALL_VMEM = 24 << 20
F32 = jnp.float32
BF16 = jnp.bfloat16
HIGHEST = lax.Precision.HIGHEST


def dot(left, right, left_dim, right_dim, precision=None):
    return lax.dot_general(
        left,
        right,
        (((left_dim,), (right_dim,)), ((), ())),
        precision=precision,
        preferred_element_type=F32,
    )


def iota(shape, dim):
    return lax.broadcasted_iota(jnp.int32, shape, dim)


def lower(length):
    return (iota((length, length), 0) >= iota((length, length), 1)).astype(F32)


def thrice(rates):
    heads, length = rates.shape
    spare = jnp.zeros((STATE - 3 * heads, length), F32)
    return jnp.concatenate([rates, rates, rates, spare], axis=0)


def three_terms(value, heads):
    lane = iota(value.shape, 1)
    first = value.astype(BF16)
    rest = value - first.astype(F32)
    second = rest.astype(BF16)
    third = (rest - second.astype(F32)).astype(BF16)
    return jnp.where(lane < heads, first, jnp.where(lane < 2 * heads, second, third))


def spreader(chunk, heads, head_size, lanes):
    row = iota((STATE, lanes), 0)
    head = (iota((STATE, lanes), 1) + chunk * lanes) // head_size
    hit = (row == head) | (row == head + heads) | (row == head + 2 * heads)
    return hit.astype(F32).astype(BF16)


def head_adder(chunk, head_size, lanes):
    head = (iota((lanes, STATE), 0) + chunk * lanes) // head_size
    return (iota((lanes, STATE), 1) == head).astype(F32).astype(BF16)


def head_sums(value, adder):
    first = value.astype(BF16)
    second = (value - first.astype(F32)).astype(BF16)
    return dot(first, adder, 1, 0) + dot(second, adder, 1, 0)


def decay_terms(rates, heads):
    length = rates.shape[1]
    running = dot(lower(length), thrice(rates), 1, 1, HIGHEST)
    last = running[length - 1 : length, :]
    return (
        running,
        three_terms(jnp.exp(last - running), heads),
        three_terms(jnp.exp(running), heads),
    )


def term_pair(value):
    first = value.astype(BF16)
    return first, (value - first.astype(F32)).astype(BF16)


def spread_rows(rows, strips, head_size):
    per_strip = STRIP // head_size
    lane = iota((strips, STRIP), 1)
    row = iota((strips, STRIP), 0)
    picked = [jnp.where(lane // per_strip == row, value, 0.0) for value in rows]
    spread = lane_spread(per_strip, head_size)
    stacked = jnp.concatenate(picked, axis=0) if len(picked) > 1 else picked[0]
    wide = dot(stacked, spread, 1, 0, HIGHEST)
    return [wide[i * strips : (i + 1) * strips, :] for i in range(len(rows))]


def lane_spread(per_strip, head_size):
    head = iota((STRIP, STRIP), 0) % per_strip
    return (iota((STRIP, STRIP), 1) // head_size == head).astype(F32)


def whole(*shape):
    return pl.BlockSpec(shape, lambda *_: (0,) * len(shape))


def lanes_of(rows):
    return pl.BlockSpec((rows, LANES), lambda c: (0, c))


SCALARS = pl.BlockSpec(memory_space=pltpu.SMEM)


def summary_kernel(
    heads, chips, place, x_ref, g_ref, write_ref, read_ref, rates_ref,
    send_ref, keep_ref, decay_ref, tail_ref, lead_ref, write_t, read_t,
):
    chunk = pl.program_id(0)
    lanes = x_ref.shape[1]
    strips = lanes // STRIP
    all_strips = strips * pl.num_programs(0)
    head_size = lanes * pl.num_programs(0) // heads
    part = STATE // chips

    @pl.when(chunk == 0)
    def _():
        running, tail, lead = decay_terms(rates_ref[...], heads)
        tail_ref[...] = tail
        lead_ref[...] = lead
        send_ref[pl.ds(all_strips * STATE, META), :] = jnp.broadcast_to(
            running[STRETCH - 1 :, :], (META, STRIP)
        )
        write_t[...] = write_ref[...].astype(F32).T.astype(BF16)
        read_t[...] = read_ref[...].astype(F32).T.astype(BF16)

    spread = spreader(chunk, heads, head_size, lanes)
    tail = dot(tail_ref[...], spread, 1, 0)
    lead = dot(lead_ref[...], spread, 1, 0)
    inputs_tail = (x_ref[...].astype(F32) * tail).astype(BF16)
    grads_lead = (g_ref[...].astype(F32) * lead).astype(BF16)
    state = dot(write_t[...], inputs_tail, 1, 0)
    back = dot(read_t[...], grads_lead, 1, 0)
    first = place[0] == 0
    send = jnp.where(first, state, back)
    keep = jnp.where(first, back, state)
    for strip in range(strips):
        at = chunk * strips + strip
        wide = slice(strip * STRIP, (strip + 1) * STRIP)
        decay_ref[pl.ds(at, 1), :] = lead[STRETCH - 1 :, wide]
        for quarter in range(chips):
            rows = pl.ds(pl.multiple_of((quarter * all_strips + at) * part, part), part)
            mine = slice(quarter * part, (quarter + 1) * part)
            send_ref[rows, :] = send[mine, wide]
            keep_ref[rows, :] = keep[mine, wide]


def summary(chips, place, x, g, write_map, read_map, rates):
    tokens, wide = x.shape
    heads = rates.shape[0]
    strips = wide // STRIP
    return pl.pallas_call(
        lambda *refs: summary_kernel(heads, chips, *refs),
        grid=(wide // LANES,),
        in_specs=[
            SCALARS,
            lanes_of(tokens),
            lanes_of(tokens),
            whole(tokens, STATE),
            whole(tokens, STATE),
            whole(heads, tokens),
        ],
        out_specs=[
            whole(strips * STATE + META, STRIP),
            whole(strips * STATE, STRIP),
            whole(strips, STRIP),
        ],
        out_shape=[
            jax.ShapeDtypeStruct((strips * STATE + META, STRIP), F32),
            jax.ShapeDtypeStruct((strips * STATE, STRIP), F32),
            jax.ShapeDtypeStruct((strips, STRIP), F32),
        ],
        scratch_shapes=[
            pltpu.VMEM((tokens, STATE), BF16),
            pltpu.VMEM((tokens, STATE), BF16),
            pltpu.VMEM((STATE, tokens), BF16),
            pltpu.VMEM((STATE, tokens), BF16),
        ],
        compiler_params=pltpu.CompilerParams(vmem_limit_bytes=BIG_VMEM),
        name="summary",
    )(place, x, g, write_map, read_map, rates)


def combine_kernel(chips, place, first_ref, keep_ref, decay_ref, rates_ref, *out_refs):
    strips = decay_ref.shape[0]
    part = STATE // chips
    size = strips * part
    own_log = jnp.sum(rates_ref[...], axis=1, keepdims=True)
    heads = own_log.shape[0]
    lane = iota((heads, STRIP), 1)
    row = iota((heads, STRIP), 0)
    own_log = jnp.sum(jnp.where(lane == row, own_log, 0.0), axis=0, keepdims=True)
    meta = first_ref[pl.ds(chips * size, META), :]
    meta = jnp.where(iota((META, STRIP), 1) < heads, meta + own_log, 0.0)
    for step, out_ref in enumerate(out_refs):
        base = (place[1] ^ step) * size
        for strip in range(strips):
            rows = pl.ds(pl.multiple_of(base + strip * part, part), part)
            out_ref[strip * part : (strip + 1) * part, :] = (
                first_ref[rows, :] * decay_ref[strip : strip + 1, :] + keep_ref[rows, :]
            )
        out_ref[size:, :] = meta


def combine(chips, place, first, keep, decay, rates):
    strips = decay.shape[0]
    size = strips * (STATE // chips)
    return pl.pallas_call(
        lambda *refs: combine_kernel(chips, *refs),
        in_specs=[
            SCALARS,
            whole(*first.shape),
            whole(*keep.shape),
            whole(*decay.shape),
            whole(*rates.shape),
        ],
        out_specs=[whole(size + META, STRIP)] * chips,
        out_shape=[jax.ShapeDtypeStruct((size + META, STRIP), F32)] * chips,
        compiler_params=pltpu.CompilerParams(vmem_limit_bytes=SMALL_VMEM),
        name="combine",
    )(place, first, keep, decay, rates)


def rank_of(place, step):
    chip = place[1] ^ step
    return jnp.where(place[0] == 1, chip, -chip)


def masked_sum(terms):
    total = None
    for hit, value in terms:
        value = jnp.where(hit, value, 0.0)
        total = value if total is None else total + value
    return total


def total_kernel(strips, head_size, place, after_ref, *refs):
    at_refs, out_ref = refs[:-1], refs[-1]
    chips = len(at_refs)
    part = STATE // chips
    size = strips * part
    rank = [rank_of(place, step) for step in range(chips)]
    logs = [ref[size : size + 1, :] for ref in at_refs]
    weights = [
        jnp.exp(masked_sum([(rank[b] > rank[a], logs[b]) for b in range(chips)]))
        for a in range(chips)
    ]
    wide = spread_rows(weights, strips, head_size)
    for strip in range(strips):
        rows = slice(strip * part, (strip + 1) * part)
        total = at_refs[0][rows, :] * wide[0][strip : strip + 1, :]
        for a in range(1, chips):
            total = total + at_refs[a][rows, :] * wide[a][strip : strip + 1, :]
        out_ref[rows, :] = total
    out_ref[size:, :] = jnp.broadcast_to(sum(logs[1:], logs[0]), (META, STRIP))


def group_total(head_size, place, after, at):
    strips = (at[0].shape[0] - META) * len(at) // STATE
    return pl.pallas_call(
        lambda *refs: total_kernel(strips, head_size, *refs),
        in_specs=[SCALARS, whole(*after.shape)] + [whole(*at[0].shape)] * len(at),
        out_specs=whole(*at[0].shape),
        out_shape=jax.ShapeDtypeStruct(at[0].shape, F32),
        compiler_params=pltpu.CompilerParams(vmem_limit_bytes=SMALL_VMEM),
        name="group_total",
    )(place, after, *at)


def enter_kernel(chips, strips, head_size, place, *refs):
    at_refs, got_refs, out_refs = refs[:chips], refs[chips:-chips], refs[-chips:]
    part = STATE // chips
    size = strips * part
    rank = [rank_of(place, step) for step in range(chips)]
    logs = [ref[size : size + 1, :] for ref in at_refs]
    zero = jnp.zeros_like(logs[0])
    rows_of = []
    passed = zero
    for ref in got_refs:
        rows_of.append(jnp.exp(passed))
        passed = passed + ref[size : size + 1, :]
    for to in range(chips):
        rows_of.append(
            jnp.exp(masked_sum([(rank[m] < rank[to], logs[m]) for m in range(chips)]))
        )
    pairs = [(to, a) for to in range(chips) for a in range(chips) if a != to]
    for to, a in pairs:
        between = masked_sum(
            [((rank[m] > rank[a]) & (rank[m] < rank[to]), logs[m]) for m in range(chips)]
        )
        rows_of.append(jnp.where(rank[a] < rank[to], jnp.exp(between), 0.0))
    wide = spread_rows(rows_of, strips, head_size)
    groups_wide = wide[: len(got_refs)]
    ahead_wide = wide[len(got_refs) : len(got_refs) + chips]
    pair_wide = dict(zip(pairs, wide[len(got_refs) + chips :]))
    for strip in range(strips):
        rows = slice(strip * part, (strip + 1) * part)
        one = slice(strip, strip + 1)
        incoming = jnp.zeros((part, STRIP), F32)
        for ref, weight in zip(got_refs, groups_wide):
            incoming = incoming + ref[rows, :] * weight[one, :]
        values = [ref[rows, :] for ref in at_refs]
        for to in range(chips):
            entering = incoming * ahead_wide[to][one, :]
            for a in range(chips):
                if a != to:
                    entering = entering + values[a] * pair_wide[to, a][one, :]
            out_refs[to][rows, :] = entering


def enter(head_size, place, at, got):
    chips = len(at)
    strips = (at[0].shape[0] - META) * chips // STATE
    size = strips * (STATE // chips)
    return pl.pallas_call(
        lambda *refs: enter_kernel(chips, strips, head_size, *refs),
        in_specs=[SCALARS] + [whole(*at[0].shape)] * (chips + len(got)),
        out_specs=[whole(size, STRIP)] * chips,
        out_shape=[jax.ShapeDtypeStruct((size, STRIP), F32)] * chips,
        compiler_params=pltpu.CompilerParams(vmem_limit_bytes=SMALL_VMEM),
        name="enter",
    )(place, *at, *got)


def intra_kernel(
    heads, after_ref, x_ref, g_ref, write_ref, read_ref, rates_ref,
    dx_ref, db_ref, dc_ref, change_ref, state_ref, back_ref,
    column_ref, row_ref, scores_ref, mask_ref, pairs_ref, tail_ref, lead_ref, write_t, read_t,
):
    chunk = pl.program_id(0)
    lanes = x_ref.shape[1]
    head_size = lanes * pl.num_programs(0) // heads
    per_chunk = lanes // head_size

    @pl.when(chunk == 0)
    def _():
        rates = rates_ref[...]
        triangle = lower(STRETCH)
        running, tail, lead = decay_terms(rates, heads)
        column_ref[...] = running
        tail_ref[...] = tail
        lead_ref[...] = lead
        row_ref[...] = dot(rates, triangle, 1, 1, HIGHEST)
        mask_ref[...] = triangle
        scores_ref[...] = dot(read_ref[...], write_ref[...], 1, 1)
        pairs_ref[...] = jnp.zeros_like(pairs_ref)
        change_ref[...] = jnp.zeros_like(change_ref)
        write_t[...] = write_ref[...].astype(F32).T.astype(BF16)
        read_t[...] = read_ref[...].astype(F32).T.astype(BF16)

    columns = pltpu.roll(column_ref[...], STATE - chunk * per_chunk, 1)
    rows = row_ref[pl.ds(pl.multiple_of(chunk * per_chunk, per_chunk), per_chunk), :]
    causal = mask_ref[...] > 0.5
    scores = scores_ref[...]
    pairs = pairs_ref[...]
    low_half = iota((STRETCH, 2 * head_size), 1) < head_size
    adder = head_adder(chunk, head_size, lanes)
    spread = spreader(chunk, heads, head_size, lanes)
    high, low = term_pair(x_ref[...].astype(F32) * dot(tail_ref[...], spread, 1, 0))
    state_ref[...] = dot(write_t[...], high, 1, 0) + dot(write_t[...], low, 1, 0)
    high, low = term_pair(g_ref[...].astype(F32) * dot(lead_ref[...], spread, 1, 0))
    back_ref[...] = dot(read_t[...], high, 1, 0) + dot(read_t[...], low, 1, 0)
    for pair in range(per_chunk // 2):
        strip = slice(pair * 2 * head_size, (pair + 1) * 2 * head_size)
        x = x_ref[:, strip]
        g = g_ref[:, strip]
        ys, dxs = [], []
        for half in range(2):
            head = 2 * pair + half
            gap = columns[:, head : head + 1] - rows[head : head + 1, :]
            decay = jnp.where(causal, jnp.exp(gap), 0.0)
            mixing = (scores * decay).astype(BF16)
            ys.append(dot(mixing, x, 1, 0))
            dxs.append(dot(mixing, g, 0, 0))
            mine = low_half if half == 0 else jnp.logical_not(low_half)
            pairs = pairs + dot(jnp.where(mine, g, jnp.zeros_like(g)), x, 1, 1) * decay
        y = jnp.where(low_half, ys[0], ys[1])
        dx = jnp.where(low_half, dxs[0], dxs[1])
        dx_ref[:, strip] = dx
        change_ref[...] += head_sums(
            g.astype(F32) * y - x.astype(F32) * dx, adder[strip, :]
        )
    pairs_ref[...] = pairs

    @pl.when(chunk == pl.num_programs(0) - 1)
    def _():
        summed = pairs_ref[...].astype(BF16)
        db_ref[...] = dot(summed, read_ref[...], 0, 0)
        dc_ref[...] = dot(summed, write_ref[...], 1, 0)


def intra(after, x, g, write_map, read_map, rates):
    tokens, wide = x.shape
    heads = rates.shape[0]
    return pl.pallas_call(
        lambda *refs: intra_kernel(heads, *refs),
        grid=(wide // LANES,),
        in_specs=[
            whole(META, STRIP),
            lanes_of(tokens),
            lanes_of(tokens),
            whole(tokens, STATE),
            whole(tokens, STATE),
            whole(heads, tokens),
        ],
        out_specs=[lanes_of(tokens)] + [whole(tokens, STATE)] * 3 + [lanes_of(STATE)] * 2,
        out_shape=[
            jax.ShapeDtypeStruct((tokens, wide), F32),
            jax.ShapeDtypeStruct((tokens, STATE), F32),
            jax.ShapeDtypeStruct((tokens, STATE), F32),
            jax.ShapeDtypeStruct((tokens, STATE), F32),
            jax.ShapeDtypeStruct((STATE, wide), F32),
            jax.ShapeDtypeStruct((STATE, wide), F32),
        ],
        scratch_shapes=[
            pltpu.VMEM((tokens, STATE), F32),
            pltpu.VMEM((heads, tokens), F32),
            pltpu.VMEM((tokens, tokens), F32),
            pltpu.VMEM((tokens, tokens), F32),
            pltpu.VMEM((tokens, tokens), F32),
            pltpu.VMEM((tokens, STATE), BF16),
            pltpu.VMEM((tokens, STATE), BF16),
            pltpu.VMEM((STATE, tokens), BF16),
            pltpu.VMEM((STATE, tokens), BF16),
        ],
        compiler_params=pltpu.CompilerParams(vmem_limit_bytes=BIG_VMEM),
        cost_estimate=pl.CostEstimate(
            flops=12_000_000_000, bytes_accessed=8_000_000, transcendentals=heads * tokens * tokens
        ),
        name="intra",
    )(after, x, g, write_map, read_map, rates)


def assemble_kernel(
    heads, chips, place, first_log, state_own, back_own, *refs,
):
    first_refs, own_refs, far_refs = (refs[i * chips : (i + 1) * chips] for i in range(3))
    state_ref, back_ref, total_ref = refs[3 * chips :]
    chunk = pl.program_id(0)
    lanes = state_ref.shape[1]
    strips = lanes // STRIP
    head_size = lanes * pl.num_programs(0) // heads
    per_strip = STRIP // head_size
    part = STATE // chips

    @pl.when(chunk == 0)
    def _():
        total_ref[...] = jnp.zeros_like(total_ref)

    lane = iota((META, STRIP), 1)
    row = iota((META, STRIP), 0) + chunk * strips
    picked = jnp.where(lane // per_strip == row, jnp.exp(first_log[...]), 0.0)
    decay = dot(picked, lane_spread(per_strip, head_size), 1, 0, HIGHEST)
    is_first = place[0] == 0
    for step in range(chips):
        quarter = place[1] ^ step
        rows = pl.ds(pl.multiple_of(quarter * part, part), part)
        for strip in range(strips):
            wide = slice(strip * STRIP, (strip + 1) * STRIP)
            here = slice(strip * part, (strip + 1) * part)
            own = own_refs[step][here, :] * decay[strip : strip + 1, :]
            own = own + first_refs[step][here, :]
            far = far_refs[step][here, :]
            state_ref[rows, wide] = jnp.where(is_first, far, own).astype(BF16)
            back_ref[rows, wide] = jnp.where(is_first, own, far).astype(BF16)
    state = state_ref[...].astype(F32)
    back = back_ref[...].astype(F32)
    row_sum = jnp.sum(state * back_own[...] - back * state_own[...], axis=0, keepdims=True)
    total_ref[...] += head_sums(
        jnp.broadcast_to(row_sum, (META, lanes)), head_adder(chunk, head_size, lanes)
    )


def assemble(heads, chips, place, first, state_own, back_own, own, far):
    wide = state_own.shape[1]
    strips = wide // STRIP
    steps = wide // LANES
    part = STATE // chips
    block = LANES // STRIP * part
    meta_at = strips * STATE // META
    piece = pl.BlockSpec((block, STRIP), lambda c, place: (c, 0))
    lanes = pl.BlockSpec((STATE, LANES), lambda c, place: (0, c))

    def quarter(step):
        return pl.BlockSpec((block, STRIP), lambda c, place: ((place[1] ^ step) * steps + c, 0))

    return pl.pallas_call(
        lambda *refs: assemble_kernel(heads, chips, *refs),
        grid_spec=pltpu.PrefetchScalarGridSpec(
            num_scalar_prefetch=1,
            grid=(steps,),
            in_specs=[pl.BlockSpec((META, STRIP), lambda c, place: (meta_at, 0)), lanes, lanes]
            + [quarter(step) for step in range(chips)]
            + [piece] * (2 * chips),
            out_specs=[lanes, lanes, whole(META, STRIP)],
        ),
        out_shape=[
            jax.ShapeDtypeStruct((STATE, wide), BF16),
            jax.ShapeDtypeStruct((STATE, wide), BF16),
            jax.ShapeDtypeStruct((META, STRIP), F32),
        ],
        compiler_params=pltpu.CompilerParams(vmem_limit_bytes=BIG_VMEM),
        name="assemble",
    )(place, first, state_own, back_own, *([first] * chips), *own, *far)


def finish_kernel(
    heads, x_ref, g_ref, write_ref, read_ref, rates_ref,
    dx_ref, db_ref, dc_ref, change_ref, state_ref, back_ref,
    grad_ref, write_out, read_out, suffix_ref, tail_ref, lead_ref, sum_ref, db_sum, dc_sum,
):
    chunk = pl.program_id(0)
    lanes = x_ref.shape[1]
    head_size = lanes * pl.num_programs(0) // heads

    @pl.when(chunk == 0)
    def _():
        _, tail, lead = decay_terms(rates_ref[...], heads)
        tail_ref[...] = tail
        lead_ref[...] = lead
        sum_ref[...] = change_ref[...]
        db_sum[...] = db_ref[...]
        dc_sum[...] = dc_ref[...]

    state = state_ref[...]
    back = back_ref[...]
    spread = spreader(chunk, heads, head_size, lanes)
    tail = dot(tail_ref[...], spread, 1, 0)
    lead = dot(lead_ref[...], spread, 1, 0)
    x = x_ref[...].astype(F32)
    g = g_ref[...].astype(F32)
    y = dot(read_ref[...], state, 1, 0) * lead
    dx = dot(write_ref[...], back, 1, 0) * tail
    grad_ref[...] = (dx_ref[...] + dx).astype(BF16)
    sum_ref[...] += head_sums(g * y - x * dx, head_adder(chunk, head_size, lanes))
    db_sum[...] += dot((x * tail).astype(BF16), back, 1, 1)
    dc_sum[...] += dot((g * lead).astype(BF16), state, 1, 1)

    @pl.when(chunk == pl.num_programs(0) - 1)
    def _():
        write_out[...] = db_sum[...].astype(BF16)
        read_out[...] = dc_sum[...].astype(BF16)
        suffix_ref[...] = dot(sum_ref[...], lower(STRETCH), 0, 0, HIGHEST)[:heads, :]


def finish(x, g, write_map, read_map, rates, parts, state, back):
    tokens, wide = x.shape
    heads = rates.shape[0]
    return pl.pallas_call(
        lambda *refs: finish_kernel(heads, *refs),
        grid=(wide // LANES,),
        in_specs=[
            lanes_of(tokens),
            lanes_of(tokens),
            whole(tokens, STATE),
            whole(tokens, STATE),
            whole(heads, tokens),
            lanes_of(tokens),
            whole(tokens, STATE),
            whole(tokens, STATE),
            whole(tokens, STATE),
            lanes_of(STATE),
            lanes_of(STATE),
        ],
        out_specs=[
            lanes_of(tokens),
            whole(tokens, STATE),
            whole(tokens, STATE),
            whole(heads, tokens),
        ],
        out_shape=[
            jax.ShapeDtypeStruct((tokens, wide), BF16),
            jax.ShapeDtypeStruct((tokens, STATE), BF16),
            jax.ShapeDtypeStruct((tokens, STATE), BF16),
            jax.ShapeDtypeStruct((heads, tokens), F32),
        ],
        scratch_shapes=[
            pltpu.VMEM((tokens, STATE), BF16),
            pltpu.VMEM((tokens, STATE), BF16),
            pltpu.VMEM((tokens, STATE), F32),
            pltpu.VMEM((tokens, STATE), F32),
            pltpu.VMEM((tokens, STATE), F32),
        ],
        compiler_params=pltpu.CompilerParams(vmem_limit_bytes=BIG_VMEM),
        cost_estimate=pl.CostEstimate(
            flops=6_000_000_000, bytes_accessed=9_000_000, transcendentals=tokens * STATE * 2
        ),
        name="finish",
    )(x, g, write_map, read_map, rates, *parts, state, back)


def per_device(inputs, out_grad, input_map, output_map, log_decay):
    heads = log_decay.shape[0]
    head_size = inputs.shape[1] // heads
    groups, shards = lax.axis_size("grp"), lax.axis_size("seq")
    chips = shards // 2
    shard = lax.axis_index("seq")
    chip, core = shard // 2, shard % 2
    place = jnp.stack([core, chip]).astype(jnp.int32)
    everyone = [(a, z, c) for a in range(groups) for z in range(chips) for c in range(2)]

    def move(value, target):
        pairs = []
        for a, z, c in everyone:
            to = target(a, z, c)
            if to is not None:
                pairs.append((a * shards + 2 * z + c, to[0] * shards + 2 * to[1] + to[2]))
        return lax.ppermute(value, ("grp", "seq"), pairs)

    def to_core(value):
        return move(value, lambda a, z, c: (a, z, 1 - c))

    def to_chip(value, step):
        return move(value, lambda a, z, c: (a, z ^ step, c)) if step else value

    def to_group(value, step, ahead):
        def target(a, z, c):
            to = a + step if ahead(c) else a - step
            return (to, z, c) if 0 <= to < groups else None

        return move(value, target)

    send, keep, decay = summary(
        chips, place, inputs, out_grad, input_map, output_map, log_decay
    )
    first = to_core(send)
    at = combine(chips, place, first, keep, decay, log_decay)
    parts = intra(at[0][-META:], inputs, out_grad, input_map, output_map, log_decay)
    at = [to_chip(value, step) for step, value in enumerate(at)]
    total = group_total(head_size, place, parts[3][:META], at)
    got = [to_group(total, step, lambda c: c == 1) for step in range(1, groups)]
    own = [to_chip(value, step) for step, value in enumerate(enter(head_size, place, at, got))]
    far = [to_core(value) for value in own]
    state, back, tally = assemble(heads, chips, place, first, parts[4], parts[5], own, far)
    grad_inputs, grad_write, grad_read, suffix = finish(
        inputs, out_grad, input_map, output_map, log_decay, parts[:4], state, back
    )

    other = to_core(tally)
    later = jnp.where(core == 0, other, 0.0)
    tally = tally + other
    steps = [to_chip(tally, step) for step in range(1, chips)]
    for step, value in enumerate(steps, 1):
        later = later + jnp.where((chip ^ step) > chip, value, 0.0)
        tally = tally + value
    for step in range(1, groups):
        later = later + to_group(tally, step, lambda c: False)
    return (grad_inputs, grad_write, grad_read, suffix + later[0, :heads][:, None])


def solution(mesh):
    tokens = P(("grp", "seq"), None)
    in_specs = (tokens, tokens, tokens, tokens, P(None, ("grp", "seq")))
    out_specs = (tokens, tokens, tokens, P(None, ("grp", "seq")))
    return jax.shard_map(
        per_device, mesh=mesh, in_specs=in_specs, out_specs=out_specs, check_vma=False
    )
```

```python
import jax
import jax.numpy as jnp
from jax import lax
from jax.experimental import pallas as pl
from jax.experimental.pallas import tpu as pltpu
from jax.sharding import PartitionSpec as P

STATE = 128
STRETCH = 256
LANES = 512
HALVES = 2
STRIP = 128
META = 8
BIG_VMEM = 56 << 20
SMALL_VMEM = 24 << 20
F32 = jnp.float32
BF16 = jnp.bfloat16
HIGHEST = lax.Precision.HIGHEST


def dot(left, right, left_dim, right_dim, precision=None):
    return lax.dot_general(
        left,
        right,
        (((left_dim,), (right_dim,)), ((), ())),
        precision=precision,
        preferred_element_type=F32,
    )


def iota(shape, dim):
    return lax.broadcasted_iota(jnp.int32, shape, dim)


def lower(length):
    return (iota((length, length), 0) >= iota((length, length), 1)).astype(F32)


def thrice(rates):
    heads, length = rates.shape
    spare = jnp.zeros((STATE - 3 * heads, length), F32)
    return jnp.concatenate([rates, rates, rates, spare], axis=0)


def three_terms(value, heads):
    lane = iota(value.shape, 1)
    first = value.astype(BF16)
    rest = value - first.astype(F32)
    second = rest.astype(BF16)
    third = (rest - second.astype(F32)).astype(BF16)
    return jnp.where(lane < heads, first, jnp.where(lane < 2 * heads, second, third))


def spreader(chunk, heads, head_size, lanes):
    row = iota((STATE, lanes), 0)
    head = (iota((STATE, lanes), 1) + chunk * lanes) // head_size
    hit = (row == head) | (row == head + heads) | (row == head + 2 * heads)
    return hit.astype(F32).astype(BF16)


def head_adder(chunk, head_size, lanes):
    head = (iota((lanes, STATE), 0) + chunk * lanes) // head_size
    return (iota((lanes, STATE), 1) == head).astype(F32).astype(BF16)


def head_sums(value, adder):
    first = value.astype(BF16)
    second = (value - first.astype(F32)).astype(BF16)
    return dot(first, adder, 1, 0) + dot(second, adder, 1, 0)


def decay_terms(rates, heads):
    length = rates.shape[1]
    running = dot(lower(length), thrice(rates), 1, 1, HIGHEST)
    last = running[length - 1 : length, :]
    return (
        running,
        three_terms(jnp.exp(last - running), heads),
        three_terms(jnp.exp(running), heads),
    )


def term_pair(value):
    first = value.astype(BF16)
    return first, (value - first.astype(F32)).astype(BF16)


def lane_spread(per_strip, head_size):
    head = iota((STRIP, STRIP), 0) % per_strip
    return (iota((STRIP, STRIP), 1) // head_size == head).astype(F32)


def spread_rows(rows, offset, strips, head_size):
    per_strip = STRIP // head_size
    lane = iota((strips, STRIP), 1)
    row = iota((strips, STRIP), 0) + offset
    picked = [jnp.where(lane // per_strip == row, value, 0.0) for value in rows]
    stacked = jnp.concatenate(picked, axis=0) if len(picked) > 1 else picked[0]
    wide = dot(stacked, lane_spread(per_strip, head_size), 1, 0, HIGHEST)
    return [wide[i * strips : (i + 1) * strips, :] for i in range(len(rows))]


def whole(*shape):
    return pl.BlockSpec(shape, lambda *_: (0,) * len(shape))


def lanes_of(rows):
    return pl.BlockSpec((rows, LANES), lambda c: (0, c))


def half_lanes(rows, lanes, half, steps):
    return pl.BlockSpec((rows, lanes), lambda c: (0, half * steps + c))


SCALARS = pl.BlockSpec(memory_space=pltpu.SMEM)
STEPS = 2


def summary_kernel(heads, chips, half, place, x_ref, g_ref, write_ref, read_ref, *refs):
    chunk = pl.program_id(0)
    lanes = x_ref.shape[1]
    strips = lanes // STRIP
    half_strips = strips * STEPS
    head_size = lanes * STEPS * HALVES // heads
    part = STATE // chips
    if half == 0:
        rates_ref, send_ref, keep_ref, decay_ref, log_ref, run_ref, tail_ref, lead_ref = refs[:8]
    else:
        log_ref, tail_ref, lead_ref, send_ref, keep_ref, decay_ref = refs[:6]
    write_t, read_t = refs[-2:]

    @pl.when(chunk == 0)
    def _():
        if half == 0:
            running, tail, lead = decay_terms(rates_ref[...], heads)
            run_ref[...] = running
            tail_ref[...] = tail
            lead_ref[...] = lead
            log_ref[...] = jnp.broadcast_to(running[STRETCH - 1 :, :], (META, STRIP))
        send_ref[pl.ds(half_strips * STATE, META), :] = log_ref[...]
        write_t[...] = write_ref[...].astype(F32).T.astype(BF16)
        read_t[...] = read_ref[...].astype(F32).T.astype(BF16)

    spread = spreader(half * STEPS + chunk, heads, head_size, lanes)
    tail = dot(tail_ref[...], spread, 1, 0)
    lead = dot(lead_ref[...], spread, 1, 0)
    inputs_tail = (x_ref[...].astype(F32) * tail).astype(BF16)
    grads_lead = (g_ref[...].astype(F32) * lead).astype(BF16)
    state = dot(write_t[...], inputs_tail, 1, 0)
    back = dot(read_t[...], grads_lead, 1, 0)
    first = place[0] == 0
    send = jnp.where(first, state, back)
    keep = jnp.where(first, back, state)
    for strip in range(strips):
        at = chunk * strips + strip
        wide = slice(strip * STRIP, (strip + 1) * STRIP)
        decay_ref[pl.ds(at, 1), :] = lead[STRETCH - 1 :, wide]
        for quarter in range(chips):
            rows = pl.ds(pl.multiple_of((quarter * half_strips + at) * part, part), part)
            mine = slice(quarter * part, (quarter + 1) * part)
            send_ref[rows, :] = send[mine, wide]
            keep_ref[rows, :] = keep[mine, wide]


def summary(chips, half, place, x, g, write_map, read_map, rates, shared):
    tokens, wide = x.shape
    heads = rates.shape[0]
    lanes = wide // (STEPS * HALVES)
    strips = wide // STRIP // HALVES
    terms = [
        jax.ShapeDtypeStruct((META, STRIP), F32),
        jax.ShapeDtypeStruct((tokens, STRIP), F32),
        jax.ShapeDtypeStruct((tokens, STRIP), BF16),
        jax.ShapeDtypeStruct((tokens, STRIP), BF16),
    ]
    out_shape = [
        jax.ShapeDtypeStruct((strips * STATE + META, STRIP), F32),
        jax.ShapeDtypeStruct((strips * STATE, STRIP), F32),
        jax.ShapeDtypeStruct((strips, STRIP), F32),
    ]
    if half == 0:
        extra = [rates]
        out_shape = out_shape + terms
    else:
        extra = [shared[0], shared[2], shared[3]]
    return pl.pallas_call(
        lambda *refs: summary_kernel(heads, chips, half, *refs),
        grid=(STEPS,),
        in_specs=[
            SCALARS,
            half_lanes(tokens, lanes, half, STEPS),
            half_lanes(tokens, lanes, half, STEPS),
            whole(tokens, STATE),
            whole(tokens, STATE),
        ]
        + [whole(*value.shape) for value in extra],
        out_specs=[whole(*out.shape) for out in out_shape],
        out_shape=out_shape,
        scratch_shapes=[
            pltpu.VMEM((STATE, tokens), BF16),
            pltpu.VMEM((STATE, tokens), BF16),
        ],
        compiler_params=pltpu.CompilerParams(vmem_limit_bytes=BIG_VMEM),
        cost_estimate=pl.CostEstimate(
            flops=1_000_000_000, bytes_accessed=3_000_000, transcendentals=0
        ),
        name="summary",
    )(place, x, g, write_map, read_map, *extra)


def combine_kernel(chips, place, after, first_ref, keep_ref, decay_ref, log_ref, *out_refs):
    strips = decay_ref.shape[0]
    part = STATE // chips
    size = strips * part
    meta = first_ref[pl.ds(chips * size, META), :] + log_ref[...]
    for step, out_ref in enumerate(out_refs):
        base = (place[1] ^ step) * size
        for strip in range(strips):
            rows = pl.ds(pl.multiple_of(base + strip * part, part), part)
            out_ref[strip * part : (strip + 1) * part, :] = (
                first_ref[rows, :] * decay_ref[strip : strip + 1, :] + keep_ref[rows, :]
            )
        out_ref[size:, :] = meta


def combine(chips, place, after, first, keep, decay, log):
    strips = decay.shape[0]
    size = strips * (STATE // chips)
    return pl.pallas_call(
        lambda *refs: combine_kernel(chips, *refs),
        in_specs=[SCALARS]
        + [whole(*value.shape) for value in (after, first, keep, decay, log)],
        out_specs=[whole(size + META, STRIP)] * chips,
        out_shape=[jax.ShapeDtypeStruct((size + META, STRIP), F32)] * chips,
        compiler_params=pltpu.CompilerParams(vmem_limit_bytes=SMALL_VMEM),
        name="combine",
    )(place, after, first, keep, decay, log)


def rank_of(place, step):
    chip = place[1] ^ step
    return jnp.where(place[0] == 1, chip, -chip)


def masked_sum(terms):
    total = None
    for hit, value in terms:
        value = jnp.where(hit, value, 0.0)
        total = value if total is None else total + value
    return total


def total_kernel(offset, strips, head_size, place, after_ref, *refs):
    at_refs, out_ref = refs[:-1], refs[-1]
    chips = len(at_refs)
    part = STATE // chips
    size = strips * part
    rank = [rank_of(place, step) for step in range(chips)]
    logs = [ref[size : size + 1, :] for ref in at_refs]
    weights = [
        jnp.exp(masked_sum([(rank[b] > rank[a], logs[b]) for b in range(chips)]))
        for a in range(chips)
    ]
    wide = spread_rows(weights, offset, strips, head_size)
    for strip in range(strips):
        rows = slice(strip * part, (strip + 1) * part)
        total = at_refs[0][rows, :] * wide[0][strip : strip + 1, :]
        for a in range(1, chips):
            total = total + at_refs[a][rows, :] * wide[a][strip : strip + 1, :]
        out_ref[rows, :] = total
    out_ref[size:, :] = jnp.broadcast_to(sum(logs[1:], logs[0]), (META, STRIP))


def group_total(half, head_size, place, after, at):
    strips = (at[0].shape[0] - META) * len(at) // STATE
    return pl.pallas_call(
        lambda *refs: total_kernel(half * strips, strips, head_size, *refs),
        in_specs=[SCALARS, whole(*after.shape)] + [whole(*at[0].shape)] * len(at),
        out_specs=whole(*at[0].shape),
        out_shape=jax.ShapeDtypeStruct(at[0].shape, F32),
        compiler_params=pltpu.CompilerParams(vmem_limit_bytes=SMALL_VMEM),
        name="group_total",
    )(place, after, *at)


def enter_kernel(chips, offset, strips, head_size, place, *refs):
    at_refs, got_refs, out_refs = refs[:chips], refs[chips:-chips], refs[-chips:]
    part = STATE // chips
    size = strips * part
    rank = [rank_of(place, step) for step in range(chips)]
    logs = [ref[size : size + 1, :] for ref in at_refs]
    zero = jnp.zeros_like(logs[0])
    rows_of = []
    passed = zero
    for ref in got_refs:
        rows_of.append(jnp.exp(passed))
        passed = passed + ref[size : size + 1, :]
    for to in range(chips):
        rows_of.append(
            jnp.exp(masked_sum([(rank[m] < rank[to], logs[m]) for m in range(chips)]))
        )
    pairs = [(to, a) for to in range(chips) for a in range(chips) if a != to]
    for to, a in pairs:
        between = masked_sum(
            [((rank[m] > rank[a]) & (rank[m] < rank[to]), logs[m]) for m in range(chips)]
        )
        rows_of.append(jnp.where(rank[a] < rank[to], jnp.exp(between), 0.0))
    wide = spread_rows(rows_of, offset, strips, head_size)
    groups_wide = wide[: len(got_refs)]
    ahead_wide = wide[len(got_refs) : len(got_refs) + chips]
    pair_wide = dict(zip(pairs, wide[len(got_refs) + chips :]))
    for strip in range(strips):
        rows = slice(strip * part, (strip + 1) * part)
        one = slice(strip, strip + 1)
        incoming = jnp.zeros((part, STRIP), F32)
        for ref, weight in zip(got_refs, groups_wide):
            incoming = incoming + ref[rows, :] * weight[one, :]
        values = [ref[rows, :] for ref in at_refs]
        for to in range(chips):
            entering = incoming * ahead_wide[to][one, :]
            for a in range(chips):
                if a != to:
                    entering = entering + values[a] * pair_wide[to, a][one, :]
            out_refs[to][rows, :] = entering


def enter(half, head_size, place, at, got):
    chips = len(at)
    strips = (at[0].shape[0] - META) * chips // STATE
    size = strips * (STATE // chips)
    return pl.pallas_call(
        lambda *refs: enter_kernel(chips, half * strips, strips, head_size, *refs),
        in_specs=[SCALARS] + [whole(*at[0].shape)] * (chips + len(got)),
        out_specs=[whole(size, STRIP)] * chips,
        out_shape=[jax.ShapeDtypeStruct((size, STRIP), F32)] * chips,
        compiler_params=pltpu.CompilerParams(vmem_limit_bytes=SMALL_VMEM),
        name="enter",
    )(place, *at, *got)


def intra_kernel(
    heads, after_ref, x_ref, g_ref, write_ref, read_ref, rates_ref, column_ref, tail_ref, lead_ref,
    dx_ref, db_ref, dc_ref, change_ref, state_ref, back_ref,
    row_ref, scores_ref, mask_ref, pairs_ref, write_t, read_t,
):
    chunk = pl.program_id(0)
    lanes = x_ref.shape[1]
    head_size = lanes * pl.num_programs(0) // heads
    per_chunk = lanes // head_size

    @pl.when(chunk == 0)
    def _():
        rates = rates_ref[...]
        triangle = lower(STRETCH)
        row_ref[...] = dot(rates, triangle, 1, 1, HIGHEST)
        mask_ref[...] = triangle
        scores_ref[...] = dot(read_ref[...], write_ref[...], 1, 1)
        pairs_ref[...] = jnp.zeros_like(pairs_ref)
        change_ref[...] = jnp.zeros_like(change_ref)
        write_t[...] = write_ref[...].astype(F32).T.astype(BF16)
        read_t[...] = read_ref[...].astype(F32).T.astype(BF16)

    columns = pltpu.roll(column_ref[...], STATE - chunk * per_chunk, 1)
    rows = row_ref[pl.ds(pl.multiple_of(chunk * per_chunk, per_chunk), per_chunk), :]
    causal = mask_ref[...] > 0.5
    scores = scores_ref[...]
    pairs = pairs_ref[...]
    low_half = iota((STRETCH, 2 * head_size), 1) < head_size
    adder = head_adder(chunk, head_size, lanes)
    spread = spreader(chunk, heads, head_size, lanes)
    high, low = term_pair(x_ref[...].astype(F32) * dot(tail_ref[...], spread, 1, 0))
    state_ref[...] = dot(write_t[...], high, 1, 0) + dot(write_t[...], low, 1, 0)
    high, low = term_pair(g_ref[...].astype(F32) * dot(lead_ref[...], spread, 1, 0))
    back_ref[...] = dot(read_t[...], high, 1, 0) + dot(read_t[...], low, 1, 0)
    for pair in range(per_chunk // 2):
        strip = slice(pair * 2 * head_size, (pair + 1) * 2 * head_size)
        x = x_ref[:, strip]
        g = g_ref[:, strip]
        ys, dxs = [], []
        for half in range(2):
            head = 2 * pair + half
            gap = columns[:, head : head + 1] - rows[head : head + 1, :]
            decay = jnp.where(causal, jnp.exp(gap), 0.0)
            mixing = (scores * decay).astype(BF16)
            ys.append(dot(mixing, x, 1, 0))
            dxs.append(dot(mixing, g, 0, 0))
            mine = low_half if half == 0 else jnp.logical_not(low_half)
            pairs = pairs + dot(jnp.where(mine, g, jnp.zeros_like(g)), x, 1, 1) * decay
        y = jnp.where(low_half, ys[0], ys[1])
        dx = jnp.where(low_half, dxs[0], dxs[1])
        dx_ref[:, strip] = dx
        change_ref[...] += head_sums(
            g.astype(F32) * y - x.astype(F32) * dx, adder[strip, :]
        )
    pairs_ref[...] = pairs

    @pl.when(chunk == pl.num_programs(0) - 1)
    def _():
        summed = pairs_ref[...].astype(BF16)
        db_ref[...] = dot(summed, read_ref[...], 0, 0)
        dc_ref[...] = dot(summed, write_ref[...], 1, 0)


def intra(after, x, g, write_map, read_map, rates, shared):
    tokens, wide = x.shape
    heads = rates.shape[0]
    return pl.pallas_call(
        lambda *refs: intra_kernel(heads, *refs),
        grid=(wide // LANES,),
        in_specs=[
            whole(META, STRIP),
            lanes_of(tokens),
            lanes_of(tokens),
            whole(tokens, STATE),
            whole(tokens, STATE),
            whole(heads, tokens),
        ]
        + [whole(tokens, STRIP)] * 3,
        out_specs=[lanes_of(tokens)] + [whole(tokens, STATE)] * 3 + [lanes_of(STATE)] * 2,
        out_shape=[
            jax.ShapeDtypeStruct((tokens, wide), F32),
            jax.ShapeDtypeStruct((tokens, STATE), F32),
            jax.ShapeDtypeStruct((tokens, STATE), F32),
            jax.ShapeDtypeStruct((tokens, STATE), F32),
            jax.ShapeDtypeStruct((STATE, wide), F32),
            jax.ShapeDtypeStruct((STATE, wide), F32),
        ],
        scratch_shapes=[
            pltpu.VMEM((heads, tokens), F32),
            pltpu.VMEM((tokens, tokens), F32),
            pltpu.VMEM((tokens, tokens), F32),
            pltpu.VMEM((tokens, tokens), F32),
            pltpu.VMEM((STATE, tokens), BF16),
            pltpu.VMEM((STATE, tokens), BF16),
        ],
        compiler_params=pltpu.CompilerParams(vmem_limit_bytes=BIG_VMEM),
        cost_estimate=pl.CostEstimate(
            flops=12_000_000_000, bytes_accessed=8_000_000, transcendentals=heads * tokens * tokens
        ),
        name="intra",
    )(after, x, g, write_map, read_map, rates, *shared[1:])


def assemble_kernel(
    heads, chips, half, head_size, place, after, first_ref, state_own, back_own, *refs,
):
    own_refs, far_refs = refs[:chips], refs[chips : 2 * chips]
    state_ref, back_ref, total_ref = refs[2 * chips :]
    lanes = state_ref.shape[1]
    strips = lanes // STRIP
    part = STATE // chips
    size = strips * part
    log = first_ref[chips * size : chips * size + 1, :]
    decay = spread_rows([jnp.exp(log)], half * strips, strips, head_size)[0]
    is_first = place[0] == 0
    sums = [None] * strips
    for step in range(chips):
        quarter = place[1] ^ step
        rows = pl.ds(pl.multiple_of(quarter * part, part), part)
        for strip in range(strips):
            wide = slice(strip * STRIP, (strip + 1) * STRIP)
            here = slice(strip * part, (strip + 1) * part)
            there = pl.ds(pl.multiple_of(quarter * size + strip * part, part), part)
            own = own_refs[step][here, :] * decay[strip : strip + 1, :] + first_ref[there, :]
            far = far_refs[step][here, :]
            state = jnp.where(is_first, far, own).astype(BF16)
            back = jnp.where(is_first, own, far).astype(BF16)
            state_ref[rows, wide] = state
            back_ref[rows, wide] = back
            gain = state.astype(F32) * back_own[rows, wide]
            gain = gain - back.astype(F32) * state_own[rows, wide]
            sums[strip] = gain if sums[strip] is None else sums[strip] + gain
    row_sum = [
        jnp.broadcast_to(jnp.sum(value, axis=0, keepdims=True), (META, STRIP)) for value in sums
    ]
    total_ref[...] = head_sums(
        jnp.concatenate(row_sum, axis=1), head_adder(half, head_size, lanes)
    )


def assemble(heads, half, place, after, first, state_own, back_own, own, far):
    chips = len(own)
    wide = state_own.shape[1]
    lanes = wide // HALVES
    mine = pl.BlockSpec((STATE, lanes), lambda c: (0, half))
    return pl.pallas_call(
        lambda *refs: assemble_kernel(heads, chips, half, wide // heads, *refs),
        grid=(1,),
        in_specs=[SCALARS, whole(*after.shape), whole(*first.shape), mine, mine]
        + [whole(*value.shape) for value in (*own, *far)],
        out_specs=[whole(STATE, lanes), whole(STATE, lanes), whole(META, STRIP)],
        out_shape=[
            jax.ShapeDtypeStruct((STATE, lanes), BF16),
            jax.ShapeDtypeStruct((STATE, lanes), BF16),
            jax.ShapeDtypeStruct((META, STRIP), F32),
        ],
        compiler_params=pltpu.CompilerParams(vmem_limit_bytes=SMALL_VMEM),
        name="assemble",
    )(place, after, first, state_own, back_own, *own, *far)


def finish_kernel(
    heads, half, x_ref, g_ref, write_ref, read_ref, tail_ref, lead_ref,
    dx_ref, db_ref, dc_ref, change_ref, state_ref, back_ref, *refs,
):
    grad_ref, db_out, dc_out, sum_out, db_sum, dc_sum = refs[-6:]
    chunk = pl.program_id(0)
    lanes = x_ref.shape[1]
    head_size = lanes * STEPS * HALVES // heads

    @pl.when(chunk == 0)
    def _():
        sum_out[...] = change_ref[...]
        db_sum[...] = db_ref[...]
        dc_sum[...] = dc_ref[...]

    state = state_ref[...]
    back = back_ref[...]
    spread = spreader(half * STEPS + chunk, heads, head_size, lanes)
    tail = dot(tail_ref[...], spread, 1, 0)
    lead = dot(lead_ref[...], spread, 1, 0)
    x = x_ref[...].astype(F32)
    g = g_ref[...].astype(F32)
    y = dot(read_ref[...], state, 1, 0) * lead
    dx = dot(write_ref[...], back, 1, 0) * tail
    grad_ref[...] = (dx_ref[...] + dx).astype(BF16)
    adder = head_adder(half * STEPS + chunk, head_size, lanes)
    sum_out[...] += head_sums(g * y - x * dx, adder)
    db_sum[...] += dot((x * tail).astype(BF16), back, 1, 1)
    dc_sum[...] += dot((g * lead).astype(BF16), state, 1, 1)

    @pl.when(chunk == STEPS - 1)
    def _():
        db_out[...] = db_sum[...].astype(db_out.dtype)
        dc_out[...] = dc_sum[...].astype(dc_out.dtype)


def finish(heads, half, x, g, write_map, read_map, shared, dx, sums, state, back, grad):
    tokens, wide = x.shape
    lanes = wide // (STEPS * HALVES)
    strip = half_lanes(tokens, lanes, half, STEPS)
    own = pl.BlockSpec((STATE, lanes), lambda c: (0, c))
    kind = BF16 if half == HALVES - 1 else F32
    earlier = [] if grad is None else [grad]
    return pl.pallas_call(
        lambda *refs: finish_kernel(heads, half, *refs),
        grid=(STEPS,),
        in_specs=[strip, strip]
        + [whole(tokens, STATE)] * 4
        + [strip]
        + [whole(tokens, STATE)] * 3
        + [own, own]
        + [pl.BlockSpec(memory_space=pl.ANY)] * len(earlier),
        out_specs=[strip] + [whole(tokens, STATE)] * 3,
        out_shape=[
            jax.ShapeDtypeStruct((tokens, wide), BF16),
            jax.ShapeDtypeStruct((tokens, STATE), kind),
            jax.ShapeDtypeStruct((tokens, STATE), kind),
            jax.ShapeDtypeStruct((tokens, STATE), F32),
        ],
        scratch_shapes=[pltpu.VMEM((tokens, STATE), F32)] * 2,
        input_output_aliases={12: 0} if earlier else {},
        compiler_params=pltpu.CompilerParams(vmem_limit_bytes=BIG_VMEM),
        cost_estimate=pl.CostEstimate(
            flops=3_000_000_000, bytes_accessed=5_000_000, transcendentals=0
        ),
        name="finish",
    )(x, g, write_map, read_map, *shared[2:], dx, *sums, state, back, *earlier)


def suffix_kernel(change_ref, later_ref, out_ref):
    heads = out_ref.shape[0]
    last = iota((STRETCH, STATE), 0) == STRETCH - 1
    change = change_ref[...] + jnp.where(last, later_ref[0:1, :], 0.0)
    out_ref[...] = dot(change, lower(STRETCH), 0, 0, HIGHEST)[:heads, :]


def suffix(heads, change, later):
    return pl.pallas_call(
        suffix_kernel,
        in_specs=[whole(*change.shape), whole(*later.shape)],
        out_specs=whole(heads, STRETCH),
        out_shape=jax.ShapeDtypeStruct((heads, STRETCH), F32),
        name="suffix",
    )(change, later)


def per_device(inputs, out_grad, input_map, output_map, log_decay):
    heads = log_decay.shape[0]
    head_size = inputs.shape[1] // heads
    groups, shards = lax.axis_size("grp"), lax.axis_size("seq")
    chips = shards // 2
    shard = lax.axis_index("seq")
    chip, core = shard // 2, shard % 2
    place = jnp.stack([core, chip]).astype(jnp.int32)
    everyone = [(a, z, c) for a in range(groups) for z in range(chips) for c in range(2)]

    def move(value, target):
        pairs = []
        for a, z, c in everyone:
            to = target(a, z, c)
            if to is not None:
                pairs.append((a * shards + 2 * z + c, to[0] * shards + 2 * to[1] + to[2]))
        return lax.ppermute(value, ("grp", "seq"), pairs)

    def to_core(value):
        return move(value, lambda a, z, c: (a, z, 1 - c))

    def to_chip(value, step):
        return move(value, lambda a, z, c: (a, z ^ step, c)) if step else value

    def to_group(value, step, ahead):
        def target(a, z, c):
            to = a + step if ahead(c) else a - step
            return (to, z, c) if 0 <= to < groups else None

        return move(value, target)

    def scan_half(half, after, at):
        at = [to_chip(value, step) for step, value in enumerate(at)]
        total = group_total(half, head_size, place, after, at)
        got = [to_group(total, step, lambda c: c == 1) for step in range(1, groups)]
        inside = enter(half, head_size, place, at, got)
        own = [to_chip(value, step) for step, value in enumerate(inside)]
        return own, [to_core(value) for value in own]

    def later_total(tally):
        other = to_core(tally)
        later = jnp.where(core == 0, other, 0.0)
        tally = tally + other
        steps = [to_chip(tally, step) for step in range(1, chips)]
        for step, value in enumerate(steps, 1):
            later = later + jnp.where((chip ^ step) > chip, value, 0.0)
            tally = tally + value
        for step in range(1, groups):
            later = later + to_group(tally, step, lambda c: False)
        return later

    maps = (inputs, out_grad, input_map, output_map)
    send, keep, decay, *shared = summary(chips, 0, place, *maps, log_decay, None)
    first = [to_core(send)]
    pieces = [combine(chips, place, shared[0], first[0], keep, decay, shared[0])]
    send, keep, decay = summary(chips, 1, place, *maps, log_decay, shared)
    first.append(to_core(send))
    dx, db, dc, change, state_own, back_own = intra(
        pieces[0][0][-META:], *maps, log_decay, shared
    )
    token = change[:META]
    pieces.append(combine(chips, place, token, first[1], keep, decay, shared[0]))
    sums, grad, later = (db, dc, change), None, None
    for half in range(HALVES):
        own, far = scan_half(half, token, pieces[half])
        state, back, tally = assemble(
            heads, half, place, sums[2][:META], first[half], state_own, back_own, own, far
        )
        grad, *sums = finish(heads, half, *maps, shared, dx, sums, state, back, grad)
        found = later_total(tally)
        later = found if later is None else later + found
    return (grad, sums[0], sums[1], suffix(heads, sums[2], later))


def solution(mesh):
    tokens = P(("grp", "seq"), None)
    in_specs = (tokens, tokens, tokens, tokens, P(None, ("grp", "seq")))
    out_specs = (tokens, tokens, tokens, P(None, ("grp", "seq")))
    return jax.shard_map(
        per_device, mesh=mesh, in_specs=in_specs, out_specs=out_specs, check_vma=False
    )
```

```python
import jax
import jax.numpy as jnp
from jax import lax
from jax.experimental import pallas as pl
from jax.experimental.pallas import tpu as pltpu
from jax.sharding import PartitionSpec as P

STATE = 128
STRETCH = 256
LANES = 512
HALVES = 2
STRIP = 128
META = 8
BIG_VMEM = 56 << 20
SMALL_VMEM = 24 << 20
F32 = jnp.float32
BF16 = jnp.bfloat16
HIGHEST = lax.Precision.HIGHEST


def dot(left, right, left_dim, right_dim, precision=None):
    return lax.dot_general(
        left,
        right,
        (((left_dim,), (right_dim,)), ((), ())),
        precision=precision,
        preferred_element_type=F32,
    )


def iota(shape, dim):
    return lax.broadcasted_iota(jnp.int32, shape, dim)


def lower(length):
    return (iota((length, length), 0) >= iota((length, length), 1)).astype(F32)


def thrice(rates):
    heads, length = rates.shape
    spare = jnp.zeros((STATE - 3 * heads, length), F32)
    return jnp.concatenate([rates, rates, rates, spare], axis=0)


def three_terms(value, heads):
    lane = iota(value.shape, 1)
    first = value.astype(BF16)
    rest = value - first.astype(F32)
    second = rest.astype(BF16)
    third = (rest - second.astype(F32)).astype(BF16)
    return jnp.where(lane < heads, first, jnp.where(lane < 2 * heads, second, third))


def spreader(chunk, heads, head_size, lanes):
    row = iota((STATE, lanes), 0)
    head = (iota((STATE, lanes), 1) + chunk * lanes) // head_size
    hit = (row == head) | (row == head + heads) | (row == head + 2 * heads)
    return hit.astype(F32).astype(BF16)


def head_adder(chunk, head_size, lanes):
    head = (iota((lanes, STATE), 0) + chunk * lanes) // head_size
    return (iota((lanes, STATE), 1) == head).astype(F32).astype(BF16)


def head_sums(value, adder):
    first = value.astype(BF16)
    second = (value - first.astype(F32)).astype(BF16)
    return dot(first, adder, 1, 0) + dot(second, adder, 1, 0)


def decay_terms(rates, heads):
    length = rates.shape[1]
    running = dot(lower(length), thrice(rates), 1, 1, HIGHEST)
    last = running[length - 1 : length, :]
    return (
        running,
        three_terms(jnp.exp(last - running), heads),
        three_terms(jnp.exp(running), heads),
    )


def term_pair(value):
    first = value.astype(BF16)
    return first, (value - first.astype(F32)).astype(BF16)


def lane_spread(per_strip, head_size):
    head = iota((STRIP, STRIP), 0) % per_strip
    return (iota((STRIP, STRIP), 1) // head_size == head).astype(F32)


def spread_rows(rows, offset, strips, head_size):
    per_strip = STRIP // head_size
    lane = iota((strips, STRIP), 1)
    row = iota((strips, STRIP), 0) + offset
    picked = [jnp.where(lane // per_strip == row, value, 0.0) for value in rows]
    stacked = jnp.concatenate(picked, axis=0) if len(picked) > 1 else picked[0]
    wide = dot(stacked, lane_spread(per_strip, head_size), 1, 0, HIGHEST)
    return [wide[i * strips : (i + 1) * strips, :] for i in range(len(rows))]


def whole(*shape):
    return pl.BlockSpec(shape, lambda *_: (0,) * len(shape))


def lanes_of(rows):
    return pl.BlockSpec((rows, LANES), lambda c: (0, c))


def half_lanes(rows, lanes, half, steps):
    return pl.BlockSpec((rows, lanes), lambda c: (0, half * steps + c))


SCALARS = pl.BlockSpec(memory_space=pltpu.SMEM)
STEPS = 2


def summary_kernel(heads, chips, half, place, x_ref, g_ref, write_ref, read_ref, *refs):
    chunk = pl.program_id(0)
    lanes = x_ref.shape[1]
    strips = lanes // STRIP
    half_strips = strips * STEPS
    head_size = lanes * STEPS * HALVES // heads
    part = STATE // chips
    if half == 0:
        rates_ref, send_ref, keep_ref, decay_ref, log_ref, run_ref, tail_ref, lead_ref = refs[:8]
    else:
        log_ref, tail_ref, lead_ref, send_ref, keep_ref, decay_ref = refs[:6]
    write_t, read_t = refs[-2:]

    @pl.when(chunk == 0)
    def _():
        if half == 0:
            running, tail, lead = decay_terms(rates_ref[...], heads)
            run_ref[...] = running
            tail_ref[...] = tail
            lead_ref[...] = lead
            log_ref[...] = jnp.broadcast_to(running[STRETCH - 1 :, :], (META, STRIP))
        send_ref[pl.ds(half_strips * STATE, META), :] = log_ref[...]
        write_t[...] = write_ref[...].astype(F32).T.astype(BF16)
        read_t[...] = read_ref[...].astype(F32).T.astype(BF16)

    spread = spreader(half * STEPS + chunk, heads, head_size, lanes)
    tail = dot(tail_ref[...], spread, 1, 0)
    lead = dot(lead_ref[...], spread, 1, 0)
    inputs_tail = (x_ref[...].astype(F32) * tail).astype(BF16)
    grads_lead = (g_ref[...].astype(F32) * lead).astype(BF16)
    state = dot(write_t[...], inputs_tail, 1, 0)
    back = dot(read_t[...], grads_lead, 1, 0)
    first = place[0] == 0
    send = jnp.where(first, state, back)
    keep = jnp.where(first, back, state)
    for strip in range(strips):
        at = chunk * strips + strip
        wide = slice(strip * STRIP, (strip + 1) * STRIP)
        decay_ref[pl.ds(at, 1), :] = lead[STRETCH - 1 :, wide]
        for quarter in range(chips):
            rows = pl.ds(pl.multiple_of((quarter * half_strips + at) * part, part), part)
            mine = slice(quarter * part, (quarter + 1) * part)
            send_ref[rows, :] = send[mine, wide]
            keep_ref[rows, :] = keep[mine, wide]


def summary(chips, half, place, x, g, write_map, read_map, rates, shared):
    tokens, wide = x.shape
    heads = rates.shape[0]
    lanes = wide // (STEPS * HALVES)
    strips = wide // STRIP // HALVES
    terms = [
        jax.ShapeDtypeStruct((META, STRIP), F32),
        jax.ShapeDtypeStruct((tokens, STRIP), F32),
        jax.ShapeDtypeStruct((tokens, STRIP), BF16),
        jax.ShapeDtypeStruct((tokens, STRIP), BF16),
    ]
    out_shape = [
        jax.ShapeDtypeStruct((strips * STATE + META, STRIP), F32),
        jax.ShapeDtypeStruct((strips * STATE, STRIP), F32),
        jax.ShapeDtypeStruct((strips, STRIP), F32),
    ]
    if half == 0:
        extra = [rates]
        out_shape = out_shape + terms
    else:
        extra = [shared[0], shared[2], shared[3]]
    return pl.pallas_call(
        lambda *refs: summary_kernel(heads, chips, half, *refs),
        grid=(STEPS,),
        in_specs=[
            SCALARS,
            half_lanes(tokens, lanes, half, STEPS),
            half_lanes(tokens, lanes, half, STEPS),
            whole(tokens, STATE),
            whole(tokens, STATE),
        ]
        + [whole(*value.shape) for value in extra],
        out_specs=[whole(*out.shape) for out in out_shape],
        out_shape=out_shape,
        scratch_shapes=[
            pltpu.VMEM((STATE, tokens), BF16),
            pltpu.VMEM((STATE, tokens), BF16),
        ],
        compiler_params=pltpu.CompilerParams(vmem_limit_bytes=BIG_VMEM),
        cost_estimate=pl.CostEstimate(
            flops=1_000_000_000, bytes_accessed=3_000_000, transcendentals=0
        ),
        name="summary",
    )(place, x, g, write_map, read_map, *extra)


def combine_kernel(chips, place, after, first_ref, keep_ref, decay_ref, log_ref, *out_refs):
    strips = decay_ref.shape[0]
    part = STATE // chips
    size = strips * part
    meta = first_ref[pl.ds(chips * size, META), :] + log_ref[...]
    for step, out_ref in enumerate(out_refs):
        base = (place[1] ^ step) * size
        for strip in range(strips):
            rows = pl.ds(pl.multiple_of(base + strip * part, part), part)
            out_ref[strip * part : (strip + 1) * part, :] = (
                first_ref[rows, :] * decay_ref[strip : strip + 1, :] + keep_ref[rows, :]
            )
        out_ref[size:, :] = meta


def combine(chips, place, after, first, keep, decay, log):
    strips = decay.shape[0]
    size = strips * (STATE // chips)
    return pl.pallas_call(
        lambda *refs: combine_kernel(chips, *refs),
        grid=(1,),
        in_specs=[SCALARS]
        + [whole(META, STRIP)]
        + [whole(*value.shape) for value in (first, keep, decay, log)],
        out_specs=[whole(size + META, STRIP)] * chips,
        out_shape=[jax.ShapeDtypeStruct((size + META, STRIP), F32)] * chips,
        compiler_params=pltpu.CompilerParams(vmem_limit_bytes=SMALL_VMEM),
        name="combine",
    )(place, after, first, keep, decay, log)


def rank_of(place, step):
    chip = place[1] ^ step
    return jnp.where(place[0] == 1, chip, -chip)


def masked_sum(terms):
    total = None
    for hit, value in terms:
        value = jnp.where(hit, value, 0.0)
        total = value if total is None else total + value
    return total


def total_kernel(offset, strips, head_size, place, after_ref, *refs):
    at_refs, out_ref = refs[:-1], refs[-1]
    chips = len(at_refs)
    part = STATE // chips
    size = strips * part
    rank = [rank_of(place, step) for step in range(chips)]
    logs = [ref[size : size + 1, :] for ref in at_refs]
    weights = [
        jnp.exp(masked_sum([(rank[b] > rank[a], logs[b]) for b in range(chips)]))
        for a in range(chips)
    ]
    wide = spread_rows(weights, offset, strips, head_size)
    for strip in range(strips):
        rows = slice(strip * part, (strip + 1) * part)
        total = at_refs[0][rows, :] * wide[0][strip : strip + 1, :]
        for a in range(1, chips):
            total = total + at_refs[a][rows, :] * wide[a][strip : strip + 1, :]
        out_ref[rows, :] = total
    out_ref[size:, :] = jnp.broadcast_to(sum(logs[1:], logs[0]), (META, STRIP))


def group_total(half, head_size, place, after, at):
    strips = (at[0].shape[0] - META) * len(at) // STATE
    return pl.pallas_call(
        lambda *refs: total_kernel(half * strips, strips, head_size, *refs),
        grid=(1,),
        in_specs=[SCALARS, whole(META, STRIP)] + [whole(*at[0].shape)] * len(at),
        out_specs=whole(*at[0].shape),
        out_shape=jax.ShapeDtypeStruct(at[0].shape, F32),
        compiler_params=pltpu.CompilerParams(vmem_limit_bytes=SMALL_VMEM),
        name="group_total",
    )(place, after, *at)


def enter_kernel(chips, offset, strips, head_size, place, *refs):
    at_refs, got_refs, out_refs = refs[:chips], refs[chips:-chips], refs[-chips:]
    part = STATE // chips
    size = strips * part
    rank = [rank_of(place, step) for step in range(chips)]
    logs = [ref[size : size + 1, :] for ref in at_refs]
    zero = jnp.zeros_like(logs[0])
    rows_of = []
    passed = zero
    for ref in got_refs:
        rows_of.append(jnp.exp(passed))
        passed = passed + ref[size : size + 1, :]
    for to in range(chips):
        rows_of.append(
            jnp.exp(masked_sum([(rank[m] < rank[to], logs[m]) for m in range(chips)]))
        )
    pairs = [(to, a) for to in range(chips) for a in range(chips) if a != to]
    for to, a in pairs:
        between = masked_sum(
            [((rank[m] > rank[a]) & (rank[m] < rank[to]), logs[m]) for m in range(chips)]
        )
        rows_of.append(jnp.where(rank[a] < rank[to], jnp.exp(between), 0.0))
    wide = spread_rows(rows_of, offset, strips, head_size)
    groups_wide = wide[: len(got_refs)]
    ahead_wide = wide[len(got_refs) : len(got_refs) + chips]
    pair_wide = dict(zip(pairs, wide[len(got_refs) + chips :]))
    for strip in range(strips):
        rows = slice(strip * part, (strip + 1) * part)
        one = slice(strip, strip + 1)
        incoming = jnp.zeros((part, STRIP), F32)
        for ref, weight in zip(got_refs, groups_wide):
            incoming = incoming + ref[rows, :] * weight[one, :]
        values = [ref[rows, :] for ref in at_refs]
        for to in range(chips):
            entering = incoming * ahead_wide[to][one, :]
            for a in range(chips):
                if a != to:
                    entering = entering + values[a] * pair_wide[to, a][one, :]
            out_refs[to][rows, :] = entering


def enter(half, head_size, place, at, got):
    chips = len(at)
    strips = (at[0].shape[0] - META) * chips // STATE
    size = strips * (STATE // chips)
    return pl.pallas_call(
        lambda *refs: enter_kernel(chips, half * strips, strips, head_size, *refs),
        in_specs=[SCALARS] + [whole(*at[0].shape)] * (chips + len(got)),
        out_specs=[whole(size, STRIP)] * chips,
        out_shape=[jax.ShapeDtypeStruct((size, STRIP), F32)] * chips,
        compiler_params=pltpu.CompilerParams(vmem_limit_bytes=SMALL_VMEM),
        name="enter",
    )(place, *at, *got)


def intra_kernel(
    heads, after_ref, x_ref, g_ref, write_ref, read_ref, rates_ref, column_ref, tail_ref, lead_ref,
    dx_ref, db_ref, dc_ref, change_ref, state_ref, back_ref,
    row_ref, scores_ref, mask_ref, pairs_ref, write_t, read_t,
):
    chunk = pl.program_id(0)
    lanes = x_ref.shape[1]
    head_size = lanes * pl.num_programs(0) // heads
    per_chunk = lanes // head_size

    @pl.when(chunk == 0)
    def _():
        rates = rates_ref[...]
        triangle = lower(STRETCH)
        row_ref[...] = dot(rates, triangle, 1, 1, HIGHEST)
        mask_ref[...] = triangle
        scores_ref[...] = dot(read_ref[...], write_ref[...], 1, 1)
        pairs_ref[...] = jnp.zeros_like(pairs_ref)
        change_ref[...] = jnp.zeros_like(change_ref)
        write_t[...] = write_ref[...].astype(F32).T.astype(BF16)
        read_t[...] = read_ref[...].astype(F32).T.astype(BF16)

    columns = pltpu.roll(column_ref[...], STATE - chunk * per_chunk, 1)
    rows = row_ref[pl.ds(pl.multiple_of(chunk * per_chunk, per_chunk), per_chunk), :]
    causal = mask_ref[...] > 0.5
    scores = scores_ref[...]
    pairs = pairs_ref[...]
    low_half = iota((STRETCH, 2 * head_size), 1) < head_size
    adder = head_adder(chunk, head_size, lanes)
    spread = spreader(chunk, heads, head_size, lanes)
    high, low = term_pair(x_ref[...].astype(F32) * dot(tail_ref[...], spread, 1, 0))
    state_ref[...] = dot(write_t[...], high, 1, 0) + dot(write_t[...], low, 1, 0)
    high, low = term_pair(g_ref[...].astype(F32) * dot(lead_ref[...], spread, 1, 0))
    back_ref[...] = dot(read_t[...], high, 1, 0) + dot(read_t[...], low, 1, 0)
    for pair in range(per_chunk // 2):
        strip = slice(pair * 2 * head_size, (pair + 1) * 2 * head_size)
        x = x_ref[:, strip]
        g = g_ref[:, strip]
        ys, dxs = [], []
        for half in range(2):
            head = 2 * pair + half
            gap = columns[:, head : head + 1] - rows[head : head + 1, :]
            decay = jnp.where(causal, jnp.exp(gap), 0.0)
            mixing = (scores * decay).astype(BF16)
            ys.append(dot(mixing, x, 1, 0))
            dxs.append(dot(mixing, g, 0, 0))
            mine = low_half if half == 0 else jnp.logical_not(low_half)
            pairs = pairs + dot(jnp.where(mine, g, jnp.zeros_like(g)), x, 1, 1) * decay
        y = jnp.where(low_half, ys[0], ys[1])
        dx = jnp.where(low_half, dxs[0], dxs[1])
        dx_ref[:, strip] = dx
        change_ref[...] += head_sums(
            g.astype(F32) * y - x.astype(F32) * dx, adder[strip, :]
        )
    pairs_ref[...] = pairs

    @pl.when(chunk == pl.num_programs(0) - 1)
    def _():
        summed = pairs_ref[...].astype(BF16)
        db_ref[...] = dot(summed, read_ref[...], 0, 0)
        dc_ref[...] = dot(summed, write_ref[...], 1, 0)


def intra(after, x, g, write_map, read_map, rates, shared):
    tokens, wide = x.shape
    heads = rates.shape[0]
    return pl.pallas_call(
        lambda *refs: intra_kernel(heads, *refs),
        grid=(wide // LANES,),
        in_specs=[
            whole(META, STRIP),
            lanes_of(tokens),
            lanes_of(tokens),
            whole(tokens, STATE),
            whole(tokens, STATE),
            whole(heads, tokens),
        ]
        + [whole(tokens, STRIP)] * 3,
        out_specs=[lanes_of(tokens)] + [whole(tokens, STATE)] * 3 + [lanes_of(STATE)] * 2,
        out_shape=[
            jax.ShapeDtypeStruct((tokens, wide), F32),
            jax.ShapeDtypeStruct((tokens, STATE), F32),
            jax.ShapeDtypeStruct((tokens, STATE), F32),
            jax.ShapeDtypeStruct((tokens, STATE), F32),
            jax.ShapeDtypeStruct((STATE, wide), F32),
            jax.ShapeDtypeStruct((STATE, wide), F32),
        ],
        scratch_shapes=[
            pltpu.VMEM((heads, tokens), F32),
            pltpu.VMEM((tokens, tokens), F32),
            pltpu.VMEM((tokens, tokens), F32),
            pltpu.VMEM((tokens, tokens), F32),
            pltpu.VMEM((STATE, tokens), BF16),
            pltpu.VMEM((STATE, tokens), BF16),
        ],
        compiler_params=pltpu.CompilerParams(vmem_limit_bytes=BIG_VMEM),
        cost_estimate=pl.CostEstimate(
            flops=12_000_000_000, bytes_accessed=8_000_000, transcendentals=heads * tokens * tokens
        ),
        name="intra",
    )(after, x, g, write_map, read_map, rates, *shared[1:])


def assemble_kernel(
    heads, chips, half, head_size, place, after, first_ref, state_own, back_own, *refs,
):
    own_refs, far_refs = refs[:chips], refs[chips : 2 * chips]
    state_ref, back_ref, total_ref = refs[2 * chips :]
    lanes = state_ref.shape[1]
    strips = lanes // STRIP
    part = STATE // chips
    size = strips * part
    log = first_ref[chips * size : chips * size + 1, :]
    decay = spread_rows([jnp.exp(log)], half * strips, strips, head_size)[0]
    is_first = place[0] == 0
    sums = [None] * strips
    for step in range(chips):
        quarter = place[1] ^ step
        rows = pl.ds(pl.multiple_of(quarter * part, part), part)
        for strip in range(strips):
            wide = slice(strip * STRIP, (strip + 1) * STRIP)
            here = slice(strip * part, (strip + 1) * part)
            there = pl.ds(pl.multiple_of(quarter * size + strip * part, part), part)
            own = own_refs[step][here, :] * decay[strip : strip + 1, :] + first_ref[there, :]
            far = far_refs[step][here, :]
            state = jnp.where(is_first, far, own).astype(BF16)
            back = jnp.where(is_first, own, far).astype(BF16)
            state_ref[rows, wide] = state
            back_ref[rows, wide] = back
            gain = state.astype(F32) * back_own[rows, wide]
            gain = gain - back.astype(F32) * state_own[rows, wide]
            sums[strip] = gain if sums[strip] is None else sums[strip] + gain
    row_sum = [
        jnp.broadcast_to(jnp.sum(value, axis=0, keepdims=True), (META, STRIP)) for value in sums
    ]
    total_ref[...] = head_sums(
        jnp.concatenate(row_sum, axis=1), head_adder(half, head_size, lanes)
    )


def assemble(heads, half, place, after, first, state_own, back_own, own, far):
    chips = len(own)
    wide = state_own.shape[1]
    lanes = wide // HALVES
    mine = pl.BlockSpec((STATE, lanes), lambda c: (0, half))
    return pl.pallas_call(
        lambda *refs: assemble_kernel(heads, chips, half, wide // heads, *refs),
        grid=(1,),
        in_specs=[SCALARS, whole(META, STRIP), whole(*first.shape), mine, mine]
        + [whole(*value.shape) for value in (*own, *far)],
        out_specs=[whole(STATE, lanes), whole(STATE, lanes), whole(META, STRIP)],
        out_shape=[
            jax.ShapeDtypeStruct((STATE, lanes), BF16),
            jax.ShapeDtypeStruct((STATE, lanes), BF16),
            jax.ShapeDtypeStruct((META, STRIP), F32),
        ],
        compiler_params=pltpu.CompilerParams(vmem_limit_bytes=SMALL_VMEM),
        name="assemble",
    )(place, after, first, state_own, back_own, *own, *far)


def finish_kernel(
    heads, start, steps, x_ref, g_ref, write_ref, read_ref, tail_ref, lead_ref,
    dx_ref, db_ref, dc_ref, change_ref, state_ref, back_ref, *refs,
):
    grad_ref, db_out, dc_out, sum_out, db_sum, dc_sum = refs[-6:]
    chunk = pl.program_id(0)
    lanes = x_ref.shape[1]
    head_size = lanes * STEPS * HALVES // heads
    wide = start + chunk

    @pl.when(chunk == 0)
    def _():
        sum_out[...] = change_ref[...]
        db_sum[...] = db_ref[...]
        dc_sum[...] = dc_ref[...]

    state = state_ref[...]
    back = back_ref[...]
    spread = spreader(wide, heads, head_size, lanes)
    tail = dot(tail_ref[...], spread, 1, 0)
    lead = dot(lead_ref[...], spread, 1, 0)
    x = x_ref[...].astype(F32)
    g = g_ref[...].astype(F32)
    y = dot(read_ref[...], state, 1, 0) * lead
    dx = dot(write_ref[...], back, 1, 0) * tail
    grad_ref[...] = (dx_ref[...] + dx).astype(BF16)
    adder = head_adder(wide, head_size, lanes)
    sum_out[...] += head_sums(g * y - x * dx, adder)
    db_sum[...] += dot((x * tail).astype(BF16), back, 1, 1)
    dc_sum[...] += dot((g * lead).astype(BF16), state, 1, 1)

    @pl.when(chunk == steps - 1)
    def _():
        db_out[...] = db_sum[...].astype(db_out.dtype)
        dc_out[...] = dc_sum[...].astype(dc_out.dtype)


def finish(heads, start, steps, x, g, write_map, read_map, shared, dx, sums, state, back, grad):
    tokens, wide = x.shape
    lanes = wide // (STEPS * HALVES)
    strip = pl.BlockSpec((tokens, lanes), lambda c: (0, start + c))
    own = pl.BlockSpec((STATE, lanes), lambda c: (0, start % STEPS + c))
    kind = BF16 if start + steps == STEPS * HALVES else F32
    earlier = [] if grad is None else [grad]
    return pl.pallas_call(
        lambda *refs: finish_kernel(heads, start, steps, *refs),
        grid=(steps,),
        in_specs=[strip, strip]
        + [whole(tokens, STATE)] * 4
        + [strip]
        + [whole(tokens, STATE)] * 3
        + [own, own]
        + [pl.BlockSpec(memory_space=pl.ANY)] * len(earlier),
        out_specs=[strip] + [whole(tokens, STATE)] * 3,
        out_shape=[
            jax.ShapeDtypeStruct((tokens, wide), BF16),
            jax.ShapeDtypeStruct((tokens, STATE), kind),
            jax.ShapeDtypeStruct((tokens, STATE), kind),
            jax.ShapeDtypeStruct((tokens, STATE), F32),
        ],
        scratch_shapes=[pltpu.VMEM((tokens, STATE), F32)] * 2,
        input_output_aliases={12: 0} if earlier else {},
        compiler_params=pltpu.CompilerParams(vmem_limit_bytes=SMALL_VMEM),
        cost_estimate=pl.CostEstimate(
            flops=3_000_000_000, bytes_accessed=5_000_000, transcendentals=0
        ),
        name="finish",
    )(x, g, write_map, read_map, *shared[2:], dx, *sums, state, back, *earlier)


def suffix_kernel(change_ref, later_ref, out_ref):
    heads = out_ref.shape[0]
    last = iota((STRETCH, STATE), 0) == STRETCH - 1
    change = change_ref[...] + jnp.where(last, later_ref[0:1, :], 0.0)
    out_ref[...] = dot(change, lower(STRETCH), 0, 0, HIGHEST)[:heads, :]


def suffix(heads, change, later):
    return pl.pallas_call(
        suffix_kernel,
        in_specs=[whole(*change.shape), whole(*later.shape)],
        out_specs=whole(heads, STRETCH),
        out_shape=jax.ShapeDtypeStruct((heads, STRETCH), F32),
        name="suffix",
    )(change, later)


def per_device(inputs, out_grad, input_map, output_map, log_decay):
    heads = log_decay.shape[0]
    head_size = inputs.shape[1] // heads
    groups, shards = lax.axis_size("grp"), lax.axis_size("seq")
    chips = shards // 2
    shard = lax.axis_index("seq")
    chip, core = shard // 2, shard % 2
    place = jnp.stack([core, chip]).astype(jnp.int32)
    everyone = [(a, z, c) for a in range(groups) for z in range(chips) for c in range(2)]

    def move(value, target):
        pairs = []
        for a, z, c in everyone:
            to = target(a, z, c)
            if to is not None:
                pairs.append((a * shards + 2 * z + c, to[0] * shards + 2 * to[1] + to[2]))
        return lax.ppermute(value, ("grp", "seq"), pairs)

    def to_core(value):
        return move(value, lambda a, z, c: (a, z, 1 - c))

    def to_chip(value, step):
        return move(value, lambda a, z, c: (a, z ^ step, c)) if step else value

    def to_group(value, step, ahead):
        def target(a, z, c):
            to = a + step if ahead(c) else a - step
            return (to, z, c) if 0 <= to < groups else None

        return move(value, target)

    def hold(value, *tokens):
        return lax.optimization_barrier((value, tokens))[0]

    maps = (inputs, out_grad, input_map, output_map)
    send, keep, decay, *shared = summary(chips, 0, place, *maps, log_decay, None)
    first = [to_core(send)]
    pieces = [combine(chips, place, shared[0], first[0], keep, decay, shared[0])]
    send, keep, decay = summary(chips, 1, place, *maps, log_decay, shared)
    first.append(to_core(send))
    dx, db, dc, change, state_own, back_own = intra(pieces[0][0], *maps, log_decay, shared)
    pieces.append(combine(chips, place, change, first[1], keep, decay, shared[0]))

    own, token = [], pieces[1][0]
    for half in range(HALVES):
        at = [to_chip(value, step) for step, value in enumerate(pieces[half])]
        total = group_total(half, head_size, place, token, at)
        got = [to_group(total, step, lambda c: c == 1) for step in range(1, groups)]
        inside = enter(half, head_size, place, at, got)
        own.append([to_chip(value, step) for step, value in enumerate(inside)])
        token = inside[0]

    def entering(half, token):
        far = [to_core(value) for value in own[half]]
        return assemble(
            heads, half, place, token, first[half], state_own, back_own, own[half], far
        )

    state, back, tally = entering(0, token)
    grad, *sums = finish(heads, 0, STEPS, *maps, shared, dx, (db, dc, change), state, back, None)
    own[1] = hold(own[1], sums[2])
    state, back, tally_b = entering(1, sums[2])
    tally = tally + tally_b

    other = to_core(tally)
    grad, *sums = finish(heads, STEPS, 1, *maps, shared, dx, sums, state, back, grad)
    other = hold(other, sums[2])
    later = jnp.where(core == 0, other, 0.0)
    tally = tally + other
    steps = [to_chip(tally, step) for step in range(1, chips)]
    sums = hold(sums, tally)
    grad, *sums = finish(heads, STEPS + 1, 1, *maps, shared, dx, sums, state, back, grad)
    steps = hold(steps, sums[2])
    for step, value in enumerate(steps, 1):
        later = later + jnp.where((chip ^ step) > chip, value, 0.0)
        tally = tally + value
    for step in range(1, groups):
        later = later + to_group(tally, step, lambda c: False)
    return (grad, sums[0], sums[1], suffix(heads, sums[2], later))


def solution(mesh):
    tokens = P(("grp", "seq"), None)
    in_specs = (tokens, tokens, tokens, tokens, P(None, ("grp", "seq")))
    out_specs = (tokens, tokens, tokens, P(None, ("grp", "seq")))
    return jax.shard_map(
        per_device, mesh=mesh, in_specs=in_specs, out_specs=out_specs, check_vma=False
    )
```

```python
import jax
import jax.numpy as jnp
from jax import lax
from jax.experimental import pallas as pl
from jax.experimental.pallas import tpu as pltpu
from jax.sharding import PartitionSpec as P

STATE = 128
STRETCH = 256
LANES = 512
HALVES = 2
STRIP = 128
META = 8
BIG_VMEM = 56 << 20
SMALL_VMEM = 24 << 20
F32 = jnp.float32
BF16 = jnp.bfloat16
HIGHEST = lax.Precision.HIGHEST


def dot(left, right, left_dim, right_dim, precision=None):
    return lax.dot_general(
        left,
        right,
        (((left_dim,), (right_dim,)), ((), ())),
        precision=precision,
        preferred_element_type=F32,
    )


def iota(shape, dim):
    return lax.broadcasted_iota(jnp.int32, shape, dim)


def lower(length):
    return (iota((length, length), 0) >= iota((length, length), 1)).astype(F32)


def thrice(rates):
    heads, length = rates.shape
    spare = jnp.zeros((STATE - 3 * heads, length), F32)
    return jnp.concatenate([rates, rates, rates, spare], axis=0)


def three_terms(value, heads):
    lane = iota(value.shape, 1)
    first = value.astype(BF16)
    rest = value - first.astype(F32)
    second = rest.astype(BF16)
    third = (rest - second.astype(F32)).astype(BF16)
    return jnp.where(lane < heads, first, jnp.where(lane < 2 * heads, second, third))


def spreader(chunk, heads, head_size, lanes):
    row = iota((STATE, lanes), 0)
    head = (iota((STATE, lanes), 1) + chunk * lanes) // head_size
    hit = (row == head) | (row == head + heads) | (row == head + 2 * heads)
    return hit.astype(F32).astype(BF16)


def head_adder(chunk, head_size, lanes):
    head = (iota((lanes, STATE), 0) + chunk * lanes) // head_size
    return (iota((lanes, STATE), 1) == head).astype(F32).astype(BF16)


def head_sums(value, adder):
    first = value.astype(BF16)
    second = (value - first.astype(F32)).astype(BF16)
    return dot(first, adder, 1, 0) + dot(second, adder, 1, 0)


def decay_terms(rates, heads):
    length = rates.shape[1]
    running = dot(lower(length), thrice(rates), 1, 1, HIGHEST)
    last = running[length - 1 : length, :]
    return (
        running,
        three_terms(jnp.exp(last - running), heads),
        three_terms(jnp.exp(running), heads),
    )


def term_pair(value):
    first = value.astype(BF16)
    return first, (value - first.astype(F32)).astype(BF16)


def lane_spread(per_strip, head_size):
    head = iota((STRIP, STRIP), 0) % per_strip
    return (iota((STRIP, STRIP), 1) // head_size == head).astype(F32)


def spread_rows(rows, offset, strips, head_size):
    per_strip = STRIP // head_size
    lane = iota((strips, STRIP), 1)
    row = iota((strips, STRIP), 0) + offset
    picked = [jnp.where(lane // per_strip == row, value, 0.0) for value in rows]
    stacked = jnp.concatenate(picked, axis=0) if len(picked) > 1 else picked[0]
    wide = dot(stacked, lane_spread(per_strip, head_size), 1, 0, HIGHEST)
    return [wide[i * strips : (i + 1) * strips, :] for i in range(len(rows))]


def whole(*shape):
    return pl.BlockSpec(shape, lambda *_: (0,) * len(shape))


def lanes_of(rows):
    return pl.BlockSpec((rows, LANES), lambda c: (0, c))


def half_lanes(rows, lanes, half, steps):
    return pl.BlockSpec((rows, lanes), lambda c: (0, half * steps + c))


LITTLE = pl.CostEstimate(flops=1, bytes_accessed=1, transcendentals=0)
SCALARS = pl.BlockSpec(memory_space=pltpu.SMEM)
STEPS = 2


def summary_kernel(heads, chips, half, place, x_ref, g_ref, write_ref, read_ref, *refs):
    chunk = pl.program_id(0)
    lanes = x_ref.shape[1]
    strips = lanes // STRIP
    half_strips = strips * STEPS
    head_size = lanes * STEPS * HALVES // heads
    part = STATE // chips
    if half == 0:
        rates_ref, send_ref, keep_ref, decay_ref, log_ref, run_ref, tail_ref, lead_ref = refs[:8]
    else:
        log_ref, tail_ref, lead_ref, send_ref, keep_ref, decay_ref = refs[:6]
    write_t, read_t = refs[-2:]

    @pl.when(chunk == 0)
    def _():
        if half == 0:
            running, tail, lead = decay_terms(rates_ref[...], heads)
            run_ref[...] = running
            tail_ref[...] = tail
            lead_ref[...] = lead
            log_ref[...] = jnp.broadcast_to(running[STRETCH - 1 :, :], (META, STRIP))
        send_ref[pl.ds(half_strips * STATE, META), :] = log_ref[...]
        write_t[...] = write_ref[...].astype(F32).T.astype(BF16)
        read_t[...] = read_ref[...].astype(F32).T.astype(BF16)

    spread = spreader(half * STEPS + chunk, heads, head_size, lanes)
    tail = dot(tail_ref[...], spread, 1, 0)
    lead = dot(lead_ref[...], spread, 1, 0)
    inputs_tail = (x_ref[...].astype(F32) * tail).astype(BF16)
    grads_lead = (g_ref[...].astype(F32) * lead).astype(BF16)
    state = dot(write_t[...], inputs_tail, 1, 0)
    back = dot(read_t[...], grads_lead, 1, 0)
    first = place[0] == 0
    send = jnp.where(first, state, back)
    keep = jnp.where(first, back, state)
    for strip in range(strips):
        at = chunk * strips + strip
        wide = slice(strip * STRIP, (strip + 1) * STRIP)
        decay_ref[pl.ds(at, 1), :] = lead[STRETCH - 1 :, wide]
        for quarter in range(chips):
            rows = pl.ds(pl.multiple_of((quarter * half_strips + at) * part, part), part)
            mine = slice(quarter * part, (quarter + 1) * part)
            send_ref[rows, :] = send[mine, wide]
            keep_ref[rows, :] = keep[mine, wide]


def summary(chips, half, place, x, g, write_map, read_map, rates, shared):
    tokens, wide = x.shape
    heads = rates.shape[0]
    lanes = wide // (STEPS * HALVES)
    strips = wide // STRIP // HALVES
    terms = [
        jax.ShapeDtypeStruct((META, STRIP), F32),
        jax.ShapeDtypeStruct((tokens, STRIP), F32),
        jax.ShapeDtypeStruct((tokens, STRIP), BF16),
        jax.ShapeDtypeStruct((tokens, STRIP), BF16),
    ]
    out_shape = [
        jax.ShapeDtypeStruct((strips * STATE + META, STRIP), F32),
        jax.ShapeDtypeStruct((strips * STATE, STRIP), F32),
        jax.ShapeDtypeStruct((strips, STRIP), F32),
    ]
    if half == 0:
        extra = [rates]
        out_shape = out_shape + terms
    else:
        extra = [shared[0], shared[2], shared[3]]
    return pl.pallas_call(
        lambda *refs: summary_kernel(heads, chips, half, *refs),
        grid=(STEPS,),
        in_specs=[
            SCALARS,
            half_lanes(tokens, lanes, half, STEPS),
            half_lanes(tokens, lanes, half, STEPS),
            whole(tokens, STATE),
            whole(tokens, STATE),
        ]
        + [whole(*value.shape) for value in extra],
        out_specs=[whole(*out.shape) for out in out_shape],
        out_shape=out_shape,
        scratch_shapes=[
            pltpu.VMEM((STATE, tokens), BF16),
            pltpu.VMEM((STATE, tokens), BF16),
        ],
        compiler_params=pltpu.CompilerParams(vmem_limit_bytes=BIG_VMEM),
        cost_estimate=LITTLE,
        name="summary",
    )(place, x, g, write_map, read_map, *extra)


def combine_kernel(chips, place, after, first_ref, keep_ref, decay_ref, log_ref, *out_refs):
    strips = decay_ref.shape[0]
    part = STATE // chips
    size = strips * part
    meta = first_ref[pl.ds(chips * size, META), :] + log_ref[...]
    for step, out_ref in enumerate(out_refs):
        base = (place[1] ^ step) * size
        for strip in range(strips):
            rows = pl.ds(pl.multiple_of(base + strip * part, part), part)
            out_ref[strip * part : (strip + 1) * part, :] = (
                first_ref[rows, :] * decay_ref[strip : strip + 1, :] + keep_ref[rows, :]
            )
        out_ref[size:, :] = meta


def combine(chips, place, after, first, keep, decay, log):
    strips = decay.shape[0]
    size = strips * (STATE // chips)
    return pl.pallas_call(
        lambda *refs: combine_kernel(chips, *refs),
        grid=(1,),
        in_specs=[SCALARS]
        + [whole(META, STRIP)]
        + [whole(*value.shape) for value in (first, keep, decay, log)],
        out_specs=[whole(size + META, STRIP)] * chips,
        out_shape=[jax.ShapeDtypeStruct((size + META, STRIP), F32)] * chips,
        compiler_params=pltpu.CompilerParams(vmem_limit_bytes=SMALL_VMEM),
        cost_estimate=LITTLE,
        name="combine",
    )(place, after, first, keep, decay, log)


def rank_of(place, step):
    chip = place[1] ^ step
    return jnp.where(place[0] == 1, chip, -chip)


def is_ahead(place, bit):
    return ((place[2] >> bit) & 1) == place[0]


def join_kernel(bit, offset, strips, head_size, place, mine_ref, got_ref, out_ref):
    size = mine_ref.shape[0] - META
    part = size // strips
    ahead = is_ahead(place, bit)
    mine_log = mine_ref[size : size + 1, :]
    got_log = got_ref[size : size + 1, :]
    mine_row = jnp.where(ahead, 1.0, jnp.exp(got_log))
    got_row = jnp.where(ahead, jnp.exp(mine_log), 1.0)
    mine_wide, got_wide = spread_rows([mine_row, got_row], offset, strips, head_size)
    for strip in range(strips):
        rows = slice(strip * part, (strip + 1) * part)
        one = slice(strip, strip + 1)
        out_ref[rows, :] = mine_ref[rows, :] * mine_wide[one, :] + got_ref[rows, :] * got_wide[one, :]
    out_ref[size:, :] = jnp.broadcast_to(mine_log + got_log, (META, STRIP))


def join(half, bit, strips, head_size, place, mine, got):
    return pl.pallas_call(
        lambda *refs: join_kernel(bit, half * strips, strips, head_size, *refs),
        in_specs=[SCALARS, whole(*mine.shape), whole(*got.shape)],
        out_specs=whole(*mine.shape),
        out_shape=jax.ShapeDtypeStruct(mine.shape, F32),
        compiler_params=pltpu.CompilerParams(vmem_limit_bytes=SMALL_VMEM),
        cost_estimate=LITTLE,
        name="join",
    )(place, mine, got)


def masked_sum(terms):
    total = None
    for hit, value in terms:
        value = jnp.where(hit, value, 0.0)
        total = value if total is None else total + value
    return total


def total_kernel(offset, strips, head_size, place, after_ref, *refs):
    at_refs, out_ref = refs[:-1], refs[-1]
    chips = len(at_refs)
    part = STATE // chips
    size = strips * part
    rank = [rank_of(place, step) for step in range(chips)]
    logs = [ref[size : size + 1, :] for ref in at_refs]
    weights = [
        jnp.exp(masked_sum([(rank[b] > rank[a], logs[b]) for b in range(chips)]))
        for a in range(chips)
    ]
    wide = spread_rows(weights, offset, strips, head_size)
    for strip in range(strips):
        rows = slice(strip * part, (strip + 1) * part)
        total = at_refs[0][rows, :] * wide[0][strip : strip + 1, :]
        for a in range(1, chips):
            total = total + at_refs[a][rows, :] * wide[a][strip : strip + 1, :]
        out_ref[rows, :] = total
    out_ref[size:, :] = jnp.broadcast_to(sum(logs[1:], logs[0]), (META, STRIP))


def group_total(half, head_size, place, after, at):
    strips = (at[0].shape[0] - META) * len(at) // STATE
    return pl.pallas_call(
        lambda *refs: total_kernel(half * strips, strips, head_size, *refs),
        grid=(1,),
        in_specs=[SCALARS, whole(META, STRIP)] + [whole(*at[0].shape)] * len(at),
        out_specs=whole(*at[0].shape),
        out_shape=jax.ShapeDtypeStruct(at[0].shape, F32),
        compiler_params=pltpu.CompilerParams(vmem_limit_bytes=SMALL_VMEM),
        cost_estimate=LITTLE,
        name="group_total",
    )(place, after, *at)


def enter_kernel(chips, offset, strips, head_size, place, after_ref, *refs):
    at_refs, got_refs, out_refs = refs[:chips], refs[chips:-chips], refs[-chips:]
    part = STATE // chips
    size = strips * part
    rank = [rank_of(place, step) for step in range(chips)]
    logs = [ref[size : size + 1, :] for ref in at_refs]
    zero = jnp.zeros_like(logs[0])
    rows_of = []
    passed = zero
    for bit, ref in enumerate(got_refs):
        ahead = is_ahead(place, bit)
        rows_of.append(jnp.where(ahead, jnp.exp(passed), 0.0))
        passed = passed + jnp.where(ahead, ref[size : size + 1, :], 0.0)
    for to in range(chips):
        rows_of.append(
            jnp.exp(masked_sum([(rank[m] < rank[to], logs[m]) for m in range(chips)]))
        )
    pairs = [(to, a) for to in range(chips) for a in range(chips) if a != to]
    for to, a in pairs:
        between = masked_sum(
            [((rank[m] > rank[a]) & (rank[m] < rank[to]), logs[m]) for m in range(chips)]
        )
        rows_of.append(jnp.where(rank[a] < rank[to], jnp.exp(between), 0.0))
    wide = spread_rows(rows_of, offset, strips, head_size)
    groups_wide = wide[: len(got_refs)]
    ahead_wide = wide[len(got_refs) : len(got_refs) + chips]
    pair_wide = dict(zip(pairs, wide[len(got_refs) + chips :]))
    for strip in range(strips):
        rows = slice(strip * part, (strip + 1) * part)
        one = slice(strip, strip + 1)
        incoming = jnp.zeros((part, STRIP), F32)
        for ref, weight in zip(got_refs, groups_wide):
            incoming = incoming + ref[rows, :] * weight[one, :]
        values = [ref[rows, :] for ref in at_refs]
        for to in range(chips):
            entering = incoming * ahead_wide[to][one, :]
            for a in range(chips):
                if a != to:
                    entering = entering + values[a] * pair_wide[to, a][one, :]
            out_refs[to][rows, :] = entering


def enter(half, head_size, place, after, at, got):
    chips = len(at)
    strips = (at[0].shape[0] - META) * chips // STATE
    size = strips * (STATE // chips)
    return pl.pallas_call(
        lambda *refs: enter_kernel(chips, half * strips, strips, head_size, *refs),
        grid=(1,),
        in_specs=[SCALARS, whole(META, STRIP)] + [whole(*at[0].shape)] * (chips + len(got)),
        out_specs=[whole(size, STRIP)] * chips,
        out_shape=[jax.ShapeDtypeStruct((size, STRIP), F32)] * chips,
        compiler_params=pltpu.CompilerParams(vmem_limit_bytes=SMALL_VMEM),
        cost_estimate=LITTLE,
        name="enter",
    )(place, after, *at, *got)


def intra_kernel(
    heads, after_ref, x_ref, g_ref, write_ref, read_ref, rates_ref, column_ref, tail_ref, lead_ref,
    dx_ref, db_ref, dc_ref, change_ref, state_ref, back_ref,
    row_ref, scores_ref, mask_ref, pairs_ref, write_t, read_t,
):
    chunk = pl.program_id(0)
    lanes = x_ref.shape[1]
    head_size = lanes * pl.num_programs(0) // heads
    per_chunk = lanes // head_size

    @pl.when(chunk == 0)
    def _():
        rates = rates_ref[...]
        triangle = lower(STRETCH)
        row_ref[...] = dot(rates, triangle, 1, 1, HIGHEST)
        mask_ref[...] = triangle
        scores_ref[...] = dot(read_ref[...], write_ref[...], 1, 1)
        pairs_ref[...] = jnp.zeros_like(pairs_ref)
        change_ref[...] = jnp.zeros_like(change_ref)
        write_t[...] = write_ref[...].astype(F32).T.astype(BF16)
        read_t[...] = read_ref[...].astype(F32).T.astype(BF16)

    columns = pltpu.roll(column_ref[...], STATE - chunk * per_chunk, 1)
    rows = row_ref[pl.ds(pl.multiple_of(chunk * per_chunk, per_chunk), per_chunk), :]
    causal = mask_ref[...] > 0.5
    scores = scores_ref[...]
    pairs = pairs_ref[...]
    low_half = iota((STRETCH, 2 * head_size), 1) < head_size
    adder = head_adder(chunk, head_size, lanes)
    spread = spreader(chunk, heads, head_size, lanes)
    high, low = term_pair(x_ref[...].astype(F32) * dot(tail_ref[...], spread, 1, 0))
    state_ref[...] = dot(write_t[...], high, 1, 0) + dot(write_t[...], low, 1, 0)
    high, low = term_pair(g_ref[...].astype(F32) * dot(lead_ref[...], spread, 1, 0))
    back_ref[...] = dot(read_t[...], high, 1, 0) + dot(read_t[...], low, 1, 0)
    for pair in range(per_chunk // 2):
        strip = slice(pair * 2 * head_size, (pair + 1) * 2 * head_size)
        x = x_ref[:, strip]
        g = g_ref[:, strip]
        ys, dxs = [], []
        for half in range(2):
            head = 2 * pair + half
            gap = columns[:, head : head + 1] - rows[head : head + 1, :]
            decay = jnp.where(causal, jnp.exp(gap), 0.0)
            mixing = (scores * decay).astype(BF16)
            ys.append(dot(mixing, x, 1, 0))
            dxs.append(dot(mixing, g, 0, 0))
            mine = low_half if half == 0 else jnp.logical_not(low_half)
            pairs = pairs + dot(jnp.where(mine, g, jnp.zeros_like(g)), x, 1, 1) * decay
        y = jnp.where(low_half, ys[0], ys[1])
        dx = jnp.where(low_half, dxs[0], dxs[1])
        dx_ref[:, strip] = dx
        change_ref[...] += head_sums(
            g.astype(F32) * y - x.astype(F32) * dx, adder[strip, :]
        )
    pairs_ref[...] = pairs

    @pl.when(chunk == pl.num_programs(0) - 1)
    def _():
        summed = pairs_ref[...].astype(BF16)
        db_ref[...] = dot(summed, read_ref[...], 0, 0)
        dc_ref[...] = dot(summed, write_ref[...], 1, 0)


def intra(after, x, g, write_map, read_map, rates, shared):
    tokens, wide = x.shape
    heads = rates.shape[0]
    return pl.pallas_call(
        lambda *refs: intra_kernel(heads, *refs),
        grid=(wide // LANES,),
        in_specs=[
            whole(META, STRIP),
            lanes_of(tokens),
            lanes_of(tokens),
            whole(tokens, STATE),
            whole(tokens, STATE),
            whole(heads, tokens),
        ]
        + [whole(tokens, STRIP)] * 3,
        out_specs=[lanes_of(tokens)] + [whole(tokens, STATE)] * 3 + [lanes_of(STATE)] * 2,
        out_shape=[
            jax.ShapeDtypeStruct((tokens, wide), F32),
            jax.ShapeDtypeStruct((tokens, STATE), F32),
            jax.ShapeDtypeStruct((tokens, STATE), F32),
            jax.ShapeDtypeStruct((tokens, STATE), F32),
            jax.ShapeDtypeStruct((STATE, wide), F32),
            jax.ShapeDtypeStruct((STATE, wide), F32),
        ],
        scratch_shapes=[
            pltpu.VMEM((heads, tokens), F32),
            pltpu.VMEM((tokens, tokens), F32),
            pltpu.VMEM((tokens, tokens), F32),
            pltpu.VMEM((tokens, tokens), F32),
            pltpu.VMEM((STATE, tokens), BF16),
            pltpu.VMEM((STATE, tokens), BF16),
        ],
        compiler_params=pltpu.CompilerParams(vmem_limit_bytes=BIG_VMEM),
        cost_estimate=LITTLE,
        name="intra",
    )(after, x, g, write_map, read_map, rates, *shared[1:])


def order_kernel(place, *refs):
    pieces, out_ref = refs[:-1], refs[-1]
    size = pieces[0].shape[0]
    for step, ref in enumerate(pieces):
        rows = pl.ds(pl.multiple_of((place[1] ^ step) * size, size), size)
        out_ref[rows, :] = ref[...]


def order(place, pieces):
    shape = (len(pieces) * pieces[0].shape[0], STRIP)
    return pl.pallas_call(
        order_kernel,
        in_specs=[SCALARS] + [whole(*value.shape) for value in pieces],
        out_specs=whole(*shape),
        out_shape=jax.ShapeDtypeStruct(shape, F32),
        compiler_params=pltpu.CompilerParams(vmem_limit_bytes=SMALL_VMEM),
        cost_estimate=LITTLE,
        name="order",
    )(place, *pieces)


def assemble_kernel(
    heads, chips, half, head_size, place, after, first_ref, state_own, back_own, own_ref, far_ref,
    state_ref, back_ref, total_ref,
):
    lanes = state_ref.shape[1]
    strips = lanes // STRIP
    part = STATE // chips
    size = strips * part
    log = first_ref[chips * size : chips * size + 1, :]
    decay = spread_rows([jnp.exp(log)], half * strips, strips, head_size)[0]
    is_first = place[0] == 0
    sums = [None] * strips
    for quarter in range(chips):
        rows = slice(quarter * part, (quarter + 1) * part)
        for strip in range(strips):
            wide = slice(strip * STRIP, (strip + 1) * STRIP)
            here = slice(quarter * size + strip * part, quarter * size + (strip + 1) * part)
            own = own_ref[here, :] * decay[strip : strip + 1, :] + first_ref[here, :]
            far = far_ref[here, :]
            state = jnp.where(is_first, far, own).astype(BF16)
            back = jnp.where(is_first, own, far).astype(BF16)
            state_ref[rows, wide] = state
            back_ref[rows, wide] = back
            gain = state.astype(F32) * back_own[rows, wide]
            gain = gain - back.astype(F32) * state_own[rows, wide]
            sums[strip] = gain if sums[strip] is None else sums[strip] + gain
    row_sum = [
        jnp.broadcast_to(jnp.sum(value, axis=0, keepdims=True), (META, STRIP)) for value in sums
    ]
    total_ref[...] = head_sums(
        jnp.concatenate(row_sum, axis=1), head_adder(half, head_size, lanes)
    )


def assemble(heads, chips, half, place, after, first, state_own, back_own, own, far):
    wide = state_own.shape[1]
    lanes = wide // HALVES
    mine = pl.BlockSpec((STATE, lanes), lambda c: (0, half))
    return pl.pallas_call(
        lambda *refs: assemble_kernel(heads, chips, half, wide // heads, *refs),
        grid=(1,),
        in_specs=[SCALARS, whole(META, STRIP), whole(*first.shape), mine, mine]
        + [whole(*own.shape), whole(*far.shape)],
        out_specs=[whole(STATE, lanes), whole(STATE, lanes), whole(META, STRIP)],
        out_shape=[
            jax.ShapeDtypeStruct((STATE, lanes), BF16),
            jax.ShapeDtypeStruct((STATE, lanes), BF16),
            jax.ShapeDtypeStruct((META, STRIP), F32),
        ],
        compiler_params=pltpu.CompilerParams(vmem_limit_bytes=SMALL_VMEM),
        cost_estimate=LITTLE,
        name="assemble",
    )(place, after, first, state_own, back_own, own, far)


def finish_kernel(
    heads, start, steps, last, x_ref, g_ref, write_ref, read_ref, tail_ref, lead_ref,
    dx_ref, db_ref, dc_ref, change_ref, state_ref, back_ref, *refs,
):
    grad_ref, db_out, dc_out, change_out, db_sum, dc_sum, sum_out = refs[-7:]
    chunk = pl.program_id(0)
    lanes = x_ref.shape[1]
    head_size = lanes * STEPS * HALVES // heads
    wide = start + chunk

    @pl.when(chunk == 0)
    def _():
        sum_out[...] = change_ref[...]
        db_sum[...] = db_ref[...]
        dc_sum[...] = dc_ref[...]

    state = state_ref[...]
    back = back_ref[...]
    spread = spreader(wide, heads, head_size, lanes)
    tail = dot(tail_ref[...], spread, 1, 0)
    lead = dot(lead_ref[...], spread, 1, 0)
    x = x_ref[...].astype(F32)
    g = g_ref[...].astype(F32)
    y = dot(read_ref[...], state, 1, 0) * lead
    dx = dot(write_ref[...], back, 1, 0) * tail
    grad_ref[...] = (dx_ref[...] + dx).astype(BF16)
    adder = head_adder(wide, head_size, lanes)
    sum_out[...] += head_sums(g * y - x * dx, adder)
    db_sum[...] += dot((x * tail).astype(BF16), back, 1, 1)
    dc_sum[...] += dot((g * lead).astype(BF16), state, 1, 1)

    @pl.when(chunk == steps - 1)
    def _():
        db_out[...] = db_sum[...].astype(db_out.dtype)
        dc_out[...] = dc_sum[...].astype(dc_out.dtype)
        if last:
            change_out[...] = dot(sum_out[...], lower(STRETCH), 0, 0, HIGHEST)[:heads, :]
        else:
            change_out[...] = sum_out[...]


def finish(heads, start, steps, x, g, write_map, read_map, shared, dx, sums, state, back, grad):
    tokens, wide = x.shape
    lanes = wide // (STEPS * HALVES)
    strip = pl.BlockSpec((tokens, lanes), lambda c: (0, start + c))
    own = pl.BlockSpec((STATE, lanes), lambda c: (0, start % STEPS + c))
    last = start + steps == STEPS * HALVES
    kind = BF16 if last else F32
    change = (heads, tokens) if last else (tokens, STATE)
    earlier = [] if grad is None else [grad]
    return pl.pallas_call(
        lambda *refs: finish_kernel(heads, start, steps, last, *refs),
        grid=(steps,),
        in_specs=[strip, strip]
        + [whole(tokens, STATE)] * 4
        + [strip]
        + [whole(tokens, STATE)] * 3
        + [own, own]
        + [pl.BlockSpec(memory_space=pl.ANY)] * len(earlier),
        out_specs=[strip] + [whole(tokens, STATE)] * 2 + [whole(*change)],
        out_shape=[
            jax.ShapeDtypeStruct((tokens, wide), BF16),
            jax.ShapeDtypeStruct((tokens, STATE), kind),
            jax.ShapeDtypeStruct((tokens, STATE), kind),
            jax.ShapeDtypeStruct(change, F32),
        ],
        scratch_shapes=[pltpu.VMEM((tokens, STATE), F32)] * 3,
        input_output_aliases={12: 0} if earlier else {},
        compiler_params=pltpu.CompilerParams(vmem_limit_bytes=SMALL_VMEM),
        cost_estimate=LITTLE,
        name="finish",
    )(x, g, write_map, read_map, *shared[2:], dx, *sums, state, back, *earlier)


def add_later_kernel(suffix_ref, later_ref, out_ref):
    heads = out_ref.shape[0]
    out_ref[...] = suffix_ref[...] + later_ref[...].T[:heads, 0:1]


def add_later(suffix, later):
    return pl.pallas_call(
        add_later_kernel,
        in_specs=[whole(*suffix.shape), whole(*later.shape)],
        out_specs=whole(*suffix.shape),
        out_shape=jax.ShapeDtypeStruct(suffix.shape, F32),
        cost_estimate=LITTLE,
        name="add_later",
    )(suffix, later)


def per_device(inputs, out_grad, input_map, output_map, log_decay):
    heads = log_decay.shape[0]
    head_size = inputs.shape[1] // heads
    groups, shards = lax.axis_size("grp"), lax.axis_size("seq")
    chips = shards // 2
    shard, group = lax.axis_index("seq"), lax.axis_index("grp")
    chip, core = shard >> 1, shard & 1
    place = jnp.stack([core, chip, group]).astype(jnp.int32)
    strips = inputs.shape[1] // STRIP // HALVES
    bits = groups.bit_length() - 1
    everyone = [(a, z, c) for a in range(groups) for z in range(chips) for c in range(2)]

    def move(value, target):
        pairs = []
        for a, z, c in everyone:
            to = target(a, z, c)
            if to is not None:
                pairs.append((a * shards + 2 * z + c, to[0] * shards + 2 * to[1] + to[2]))
        return lax.ppermute(value, ("grp", "seq"), pairs)

    def to_core(value):
        return move(value, lambda a, z, c: (a, z, 1 - c))

    def to_chip(value, step):
        return move(value, lambda a, z, c: (a, z ^ step, c)) if step else value

    def to_group(value, step):
        return move(value, lambda a, z, c: (a ^ step, z, c))

    def hold(value, *tokens):
        return lax.optimization_barrier((value, tokens))[0]

    maps = (inputs, out_grad, input_map, output_map)
    send, keep, decay, *shared = summary(chips, 0, place, *maps, log_decay, None)
    first = [to_core(send)]
    pieces = [combine(chips, place, shared[0], first[0], keep, decay, shared[0])]
    send, keep, decay = summary(chips, 1, place, *maps, log_decay, shared)
    first.append(to_core(send))
    dx, db, dc, change, state_own, back_own = intra(pieces[0][0], *maps, log_decay, shared)
    pieces.append(combine(chips, place, change, first[1], keep, decay, shared[0]))

    at, total, token = [], [], pieces[1][0]
    for half in range(HALVES):
        at.append([to_chip(value, step) for step, value in enumerate(pieces[half])])
        total.append(group_total(half, head_size, place, token, at[half]))
        token = total[half]
    own = []
    for half in range(HALVES):
        block, got = total[half], []
        for bit in range(bits):
            got.append(to_group(block, 1 << bit))
            if bit < bits - 1:
                block = join(half, bit, strips, head_size, place, block, got[bit])
        inside = enter(half, head_size, place, token, at[half], got)
        token = inside[0]
        own.append([to_chip(value, step) for step, value in enumerate(inside)])

    own[0] = hold(own[0], token)

    def entering(half, token):
        mine = order(place, own[half])
        return assemble(
            heads, chips, half, place, token, first[half], state_own, back_own, mine, to_core(mine)
        )

    state, back, tally = entering(0, token)
    grad, *sums = finish(heads, 0, STEPS, *maps, shared, dx, (db, dc, change), state, back, None)
    own[1] = hold(own[1], sums[2])
    state, back, tally_b = entering(1, sums[2])
    tally = tally + tally_b

    def count(later, tally, got, bit, index):
        return later + jnp.where((index >> bit) & 1 == 0, got, 0.0), tally + got

    got = to_core(tally)
    grad, *sums = finish(heads, STEPS, 1, *maps, shared, dx, sums, state, back, grad)
    later, tally = count(0.0, tally, hold(got, sums[2]), 0, core)
    got = to_chip(tally, 1)
    sums = hold(sums, tally)
    grad, *sums = finish(heads, STEPS + 1, 1, *maps, shared, dx, sums, state, back, grad)
    later, tally = count(later, tally, hold(got, sums[2]), 0, chip)
    for bit in range(1, chips.bit_length() - 1):
        later, tally = count(later, tally, to_chip(tally, 1 << bit), bit, chip)
    for bit in range(bits):
        later, tally = count(later, tally, to_group(tally, 1 << bit), bit, group)
    return (grad, sums[0], sums[1], add_later(sums[2], later))


def solution(mesh):
    tokens = P(("grp", "seq"), None)
    in_specs = (tokens, tokens, tokens, tokens, P(None, ("grp", "seq")))
    out_specs = (tokens, tokens, tokens, P(None, ("grp", "seq")))
    return jax.shard_map(
        per_device, mesh=mesh, in_specs=in_specs, out_specs=out_specs, check_vma=False
    )
```

```python
import jax
import jax.numpy as jnp
from jax import lax
from jax.experimental import pallas as pl
from jax.experimental.pallas import tpu as pltpu
from jax.sharding import PartitionSpec as P

STATE = 128
STRETCH = 256
LANES = 512
HALVES = 2
STRIP = 128
META = 8
BIG_VMEM = 56 << 20
SMALL_VMEM = 24 << 20
F32 = jnp.float32
BF16 = jnp.bfloat16
HIGHEST = lax.Precision.HIGHEST


def dot(left, right, left_dim, right_dim, precision=None):
    return lax.dot_general(
        left,
        right,
        (((left_dim,), (right_dim,)), ((), ())),
        precision=precision,
        preferred_element_type=F32,
    )


def iota(shape, dim):
    return lax.broadcasted_iota(jnp.int32, shape, dim)


def lower(length):
    return (iota((length, length), 0) >= iota((length, length), 1)).astype(F32)


def thrice(rates):
    heads, length = rates.shape
    spare = jnp.zeros((STATE - 3 * heads, length), F32)
    return jnp.concatenate([rates, rates, rates, spare], axis=0)


def three_terms(value, heads):
    lane = iota(value.shape, 1)
    first = value.astype(BF16)
    rest = value - first.astype(F32)
    second = rest.astype(BF16)
    third = (rest - second.astype(F32)).astype(BF16)
    return jnp.where(lane < heads, first, jnp.where(lane < 2 * heads, second, third))


def spreader(chunk, heads, head_size, lanes):
    row = iota((STATE, lanes), 0)
    head = (iota((STATE, lanes), 1) + chunk * lanes) // head_size
    hit = (row == head) | (row == head + heads) | (row == head + 2 * heads)
    return hit.astype(F32).astype(BF16)


def head_adder(chunk, head_size, lanes):
    head = (iota((lanes, STATE), 0) + chunk * lanes) // head_size
    return (iota((lanes, STATE), 1) == head).astype(F32).astype(BF16)


def head_sums(value, adder):
    first = value.astype(BF16)
    second = (value - first.astype(F32)).astype(BF16)
    return dot(first, adder, 1, 0) + dot(second, adder, 1, 0)


def decay_terms(rates, heads):
    length = rates.shape[1]
    running = dot(lower(length), thrice(rates), 1, 1, HIGHEST)
    last = running[length - 1 : length, :]
    return (
        running,
        three_terms(jnp.exp(last - running), heads),
        three_terms(jnp.exp(running), heads),
    )


def term_pair(value):
    first = value.astype(BF16)
    return first, (value - first.astype(F32)).astype(BF16)


def lane_spread(per_strip, head_size):
    head = iota((STRIP, STRIP), 0) % per_strip
    return (iota((STRIP, STRIP), 1) // head_size == head).astype(F32)


def spread_rows(rows, offset, strips, head_size):
    per_strip = STRIP // head_size
    lane = iota((strips, STRIP), 1)
    row = iota((strips, STRIP), 0) + offset
    picked = [jnp.where(lane // per_strip == row, value, 0.0) for value in rows]
    stacked = jnp.concatenate(picked, axis=0) if len(picked) > 1 else picked[0]
    wide = dot(stacked, lane_spread(per_strip, head_size), 1, 0, HIGHEST)
    return [wide[i * strips : (i + 1) * strips, :] for i in range(len(rows))]


def whole(*shape):
    return pl.BlockSpec(shape, lambda *_: (0,) * len(shape))


def lanes_of(rows):
    return pl.BlockSpec((rows, LANES), lambda c: (0, c))


def half_lanes(rows, lanes, half, steps):
    return pl.BlockSpec((rows, lanes), lambda c: (0, half * steps + c))


LITTLE = pl.CostEstimate(flops=1, bytes_accessed=1, transcendentals=0)
SCALARS = pl.BlockSpec(memory_space=pltpu.SMEM)
STEPS = 2


def summary_kernel(heads, chips, half, place, x_ref, g_ref, write_ref, read_ref, *refs):
    chunk = pl.program_id(0)
    lanes = x_ref.shape[1]
    strips = lanes // STRIP
    half_strips = strips * STEPS
    head_size = lanes * STEPS * HALVES // heads
    part = STATE // chips
    if half == 0:
        rates_ref, send_ref, keep_ref, decay_ref, log_ref, run_ref, tail_ref, lead_ref = refs[:8]
    else:
        log_ref, tail_ref, lead_ref, send_ref, keep_ref, decay_ref = refs[:6]
    write_t, read_t = refs[-2:]

    @pl.when(chunk == 0)
    def _():
        if half == 0:
            running, tail, lead = decay_terms(rates_ref[...], heads)
            run_ref[...] = running
            tail_ref[...] = tail
            lead_ref[...] = lead
            log_ref[...] = jnp.broadcast_to(running[STRETCH - 1 :, :], (META, STRIP))
        send_ref[pl.ds(half_strips * STATE, META), :] = log_ref[...]
        write_t[...] = write_ref[...].astype(F32).T.astype(BF16)
        read_t[...] = read_ref[...].astype(F32).T.astype(BF16)

    spread = spreader(half * STEPS + chunk, heads, head_size, lanes)
    tail = dot(tail_ref[...], spread, 1, 0)
    lead = dot(lead_ref[...], spread, 1, 0)
    inputs_tail = (x_ref[...].astype(F32) * tail).astype(BF16)
    grads_lead = (g_ref[...].astype(F32) * lead).astype(BF16)
    state = dot(write_t[...], inputs_tail, 1, 0)
    back = dot(read_t[...], grads_lead, 1, 0)
    first = place[0] == 0
    send = jnp.where(first, state, back)
    keep = jnp.where(first, back, state)
    for strip in range(strips):
        at = chunk * strips + strip
        wide = slice(strip * STRIP, (strip + 1) * STRIP)
        decay_ref[pl.ds(at, 1), :] = lead[STRETCH - 1 :, wide]
        for quarter in range(chips):
            rows = pl.ds(pl.multiple_of((quarter * half_strips + at) * part, part), part)
            mine = slice(quarter * part, (quarter + 1) * part)
            send_ref[rows, :] = send[mine, wide]
            keep_ref[rows, :] = keep[mine, wide]


def summary(chips, half, place, x, g, write_map, read_map, rates, shared):
    tokens, wide = x.shape
    heads = rates.shape[0]
    lanes = wide // (STEPS * HALVES)
    strips = wide // STRIP // HALVES
    terms = [
        jax.ShapeDtypeStruct((META, STRIP), F32),
        jax.ShapeDtypeStruct((tokens, STRIP), F32),
        jax.ShapeDtypeStruct((tokens, STRIP), BF16),
        jax.ShapeDtypeStruct((tokens, STRIP), BF16),
    ]
    out_shape = [
        jax.ShapeDtypeStruct((strips * STATE + META, STRIP), F32),
        jax.ShapeDtypeStruct((strips * STATE, STRIP), F32),
        jax.ShapeDtypeStruct((strips, STRIP), F32),
    ]
    if half == 0:
        extra = [rates]
        out_shape = out_shape + terms
    else:
        extra = [shared[0], shared[2], shared[3]]
    return pl.pallas_call(
        lambda *refs: summary_kernel(heads, chips, half, *refs),
        grid=(STEPS,),
        in_specs=[
            SCALARS,
            half_lanes(tokens, lanes, half, STEPS),
            half_lanes(tokens, lanes, half, STEPS),
            whole(tokens, STATE),
            whole(tokens, STATE),
        ]
        + [whole(*value.shape) for value in extra],
        out_specs=[whole(*out.shape) for out in out_shape],
        out_shape=out_shape,
        scratch_shapes=[
            pltpu.VMEM((STATE, tokens), BF16),
            pltpu.VMEM((STATE, tokens), BF16),
        ],
        compiler_params=pltpu.CompilerParams(vmem_limit_bytes=BIG_VMEM),
        cost_estimate=LITTLE,
        name="summary",
    )(place, x, g, write_map, read_map, *extra)


def combine_kernel(chips, place, after, first_ref, keep_ref, decay_ref, log_ref, *out_refs):
    strips = decay_ref.shape[0]
    part = STATE // chips
    size = strips * part
    meta = first_ref[pl.ds(chips * size, META), :] + log_ref[...]
    for step, out_ref in enumerate(out_refs):
        base = (place[1] ^ step) * size
        for strip in range(strips):
            rows = pl.ds(pl.multiple_of(base + strip * part, part), part)
            out_ref[strip * part : (strip + 1) * part, :] = (
                first_ref[rows, :] * decay_ref[strip : strip + 1, :] + keep_ref[rows, :]
            )
        out_ref[size:, :] = meta


def combine(chips, place, after, first, keep, decay, log):
    strips = decay.shape[0]
    size = strips * (STATE // chips)
    return pl.pallas_call(
        lambda *refs: combine_kernel(chips, *refs),
        grid=(1,),
        in_specs=[SCALARS]
        + [whole(META, STRIP)]
        + [whole(*value.shape) for value in (first, keep, decay, log)],
        out_specs=[whole(size + META, STRIP)] * chips,
        out_shape=[jax.ShapeDtypeStruct((size + META, STRIP), F32)] * chips,
        compiler_params=pltpu.CompilerParams(vmem_limit_bytes=SMALL_VMEM),
        cost_estimate=LITTLE,
        name="combine",
    )(place, after, first, keep, decay, log)


def rank_of(place, step):
    chip = place[1] ^ step
    return jnp.where(place[0] == 1, chip, -chip)


def masked_sum(terms):
    total = None
    for hit, value in terms:
        value = jnp.where(hit, value, 0.0)
        total = value if total is None else total + value
    return total


def total_kernel(offset, strips, head_size, place, after_ref, *refs):
    at_refs, out_ref = refs[:-1], refs[-1]
    chips = len(at_refs)
    part = STATE // chips
    size = strips * part
    rank = [rank_of(place, step) for step in range(chips)]
    logs = [ref[size : size + 1, :] for ref in at_refs]
    weights = [
        jnp.exp(masked_sum([(rank[b] > rank[a], logs[b]) for b in range(chips)]))
        for a in range(chips)
    ]
    wide = spread_rows(weights, offset, strips, head_size)
    for strip in range(strips):
        rows = slice(strip * part, (strip + 1) * part)
        total = at_refs[0][rows, :] * wide[0][strip : strip + 1, :]
        for a in range(1, chips):
            total = total + at_refs[a][rows, :] * wide[a][strip : strip + 1, :]
        out_ref[rows, :] = total
    out_ref[size:, :] = jnp.broadcast_to(sum(logs[1:], logs[0]), (META, STRIP))


def group_total(half, head_size, place, after, at):
    strips = (at[0].shape[0] - META) * len(at) // STATE
    return pl.pallas_call(
        lambda *refs: total_kernel(half * strips, strips, head_size, *refs),
        grid=(1,),
        in_specs=[SCALARS, whole(META, STRIP)] + [whole(*at[0].shape)] * len(at),
        out_specs=whole(*at[0].shape),
        out_shape=jax.ShapeDtypeStruct(at[0].shape, F32),
        compiler_params=pltpu.CompilerParams(vmem_limit_bytes=SMALL_VMEM),
        cost_estimate=LITTLE,
        name="group_total",
    )(place, after, *at)


def enter_kernel(chips, offset, strips, head_size, place, after_ref, *refs):
    at_refs, got_refs, out_refs = refs[:chips], refs[chips:-chips], refs[-chips:]
    part = STATE // chips
    size = strips * part
    rank = [rank_of(place, step) for step in range(chips)]
    logs = [ref[size : size + 1, :] for ref in at_refs]
    zero = jnp.zeros_like(logs[0])
    rows_of = []
    passed = zero
    for ref in got_refs:
        rows_of.append(jnp.exp(passed))
        passed = passed + ref[size : size + 1, :]
    for to in range(chips):
        rows_of.append(
            jnp.exp(masked_sum([(rank[m] < rank[to], logs[m]) for m in range(chips)]))
        )
    pairs = [(to, a) for to in range(chips) for a in range(chips) if a != to]
    for to, a in pairs:
        between = masked_sum(
            [((rank[m] > rank[a]) & (rank[m] < rank[to]), logs[m]) for m in range(chips)]
        )
        rows_of.append(jnp.where(rank[a] < rank[to], jnp.exp(between), 0.0))
    wide = spread_rows(rows_of, offset, strips, head_size)
    groups_wide = wide[: len(got_refs)]
    ahead_wide = wide[len(got_refs) : len(got_refs) + chips]
    pair_wide = dict(zip(pairs, wide[len(got_refs) + chips :]))
    for strip in range(strips):
        rows = slice(strip * part, (strip + 1) * part)
        one = slice(strip, strip + 1)
        incoming = jnp.zeros((part, STRIP), F32)
        for ref, weight in zip(got_refs, groups_wide):
            incoming = incoming + ref[rows, :] * weight[one, :]
        values = [ref[rows, :] for ref in at_refs]
        for to in range(chips):
            entering = incoming * ahead_wide[to][one, :]
            for a in range(chips):
                if a != to:
                    entering = entering + values[a] * pair_wide[to, a][one, :]
            out_refs[to][rows, :] = entering


def enter(half, head_size, place, after, at, got):
    chips = len(at)
    strips = (at[0].shape[0] - META) * chips // STATE
    size = strips * (STATE // chips)
    return pl.pallas_call(
        lambda *refs: enter_kernel(chips, half * strips, strips, head_size, *refs),
        grid=(1,),
        in_specs=[SCALARS, whole(META, STRIP)] + [whole(*at[0].shape)] * (chips + len(got)),
        out_specs=[whole(size, STRIP)] * chips,
        out_shape=[jax.ShapeDtypeStruct((size, STRIP), F32)] * chips,
        compiler_params=pltpu.CompilerParams(vmem_limit_bytes=SMALL_VMEM),
        cost_estimate=LITTLE,
        name="enter",
    )(place, after, *at, *got)


def intra_kernel(
    heads, after_ref, x_ref, g_ref, write_ref, read_ref, rates_ref, column_ref, tail_ref, lead_ref,
    dx_ref, db_ref, dc_ref, change_ref, state_ref, back_ref,
    row_ref, scores_ref, mask_ref, pairs_ref, write_t, read_t,
):
    chunk = pl.program_id(0)
    lanes = x_ref.shape[1]
    head_size = lanes * pl.num_programs(0) // heads
    per_chunk = lanes // head_size

    @pl.when(chunk == 0)
    def _():
        rates = rates_ref[...]
        triangle = lower(STRETCH)
        row_ref[...] = dot(rates, triangle, 1, 1, HIGHEST)
        mask_ref[...] = triangle
        scores_ref[...] = dot(read_ref[...], write_ref[...], 1, 1)
        pairs_ref[...] = jnp.zeros_like(pairs_ref)
        change_ref[...] = jnp.zeros_like(change_ref)
        write_t[...] = write_ref[...].astype(F32).T.astype(BF16)
        read_t[...] = read_ref[...].astype(F32).T.astype(BF16)

    columns = pltpu.roll(column_ref[...], STATE - chunk * per_chunk, 1)
    rows = row_ref[pl.ds(pl.multiple_of(chunk * per_chunk, per_chunk), per_chunk), :]
    causal = mask_ref[...] > 0.5
    scores = scores_ref[...]
    pairs = pairs_ref[...]
    low_half = iota((STRETCH, 2 * head_size), 1) < head_size
    adder = head_adder(chunk, head_size, lanes)
    spread = spreader(chunk, heads, head_size, lanes)
    high, low = term_pair(x_ref[...].astype(F32) * dot(tail_ref[...], spread, 1, 0))
    state_ref[...] = dot(write_t[...], high, 1, 0) + dot(write_t[...], low, 1, 0)
    high, low = term_pair(g_ref[...].astype(F32) * dot(lead_ref[...], spread, 1, 0))
    back_ref[...] = dot(read_t[...], high, 1, 0) + dot(read_t[...], low, 1, 0)
    for pair in range(per_chunk // 2):
        strip = slice(pair * 2 * head_size, (pair + 1) * 2 * head_size)
        x = x_ref[:, strip]
        g = g_ref[:, strip]
        ys, dxs = [], []
        for half in range(2):
            head = 2 * pair + half
            gap = columns[:, head : head + 1] - rows[head : head + 1, :]
            decay = jnp.where(causal, jnp.exp(gap), 0.0)
            mixing = (scores * decay).astype(BF16)
            ys.append(dot(mixing, x, 1, 0))
            dxs.append(dot(mixing, g, 0, 0))
            mine = low_half if half == 0 else jnp.logical_not(low_half)
            pairs = pairs + dot(jnp.where(mine, g, jnp.zeros_like(g)), x, 1, 1) * decay
        y = jnp.where(low_half, ys[0], ys[1])
        dx = jnp.where(low_half, dxs[0], dxs[1])
        dx_ref[:, strip] = dx
        change_ref[...] += head_sums(
            g.astype(F32) * y - x.astype(F32) * dx, adder[strip, :]
        )
    pairs_ref[...] = pairs

    @pl.when(chunk == pl.num_programs(0) - 1)
    def _():
        summed = pairs_ref[...].astype(BF16)
        db_ref[...] = dot(summed, read_ref[...], 0, 0)
        dc_ref[...] = dot(summed, write_ref[...], 1, 0)


def intra(after, x, g, write_map, read_map, rates, shared):
    tokens, wide = x.shape
    heads = rates.shape[0]
    return pl.pallas_call(
        lambda *refs: intra_kernel(heads, *refs),
        grid=(wide // LANES,),
        in_specs=[
            whole(META, STRIP),
            lanes_of(tokens),
            lanes_of(tokens),
            whole(tokens, STATE),
            whole(tokens, STATE),
            whole(heads, tokens),
        ]
        + [whole(tokens, STRIP)] * 3,
        out_specs=[lanes_of(tokens)] + [whole(tokens, STATE)] * 3 + [lanes_of(STATE)] * 2,
        out_shape=[
            jax.ShapeDtypeStruct((tokens, wide), F32),
            jax.ShapeDtypeStruct((tokens, STATE), F32),
            jax.ShapeDtypeStruct((tokens, STATE), F32),
            jax.ShapeDtypeStruct((tokens, STATE), F32),
            jax.ShapeDtypeStruct((STATE, wide), F32),
            jax.ShapeDtypeStruct((STATE, wide), F32),
        ],
        scratch_shapes=[
            pltpu.VMEM((heads, tokens), F32),
            pltpu.VMEM((tokens, tokens), F32),
            pltpu.VMEM((tokens, tokens), F32),
            pltpu.VMEM((tokens, tokens), F32),
            pltpu.VMEM((STATE, tokens), BF16),
            pltpu.VMEM((STATE, tokens), BF16),
        ],
        compiler_params=pltpu.CompilerParams(vmem_limit_bytes=BIG_VMEM),
        cost_estimate=LITTLE,
        name="intra",
    )(after, x, g, write_map, read_map, rates, *shared[1:])


def order_kernel(place, *refs):
    pieces, out_ref = refs[:-1], refs[-1]
    size = pieces[0].shape[0]
    for step, ref in enumerate(pieces):
        rows = pl.ds(pl.multiple_of((place[1] ^ step) * size, size), size)
        out_ref[rows, :] = ref[...]


def order(place, pieces):
    shape = (len(pieces) * pieces[0].shape[0], STRIP)
    return pl.pallas_call(
        order_kernel,
        in_specs=[SCALARS] + [whole(*value.shape) for value in pieces],
        out_specs=whole(*shape),
        out_shape=jax.ShapeDtypeStruct(shape, F32),
        compiler_params=pltpu.CompilerParams(vmem_limit_bytes=SMALL_VMEM),
        cost_estimate=LITTLE,
        name="order",
    )(place, *pieces)


def assemble_kernel(
    heads, chips, half, head_size, place, after, first_ref, state_own, back_own, own_ref, far_ref,
    state_ref, back_ref, total_ref,
):
    lanes = state_ref.shape[1]
    strips = lanes // STRIP
    part = STATE // chips
    size = strips * part
    log = first_ref[chips * size : chips * size + 1, :]
    decay = spread_rows([jnp.exp(log)], half * strips, strips, head_size)[0]
    is_first = place[0] == 0
    sums = [None] * strips
    for quarter in range(chips):
        rows = slice(quarter * part, (quarter + 1) * part)
        for strip in range(strips):
            wide = slice(strip * STRIP, (strip + 1) * STRIP)
            here = slice(quarter * size + strip * part, quarter * size + (strip + 1) * part)
            own = own_ref[here, :] * decay[strip : strip + 1, :] + first_ref[here, :]
            far = far_ref[here, :]
            state = jnp.where(is_first, far, own).astype(BF16)
            back = jnp.where(is_first, own, far).astype(BF16)
            state_ref[rows, wide] = state
            back_ref[rows, wide] = back
            gain = state.astype(F32) * back_own[rows, wide]
            gain = gain - back.astype(F32) * state_own[rows, wide]
            sums[strip] = gain if sums[strip] is None else sums[strip] + gain
    row_sum = [
        jnp.broadcast_to(jnp.sum(value, axis=0, keepdims=True), (META, STRIP)) for value in sums
    ]
    total_ref[...] = head_sums(
        jnp.concatenate(row_sum, axis=1), head_adder(half, head_size, lanes)
    )


def assemble(heads, chips, half, place, after, first, state_own, back_own, own, far):
    wide = state_own.shape[1]
    lanes = wide // HALVES
    mine = pl.BlockSpec((STATE, lanes), lambda c: (0, half))
    return pl.pallas_call(
        lambda *refs: assemble_kernel(heads, chips, half, wide // heads, *refs),
        grid=(1,),
        in_specs=[SCALARS, whole(META, STRIP), whole(*first.shape), mine, mine]
        + [whole(*own.shape), whole(*far.shape)],
        out_specs=[whole(STATE, lanes), whole(STATE, lanes), whole(META, STRIP)],
        out_shape=[
            jax.ShapeDtypeStruct((STATE, lanes), BF16),
            jax.ShapeDtypeStruct((STATE, lanes), BF16),
            jax.ShapeDtypeStruct((META, STRIP), F32),
        ],
        compiler_params=pltpu.CompilerParams(vmem_limit_bytes=SMALL_VMEM),
        cost_estimate=LITTLE,
        name="assemble",
    )(place, after, first, state_own, back_own, own, far)


def finish_kernel(
    heads, start, steps, last, x_ref, g_ref, write_ref, read_ref, tail_ref, lead_ref,
    dx_ref, db_ref, dc_ref, change_ref, state_ref, back_ref, *refs,
):
    grad_ref, db_out, dc_out, change_out, db_sum, dc_sum, sum_out = refs[-7:]
    chunk = pl.program_id(0)
    lanes = x_ref.shape[1]
    head_size = lanes * STEPS * HALVES // heads
    wide = start + chunk

    @pl.when(chunk == 0)
    def _():
        sum_out[...] = change_ref[...]
        db_sum[...] = db_ref[...]
        dc_sum[...] = dc_ref[...]

    state = state_ref[...]
    back = back_ref[...]
    spread = spreader(wide, heads, head_size, lanes)
    tail = dot(tail_ref[...], spread, 1, 0)
    lead = dot(lead_ref[...], spread, 1, 0)
    x = x_ref[...].astype(F32)
    g = g_ref[...].astype(F32)
    y = dot(read_ref[...], state, 1, 0) * lead
    dx = dot(write_ref[...], back, 1, 0) * tail
    grad_ref[...] = (dx_ref[...] + dx).astype(BF16)
    adder = head_adder(wide, head_size, lanes)
    sum_out[...] += head_sums(g * y - x * dx, adder)
    db_sum[...] += dot((x * tail).astype(BF16), back, 1, 1)
    dc_sum[...] += dot((g * lead).astype(BF16), state, 1, 1)

    @pl.when(chunk == steps - 1)
    def _():
        db_out[...] = db_sum[...].astype(db_out.dtype)
        dc_out[...] = dc_sum[...].astype(dc_out.dtype)
        if last:
            change_out[...] = dot(sum_out[...], lower(STRETCH), 0, 0, HIGHEST)[:heads, :]
        else:
            change_out[...] = sum_out[...]


def finish(heads, start, steps, x, g, write_map, read_map, shared, dx, sums, state, back, grad):
    tokens, wide = x.shape
    lanes = wide // (STEPS * HALVES)
    strip = pl.BlockSpec((tokens, lanes), lambda c: (0, start + c))
    own = pl.BlockSpec((STATE, lanes), lambda c: (0, start % STEPS + c))
    last = start + steps == STEPS * HALVES
    kind = BF16 if last else F32
    change = (heads, tokens) if last else (tokens, STATE)
    earlier = [] if grad is None else [grad]
    return pl.pallas_call(
        lambda *refs: finish_kernel(heads, start, steps, last, *refs),
        grid=(steps,),
        in_specs=[strip, strip]
        + [whole(tokens, STATE)] * 4
        + [strip]
        + [whole(tokens, STATE)] * 3
        + [own, own]
        + [pl.BlockSpec(memory_space=pl.ANY)] * len(earlier),
        out_specs=[strip] + [whole(tokens, STATE)] * 2 + [whole(*change)],
        out_shape=[
            jax.ShapeDtypeStruct((tokens, wide), BF16),
            jax.ShapeDtypeStruct((tokens, STATE), kind),
            jax.ShapeDtypeStruct((tokens, STATE), kind),
            jax.ShapeDtypeStruct(change, F32),
        ],
        scratch_shapes=[pltpu.VMEM((tokens, STATE), F32)] * 3,
        input_output_aliases={12: 0} if earlier else {},
        compiler_params=pltpu.CompilerParams(vmem_limit_bytes=SMALL_VMEM),
        cost_estimate=LITTLE,
        name="finish",
    )(x, g, write_map, read_map, *shared[2:], dx, *sums, state, back, *earlier)


def add_later_kernel(suffix_ref, later_ref, out_ref):
    heads = out_ref.shape[0]
    out_ref[...] = suffix_ref[...] + later_ref[...].T[:heads, 0:1]


def add_later(suffix, later):
    return pl.pallas_call(
        add_later_kernel,
        in_specs=[whole(*suffix.shape), whole(*later.shape)],
        out_specs=whole(*suffix.shape),
        out_shape=jax.ShapeDtypeStruct(suffix.shape, F32),
        cost_estimate=LITTLE,
        name="add_later",
    )(suffix, later)


def per_device(inputs, out_grad, input_map, output_map, log_decay):
    heads = log_decay.shape[0]
    head_size = inputs.shape[1] // heads
    groups, shards = lax.axis_size("grp"), lax.axis_size("seq")
    chips = shards // 2
    shard, group = lax.axis_index("seq"), lax.axis_index("grp")
    chip, core = shard >> 1, shard & 1
    place = jnp.stack([core, chip, group]).astype(jnp.int32)
    strips = inputs.shape[1] // STRIP // HALVES
    bits = groups.bit_length() - 1
    everyone = [(a, z, c) for a in range(groups) for z in range(chips) for c in range(2)]

    def move(value, target):
        pairs = []
        for a, z, c in everyone:
            to = target(a, z, c)
            if to is not None:
                pairs.append((a * shards + 2 * z + c, to[0] * shards + 2 * to[1] + to[2]))
        return lax.ppermute(value, ("grp", "seq"), pairs)

    def to_core(value):
        return move(value, lambda a, z, c: (a, z, 1 - c))

    def to_chip(value, step):
        return move(value, lambda a, z, c: (a, z ^ step, c)) if step else value

    def to_group(value, step):
        return move(value, lambda a, z, c: (a ^ step, z, c))

    def to_later(value, step):
        def target(a, z, c):
            to = a + step if c == 1 else a - step
            return (to, z, c) if 0 <= to < groups else None

        return move(value, target)

    def hold(value, *tokens):
        return lax.optimization_barrier((value, tokens))[0]

    maps = (inputs, out_grad, input_map, output_map)
    send, keep, decay, *shared = summary(chips, 0, place, *maps, log_decay, None)
    first = [to_core(send)]
    pieces = [combine(chips, place, shared[0], first[0], keep, decay, shared[0])]
    send, keep, decay = summary(chips, 1, place, *maps, log_decay, shared)
    first.append(to_core(send))
    dx, db, dc, change, state_own, back_own = intra(pieces[0][0], *maps, log_decay, shared)
    pieces.append(combine(chips, place, change, first[1], keep, decay, shared[0]))

    def trade(values):
        return [to_chip(value, step) for step, value in enumerate(values)]

    def to_groups(half, token, at):
        total = group_total(half, head_size, place, token, at)
        return [to_later(total, step) for step in range(1, groups)]

    at_a = trade(pieces[0])
    at_b = trade(pieces[1])
    got_a = to_groups(0, pieces[1][0], at_a)
    got_a, at_b = lax.optimization_barrier((got_a, at_b))
    own_a = trade(enter(0, head_size, place, change, at_a, got_a))
    got_b = to_groups(1, change, at_b)
    own_a, got_b = lax.optimization_barrier((own_a, got_b))
    own_b = trade(enter(1, head_size, place, change, at_b, got_b))

    def entering(half, token, own):
        mine = order(place, own)
        return assemble(
            heads, chips, half, place, token, first[half], state_own, back_own, mine, to_core(mine)
        )

    state, back, tally = entering(0, change, own_a)
    grad, *sums = finish(heads, 0, STEPS, *maps, shared, dx, (db, dc, change), state, back, None)
    own_b = hold(own_b, sums[2])
    state, back, tally_b = entering(1, sums[2], own_b)
    tally = tally + tally_b

    def count(later, tally, got, bit, index):
        return later + jnp.where((index >> bit) & 1 == 0, got, 0.0), tally + got

    got = to_core(tally)
    grad, *sums = finish(heads, STEPS, 1, *maps, shared, dx, sums, state, back, grad)
    later, tally = count(0.0, tally, hold(got, sums[2]), 0, core)
    got = to_chip(tally, 1)
    sums = hold(sums, tally)
    grad, *sums = finish(heads, STEPS + 1, 1, *maps, shared, dx, sums, state, back, grad)
    later, tally = count(later, tally, hold(got, sums[2]), 0, chip)
    for bit in range(1, chips.bit_length() - 1):
        later, tally = count(later, tally, to_chip(tally, 1 << bit), bit, chip)
    for bit in range(bits):
        later, tally = count(later, tally, to_group(tally, 1 << bit), bit, group)
    return (grad, sums[0], sums[1], add_later(sums[2], later))


def solution(mesh):
    tokens = P(("grp", "seq"), None)
    in_specs = (tokens, tokens, tokens, tokens, P(None, ("grp", "seq")))
    out_specs = (tokens, tokens, tokens, P(None, ("grp", "seq")))
    return jax.shard_map(
        per_device, mesh=mesh, in_specs=in_specs, out_specs=out_specs, check_vma=False
    )
```

```python
import jax
import jax.numpy as jnp
from jax import lax
from jax.experimental import pallas as pl
from jax.experimental.pallas import tpu as pltpu
from jax.sharding import PartitionSpec as P

STATE = 128
STRETCH = 256
LANES = 512
HALVES = 2
STRIP = 128
META = 8
BIG_VMEM = 56 << 20
SMALL_VMEM = 24 << 20
F32 = jnp.float32
BF16 = jnp.bfloat16
HIGHEST = lax.Precision.HIGHEST


def dot(left, right, left_dim, right_dim, precision=None):
    return lax.dot_general(
        left,
        right,
        (((left_dim,), (right_dim,)), ((), ())),
        precision=precision,
        preferred_element_type=F32,
    )


def iota(shape, dim):
    return lax.broadcasted_iota(jnp.int32, shape, dim)


def lower(length):
    return (iota((length, length), 0) >= iota((length, length), 1)).astype(F32)


def thrice(rates):
    heads, length = rates.shape
    spare = jnp.zeros((STATE - 3 * heads, length), F32)
    return jnp.concatenate([rates, rates, rates, spare], axis=0)


def three_terms(value, heads):
    lane = iota(value.shape, 1)
    first = value.astype(BF16)
    rest = value - first.astype(F32)
    second = rest.astype(BF16)
    third = (rest - second.astype(F32)).astype(BF16)
    return jnp.where(lane < heads, first, jnp.where(lane < 2 * heads, second, third))


def spreader(chunk, heads, head_size, lanes):
    row = iota((STATE, lanes), 0)
    head = (iota((STATE, lanes), 1) + chunk * lanes) // head_size
    hit = (row == head) | (row == head + heads) | (row == head + 2 * heads)
    return hit.astype(F32).astype(BF16)


def head_adder(chunk, head_size, lanes):
    head = (iota((lanes, STATE), 0) + chunk * lanes) // head_size
    return (iota((lanes, STATE), 1) == head).astype(F32).astype(BF16)


def head_sums(value, adder):
    first = value.astype(BF16)
    second = (value - first.astype(F32)).astype(BF16)
    return dot(first, adder, 1, 0) + dot(second, adder, 1, 0)


def decay_terms(rates, heads):
    length = rates.shape[1]
    running = dot(lower(length), thrice(rates), 1, 1, HIGHEST)
    last = running[length - 1 : length, :]
    return (
        running,
        three_terms(jnp.exp(last - running), heads),
        three_terms(jnp.exp(running), heads),
    )


def term_pair(value):
    first = value.astype(BF16)
    return first, (value - first.astype(F32)).astype(BF16)


def lane_spread(per_strip, head_size):
    head = iota((STRIP, STRIP), 0) % per_strip
    return (iota((STRIP, STRIP), 1) // head_size == head).astype(F32)


def spread_rows(rows, offset, strips, head_size):
    per_strip = STRIP // head_size
    lane = iota((strips, STRIP), 1)
    row = iota((strips, STRIP), 0) + offset
    picked = [jnp.where(lane // per_strip == row, value, 0.0) for value in rows]
    stacked = jnp.concatenate(picked, axis=0) if len(picked) > 1 else picked[0]
    wide = dot(stacked, lane_spread(per_strip, head_size), 1, 0, HIGHEST)
    return [wide[i * strips : (i + 1) * strips, :] for i in range(len(rows))]


def whole(*shape):
    return pl.BlockSpec(shape, lambda *_: (0,) * len(shape))


def lanes_of(rows):
    return pl.BlockSpec((rows, LANES), lambda c: (0, c))


def half_lanes(rows, lanes, half, steps):
    return pl.BlockSpec((rows, lanes), lambda c: (0, half * steps + c))


LITTLE = pl.CostEstimate(flops=1, bytes_accessed=1, transcendentals=0)
SCALARS = pl.BlockSpec(memory_space=pltpu.SMEM)
STEPS = 2


def summary_kernel(heads, chips, half, place, x_ref, g_ref, write_ref, read_ref, *refs):
    chunk = pl.program_id(0)
    lanes = x_ref.shape[1]
    strips = lanes // STRIP
    half_strips = strips * STEPS
    head_size = lanes * STEPS * HALVES // heads
    part = STATE // chips
    if half == 0:
        rates_ref, send_ref, keep_ref, decay_ref, log_ref, run_ref, tail_ref, lead_ref = refs[:8]
    else:
        log_ref, tail_ref, lead_ref, send_ref, keep_ref, decay_ref = refs[:6]
    write_t, read_t = refs[-2:]

    @pl.when(chunk == 0)
    def _():
        if half == 0:
            running, tail, lead = decay_terms(rates_ref[...], heads)
            run_ref[...] = running
            tail_ref[...] = tail
            lead_ref[...] = lead
            log_ref[...] = jnp.broadcast_to(running[STRETCH - 1 :, :], (META, STRIP))
        send_ref[pl.ds(half_strips * STATE, META), :] = log_ref[...]
        write_t[...] = write_ref[...].astype(F32).T.astype(BF16)
        read_t[...] = read_ref[...].astype(F32).T.astype(BF16)

    spread = spreader(half * STEPS + chunk, heads, head_size, lanes)
    tail = dot(tail_ref[...], spread, 1, 0)
    lead = dot(lead_ref[...], spread, 1, 0)
    inputs_tail = (x_ref[...].astype(F32) * tail).astype(BF16)
    grads_lead = (g_ref[...].astype(F32) * lead).astype(BF16)
    state = dot(write_t[...], inputs_tail, 1, 0)
    back = dot(read_t[...], grads_lead, 1, 0)
    first = place[0] == 0
    send = jnp.where(first, state, back)
    keep = jnp.where(first, back, state)
    for strip in range(strips):
        at = chunk * strips + strip
        wide = slice(strip * STRIP, (strip + 1) * STRIP)
        decay_ref[pl.ds(at, 1), :] = lead[STRETCH - 1 :, wide]
        for quarter in range(chips):
            rows = pl.ds(pl.multiple_of((quarter * half_strips + at) * part, part), part)
            mine = slice(quarter * part, (quarter + 1) * part)
            send_ref[rows, :] = send[mine, wide]
            keep_ref[rows, :] = keep[mine, wide]


def summary(chips, half, place, x, g, write_map, read_map, rates, shared):
    tokens, wide = x.shape
    heads = rates.shape[0]
    lanes = wide // (STEPS * HALVES)
    strips = wide // STRIP // HALVES
    terms = [
        jax.ShapeDtypeStruct((META, STRIP), F32),
        jax.ShapeDtypeStruct((tokens, STRIP), F32),
        jax.ShapeDtypeStruct((tokens, STRIP), BF16),
        jax.ShapeDtypeStruct((tokens, STRIP), BF16),
    ]
    out_shape = [
        jax.ShapeDtypeStruct((strips * STATE + META, STRIP), F32),
        jax.ShapeDtypeStruct((strips * STATE, STRIP), F32),
        jax.ShapeDtypeStruct((strips, STRIP), F32),
    ]
    if half == 0:
        extra = [rates]
        out_shape = out_shape + terms
    else:
        extra = [shared[0], shared[2], shared[3]]
    return pl.pallas_call(
        lambda *refs: summary_kernel(heads, chips, half, *refs),
        grid=(STEPS,),
        in_specs=[
            SCALARS,
            half_lanes(tokens, lanes, half, STEPS),
            half_lanes(tokens, lanes, half, STEPS),
            whole(tokens, STATE),
            whole(tokens, STATE),
        ]
        + [whole(*value.shape) for value in extra],
        out_specs=[whole(*out.shape) for out in out_shape],
        out_shape=out_shape,
        scratch_shapes=[
            pltpu.VMEM((STATE, tokens), BF16),
            pltpu.VMEM((STATE, tokens), BF16),
        ],
        compiler_params=pltpu.CompilerParams(vmem_limit_bytes=BIG_VMEM),
        cost_estimate=LITTLE,
        name="summary",
    )(place, x, g, write_map, read_map, *extra)


def combine_kernel(chips, place, first_ref, keep_ref, decay_ref, log_ref, mine_ref, send_ref):
    strips = decay_ref.shape[0]
    part = STATE // chips
    size = mine_ref.shape[0]
    bit = place[1] & 1
    for base, out_ref in ((bit * size, mine_ref), ((1 - bit) * size, send_ref)):
        for strip in range(strips):
            decay = decay_ref[strip : strip + 1, :]
            for at in range(strip * part, size, strips * part):
                rows = pl.ds(pl.multiple_of(base + at, part), part)
                out_ref[at : at + part, :] = first_ref[rows, :] * decay + keep_ref[rows, :]
    send_ref[size:, :] = first_ref[2 * size :, :] + log_ref[...]


def halves(size):
    return (
        [whole(size, STRIP), whole(size + META, STRIP)],
        [
            jax.ShapeDtypeStruct((size, STRIP), F32),
            jax.ShapeDtypeStruct((size + META, STRIP), F32),
        ],
    )


def combine(chips, place, first, keep, decay, log):
    out_specs, out_shape = halves(keep.shape[0] // 2)
    return pl.pallas_call(
        lambda *refs: combine_kernel(chips, *refs),
        in_specs=[SCALARS] + [whole(*value.shape) for value in (first, keep, decay, log)],
        out_specs=out_specs,
        out_shape=out_shape,
        compiler_params=pltpu.CompilerParams(vmem_limit_bytes=SMALL_VMEM),
        cost_estimate=LITTLE,
        name="combine",
    )(place, first, keep, decay, log)


def is_ahead(place, level):
    return ((place[1] >> level) & 1) == place[0]


def tail_block(value):
    return pl.BlockSpec((META, STRIP), lambda c: (value.shape[0] // META - 1, 0))


def up_kernel(level, last, part, offset, strips, head_size, place, mine_ref, log_ref, got_ref, *outs):
    size = mine_ref.shape[0]
    ahead = is_ahead(place, level)
    mine_log, got_log = log_ref[0:1, :], got_ref[size : size + 1, :]
    mine_wide, got_wide = spread_rows(
        [jnp.where(ahead, 1.0, jnp.exp(got_log)), jnp.where(ahead, jnp.exp(mine_log), 1.0)],
        offset,
        strips,
        head_size,
    )
    bit = (place[1] >> (level + 1)) & 1
    half = size if last else size // 2
    targets = ((0, outs[0]),) if last else ((bit * half, outs[0]), ((1 - bit) * half, outs[1]))
    for base, out_ref in targets:
        for strip in range(strips):
            one = slice(strip, strip + 1)
            for at in range(strip * part, half, strips * part):
                rows = slice(at, at + part)
                if not last:
                    rows = pl.ds(pl.multiple_of(base + at, part), part)
                out_ref[at : at + part, :] = (
                    mine_ref[rows, :] * mine_wide[one, :] + got_ref[rows, :] * got_wide[one, :]
                )
    outs[-1][half:, :] = jnp.broadcast_to(mine_log + got_log, (META, STRIP))


def up(level, chips, half, strips, head_size, place, mine, send, got):
    size = mine.shape[0]
    last = 2 << level == chips
    out_specs, out_shape = halves(size if last else size // 2)
    if last:
        out_specs, out_shape = out_specs[1:], out_shape[1:]
    return pl.pallas_call(
        lambda *refs: up_kernel(
            level, last, STATE // chips, half * strips, strips, head_size, *refs
        ),
        grid=(1,),
        in_specs=[SCALARS, whole(size, STRIP), tail_block(send), whole(size + META, STRIP)],
        out_specs=out_specs,
        out_shape=out_shape,
        compiler_params=pltpu.CompilerParams(vmem_limit_bytes=SMALL_VMEM),
        cost_estimate=LITTLE,
        name="up",
    )(place, mine, send, got)


def down_kernel(level, top, part, offset, strips, head_size, place, mine_ref, log_ref, got_ref, *refs):
    sources, (here_ref, there_ref) = refs[:-2], refs[-2:]
    size = mine_ref.shape[0]
    ahead = is_ahead(place, level)
    rows_of = [
        jnp.where(ahead, jnp.exp(got_ref[size : size + 1, :]), 1.0),
        jnp.where(ahead, 1.0, jnp.exp(log_ref[0:1, :])),
    ]
    if top:
        passed = jnp.zeros_like(rows_of[0])
        for ref in sources:
            rows_of.append(jnp.exp(passed))
            passed = passed + ref[size : size + 1, :]
        bases, length = (0,), size
    else:
        length = size // 2
        bit = (place[1] >> (level + 1)) & 1
        bases = (bit * length, (1 - bit) * length)
    here_wide, there_wide, *group_wide = spread_rows(rows_of, offset, strips, head_size)
    for index, base in enumerate(bases):
        for strip in range(strips):
            one = slice(strip, strip + 1)
            for at in range(strip * part, length, strips * part):
                rows = slice(at, at + part)
                if top:
                    entering = sources[0][rows, :] * group_wide[0][one, :]
                    for ref, wide in zip(sources[1:], group_wide[1:]):
                        entering = entering + ref[rows, :] * wide[one, :]
                else:
                    entering = sources[index][rows, :]
                    rows = pl.ds(pl.multiple_of(base + at, part), part)
                got = jnp.where(ahead, got_ref[rows, :], 0.0)
                mine = jnp.where(ahead, 0.0, mine_ref[rows, :])
                here_ref[rows, :] = entering * here_wide[one, :] + got
                there_ref[rows, :] = entering * there_wide[one, :] + mine


def down(level, chips, half, strips, head_size, place, mine, send, got, sources):
    size = mine.shape[0]
    top = 2 << level == chips
    return pl.pallas_call(
        lambda *refs: down_kernel(
            level, top, STATE // chips, half * strips, strips, head_size, *refs
        ),
        grid=(1,),
        in_specs=[SCALARS, whole(size, STRIP), tail_block(send), whole(size + META, STRIP)]
        + [whole(*value.shape) for value in sources],
        out_specs=[whole(size, STRIP)] * 2,
        out_shape=[jax.ShapeDtypeStruct((size, STRIP), F32)] * 2,
        compiler_params=pltpu.CompilerParams(vmem_limit_bytes=SMALL_VMEM),
        cost_estimate=LITTLE,
        name="down",
    )(place, mine, send, got, *sources)


def intra_kernel(
    heads, head_size, start, last,
    after_ref, x_ref, g_ref, write_ref, read_ref, rates_ref, column_ref, tail_ref, lead_ref, *refs,
):
    dx_ref, state_ref, back_ref, change_ref, *sums, row_ref, scores_ref, mask_ref, pairs_ref, \
        write_t, read_t = refs[5 if start else 0 :]
    step = pl.program_id(0)
    chunk = start + step
    lanes = x_ref.shape[1]
    per_chunk = lanes // head_size

    @pl.when(step == 0)
    def _():
        rates = rates_ref[...]
        triangle = lower(STRETCH)
        row_ref[...] = dot(rates, triangle, 1, 1, HIGHEST)
        mask_ref[...] = triangle
        scores_ref[...] = dot(read_ref[...], write_ref[...], 1, 1)
        pairs_ref[...] = refs[4][...] if start else jnp.zeros_like(pairs_ref)
        change_ref[...] = refs[3][...] if start else jnp.zeros_like(change_ref)
        write_t[...] = write_ref[...].astype(F32).T.astype(BF16)
        read_t[...] = read_ref[...].astype(F32).T.astype(BF16)

    columns = pltpu.roll(column_ref[...], STATE - chunk * per_chunk, 1)
    rows = row_ref[pl.ds(pl.multiple_of(chunk * per_chunk, per_chunk), per_chunk), :]
    causal = mask_ref[...] > 0.5
    scores = scores_ref[...]
    pairs = pairs_ref[...]
    low_half = iota((STRETCH, 2 * head_size), 1) < head_size
    adder = head_adder(chunk, head_size, lanes)
    spread = spreader(chunk, heads, head_size, lanes)
    high, low = term_pair(x_ref[...].astype(F32) * dot(tail_ref[...], spread, 1, 0))
    state_ref[...] = dot(write_t[...], high, 1, 0) + dot(write_t[...], low, 1, 0)
    high, low = term_pair(g_ref[...].astype(F32) * dot(lead_ref[...], spread, 1, 0))
    back_ref[...] = dot(read_t[...], high, 1, 0) + dot(read_t[...], low, 1, 0)
    for pair in range(per_chunk // 2):
        strip = slice(pair * 2 * head_size, (pair + 1) * 2 * head_size)
        x = x_ref[:, strip]
        g = g_ref[:, strip]
        ys, dxs = [], []
        for half in range(2):
            head = 2 * pair + half
            gap = columns[:, head : head + 1] - rows[head : head + 1, :]
            decay = jnp.where(causal, jnp.exp(gap), 0.0)
            mixing = (scores * decay).astype(BF16)
            ys.append(dot(mixing, x, 1, 0))
            dxs.append(dot(mixing, g, 0, 0))
            mine = low_half if half == 0 else jnp.logical_not(low_half)
            pairs = pairs + dot(jnp.where(mine, g, jnp.zeros_like(g)), x, 1, 1) * decay
        y = jnp.where(low_half, ys[0], ys[1])
        dx = jnp.where(low_half, dxs[0], dxs[1])
        dx_ref[:, strip] = dx
        change_ref[...] += head_sums(
            g.astype(F32) * y - x.astype(F32) * dx, adder[strip, :]
        )
    pairs_ref[...] = pairs

    @pl.when(step == pl.num_programs(0) - 1)
    def _():
        if last:
            summed = pairs_ref[...].astype(BF16)
            sums[0][...] = dot(summed, read_ref[...], 0, 0)
            sums[1][...] = dot(summed, write_ref[...], 1, 0)
        else:
            sums[0][...] = pairs_ref[...]


def intra(start, steps, after, x, g, write_map, read_map, rates, shared, earlier):
    tokens, wide = x.shape
    heads = rates.shape[0]
    last = (start + steps) * LANES == wide
    lanes = lambda rows: pl.BlockSpec((rows, LANES), lambda c: (0, start + c))
    anywhere = pl.BlockSpec(memory_space=pl.ANY)
    sums = [(tokens, STATE)] * 2 if last else [(tokens, tokens)]
    return pl.pallas_call(
        lambda *refs: intra_kernel(heads, wide // heads, start, last, *refs),
        grid=(steps,),
        in_specs=[
            whole(META, STRIP),
            lanes(tokens),
            lanes(tokens),
            whole(tokens, STATE),
            whole(tokens, STATE),
            whole(heads, tokens),
        ]
        + [whole(tokens, STRIP)] * 3
        + ([anywhere] * 3 + [whole(tokens, STATE), whole(tokens, tokens)] if earlier else []),
        out_specs=[lanes(tokens), lanes(STATE), lanes(STATE), whole(tokens, STATE)]
        + [whole(*shape) for shape in sums],
        out_shape=[
            jax.ShapeDtypeStruct((tokens, wide), F32),
            jax.ShapeDtypeStruct((STATE, wide), F32),
            jax.ShapeDtypeStruct((STATE, wide), F32),
            jax.ShapeDtypeStruct((tokens, STATE), F32),
        ]
        + [jax.ShapeDtypeStruct(shape, F32) for shape in sums],
        scratch_shapes=[
            pltpu.VMEM((heads, tokens), F32),
            pltpu.VMEM((tokens, tokens), F32),
            pltpu.VMEM((tokens, tokens), F32),
            pltpu.VMEM((tokens, tokens), F32),
            pltpu.VMEM((STATE, tokens), BF16),
            pltpu.VMEM((STATE, tokens), BF16),
        ],
        input_output_aliases={9: 0, 10: 1, 11: 2} if earlier else {},
        compiler_params=pltpu.CompilerParams(vmem_limit_bytes=SMALL_VMEM),
        cost_estimate=LITTLE,
        name="intra",
    )(after, x, g, write_map, read_map, rates, *shared[1:], *earlier)


def order_kernel(place, here_ref, got_ref, out_ref):
    size = here_ref.shape[0]
    bit = place[1] & 1
    out_ref[pl.ds(pl.multiple_of(bit * size, size), size), :] = here_ref[...]
    out_ref[pl.ds(pl.multiple_of((1 - bit) * size, size), size), :] = got_ref[...]


def order(place, here, got):
    shape = (2 * here.shape[0], STRIP)
    return pl.pallas_call(
        order_kernel,
        in_specs=[SCALARS, whole(*here.shape), whole(*got.shape)],
        out_specs=whole(*shape),
        out_shape=jax.ShapeDtypeStruct(shape, F32),
        compiler_params=pltpu.CompilerParams(vmem_limit_bytes=SMALL_VMEM),
        cost_estimate=LITTLE,
        name="order",
    )(place, here, got)


def assemble_kernel(
    heads, chips, half, head_size, place, after, first_ref, state_own, back_own, own_ref, far_ref,
    state_ref, back_ref, total_ref,
):
    lanes = state_ref.shape[1]
    strips = lanes // STRIP
    part = STATE // chips
    size = strips * part
    log = first_ref[chips * size : chips * size + 1, :]
    decay = spread_rows([jnp.exp(log)], half * strips, strips, head_size)[0]
    is_first = place[0] == 0
    sums = [None] * strips
    for quarter in range(chips):
        rows = slice(quarter * part, (quarter + 1) * part)
        for strip in range(strips):
            wide = slice(strip * STRIP, (strip + 1) * STRIP)
            here = slice(quarter * size + strip * part, quarter * size + (strip + 1) * part)
            own = own_ref[here, :] * decay[strip : strip + 1, :] + first_ref[here, :]
            far = far_ref[here, :]
            state = jnp.where(is_first, far, own).astype(BF16)
            back = jnp.where(is_first, own, far).astype(BF16)
            state_ref[rows, wide] = state
            back_ref[rows, wide] = back
            gain = state.astype(F32) * back_own[rows, wide]
            gain = gain - back.astype(F32) * state_own[rows, wide]
            sums[strip] = gain if sums[strip] is None else sums[strip] + gain
    row_sum = [
        jnp.broadcast_to(jnp.sum(value, axis=0, keepdims=True), (META, STRIP)) for value in sums
    ]
    total_ref[...] = head_sums(
        jnp.concatenate(row_sum, axis=1), head_adder(half, head_size, lanes)
    )


def assemble(heads, chips, half, place, after, first, state_own, back_own, own, far):
    wide = state_own.shape[1]
    lanes = wide // HALVES
    mine = pl.BlockSpec((STATE, lanes), lambda c: (0, half))
    return pl.pallas_call(
        lambda *refs: assemble_kernel(heads, chips, half, wide // heads, *refs),
        grid=(1,),
        in_specs=[SCALARS, whole(META, STRIP), whole(*first.shape), mine, mine]
        + [whole(*own.shape), whole(*far.shape)],
        out_specs=[whole(STATE, lanes), whole(STATE, lanes), whole(META, STRIP)],
        out_shape=[
            jax.ShapeDtypeStruct((STATE, lanes), BF16),
            jax.ShapeDtypeStruct((STATE, lanes), BF16),
            jax.ShapeDtypeStruct((META, STRIP), F32),
        ],
        compiler_params=pltpu.CompilerParams(vmem_limit_bytes=SMALL_VMEM),
        cost_estimate=LITTLE,
        name="assemble",
    )(place, after, first, state_own, back_own, own, far)


def finish_kernel(
    heads, start, steps, last, x_ref, g_ref, write_ref, read_ref, tail_ref, lead_ref,
    dx_ref, db_ref, dc_ref, change_ref, state_ref, back_ref, *refs,
):
    grad_ref, db_out, dc_out, change_out, db_sum, dc_sum, sum_out = refs[-7:]
    chunk = pl.program_id(0)
    lanes = x_ref.shape[1]
    head_size = lanes * STEPS * HALVES // heads
    wide = start + chunk

    @pl.when(chunk == 0)
    def _():
        sum_out[...] = change_ref[...]
        db_sum[...] = db_ref[...]
        dc_sum[...] = dc_ref[...]

    state = state_ref[...]
    back = back_ref[...]
    spread = spreader(wide, heads, head_size, lanes)
    tail = dot(tail_ref[...], spread, 1, 0)
    lead = dot(lead_ref[...], spread, 1, 0)
    x = x_ref[...].astype(F32)
    g = g_ref[...].astype(F32)
    y = dot(read_ref[...], state, 1, 0) * lead
    dx = dot(write_ref[...], back, 1, 0) * tail
    grad_ref[...] = (dx_ref[...] + dx).astype(BF16)
    adder = head_adder(wide, head_size, lanes)
    sum_out[...] += head_sums(g * y - x * dx, adder)
    db_sum[...] += dot((x * tail).astype(BF16), back, 1, 1)
    dc_sum[...] += dot((g * lead).astype(BF16), state, 1, 1)

    @pl.when(chunk == steps - 1)
    def _():
        db_out[...] = db_sum[...].astype(db_out.dtype)
        dc_out[...] = dc_sum[...].astype(dc_out.dtype)
        if last:
            change_out[...] = dot(sum_out[...], lower(STRETCH), 0, 0, HIGHEST)[:heads, :]
        else:
            change_out[...] = sum_out[...]


def finish(heads, start, steps, x, g, write_map, read_map, shared, dx, sums, state, back, grad):
    tokens, wide = x.shape
    lanes = wide // (STEPS * HALVES)
    strip = pl.BlockSpec((tokens, lanes), lambda c: (0, start + c))
    own = pl.BlockSpec((STATE, lanes), lambda c: (0, start % STEPS + c))
    last = start + steps == STEPS * HALVES
    kind = BF16 if last else F32
    change = (heads, tokens) if last else (tokens, STATE)
    earlier = [] if grad is None else [grad]
    return pl.pallas_call(
        lambda *refs: finish_kernel(heads, start, steps, last, *refs),
        grid=(steps,),
        in_specs=[strip, strip]
        + [whole(tokens, STATE)] * 4
        + [strip]
        + [whole(tokens, STATE)] * 3
        + [own, own]
        + [pl.BlockSpec(memory_space=pl.ANY)] * len(earlier),
        out_specs=[strip] + [whole(tokens, STATE)] * 2 + [whole(*change)],
        out_shape=[
            jax.ShapeDtypeStruct((tokens, wide), BF16),
            jax.ShapeDtypeStruct((tokens, STATE), kind),
            jax.ShapeDtypeStruct((tokens, STATE), kind),
            jax.ShapeDtypeStruct(change, F32),
        ],
        scratch_shapes=[pltpu.VMEM((tokens, STATE), F32)] * 3,
        input_output_aliases={12: 0} if earlier else {},
        compiler_params=pltpu.CompilerParams(vmem_limit_bytes=SMALL_VMEM),
        cost_estimate=LITTLE,
        name="finish",
    )(x, g, write_map, read_map, *shared[2:], dx, *sums, state, back, *earlier)


def add_later_kernel(suffix_ref, later_ref, out_ref):
    heads = out_ref.shape[0]
    out_ref[...] = suffix_ref[...] + later_ref[...].T[:heads, 0:1]


def add_later(suffix, later):
    return pl.pallas_call(
        add_later_kernel,
        in_specs=[whole(*suffix.shape), whole(*later.shape)],
        out_specs=whole(*suffix.shape),
        out_shape=jax.ShapeDtypeStruct(suffix.shape, F32),
        cost_estimate=LITTLE,
        name="add_later",
    )(suffix, later)


def per_device(inputs, out_grad, input_map, output_map, log_decay):
    heads = log_decay.shape[0]
    head_size = inputs.shape[1] // heads
    groups, shards = lax.axis_size("grp"), lax.axis_size("seq")
    chips = shards // 2
    shard, group = lax.axis_index("seq"), lax.axis_index("grp")
    chip, core = shard >> 1, shard & 1
    place = jnp.stack([core, chip, group]).astype(jnp.int32)
    strips = inputs.shape[1] // STRIP // HALVES
    bits = groups.bit_length() - 1
    everyone = [(a, z, c) for a in range(groups) for z in range(chips) for c in range(2)]

    def move(value, target):
        pairs = []
        for a, z, c in everyone:
            to = target(a, z, c)
            if to is not None:
                pairs.append((a * shards + 2 * z + c, to[0] * shards + 2 * to[1] + to[2]))
        return lax.ppermute(value, ("grp", "seq"), pairs)

    def to_core(value):
        return move(value, lambda a, z, c: (a, z, 1 - c))

    def to_chip(value, step):
        return move(value, lambda a, z, c: (a, z ^ step, c)) if step else value

    def to_group(value, step):
        return move(value, lambda a, z, c: (a ^ step, z, c))

    def to_later(value, step):
        def target(a, z, c):
            to = a + step if c == 1 else a - step
            return (to, z, c) if 0 <= to < groups else None

        return move(value, target)

    def hold(value, *tokens):
        return lax.optimization_barrier((value, tokens))[0]

    maps = (inputs, out_grad, input_map, output_map)
    send, keep, decay, *shared = summary(chips, 0, place, *maps, log_decay, None)
    first = [to_core(send)]
    kept, decays = [keep], [decay]
    send, keep, decay = summary(chips, 1, place, *maps, log_decay, shared)
    first.append(to_core(send))
    kept.append(keep)
    decays.append(decay)

    levels = chips.bit_length() - 1
    held = [[], []]
    waiting = [None, None]

    def advance(half, step):
        fixed = (chips, half, strips, head_size, place)
        if step == 0:
            mine, send = combine(
                chips, place, first[half], kept[half], decays[half], shared[0]
            )
        elif step < levels:
            held[half][-1] += (waiting[half],)
            mine, send = up(step - 1, *fixed, *held[half][-1])
        elif step == levels:
            held[half][-1] += (waiting[half],)
            (send,) = up(step - 1, *fixed, *held[half][-1])
            waiting[half] = [to_later(send, far) for far in range(1, groups)]
            return send
        elif step <= 2 * levels:
            level = 2 * levels - step
            if level < levels - 1:
                waiting[half] = (held[half][level + 1], waiting[half])
            mine, send = down(level, *fixed, *held[half][level], waiting[half])
            held[half][level] = mine
            waiting[half] = to_chip(send, 1 << level)
            return send
        else:
            send = order(place, held[half][0], waiting[half])
            held[half] = send
            waiting[half] = to_core(send)
            return send
        held[half].append((mine, send))
        waiting[half] = to_chip(send, 1 << step)
        return send

    def entering(half, token):
        return assemble(
            heads, chips, half, place, token, first[half], state_own, back_own,
            held[half], waiting[half],
        )

    chunks = inputs.shape[1] // LANES
    rounds = 2 * levels + 2
    block, ready = (), 0
    for step in range(rounds):
        token = advance(0, step)
        if step:
            advance(1, step - 1)
        if step < 3:
            more = pl.cdiv(chunks - ready, 3 - step)
            block = intra(ready, more, token, *maps, log_decay, shared, block)
            ready += more
            waiting[0], waiting[1], first[1], block = lax.optimization_barrier(
                (waiting[0], waiting[1], first[1], block)
            )
        elif step < rounds - 1:
            waiting[0], waiting[1] = lax.optimization_barrier((waiting[0], waiting[1]))
    dx, state_own, back_own, change, db, dc = block
    state, back, tally = entering(0, change)
    grad, *sums = finish(heads, 0, STEPS, *maps, shared, dx, (db, dc, change), state, back, None)
    waiting[1] = hold(waiting[1], sums[2])
    advance(1, rounds - 1)
    state, back, tally_b = entering(1, sums[2])
    tally = tally + tally_b

    def count(later, tally, got, bit, index):
        return later + jnp.where((index >> bit) & 1 == 0, got, 0.0), tally + got

    got = to_core(tally)
    grad, *sums = finish(heads, STEPS, 1, *maps, shared, dx, sums, state, back, grad)
    later, tally = count(0.0, tally, hold(got, sums[2]), 0, core)
    got = to_chip(tally, 1)
    sums = hold(sums, tally)
    grad, *sums = finish(heads, STEPS + 1, 1, *maps, shared, dx, sums, state, back, grad)
    later, tally = count(later, tally, hold(got, sums[2]), 0, chip)
    for bit in range(1, chips.bit_length() - 1):
        later, tally = count(later, tally, to_chip(tally, 1 << bit), bit, chip)
    for bit in range(bits):
        later, tally = count(later, tally, to_group(tally, 1 << bit), bit, group)
    return (grad, sums[0], sums[1], add_later(sums[2], later))


def solution(mesh):
    tokens = P(("grp", "seq"), None)
    in_specs = (tokens, tokens, tokens, tokens, P(None, ("grp", "seq")))
    out_specs = (tokens, tokens, tokens, P(None, ("grp", "seq")))
    return jax.shard_map(
        per_device, mesh=mesh, in_specs=in_specs, out_specs=out_specs, check_vma=False
    )
```

```python
import jax
import jax.numpy as jnp
from jax import lax
from jax.experimental import pallas as pl
from jax.experimental.pallas import tpu as pltpu
from jax.sharding import PartitionSpec as P

STATE = 128
STRETCH = 256
LANES = 512
HALVES = 2
STRIP = 128
META = 8
BIG_VMEM = 56 << 20
SMALL_VMEM = 24 << 20
F32 = jnp.float32
BF16 = jnp.bfloat16
HIGHEST = lax.Precision.HIGHEST


def dot(left, right, left_dim, right_dim, precision=None):
    return lax.dot_general(
        left,
        right,
        (((left_dim,), (right_dim,)), ((), ())),
        precision=precision,
        preferred_element_type=F32,
    )


def iota(shape, dim):
    return lax.broadcasted_iota(jnp.int32, shape, dim)


def lower(length):
    return (iota((length, length), 0) >= iota((length, length), 1)).astype(F32)


def thrice(rates):
    heads, length = rates.shape
    spare = jnp.zeros((STATE - 3 * heads, length), F32)
    return jnp.concatenate([rates, rates, rates, spare], axis=0)


def three_terms(value, heads):
    lane = iota(value.shape, 1)
    first = value.astype(BF16)
    rest = value - first.astype(F32)
    second = rest.astype(BF16)
    third = (rest - second.astype(F32)).astype(BF16)
    return jnp.where(lane < heads, first, jnp.where(lane < 2 * heads, second, third))


def spreader(chunk, heads, head_size, lanes):
    row = iota((STATE, lanes), 0)
    head = (iota((STATE, lanes), 1) + chunk * lanes) // head_size
    hit = (row == head) | (row == head + heads) | (row == head + 2 * heads)
    return hit.astype(F32).astype(BF16)


def head_adder(chunk, head_size, lanes):
    head = (iota((lanes, STATE), 0) + chunk * lanes) // head_size
    return (iota((lanes, STATE), 1) == head).astype(F32).astype(BF16)


def head_sums(value, adder):
    first = value.astype(BF16)
    second = (value - first.astype(F32)).astype(BF16)
    return dot(first, adder, 1, 0) + dot(second, adder, 1, 0)


def decay_terms(rates, heads):
    length = rates.shape[1]
    running = dot(lower(length), thrice(rates), 1, 1, HIGHEST)
    last = running[length - 1 : length, :]
    return (
        running,
        three_terms(jnp.exp(last - running), heads),
        three_terms(jnp.exp(running), heads),
    )


def term_pair(value):
    first = value.astype(BF16)
    return first, (value - first.astype(F32)).astype(BF16)


def lane_spread(per_strip, head_size):
    head = iota((STRIP, STRIP), 0) % per_strip
    return (iota((STRIP, STRIP), 1) // head_size == head).astype(F32)


def spread_rows(rows, offset, strips, head_size):
    per_strip = STRIP // head_size
    lane = iota((strips, STRIP), 1)
    row = iota((strips, STRIP), 0) + offset
    picked = [jnp.where(lane // per_strip == row, value, 0.0) for value in rows]
    stacked = jnp.concatenate(picked, axis=0) if len(picked) > 1 else picked[0]
    wide = dot(stacked, lane_spread(per_strip, head_size), 1, 0, HIGHEST)
    return [wide[i * strips : (i + 1) * strips, :] for i in range(len(rows))]


def whole(*shape):
    return pl.BlockSpec(shape, lambda *_: (0,) * len(shape))


def lanes_of(rows):
    return pl.BlockSpec((rows, LANES), lambda c: (0, c))


def half_lanes(rows, lanes, half, steps):
    return pl.BlockSpec((rows, lanes), lambda c: (0, half * steps + c))


LITTLE = pl.CostEstimate(flops=1, bytes_accessed=1, transcendentals=0)
SCALARS = pl.BlockSpec(memory_space=pltpu.SMEM)
STEPS = 2


def summary_kernel(heads, chips, half, place, x_ref, g_ref, write_ref, read_ref, *refs):
    chunk = pl.program_id(0)
    lanes = x_ref.shape[1]
    strips = lanes // STRIP
    half_strips = strips * STEPS
    head_size = lanes * STEPS * HALVES // heads
    part = STATE // chips
    if half == 0:
        rates_ref, send_ref, keep_ref, decay_ref, log_ref, run_ref, tail_ref, lead_ref = refs[:8]
    else:
        log_ref, tail_ref, lead_ref, send_ref, keep_ref, decay_ref = refs[:6]
    write_t, read_t = refs[-2:]

    @pl.when(chunk == 0)
    def _():
        if half == 0:
            running, tail, lead = decay_terms(rates_ref[...], heads)
            run_ref[...] = running
            tail_ref[...] = tail
            lead_ref[...] = lead
            log_ref[...] = jnp.broadcast_to(running[STRETCH - 1 :, :], (META, STRIP))
        send_ref[pl.ds(half_strips * STATE, META), :] = log_ref[...]
        write_t[...] = write_ref[...].astype(F32).T.astype(BF16)
        read_t[...] = read_ref[...].astype(F32).T.astype(BF16)

    spread = spreader(half * STEPS + chunk, heads, head_size, lanes)
    tail = dot(tail_ref[...], spread, 1, 0)
    lead = dot(lead_ref[...], spread, 1, 0)
    inputs_tail = (x_ref[...].astype(F32) * tail).astype(BF16)
    grads_lead = (g_ref[...].astype(F32) * lead).astype(BF16)
    state = dot(write_t[...], inputs_tail, 1, 0)
    back = dot(read_t[...], grads_lead, 1, 0)
    first = place[0] == 0
    send = jnp.where(first, state, back)
    keep = jnp.where(first, back, state)
    for strip in range(strips):
        at = chunk * strips + strip
        wide = slice(strip * STRIP, (strip + 1) * STRIP)
        decay_ref[pl.ds(at, 1), :] = lead[STRETCH - 1 :, wide]
        for quarter in range(chips):
            rows = pl.ds(pl.multiple_of((quarter * half_strips + at) * part, part), part)
            mine = slice(quarter * part, (quarter + 1) * part)
            send_ref[rows, :] = send[mine, wide]
            keep_ref[rows, :] = keep[mine, wide]


def summary(chips, half, place, x, g, write_map, read_map, rates, shared):
    tokens, wide = x.shape
    heads = rates.shape[0]
    lanes = wide // (STEPS * HALVES)
    strips = wide // STRIP // HALVES
    terms = [
        jax.ShapeDtypeStruct((META, STRIP), F32),
        jax.ShapeDtypeStruct((tokens, STRIP), F32),
        jax.ShapeDtypeStruct((tokens, STRIP), BF16),
        jax.ShapeDtypeStruct((tokens, STRIP), BF16),
    ]
    out_shape = [
        jax.ShapeDtypeStruct((strips * STATE + META, STRIP), F32),
        jax.ShapeDtypeStruct((strips * STATE, STRIP), F32),
        jax.ShapeDtypeStruct((strips, STRIP), F32),
    ]
    if half == 0:
        extra = [rates]
        out_shape = out_shape + terms
    else:
        extra = [shared[0], shared[2], shared[3]]
    return pl.pallas_call(
        lambda *refs: summary_kernel(heads, chips, half, *refs),
        grid=(STEPS,),
        in_specs=[
            SCALARS,
            half_lanes(tokens, lanes, half, STEPS),
            half_lanes(tokens, lanes, half, STEPS),
            whole(tokens, STATE),
            whole(tokens, STATE),
        ]
        + [whole(*value.shape) for value in extra],
        out_specs=[whole(*out.shape) for out in out_shape],
        out_shape=out_shape,
        scratch_shapes=[
            pltpu.VMEM((STATE, tokens), BF16),
            pltpu.VMEM((STATE, tokens), BF16),
        ],
        compiler_params=pltpu.CompilerParams(vmem_limit_bytes=BIG_VMEM),
        cost_estimate=LITTLE,
        name="summary",
    )(place, x, g, write_map, read_map, *extra)


def combine_kernel(chips, place, first_ref, keep_ref, decay_ref, log_ref, mine_ref, send_ref):
    strips = decay_ref.shape[0]
    part = STATE // chips
    size = mine_ref.shape[0]
    bit = place[1] & 1
    for base, out_ref in ((bit * size, mine_ref), ((1 - bit) * size, send_ref)):
        for strip in range(strips):
            decay = decay_ref[strip : strip + 1, :]
            for at in range(strip * part, size, strips * part):
                rows = pl.ds(pl.multiple_of(base + at, part), part)
                out_ref[at : at + part, :] = first_ref[rows, :] * decay + keep_ref[rows, :]
    send_ref[size:, :] = first_ref[2 * size :, :] + log_ref[...]


def halves(size):
    return (
        [whole(size, STRIP), whole(size + META, STRIP)],
        [
            jax.ShapeDtypeStruct((size, STRIP), F32),
            jax.ShapeDtypeStruct((size + META, STRIP), F32),
        ],
    )


def combine(chips, place, first, keep, decay, log):
    out_specs, out_shape = halves(keep.shape[0] // 2)
    return pl.pallas_call(
        lambda *refs: combine_kernel(chips, *refs),
        in_specs=[SCALARS] + [whole(*value.shape) for value in (first, keep, decay, log)],
        out_specs=out_specs,
        out_shape=out_shape,
        compiler_params=pltpu.CompilerParams(vmem_limit_bytes=SMALL_VMEM),
        cost_estimate=LITTLE,
        name="combine",
    )(place, first, keep, decay, log)


def is_ahead(place, level):
    return ((place[1] >> level) & 1) == place[0]


def tail_block(value):
    return pl.BlockSpec((META, STRIP), lambda c: (value.shape[0] // META - 1, 0))


def up_kernel(level, last, part, offset, strips, head_size, place, mine_ref, log_ref, got_ref, *outs):
    size = mine_ref.shape[0]
    ahead = is_ahead(place, level)
    mine_log, got_log = log_ref[0:1, :], got_ref[size : size + 1, :]
    mine_wide, got_wide = spread_rows(
        [jnp.where(ahead, 1.0, jnp.exp(got_log)), jnp.where(ahead, jnp.exp(mine_log), 1.0)],
        offset,
        strips,
        head_size,
    )
    bit = (place[1] >> (level + 1)) & 1
    half = size if last else size // 2
    targets = ((0, outs[0]),) if last else ((bit * half, outs[0]), ((1 - bit) * half, outs[1]))
    for base, out_ref in targets:
        for strip in range(strips):
            one = slice(strip, strip + 1)
            for at in range(strip * part, half, strips * part):
                rows = slice(at, at + part)
                if not last:
                    rows = pl.ds(pl.multiple_of(base + at, part), part)
                out_ref[at : at + part, :] = (
                    mine_ref[rows, :] * mine_wide[one, :] + got_ref[rows, :] * got_wide[one, :]
                )
    outs[-1][half:, :] = jnp.broadcast_to(mine_log + got_log, (META, STRIP))


def up(level, chips, half, strips, head_size, place, mine, send, got):
    size = mine.shape[0]
    last = 2 << level == chips
    out_specs, out_shape = halves(size if last else size // 2)
    if last:
        out_specs, out_shape = out_specs[1:], out_shape[1:]
    return pl.pallas_call(
        lambda *refs: up_kernel(
            level, last, STATE // chips, half * strips, strips, head_size, *refs
        ),
        grid=(1,),
        in_specs=[SCALARS, whole(size, STRIP), tail_block(send), whole(size + META, STRIP)],
        out_specs=out_specs,
        out_shape=out_shape,
        compiler_params=pltpu.CompilerParams(vmem_limit_bytes=SMALL_VMEM),
        cost_estimate=LITTLE,
        name="up",
    )(place, mine, send, got)


def down_kernel(level, top, part, offset, strips, head_size, place, mine_ref, log_ref, got_ref, *refs):
    sources, (here_ref, there_ref) = refs[:-2], refs[-2:]
    size = mine_ref.shape[0]
    ahead = is_ahead(place, level)
    rows_of = [
        jnp.where(ahead, jnp.exp(got_ref[size : size + 1, :]), 1.0),
        jnp.where(ahead, 1.0, jnp.exp(log_ref[0:1, :])),
    ]
    if top:
        passed = jnp.zeros_like(rows_of[0])
        for ref in sources:
            rows_of.append(jnp.exp(passed))
            passed = passed + ref[size : size + 1, :]
        bases, length = (0,), size
    else:
        length = size // 2
        bit = (place[1] >> (level + 1)) & 1
        bases = (bit * length, (1 - bit) * length)
    here_wide, there_wide, *group_wide = spread_rows(rows_of, offset, strips, head_size)
    for index, base in enumerate(bases):
        for strip in range(strips):
            one = slice(strip, strip + 1)
            for at in range(strip * part, length, strips * part):
                rows = slice(at, at + part)
                if top:
                    entering = sources[0][rows, :] * group_wide[0][one, :]
                    for ref, wide in zip(sources[1:], group_wide[1:]):
                        entering = entering + ref[rows, :] * wide[one, :]
                else:
                    entering = sources[index][rows, :]
                    rows = pl.ds(pl.multiple_of(base + at, part), part)
                got = jnp.where(ahead, got_ref[rows, :], 0.0)
                mine = jnp.where(ahead, 0.0, mine_ref[rows, :])
                here_ref[rows, :] = entering * here_wide[one, :] + got
                there_ref[rows, :] = entering * there_wide[one, :] + mine


def down(level, chips, half, strips, head_size, place, mine, send, got, sources):
    size = mine.shape[0]
    top = 2 << level == chips
    return pl.pallas_call(
        lambda *refs: down_kernel(
            level, top, STATE // chips, half * strips, strips, head_size, *refs
        ),
        grid=(1,),
        in_specs=[SCALARS, whole(size, STRIP), tail_block(send), whole(size + META, STRIP)]
        + [whole(*value.shape) for value in sources],
        out_specs=[whole(size, STRIP)] * 2,
        out_shape=[jax.ShapeDtypeStruct((size, STRIP), F32)] * 2,
        compiler_params=pltpu.CompilerParams(vmem_limit_bytes=SMALL_VMEM),
        cost_estimate=LITTLE,
        name="down",
    )(place, mine, send, got, *sources)


def intra_kernel(
    heads, head_size, start, last,
    place, after_ref, x_ref, g_ref, write_ref, read_ref, rates_ref, column_ref, tail_ref, lead_ref, *refs,
):
    dx_ref, mine_ref, other_ref, change_ref, *sums, row_ref, scores_ref, mask_ref, pairs_ref, \
        write_t, read_t = refs[5 if start else 0 :]
    step = pl.program_id(0)
    chunk = start + step
    lanes = x_ref.shape[1]
    per_chunk = lanes // head_size

    @pl.when(step == 0)
    def _():
        rates = rates_ref[...]
        triangle = lower(STRETCH)
        row_ref[...] = dot(rates, triangle, 1, 1, HIGHEST)
        mask_ref[...] = triangle
        scores_ref[...] = dot(read_ref[...], write_ref[...], 1, 1)
        pairs_ref[...] = refs[4][...] if start else jnp.zeros_like(pairs_ref)
        change_ref[...] = refs[3][...] if start else jnp.zeros_like(change_ref)
        write_t[...] = write_ref[...].astype(F32).T.astype(BF16)
        read_t[...] = read_ref[...].astype(F32).T.astype(BF16)

    columns = pltpu.roll(column_ref[...], STATE - chunk * per_chunk, 1)
    rows = row_ref[pl.ds(pl.multiple_of(chunk * per_chunk, per_chunk), per_chunk), :]
    causal = mask_ref[...] > 0.5
    scores = scores_ref[...]
    pairs = pairs_ref[...]
    low_half = iota((STRETCH, 2 * head_size), 1) < head_size
    adder = head_adder(chunk, head_size, lanes)
    spread = spreader(chunk, heads, head_size, lanes)
    high, low = term_pair(x_ref[...].astype(F32) * dot(tail_ref[...], spread, 1, 0))
    state = dot(write_t[...], high, 1, 0) + dot(write_t[...], low, 1, 0)
    high, low = term_pair(g_ref[...].astype(F32) * dot(lead_ref[...], spread, 1, 0))
    back = dot(read_t[...], high, 1, 0) + dot(read_t[...], low, 1, 0)
    is_first = place[0] == 0
    mine_ref[...] = jnp.where(is_first, state, back)
    other_ref[...] = jnp.where(is_first, back, state)
    for pair in range(per_chunk // 2):
        strip = slice(pair * 2 * head_size, (pair + 1) * 2 * head_size)
        x = x_ref[:, strip]
        g = g_ref[:, strip]
        ys, dxs = [], []
        for half in range(2):
            head = 2 * pair + half
            gap = columns[:, head : head + 1] - rows[head : head + 1, :]
            decay = jnp.where(causal, jnp.exp(gap), 0.0)
            mixing = (scores * decay).astype(BF16)
            ys.append(dot(mixing, x, 1, 0))
            dxs.append(dot(mixing, g, 0, 0))
            mine = low_half if half == 0 else jnp.logical_not(low_half)
            pairs = pairs + dot(jnp.where(mine, g, jnp.zeros_like(g)), x, 1, 1) * decay
        y = jnp.where(low_half, ys[0], ys[1])
        dx = jnp.where(low_half, dxs[0], dxs[1])
        dx_ref[:, strip] = dx
        change_ref[...] += head_sums(
            g.astype(F32) * y - x.astype(F32) * dx, adder[strip, :]
        )
    pairs_ref[...] = pairs

    @pl.when(step == pl.num_programs(0) - 1)
    def _():
        if last:
            summed = pairs_ref[...].astype(BF16)
            sums[0][...] = dot(summed, read_ref[...], 0, 0)
            sums[1][...] = dot(summed, write_ref[...], 1, 0)
        else:
            sums[0][...] = pairs_ref[...]


def intra(start, steps, place, after, x, g, write_map, read_map, rates, shared, earlier):
    tokens, wide = x.shape
    heads = rates.shape[0]
    last = (start + steps) * LANES == wide
    lanes = lambda rows: pl.BlockSpec((rows, LANES), lambda c: (0, start + c))
    anywhere = pl.BlockSpec(memory_space=pl.ANY)
    sums = [(tokens, STATE)] * 2 if last else [(tokens, tokens)]
    return pl.pallas_call(
        lambda *refs: intra_kernel(heads, wide // heads, start, last, *refs),
        grid=(steps,),
        in_specs=[
            SCALARS,
            whole(META, STRIP),
            lanes(tokens),
            lanes(tokens),
            whole(tokens, STATE),
            whole(tokens, STATE),
            whole(heads, tokens),
        ]
        + [whole(tokens, STRIP)] * 3
        + ([anywhere] * 3 + [whole(tokens, STATE), whole(tokens, tokens)] if earlier else []),
        out_specs=[lanes(tokens), lanes(STATE), lanes(STATE), whole(tokens, STATE)]
        + [whole(*shape) for shape in sums],
        out_shape=[
            jax.ShapeDtypeStruct((tokens, wide), F32),
            jax.ShapeDtypeStruct((STATE, wide), F32),
            jax.ShapeDtypeStruct((STATE, wide), F32),
            jax.ShapeDtypeStruct((tokens, STATE), F32),
        ]
        + [jax.ShapeDtypeStruct(shape, F32) for shape in sums],
        scratch_shapes=[
            pltpu.VMEM((heads, tokens), F32),
            pltpu.VMEM((tokens, tokens), F32),
            pltpu.VMEM((tokens, tokens), F32),
            pltpu.VMEM((tokens, tokens), F32),
            pltpu.VMEM((STATE, tokens), BF16),
            pltpu.VMEM((STATE, tokens), BF16),
        ],
        input_output_aliases={10: 0, 11: 1, 12: 2} if earlier else {},
        compiler_params=pltpu.CompilerParams(vmem_limit_bytes=SMALL_VMEM),
        cost_estimate=LITTLE,
        name="intra",
    )(place, after, x, g, write_map, read_map, rates, *shared[1:], *earlier)


def order_kernel(place, here_ref, got_ref, out_ref):
    size = here_ref.shape[0]
    bit = place[1] & 1
    out_ref[pl.ds(pl.multiple_of(bit * size, size), size), :] = here_ref[...]
    out_ref[pl.ds(pl.multiple_of((1 - bit) * size, size), size), :] = got_ref[...]


def order(place, here, got):
    shape = (2 * here.shape[0], STRIP)
    return pl.pallas_call(
        order_kernel,
        in_specs=[SCALARS, whole(*here.shape), whole(*got.shape)],
        out_specs=whole(*shape),
        out_shape=jax.ShapeDtypeStruct(shape, F32),
        compiler_params=pltpu.CompilerParams(vmem_limit_bytes=SMALL_VMEM),
        cost_estimate=LITTLE,
        name="order",
    )(place, here, got)


def tally_kernel(
    heads, chips, half, head_size, place, first_ref, enter_ref, mine_ref, other_ref, out_ref
):
    lanes = mine_ref.shape[1]
    strips = lanes // STRIP
    part = STATE // chips
    size = strips * part
    log = first_ref[chips * size : chips * size + 1, :]
    decay = spread_rows([jnp.exp(log)], half * strips, strips, head_size)[0]
    sums = [[], []]
    for strip in range(strips):
        wide = slice(strip * STRIP, (strip + 1) * STRIP)
        near_sum = far_sum = None
        for quarter in range(chips):
            rows = slice(quarter * part, (quarter + 1) * part)
            here = slice(quarter * size + strip * part, quarter * size + (strip + 1) * part)
            far = enter_ref[here, :]
            near = far * decay[strip : strip + 1, :] + first_ref[here, :]
            near = near.astype(BF16).astype(F32) * mine_ref[rows, wide]
            far = far.astype(BF16).astype(F32) * other_ref[rows, wide]
            near_sum = near if near_sum is None else near_sum + near
            far_sum = far if far_sum is None else far_sum + far
        for found, value in zip(sums, (near_sum, far_sum)):
            found.append(jnp.sum(value, axis=0, keepdims=True))
    near, far = (jnp.concatenate(found, axis=1) for found in sums)
    sign = jnp.where(place[0] == 1, 1.0, -1.0)
    second = jnp.where(place[0] == 1, near, far) * sign
    chip = (near + far) * sign
    both = jnp.where(iota((META, lanes), 0) < META // 2, chip, second)
    out_ref[...] = head_sums(both, head_adder(half, head_size, lanes))


def tally(heads, chips, half, place, first, entering, mine, other):
    wide = mine.shape[1]
    ours = pl.BlockSpec((STATE, wide // HALVES), lambda c: (0, half))
    return pl.pallas_call(
        lambda *refs: tally_kernel(heads, chips, half, wide // heads, *refs),
        grid=(1,),
        in_specs=[SCALARS, whole(*first.shape), whole(*entering.shape), ours, ours],
        out_specs=whole(META, STRIP),
        out_shape=jax.ShapeDtypeStruct((META, STRIP), F32),
        compiler_params=pltpu.CompilerParams(vmem_limit_bytes=SMALL_VMEM),
        cost_estimate=LITTLE,
        name="tally",
    )(place, first, entering, mine, other)


def assemble_kernel(
    chips, half, head_size, place, after, first_ref, own_ref, far_ref, state_ref, back_ref
):
    strips = state_ref.shape[1] // STRIP
    part = STATE // chips
    size = strips * part
    log = first_ref[chips * size : chips * size + 1, :]
    decay = spread_rows([jnp.exp(log)], half * strips, strips, head_size)[0]
    is_first = place[0] == 0
    for quarter in range(chips):
        rows = slice(quarter * part, (quarter + 1) * part)
        for strip in range(strips):
            wide = slice(strip * STRIP, (strip + 1) * STRIP)
            here = slice(quarter * size + strip * part, quarter * size + (strip + 1) * part)
            own = own_ref[here, :] * decay[strip : strip + 1, :] + first_ref[here, :]
            far = far_ref[here, :]
            state_ref[rows, wide] = jnp.where(is_first, far, own).astype(BF16)
            back_ref[rows, wide] = jnp.where(is_first, own, far).astype(BF16)


def assemble(heads, chips, half, place, after, first, own, far):
    strips = own.shape[0] // STATE
    lanes = strips * STRIP
    return pl.pallas_call(
        lambda *refs: assemble_kernel(chips, half, lanes * HALVES // heads, *refs),
        grid=(1,),
        in_specs=[SCALARS, whole(META, STRIP)]
        + [whole(*value.shape) for value in (first, own, far)],
        out_specs=[whole(STATE, lanes), whole(STATE, lanes)],
        out_shape=[jax.ShapeDtypeStruct((STATE, lanes), BF16)] * 2,
        compiler_params=pltpu.CompilerParams(vmem_limit_bytes=SMALL_VMEM),
        cost_estimate=LITTLE,
        name="assemble",
    )(place, after, first, own, far)


def finish_kernel(
    heads, start, steps, last, x_ref, g_ref, write_ref, read_ref, tail_ref, lead_ref,
    dx_ref, db_ref, dc_ref, change_ref, state_ref, back_ref, *refs,
):
    grad_ref, db_out, dc_out, change_out, db_sum, dc_sum, sum_out = refs[-7:]
    chunk = pl.program_id(0)
    lanes = x_ref.shape[1]
    head_size = lanes * STEPS * HALVES // heads
    wide = start + chunk

    @pl.when(chunk == 0)
    def _():
        sum_out[...] = change_ref[...]
        db_sum[...] = db_ref[...]
        dc_sum[...] = dc_ref[...]

    state = state_ref[...]
    back = back_ref[...]
    spread = spreader(wide, heads, head_size, lanes)
    tail = dot(tail_ref[...], spread, 1, 0)
    lead = dot(lead_ref[...], spread, 1, 0)
    x = x_ref[...].astype(F32)
    g = g_ref[...].astype(F32)
    y = dot(read_ref[...], state, 1, 0) * lead
    dx = dot(write_ref[...], back, 1, 0) * tail
    grad_ref[...] = (dx_ref[...] + dx).astype(BF16)
    adder = head_adder(wide, head_size, lanes)
    sum_out[...] += head_sums(g * y - x * dx, adder)
    db_sum[...] += dot((x * tail).astype(BF16), back, 1, 1)
    dc_sum[...] += dot((g * lead).astype(BF16), state, 1, 1)

    @pl.when(chunk == steps - 1)
    def _():
        db_out[...] = db_sum[...].astype(db_out.dtype)
        dc_out[...] = dc_sum[...].astype(dc_out.dtype)
        if last:
            change_out[...] = dot(sum_out[...], lower(STRETCH), 0, 0, HIGHEST)[:heads, :]
        else:
            change_out[...] = sum_out[...]


def finish(heads, start, steps, x, g, write_map, read_map, shared, dx, sums, state, back, grad):
    tokens, wide = x.shape
    lanes = wide // (STEPS * HALVES)
    strip = pl.BlockSpec((tokens, lanes), lambda c: (0, start + c))
    own = pl.BlockSpec((STATE, lanes), lambda c: (0, start % STEPS + c))
    last = start + steps == STEPS * HALVES
    kind = BF16 if last else F32
    change = (heads, tokens) if last else (tokens, STATE)
    earlier = [] if grad is None else [grad]
    return pl.pallas_call(
        lambda *refs: finish_kernel(heads, start, steps, last, *refs),
        grid=(steps,),
        in_specs=[strip, strip]
        + [whole(tokens, STATE)] * 4
        + [strip]
        + [whole(tokens, STATE)] * 3
        + [own, own]
        + [pl.BlockSpec(memory_space=pl.ANY)] * len(earlier),
        out_specs=[strip] + [whole(tokens, STATE)] * 2 + [whole(*change)],
        out_shape=[
            jax.ShapeDtypeStruct((tokens, wide), BF16),
            jax.ShapeDtypeStruct((tokens, STATE), kind),
            jax.ShapeDtypeStruct((tokens, STATE), kind),
            jax.ShapeDtypeStruct(change, F32),
        ],
        scratch_shapes=[pltpu.VMEM((tokens, STATE), F32)] * 3,
        input_output_aliases={12: 0} if earlier else {},
        compiler_params=pltpu.CompilerParams(vmem_limit_bytes=SMALL_VMEM),
        cost_estimate=LITTLE,
        name="finish",
    )(x, g, write_map, read_map, *shared[2:], dx, *sums, state, back, *earlier)


def add_later_kernel(place, suffix_ref, mine_ref, other_ref, out_ref):
    heads = out_ref.shape[0]
    later = (mine_ref[...] + other_ref[...]).T[:heads, :]
    second = later[:, META // 2 : META // 2 + 1]
    out_ref[...] = suffix_ref[...] + later[:, 0:1] + jnp.where(place[0] == 0, second, 0.0)


def add_later(place, suffix, mine, other):
    return pl.pallas_call(
        add_later_kernel,
        in_specs=[SCALARS] + [whole(*value.shape) for value in (suffix, mine, other)],
        out_specs=whole(*suffix.shape),
        out_shape=jax.ShapeDtypeStruct(suffix.shape, F32),
        cost_estimate=LITTLE,
        name="add_later",
    )(place, suffix, mine, other)


def per_device(inputs, out_grad, input_map, output_map, log_decay):
    heads = log_decay.shape[0]
    head_size = inputs.shape[1] // heads
    groups, shards = lax.axis_size("grp"), lax.axis_size("seq")
    chips = shards // 2
    shard, group = lax.axis_index("seq"), lax.axis_index("grp")
    chip, core = shard >> 1, shard & 1
    place = jnp.stack([core, chip, group]).astype(jnp.int32)
    strips = inputs.shape[1] // STRIP // HALVES
    everyone = [(a, z, c) for a in range(groups) for z in range(chips) for c in range(2)]

    def move(value, target):
        pairs = []
        for a, z, c in everyone:
            to = target(a, z, c)
            if to is not None:
                pairs.append((a * shards + 2 * z + c, to[0] * shards + 2 * to[1] + to[2]))
        return lax.ppermute(value, ("grp", "seq"), pairs)

    def to_core(value):
        return move(value, lambda a, z, c: (a, z, 1 - c))

    def to_chip(value, step):
        return move(value, lambda a, z, c: (a, z ^ step, c)) if step else value

    def to_earlier(value, step):
        return move(value, lambda a, z, c: (a - step, z, c) if a >= step else None)

    def to_later(value, step):
        def target(a, z, c):
            to = a + step if c == 1 else a - step
            return (to, z, c) if 0 <= to < groups else None

        return move(value, target)

    def hold(value, *tokens):
        return lax.optimization_barrier((value, tokens))[0]

    maps = (inputs, out_grad, input_map, output_map)
    send, keep, decay, *shared = summary(chips, 0, place, *maps, log_decay, None)
    first = [to_core(send)]
    kept, decays = [keep], [decay]
    send, keep, decay = summary(chips, 1, place, *maps, log_decay, shared)
    first.append(to_core(send))
    kept.append(keep)
    decays.append(decay)

    levels = chips.bit_length() - 1
    held = [[], []]
    waiting = [None, None]

    def advance(half, step):
        fixed = (chips, half, strips, head_size, place)
        if step == 0:
            mine, send = combine(
                chips, place, first[half], kept[half], decays[half], shared[0]
            )
        elif step < levels:
            held[half][-1] += (waiting[half],)
            mine, send = up(step - 1, *fixed, *held[half][-1])
        elif step == levels:
            held[half][-1] += (waiting[half],)
            (send,) = up(step - 1, *fixed, *held[half][-1])
            waiting[half] = [to_later(send, far) for far in range(1, groups)]
            return send
        elif step <= 2 * levels:
            level = 2 * levels - step
            if level < levels - 1:
                waiting[half] = (held[half][level + 1], waiting[half])
            mine, send = down(level, *fixed, *held[half][level], waiting[half])
            held[half][level] = mine
            waiting[half] = to_chip(send, 1 << level)
            return send
        else:
            send = order(place, held[half][0], waiting[half])
            held[half] = send
            waiting[half] = to_core(send)
            return send
        held[half].append((mine, send))
        waiting[half] = to_chip(send, 1 << step)
        return send

    def entering(half, token):
        return assemble(
            heads, chips, half, place, token, first[half], held[half], waiting[half]
        )

    chunks = inputs.shape[1] // LANES
    rounds = 2 * levels + 2
    block, ready = (), 0
    for step in range(rounds):
        if step == rounds - 1:
            waiting[0] = hold(waiting[0], advance(1, step - 1))
            advance(0, step)
            continue
        token = advance(0, step)
        if step == levels + 1:
            waiting[1] = hold(waiting[1], token)
        if step:
            advance(1, step - 1)
        if step < 3:
            more = pl.cdiv(chunks - ready, 3 - step)
            block = intra(ready, more, place, token, *maps, log_decay, shared, block)
            ready += more
            waiting[0], waiting[1], first[1], block = lax.optimization_barrier(
                (waiting[0], waiting[1], first[1], block)
            )
        else:
            waiting[0], waiting[1] = lax.optimization_barrier((waiting[0], waiting[1]))
    dx, mine, other, change, db, dc = block
    other = to_core(other)

    def count(half):
        return tally(heads, chips, half, place, first[half], held[half], mine, other)

    state, back = entering(0, change)
    grad, *sums = finish(heads, 0, STEPS, *maps, shared, dx, (db, dc, change), state, back, None)
    counted = count(0)
    waiting[1] = hold(waiting[1], sums[2], counted)
    advance(1, rounds - 1)
    counted = counted + count(1)

    reached = [to_chip(counted, step) for step in range(1, chips)]
    state, back = entering(1, counted)
    grad, *sums = finish(heads, STEPS, 1, *maps, shared, dx, sums, state, back, grad)
    reached = hold(reached, sums[2])
    later, whole_group = jnp.zeros_like(counted), counted
    for step, value in enumerate(reached, 1):
        later = later + jnp.where((chip ^ step) > chip, value, 0.0)
        whole_group = whole_group + value
    reached = [to_earlier(whole_group, step) for step in range(1, groups)]
    sums = hold(sums, whole_group)
    grad, *sums = finish(heads, STEPS + 1, 1, *maps, shared, dx, sums, state, back, grad)
    reached = hold(reached, sums[2])
    later = sum(reached, later)
    row = lax.broadcasted_iota(jnp.int32, later.shape, 0)
    counted = jnp.where(row < META // 2, later, counted)
    return (grad, sums[0], sums[1], add_later(place, sums[2], counted, to_core(counted)))


def solution(mesh):
    tokens = P(("grp", "seq"), None)
    in_specs = (tokens, tokens, tokens, tokens, P(None, ("grp", "seq")))
    out_specs = (tokens, tokens, tokens, P(None, ("grp", "seq")))
    return jax.shard_map(
        per_device, mesh=mesh, in_specs=in_specs, out_specs=out_specs, check_vma=False
    )
```

```python
import jax
import jax.numpy as jnp
from jax import lax
from jax.experimental import pallas as pl
from jax.experimental.pallas import tpu as pltpu
from jax.sharding import PartitionSpec as P

STATE = 128
STRETCH = 256
LANES = 512
HALVES = 2
STRIP = 128
META = 8
BIG_VMEM = 56 << 20
SMALL_VMEM = 24 << 20
F32 = jnp.float32
BF16 = jnp.bfloat16
HIGHEST = lax.Precision.HIGHEST


def dot(left, right, left_dim, right_dim, precision=None):
    return lax.dot_general(
        left,
        right,
        (((left_dim,), (right_dim,)), ((), ())),
        precision=precision,
        preferred_element_type=F32,
    )


def iota(shape, dim):
    return lax.broadcasted_iota(jnp.int32, shape, dim)


def lower(length):
    return (iota((length, length), 0) >= iota((length, length), 1)).astype(F32)


def thrice(rates):
    heads, length = rates.shape
    spare = jnp.zeros((STATE - 3 * heads, length), F32)
    return jnp.concatenate([rates, rates, rates, spare], axis=0)


def three_terms(value, heads):
    lane = iota(value.shape, 1)
    first = value.astype(BF16)
    rest = value - first.astype(F32)
    second = rest.astype(BF16)
    third = (rest - second.astype(F32)).astype(BF16)
    return jnp.where(lane < heads, first, jnp.where(lane < 2 * heads, second, third))


def spreader(chunk, heads, head_size, lanes):
    row = iota((STATE, lanes), 0)
    head = (iota((STATE, lanes), 1) + chunk * lanes) // head_size
    hit = (row == head) | (row == head + heads) | (row == head + 2 * heads)
    return hit.astype(F32).astype(BF16)


def head_adder(chunk, head_size, lanes):
    head = (iota((lanes, STATE), 0) + chunk * lanes) // head_size
    return (iota((lanes, STATE), 1) == head).astype(F32).astype(BF16)


def head_sums(value, adder):
    first = value.astype(BF16)
    second = (value - first.astype(F32)).astype(BF16)
    return dot(first, adder, 1, 0) + dot(second, adder, 1, 0)


def decay_terms(rates, heads):
    length = rates.shape[1]
    running = dot(lower(length), thrice(rates), 1, 1, HIGHEST)
    last = running[length - 1 : length, :]
    return (
        running,
        three_terms(jnp.exp(last - running), heads),
        three_terms(jnp.exp(running), heads),
    )


def term_pair(value):
    first = value.astype(BF16)
    return first, (value - first.astype(F32)).astype(BF16)


def lane_spread(per_strip, head_size):
    head = iota((STRIP, STRIP), 0) % per_strip
    return (iota((STRIP, STRIP), 1) // head_size == head).astype(F32)


def spread_rows(rows, offset, strips, head_size):
    per_strip = STRIP // head_size
    lane = iota((strips, STRIP), 1)
    row = iota((strips, STRIP), 0) + offset
    picked = [jnp.where(lane // per_strip == row, value, 0.0) for value in rows]
    stacked = jnp.concatenate(picked, axis=0) if len(picked) > 1 else picked[0]
    wide = dot(stacked, lane_spread(per_strip, head_size), 1, 0, HIGHEST)
    return [wide[i * strips : (i + 1) * strips, :] for i in range(len(rows))]


def whole(*shape):
    return pl.BlockSpec(shape, lambda *_: (0,) * len(shape))


def lanes_of(rows):
    return pl.BlockSpec((rows, LANES), lambda c: (0, c))


def half_lanes(rows, lanes, half, steps):
    return pl.BlockSpec((rows, lanes), lambda c: (0, half * steps + c))


LITTLE = pl.CostEstimate(flops=1, bytes_accessed=1, transcendentals=0)
SCALARS = pl.BlockSpec(memory_space=pltpu.SMEM)
STEPS = 2


def summary_kernel(heads, chips, half, place, x_ref, g_ref, write_ref, read_ref, *refs):
    chunk = pl.program_id(0)
    lanes = x_ref.shape[1]
    strips = lanes // STRIP
    half_strips = strips * STEPS
    head_size = lanes * STEPS * HALVES // heads
    part = STATE // chips
    if half == 0:
        rates_ref, send_ref, keep_ref, decay_ref, log_ref, run_ref, tail_ref, lead_ref = refs[:8]
    else:
        log_ref, tail_ref, lead_ref, send_ref, keep_ref, decay_ref = refs[:6]
    write_t, read_t = refs[-2:]

    @pl.when(chunk == 0)
    def _():
        if half == 0:
            running, tail, lead = decay_terms(rates_ref[...], heads)
            run_ref[...] = running
            tail_ref[...] = tail
            lead_ref[...] = lead
            log_ref[...] = jnp.broadcast_to(running[STRETCH - 1 :, :], (META, STRIP))
        send_ref[pl.ds(half_strips * STATE, META), :] = log_ref[...]
        write_t[...] = write_ref[...].astype(F32).T.astype(BF16)
        read_t[...] = read_ref[...].astype(F32).T.astype(BF16)

    spread = spreader(half * STEPS + chunk, heads, head_size, lanes)
    tail = dot(tail_ref[...], spread, 1, 0)
    lead = dot(lead_ref[...], spread, 1, 0)
    inputs_tail = (x_ref[...].astype(F32) * tail).astype(BF16)
    grads_lead = (g_ref[...].astype(F32) * lead).astype(BF16)
    state = dot(write_t[...], inputs_tail, 1, 0)
    back = dot(read_t[...], grads_lead, 1, 0)
    first = place[0] == 0
    send = jnp.where(first, state, back)
    keep = jnp.where(first, back, state)
    for strip in range(strips):
        at = chunk * strips + strip
        wide = slice(strip * STRIP, (strip + 1) * STRIP)
        decay_ref[pl.ds(at, 1), :] = lead[STRETCH - 1 :, wide]
        for quarter in range(chips):
            rows = pl.ds(pl.multiple_of((quarter * half_strips + at) * part, part), part)
            mine = slice(quarter * part, (quarter + 1) * part)
            send_ref[rows, :] = send[mine, wide]
            keep_ref[rows, :] = keep[mine, wide]


def summary(chips, half, place, x, g, write_map, read_map, rates, shared):
    tokens, wide = x.shape
    heads = rates.shape[0]
    lanes = wide // (STEPS * HALVES)
    strips = wide // STRIP // HALVES
    terms = [
        jax.ShapeDtypeStruct((META, STRIP), F32),
        jax.ShapeDtypeStruct((tokens, STRIP), F32),
        jax.ShapeDtypeStruct((tokens, STRIP), BF16),
        jax.ShapeDtypeStruct((tokens, STRIP), BF16),
    ]
    out_shape = [
        jax.ShapeDtypeStruct((strips * STATE + META, STRIP), F32),
        jax.ShapeDtypeStruct((strips * STATE, STRIP), F32),
        jax.ShapeDtypeStruct((strips, STRIP), F32),
    ]
    if half == 0:
        extra = [rates]
        out_shape = out_shape + terms
    else:
        extra = [shared[0], shared[2], shared[3]]
    return pl.pallas_call(
        lambda *refs: summary_kernel(heads, chips, half, *refs),
        grid=(STEPS,),
        in_specs=[
            SCALARS,
            half_lanes(tokens, lanes, half, STEPS),
            half_lanes(tokens, lanes, half, STEPS),
            whole(tokens, STATE),
            whole(tokens, STATE),
        ]
        + [whole(*value.shape) for value in extra],
        out_specs=[whole(*out.shape) for out in out_shape],
        out_shape=out_shape,
        scratch_shapes=[
            pltpu.VMEM((STATE, tokens), BF16),
            pltpu.VMEM((STATE, tokens), BF16),
        ],
        compiler_params=pltpu.CompilerParams(vmem_limit_bytes=BIG_VMEM),
        cost_estimate=LITTLE,
        name="summary",
    )(place, x, g, write_map, read_map, *extra)


def combine_kernel(chips, place, first_ref, keep_ref, decay_ref, log_ref, mine_ref, send_ref):
    strips = decay_ref.shape[0]
    part = STATE // chips
    size = mine_ref.shape[0]
    bit = place[1] & 1
    for base, out_ref in ((bit * size, mine_ref), ((1 - bit) * size, send_ref)):
        for strip in range(strips):
            decay = decay_ref[strip : strip + 1, :]
            for at in range(strip * part, size, strips * part):
                rows = pl.ds(pl.multiple_of(base + at, part), part)
                out_ref[at : at + part, :] = first_ref[rows, :] * decay + keep_ref[rows, :]
    send_ref[size:, :] = first_ref[2 * size :, :] + log_ref[...]


def halves(size):
    return (
        [whole(size, STRIP), whole(size + META, STRIP)],
        [
            jax.ShapeDtypeStruct((size, STRIP), F32),
            jax.ShapeDtypeStruct((size + META, STRIP), F32),
        ],
    )


def combine(chips, place, first, keep, decay, log):
    out_specs, out_shape = halves(keep.shape[0] // 2)
    return pl.pallas_call(
        lambda *refs: combine_kernel(chips, *refs),
        in_specs=[SCALARS] + [whole(*value.shape) for value in (first, keep, decay, log)],
        out_specs=out_specs,
        out_shape=out_shape,
        compiler_params=pltpu.CompilerParams(vmem_limit_bytes=SMALL_VMEM),
        cost_estimate=LITTLE,
        name="combine",
    )(place, first, keep, decay, log)


def is_ahead(place, level):
    return ((place[1] >> level) & 1) == place[0]


def tail_block(value):
    return pl.BlockSpec((META, STRIP), lambda c: (value.shape[0] // META - 1, 0))


def up_kernel(level, last, part, offset, strips, head_size, place, mine_ref, log_ref, got_ref, *outs):
    size = mine_ref.shape[0]
    ahead = is_ahead(place, level)
    mine_log, got_log = log_ref[0:1, :], got_ref[size : size + 1, :]
    mine_wide, got_wide = spread_rows(
        [jnp.where(ahead, 1.0, jnp.exp(got_log)), jnp.where(ahead, jnp.exp(mine_log), 1.0)],
        offset,
        strips,
        head_size,
    )
    bit = (place[1] >> (level + 1)) & 1
    half = size if last else size // 2
    targets = ((0, outs[0]),) if last else ((bit * half, outs[0]), ((1 - bit) * half, outs[1]))
    for base, out_ref in targets:
        for strip in range(strips):
            one = slice(strip, strip + 1)
            for at in range(strip * part, half, strips * part):
                rows = slice(at, at + part)
                if not last:
                    rows = pl.ds(pl.multiple_of(base + at, part), part)
                out_ref[at : at + part, :] = (
                    mine_ref[rows, :] * mine_wide[one, :] + got_ref[rows, :] * got_wide[one, :]
                )
    outs[-1][half:, :] = jnp.broadcast_to(mine_log + got_log, (META, STRIP))


def up(level, chips, half, strips, head_size, place, mine, send, got):
    size = mine.shape[0]
    last = 2 << level == chips
    out_specs, out_shape = halves(size if last else size // 2)
    if last:
        out_specs, out_shape = out_specs[1:], out_shape[1:]
    return pl.pallas_call(
        lambda *refs: up_kernel(
            level, last, STATE // chips, half * strips, strips, head_size, *refs
        ),
        grid=(1,),
        in_specs=[SCALARS, whole(size, STRIP), tail_block(send), whole(size + META, STRIP)],
        out_specs=out_specs,
        out_shape=out_shape,
        compiler_params=pltpu.CompilerParams(vmem_limit_bytes=SMALL_VMEM),
        cost_estimate=LITTLE,
        name="up",
    )(place, mine, send, got)


def down_kernel(level, top, part, offset, strips, head_size, place, mine_ref, log_ref, got_ref, *refs):
    sources, (here_ref, there_ref) = refs[:-2], refs[-2:]
    size = mine_ref.shape[0]
    ahead = is_ahead(place, level)
    rows_of = [
        jnp.where(ahead, jnp.exp(got_ref[size : size + 1, :]), 1.0),
        jnp.where(ahead, 1.0, jnp.exp(log_ref[0:1, :])),
    ]
    if top:
        passed = jnp.zeros_like(rows_of[0])
        for ref in sources:
            rows_of.append(jnp.exp(passed))
            passed = passed + ref[size : size + 1, :]
        bases, length = (0,), size
    else:
        length = size // 2
        bit = (place[1] >> (level + 1)) & 1
        bases = (bit * length, (1 - bit) * length)
    here_wide, there_wide, *group_wide = spread_rows(rows_of, offset, strips, head_size)
    for index, base in enumerate(bases):
        for strip in range(strips):
            one = slice(strip, strip + 1)
            for at in range(strip * part, length, strips * part):
                rows = slice(at, at + part)
                if top:
                    entering = sources[0][rows, :] * group_wide[0][one, :]
                    for ref, wide in zip(sources[1:], group_wide[1:]):
                        entering = entering + ref[rows, :] * wide[one, :]
                else:
                    entering = sources[index][rows, :]
                    rows = pl.ds(pl.multiple_of(base + at, part), part)
                got = jnp.where(ahead, got_ref[rows, :], 0.0)
                mine = jnp.where(ahead, 0.0, mine_ref[rows, :])
                here_ref[rows, :] = entering * here_wide[one, :] + got
                there_ref[rows, :] = entering * there_wide[one, :] + mine


def down(level, chips, half, strips, head_size, place, mine, send, got, sources):
    size = mine.shape[0]
    top = 2 << level == chips
    return pl.pallas_call(
        lambda *refs: down_kernel(
            level, top, STATE // chips, half * strips, strips, head_size, *refs
        ),
        grid=(1,),
        in_specs=[SCALARS, whole(size, STRIP), tail_block(send), whole(size + META, STRIP)]
        + [whole(*value.shape) for value in sources],
        out_specs=[whole(size, STRIP)] * 2,
        out_shape=[jax.ShapeDtypeStruct((size, STRIP), F32)] * 2,
        compiler_params=pltpu.CompilerParams(vmem_limit_bytes=SMALL_VMEM),
        cost_estimate=LITTLE,
        name="down",
    )(place, mine, send, got, *sources)


def intra_kernel(
    heads, head_size, start, last,
    place, after_ref, x_ref, g_ref, write_ref, read_ref, rates_ref, column_ref, tail_ref, lead_ref, *refs,
):
    dx_ref, mine_ref, other_ref, change_ref, *sums, row_ref, scores_ref, mask_ref, pairs_ref, \
        write_t, read_t = refs[5 if start else 0 :]
    step = pl.program_id(0)
    chunk = start + step
    lanes = x_ref.shape[1]
    per_chunk = lanes // head_size

    @pl.when(step == 0)
    def _():
        rates = rates_ref[...]
        triangle = lower(STRETCH)
        row_ref[...] = dot(rates, triangle, 1, 1, HIGHEST)
        mask_ref[...] = triangle
        scores_ref[...] = dot(read_ref[...], write_ref[...], 1, 1)
        pairs_ref[...] = refs[4][...] if start else jnp.zeros_like(pairs_ref)
        change_ref[...] = refs[3][...] if start else jnp.zeros_like(change_ref)
        write_t[...] = write_ref[...].astype(F32).T.astype(BF16)
        read_t[...] = read_ref[...].astype(F32).T.astype(BF16)

    columns = pltpu.roll(column_ref[...], STATE - chunk * per_chunk, 1)
    rows = row_ref[pl.ds(pl.multiple_of(chunk * per_chunk, per_chunk), per_chunk), :]
    causal = mask_ref[...] > 0.5
    scores = scores_ref[...]
    pairs = pairs_ref[...]
    low_half = iota((STRETCH, 2 * head_size), 1) < head_size
    adder = head_adder(chunk, head_size, lanes)
    spread = spreader(chunk, heads, head_size, lanes)
    high, low = term_pair(x_ref[...].astype(F32) * dot(tail_ref[...], spread, 1, 0))
    state = dot(write_t[...], high, 1, 0) + dot(write_t[...], low, 1, 0)
    high, low = term_pair(g_ref[...].astype(F32) * dot(lead_ref[...], spread, 1, 0))
    back = dot(read_t[...], high, 1, 0) + dot(read_t[...], low, 1, 0)
    is_first = place[0] == 0
    mine_ref[...] = jnp.where(is_first, state, back)
    other_ref[...] = jnp.where(is_first, back, state)
    for pair in range(per_chunk // 2):
        strip = slice(pair * 2 * head_size, (pair + 1) * 2 * head_size)
        x = x_ref[:, strip]
        g = g_ref[:, strip]
        ys, dxs = [], []
        for half in range(2):
            head = 2 * pair + half
            gap = columns[:, head : head + 1] - rows[head : head + 1, :]
            decay = jnp.where(causal, jnp.exp(gap), 0.0)
            mixing = (scores * decay).astype(BF16)
            ys.append(dot(mixing, x, 1, 0))
            dxs.append(dot(mixing, g, 0, 0))
            mine = low_half if half == 0 else jnp.logical_not(low_half)
            pairs = pairs + dot(jnp.where(mine, g, jnp.zeros_like(g)), x, 1, 1) * decay
        y = jnp.where(low_half, ys[0], ys[1])
        dx = jnp.where(low_half, dxs[0], dxs[1])
        dx_ref[:, strip] = dx
        change_ref[...] += head_sums(
            g.astype(F32) * y - x.astype(F32) * dx, adder[strip, :]
        )
    pairs_ref[...] = pairs

    @pl.when(step == pl.num_programs(0) - 1)
    def _():
        if last:
            summed = pairs_ref[...].astype(BF16)
            sums[0][...] = dot(summed, read_ref[...], 0, 0)
            sums[1][...] = dot(summed, write_ref[...], 1, 0)
        else:
            sums[0][...] = pairs_ref[...]


def intra(start, steps, place, after, x, g, write_map, read_map, rates, shared, earlier):
    tokens, wide = x.shape
    heads = rates.shape[0]
    last = (start + steps) * LANES == wide
    lanes = lambda rows: pl.BlockSpec((rows, LANES), lambda c: (0, start + c))
    anywhere = pl.BlockSpec(memory_space=pl.ANY)
    sums = [(tokens, STATE)] * 2 if last else [(tokens, tokens)]
    return pl.pallas_call(
        lambda *refs: intra_kernel(heads, wide // heads, start, last, *refs),
        grid=(steps,),
        in_specs=[
            SCALARS,
            whole(META, STRIP),
            lanes(tokens),
            lanes(tokens),
            whole(tokens, STATE),
            whole(tokens, STATE),
            whole(heads, tokens),
        ]
        + [whole(tokens, STRIP)] * 3
        + ([anywhere] * 3 + [whole(tokens, STATE), whole(tokens, tokens)] if earlier else []),
        out_specs=[lanes(tokens), lanes(STATE), lanes(STATE), whole(tokens, STATE)]
        + [whole(*shape) for shape in sums],
        out_shape=[
            jax.ShapeDtypeStruct((tokens, wide), F32),
            jax.ShapeDtypeStruct((STATE, wide), F32),
            jax.ShapeDtypeStruct((STATE, wide), F32),
            jax.ShapeDtypeStruct((tokens, STATE), F32),
        ]
        + [jax.ShapeDtypeStruct(shape, F32) for shape in sums],
        scratch_shapes=[
            pltpu.VMEM((heads, tokens), F32),
            pltpu.VMEM((tokens, tokens), F32),
            pltpu.VMEM((tokens, tokens), F32),
            pltpu.VMEM((tokens, tokens), F32),
            pltpu.VMEM((STATE, tokens), BF16),
            pltpu.VMEM((STATE, tokens), BF16),
        ],
        input_output_aliases={10: 0, 11: 1, 12: 2} if earlier else {},
        compiler_params=pltpu.CompilerParams(vmem_limit_bytes=SMALL_VMEM),
        cost_estimate=LITTLE,
        name="intra",
    )(place, after, x, g, write_map, read_map, rates, *shared[1:], *earlier)


def order_kernel(place, after_ref, here_ref, got_ref, out_ref):
    size = here_ref.shape[0]
    bit = place[1] & 1
    out_ref[pl.ds(pl.multiple_of(bit * size, size), size), :] = here_ref[...]
    out_ref[pl.ds(pl.multiple_of((1 - bit) * size, size), size), :] = got_ref[...]


def order(place, after, here, got):
    shape = (2 * here.shape[0], STRIP)
    return pl.pallas_call(
        order_kernel,
        in_specs=[SCALARS, whole(META, STRIP), whole(*here.shape), whole(*got.shape)],
        out_specs=whole(*shape),
        out_shape=jax.ShapeDtypeStruct(shape, F32),
        compiler_params=pltpu.CompilerParams(vmem_limit_bytes=SMALL_VMEM),
        cost_estimate=LITTLE,
        name="order",
    )(place, after, here, got)


def tally_kernel(
    heads, chips, half, head_size, place, first_ref, enter_ref, mine_ref, other_ref, out_ref
):
    lanes = mine_ref.shape[1]
    strips = lanes // STRIP
    part = STATE // chips
    size = strips * part
    log = first_ref[chips * size : chips * size + 1, :]
    decay = spread_rows([jnp.exp(log)], half * strips, strips, head_size)[0]
    sums = [[], []]
    for strip in range(strips):
        wide = slice(strip * STRIP, (strip + 1) * STRIP)
        near_sum = far_sum = None
        for quarter in range(chips):
            rows = slice(quarter * part, (quarter + 1) * part)
            here = slice(quarter * size + strip * part, quarter * size + (strip + 1) * part)
            far = enter_ref[here, :]
            near = far * decay[strip : strip + 1, :] + first_ref[here, :]
            near = near.astype(BF16).astype(F32) * mine_ref[rows, wide]
            far = far.astype(BF16).astype(F32) * other_ref[rows, wide]
            near_sum = near if near_sum is None else near_sum + near
            far_sum = far if far_sum is None else far_sum + far
        for found, value in zip(sums, (near_sum, far_sum)):
            found.append(jnp.sum(value, axis=0, keepdims=True))
    near, far = (jnp.concatenate(found, axis=1) for found in sums)
    sign = jnp.where(place[0] == 1, 1.0, -1.0)
    second = jnp.where(place[0] == 1, near, far) * sign
    chip = (near + far) * sign
    both = jnp.where(iota((META, lanes), 0) < META // 2, chip, second)
    out_ref[...] = head_sums(both, head_adder(half, head_size, lanes))


def tally(heads, chips, half, place, first, entering, mine, other):
    wide = mine.shape[1]
    ours = pl.BlockSpec((STATE, wide // HALVES), lambda c: (0, half))
    return pl.pallas_call(
        lambda *refs: tally_kernel(heads, chips, half, wide // heads, *refs),
        grid=(1,),
        in_specs=[SCALARS, whole(*first.shape), whole(*entering.shape), ours, ours],
        out_specs=whole(META, STRIP),
        out_shape=jax.ShapeDtypeStruct((META, STRIP), F32),
        compiler_params=pltpu.CompilerParams(vmem_limit_bytes=SMALL_VMEM),
        cost_estimate=LITTLE,
        name="tally",
    )(place, first, entering, mine, other)


def assemble_kernel(
    chips, half, head_size, place, after, first_ref, own_ref, far_ref, state_ref, back_ref
):
    strips = state_ref.shape[1] // STRIP
    part = STATE // chips
    size = strips * part
    log = first_ref[chips * size : chips * size + 1, :]
    decay = spread_rows([jnp.exp(log)], half * strips, strips, head_size)[0]
    is_first = place[0] == 0
    for quarter in range(chips):
        rows = slice(quarter * part, (quarter + 1) * part)
        for strip in range(strips):
            wide = slice(strip * STRIP, (strip + 1) * STRIP)
            here = slice(quarter * size + strip * part, quarter * size + (strip + 1) * part)
            own = own_ref[here, :] * decay[strip : strip + 1, :] + first_ref[here, :]
            far = far_ref[here, :]
            state_ref[rows, wide] = jnp.where(is_first, far, own).astype(BF16)
            back_ref[rows, wide] = jnp.where(is_first, own, far).astype(BF16)


def assemble(heads, chips, half, place, after, first, own, far):
    strips = own.shape[0] // STATE
    lanes = strips * STRIP
    return pl.pallas_call(
        lambda *refs: assemble_kernel(chips, half, lanes * HALVES // heads, *refs),
        grid=(1,),
        in_specs=[SCALARS, whole(META, STRIP)]
        + [whole(*value.shape) for value in (first, own, far)],
        out_specs=[whole(STATE, lanes), whole(STATE, lanes)],
        out_shape=[jax.ShapeDtypeStruct((STATE, lanes), BF16)] * 2,
        compiler_params=pltpu.CompilerParams(vmem_limit_bytes=SMALL_VMEM),
        cost_estimate=LITTLE,
        name="assemble",
    )(place, after, first, own, far)


def finish_kernel(
    heads, start, steps, last, after_ref, x_ref, g_ref, write_ref, read_ref, tail_ref, lead_ref,
    dx_ref, db_ref, dc_ref, change_ref, state_ref, back_ref, *refs,
):
    grad_ref, db_out, dc_out, change_out, token_ref, db_sum, dc_sum, sum_out = refs[-8:]
    chunk = pl.program_id(0)
    lanes = x_ref.shape[1]
    head_size = lanes * STEPS * HALVES // heads
    wide = start + chunk

    @pl.when(chunk == 0)
    def _():
        sum_out[...] = change_ref[...]
        db_sum[...] = db_ref[...]
        dc_sum[...] = dc_ref[...]

    state = state_ref[...]
    back = back_ref[...]
    spread = spreader(wide, heads, head_size, lanes)
    tail = dot(tail_ref[...], spread, 1, 0)
    lead = dot(lead_ref[...], spread, 1, 0)
    x = x_ref[...].astype(F32)
    g = g_ref[...].astype(F32)
    y = dot(read_ref[...], state, 1, 0) * lead
    dx = dot(write_ref[...], back, 1, 0) * tail
    grad_ref[...] = (dx_ref[...] + dx).astype(BF16)
    adder = head_adder(wide, head_size, lanes)
    sum_out[...] += head_sums(g * y - x * dx, adder)
    db_sum[...] += dot((x * tail).astype(BF16), back, 1, 1)
    dc_sum[...] += dot((g * lead).astype(BF16), state, 1, 1)

    @pl.when(chunk == steps - 1)
    def _():
        token_ref[...] = jnp.zeros_like(token_ref)
        db_out[...] = db_sum[...].astype(db_out.dtype)
        dc_out[...] = dc_sum[...].astype(dc_out.dtype)
        if last:
            change_out[...] = dot(sum_out[...], lower(STRETCH), 0, 0, HIGHEST)[:heads, :]
        else:
            change_out[...] = sum_out[...]


def finish(heads, start, steps, after, x, g, write_map, read_map, shared, dx, sums, state, back, grad):
    tokens, wide = x.shape
    lanes = wide // (STEPS * HALVES)
    strip = pl.BlockSpec((tokens, lanes), lambda c: (0, start + c))
    own = pl.BlockSpec((STATE, lanes), lambda c: (0, start % STEPS + c))
    last = start + steps == STEPS * HALVES
    kind = BF16 if last else F32
    change = (heads, tokens) if last else (tokens, STATE)
    earlier = [] if grad is None else [grad]
    return pl.pallas_call(
        lambda *refs: finish_kernel(heads, start, steps, last, *refs),
        grid=(steps,),
        in_specs=[whole(META, STRIP), strip, strip]
        + [whole(tokens, STATE)] * 4
        + [strip]
        + [whole(tokens, STATE)] * 3
        + [own, own]
        + [pl.BlockSpec(memory_space=pl.ANY)] * len(earlier),
        out_specs=[strip] + [whole(tokens, STATE)] * 2 + [whole(*change), whole(META, STRIP)],
        out_shape=[
            jax.ShapeDtypeStruct((tokens, wide), BF16),
            jax.ShapeDtypeStruct((tokens, STATE), kind),
            jax.ShapeDtypeStruct((tokens, STATE), kind),
            jax.ShapeDtypeStruct(change, F32),
            jax.ShapeDtypeStruct((META, STRIP), F32),
        ],
        scratch_shapes=[pltpu.VMEM((tokens, STATE), F32)] * 3,
        input_output_aliases={13: 0} if earlier else {},
        compiler_params=pltpu.CompilerParams(vmem_limit_bytes=SMALL_VMEM),
        cost_estimate=LITTLE,
        name="finish",
    )(after, x, g, write_map, read_map, *shared[2:], dx, *sums, state, back, *earlier)


def add_later_kernel(place, suffix_ref, mine_ref, other_ref, out_ref):
    heads = out_ref.shape[0]
    later = (mine_ref[...] + other_ref[...]).T[:heads, :]
    second = later[:, META // 2 : META // 2 + 1]
    out_ref[...] = suffix_ref[...] + later[:, 0:1] + jnp.where(place[0] == 0, second, 0.0)


def add_later(place, suffix, mine, other):
    return pl.pallas_call(
        add_later_kernel,
        in_specs=[SCALARS] + [whole(*value.shape) for value in (suffix, mine, other)],
        out_specs=whole(*suffix.shape),
        out_shape=jax.ShapeDtypeStruct(suffix.shape, F32),
        cost_estimate=LITTLE,
        name="add_later",
    )(place, suffix, mine, other)


def per_device(inputs, out_grad, input_map, output_map, log_decay):
    heads = log_decay.shape[0]
    head_size = inputs.shape[1] // heads
    groups, shards = lax.axis_size("grp"), lax.axis_size("seq")
    chips = shards // 2
    shard, group = lax.axis_index("seq"), lax.axis_index("grp")
    chip, core = shard >> 1, shard & 1
    place = jnp.stack([core, chip, group]).astype(jnp.int32)
    strips = inputs.shape[1] // STRIP // HALVES
    everyone = [(a, z, c) for a in range(groups) for z in range(chips) for c in range(2)]

    def move(value, target):
        pairs = []
        for a, z, c in everyone:
            to = target(a, z, c)
            if to is not None:
                pairs.append((a * shards + 2 * z + c, to[0] * shards + 2 * to[1] + to[2]))
        return lax.ppermute(value, ("grp", "seq"), pairs)

    def to_core(value):
        return move(value, lambda a, z, c: (a, z, 1 - c))

    def to_chip(value, step):
        return move(value, lambda a, z, c: (a, z ^ step, c)) if step else value

    def to_earlier(value, step):
        return move(value, lambda a, z, c: (a - step, z, c) if a >= step else None)

    def to_later(value, step):
        def target(a, z, c):
            to = a + step if c == 1 else a - step
            return (to, z, c) if 0 <= to < groups else None

        return move(value, target)

    maps = (inputs, out_grad, input_map, output_map)
    send, keep, decay, *shared = summary(chips, 0, place, *maps, log_decay, None)
    first = [to_core(send)]
    kept, decays = [keep], [decay]
    send, keep, decay = summary(chips, 1, place, *maps, log_decay, shared)
    first.append(to_core(send))
    kept.append(keep)
    decays.append(decay)

    levels = chips.bit_length() - 1
    held = [[], []]
    waiting = [None, None]

    def advance(half, step, after=None):
        fixed = (chips, half, strips, head_size, place)
        if step == 0:
            mine, send = combine(
                chips, place, first[half], kept[half], decays[half], shared[0]
            )
        elif step < levels:
            held[half][-1] += (waiting[half],)
            mine, send = up(step - 1, *fixed, *held[half][-1])
        elif step == levels:
            held[half][-1] += (waiting[half],)
            (send,) = up(step - 1, *fixed, *held[half][-1])
            waiting[half] = [to_later(send, far) for far in range(1, groups)]
            return send
        elif step <= 2 * levels:
            level = 2 * levels - step
            if level < levels - 1:
                waiting[half] = (held[half][level + 1], waiting[half])
            mine, send = down(level, *fixed, *held[half][level], waiting[half])
            held[half][level] = mine
            waiting[half] = to_chip(send, 1 << level)
            return send
        else:
            send = order(place, after, held[half][0], waiting[half])
            held[half] = send
            waiting[half] = to_core(send)
            return send
        held[half].append((mine, send))
        waiting[half] = to_chip(send, 1 << step)
        return send

    def entering(half, token):
        return assemble(
            heads, chips, half, place, token, first[half], held[half], waiting[half]
        )

    chunks = inputs.shape[1] // LANES
    rounds = 2 * levels + 2
    spare = chunks - 3
    parts = {0: spare - spare // 2, 1: 1 + spare // 2, levels: 1, levels + 1: 1}
    block, ready = (), 0
    for step in range(rounds):
        token = advance(0, step, shared[0])
        if step:
            behind = advance(1, step - 1)
            token = behind if step == levels + 1 else token
        if step in parts:
            block = intra(ready, parts[step], place, token, *maps, log_decay, shared, block)
            ready += parts[step]
            waiting[0], waiting[1], first[1], block = lax.optimization_barrier(
                (waiting[0], waiting[1], first[1], block)
            )
        elif step < rounds - 1:
            waiting[0], waiting[1] = lax.optimization_barrier((waiting[0], waiting[1]))
    dx, mine, other, change, db, dc = block
    other = to_core(other)

    def count(half):
        return tally(heads, chips, half, place, first[half], held[half], mine, other)

    counted = count(0)
    state, back = entering(0, counted)
    grad, *sums, token = finish(
        heads, 0, STEPS, counted, *maps, shared, dx, (db, dc, change), state, back, None
    )
    advance(1, rounds - 1, token)
    counted = counted + count(1)

    reached = [to_chip(counted, step) for step in range(1, chips)]
    state, back = entering(1, counted)
    grad, *sums, token = finish(
        heads, STEPS, 1, counted, *maps, shared, dx, sums, state, back, grad
    )
    later, whole_group = jnp.zeros_like(counted), counted + token
    for step, value in enumerate(reached, 1):
        later = later + jnp.where((chip ^ step) > chip, value, 0.0)
        whole_group = whole_group + value
    reached = [to_earlier(whole_group, step) for step in range(1, groups)]
    grad, *sums, token = finish(
        heads, STEPS + 1, 1, whole_group, *maps, shared, dx, sums, state, back, grad
    )
    later = sum(reached, later + token)
    row = lax.broadcasted_iota(jnp.int32, later.shape, 0)
    counted = jnp.where(row < META // 2, later, counted)
    return (grad, sums[0], sums[1], add_later(place, sums[2], counted, to_core(counted)))


def solution(mesh):
    tokens = P(("grp", "seq"), None)
    in_specs = (tokens, tokens, tokens, tokens, P(None, ("grp", "seq")))
    out_specs = (tokens, tokens, tokens, P(None, ("grp", "seq")))
    return jax.shard_map(
        per_device, mesh=mesh, in_specs=in_specs, out_specs=out_specs, check_vma=False
    )
```

```python
import jax
import jax.numpy as jnp
from jax import lax
from jax.experimental import pallas as pl
from jax.experimental.pallas import tpu as pltpu
from jax.sharding import PartitionSpec as P

STATE = 128
STRETCH = 256
LANES = 512
HALVES = 2
STRIP = 128
META = 8
BIG_VMEM = 56 << 20
SMALL_VMEM = 24 << 20
F32 = jnp.float32
BF16 = jnp.bfloat16
HIGHEST = lax.Precision.HIGHEST


def dot(left, right, left_dim, right_dim, precision=None):
    return lax.dot_general(
        left,
        right,
        (((left_dim,), (right_dim,)), ((), ())),
        precision=precision,
        preferred_element_type=F32,
    )


def iota(shape, dim):
    return lax.broadcasted_iota(jnp.int32, shape, dim)


def lower(length):
    return (iota((length, length), 0) >= iota((length, length), 1)).astype(F32)


def thrice(rates):
    heads, length = rates.shape
    spare = jnp.zeros((STATE - 3 * heads, length), F32)
    return jnp.concatenate([rates, rates, rates, spare], axis=0)


def three_terms(value, heads):
    lane = iota(value.shape, 1)
    first = value.astype(BF16)
    rest = value - first.astype(F32)
    second = rest.astype(BF16)
    third = (rest - second.astype(F32)).astype(BF16)
    return jnp.where(lane < heads, first, jnp.where(lane < 2 * heads, second, third))


def spreader(chunk, heads, head_size, lanes):
    row = iota((STATE, lanes), 0)
    head = (iota((STATE, lanes), 1) + chunk * lanes) // head_size
    hit = (row == head) | (row == head + heads) | (row == head + 2 * heads)
    return hit.astype(F32).astype(BF16)


def head_adder(chunk, head_size, lanes):
    head = (iota((lanes, STATE), 0) + chunk * lanes) // head_size
    return (iota((lanes, STATE), 1) == head).astype(F32).astype(BF16)


def head_sums(value, adder):
    first = value.astype(BF16)
    second = (value - first.astype(F32)).astype(BF16)
    return dot(first, adder, 1, 0) + dot(second, adder, 1, 0)


def decay_terms(rates, heads):
    length = rates.shape[1]
    running = dot(lower(length), thrice(rates), 1, 1, HIGHEST)
    last = running[length - 1 : length, :]
    return (
        running,
        three_terms(jnp.exp(last - running), heads),
        three_terms(jnp.exp(running), heads),
    )


def term_pair(value):
    first = value.astype(BF16)
    return first, (value - first.astype(F32)).astype(BF16)


def lane_spread(per_strip, head_size):
    head = iota((STRIP, STRIP), 0) % per_strip
    return (iota((STRIP, STRIP), 1) // head_size == head).astype(F32)


def spread_rows(rows, offset, strips, head_size):
    per_strip = STRIP // head_size
    lane = iota((strips, STRIP), 1)
    row = iota((strips, STRIP), 0) + offset
    picked = [jnp.where(lane // per_strip == row, value, 0.0) for value in rows]
    stacked = jnp.concatenate(picked, axis=0) if len(picked) > 1 else picked[0]
    wide = dot(stacked, lane_spread(per_strip, head_size), 1, 0, HIGHEST)
    return [wide[i * strips : (i + 1) * strips, :] for i in range(len(rows))]


def whole(*shape):
    return pl.BlockSpec(shape, lambda *_: (0,) * len(shape))


def lanes_of(rows):
    return pl.BlockSpec((rows, LANES), lambda c: (0, c))


def half_lanes(rows, lanes, half, steps):
    return pl.BlockSpec((rows, lanes), lambda c: (0, half * steps + c))


LITTLE = pl.CostEstimate(flops=1, bytes_accessed=1, transcendentals=0)
SCALARS = pl.BlockSpec(memory_space=pltpu.SMEM)
STEPS = 2


def summary_kernel(heads, chips, half, place, x_ref, g_ref, write_ref, read_ref, *refs):
    chunk = pl.program_id(0)
    lanes = x_ref.shape[1]
    strips = lanes // STRIP
    half_strips = strips * STEPS
    head_size = lanes * STEPS * HALVES // heads
    part = STATE // chips
    if half == 0:
        rates_ref, send_ref, keep_ref, decay_ref, log_ref, run_ref, tail_ref, lead_ref = refs[:8]
    else:
        log_ref, tail_ref, lead_ref, send_ref, keep_ref, decay_ref = refs[:6]
    write_t, read_t = refs[-2:]

    @pl.when(chunk == 0)
    def _():
        if half == 0:
            running, tail, lead = decay_terms(rates_ref[...], heads)
            run_ref[...] = running
            tail_ref[...] = tail
            lead_ref[...] = lead
            log_ref[...] = jnp.broadcast_to(running[STRETCH - 1 :, :], (META, STRIP))
        send_ref[pl.ds(half_strips * STATE, META), :] = log_ref[...]
        write_t[...] = write_ref[...].astype(F32).T.astype(BF16)
        read_t[...] = read_ref[...].astype(F32).T.astype(BF16)

    spread = spreader(half * STEPS + chunk, heads, head_size, lanes)
    tail = dot(tail_ref[...], spread, 1, 0)
    lead = dot(lead_ref[...], spread, 1, 0)
    inputs_tail = (x_ref[...].astype(F32) * tail).astype(BF16)
    grads_lead = (g_ref[...].astype(F32) * lead).astype(BF16)
    state = dot(write_t[...], inputs_tail, 1, 0)
    back = dot(read_t[...], grads_lead, 1, 0)
    first = place[0] == 0
    send = jnp.where(first, state, back)
    keep = jnp.where(first, back, state)
    for strip in range(strips):
        at = chunk * strips + strip
        wide = slice(strip * STRIP, (strip + 1) * STRIP)
        decay_ref[pl.ds(at, 1), :] = lead[STRETCH - 1 :, wide]
        for quarter in range(chips):
            rows = pl.ds(pl.multiple_of((quarter * half_strips + at) * part, part), part)
            mine = slice(quarter * part, (quarter + 1) * part)
            send_ref[rows, :] = send[mine, wide]
            keep_ref[rows, :] = keep[mine, wide]


def summary(chips, half, place, x, g, write_map, read_map, rates, shared):
    tokens, wide = x.shape
    heads = rates.shape[0]
    lanes = wide // (STEPS * HALVES)
    strips = wide // STRIP // HALVES
    terms = [
        jax.ShapeDtypeStruct((META, STRIP), F32),
        jax.ShapeDtypeStruct((tokens, STRIP), F32),
        jax.ShapeDtypeStruct((tokens, STRIP), BF16),
        jax.ShapeDtypeStruct((tokens, STRIP), BF16),
    ]
    out_shape = [
        jax.ShapeDtypeStruct((strips * STATE + META, STRIP), F32),
        jax.ShapeDtypeStruct((strips * STATE, STRIP), F32),
        jax.ShapeDtypeStruct((strips, STRIP), F32),
    ]
    if half == 0:
        extra = [rates]
        out_shape = out_shape + terms
    else:
        extra = [shared[0], shared[2], shared[3]]
    return pl.pallas_call(
        lambda *refs: summary_kernel(heads, chips, half, *refs),
        grid=(STEPS,),
        in_specs=[
            SCALARS,
            half_lanes(tokens, lanes, half, STEPS),
            half_lanes(tokens, lanes, half, STEPS),
            whole(tokens, STATE),
            whole(tokens, STATE),
        ]
        + [whole(*value.shape) for value in extra],
        out_specs=[whole(*out.shape) for out in out_shape],
        out_shape=out_shape,
        scratch_shapes=[
            pltpu.VMEM((STATE, tokens), BF16),
            pltpu.VMEM((STATE, tokens), BF16),
        ],
        compiler_params=pltpu.CompilerParams(vmem_limit_bytes=BIG_VMEM),
        cost_estimate=LITTLE,
        name="summary",
    )(place, x, g, write_map, read_map, *extra)


def combine_kernel(chips, place, first_ref, keep_ref, decay_ref, log_ref, mine_ref, send_ref):
    strips = decay_ref.shape[0]
    part = STATE // chips
    size = mine_ref.shape[0]
    bit = place[1] & 1
    for base, out_ref in ((bit * size, mine_ref), ((1 - bit) * size, send_ref)):
        for strip in range(strips):
            decay = decay_ref[strip : strip + 1, :]
            for at in range(strip * part, size, strips * part):
                rows = pl.ds(pl.multiple_of(base + at, part), part)
                out_ref[at : at + part, :] = first_ref[rows, :] * decay + keep_ref[rows, :]
    send_ref[size:, :] = first_ref[2 * size :, :] + log_ref[...]


def halves(size):
    return (
        [whole(size, STRIP), whole(size + META, STRIP)],
        [
            jax.ShapeDtypeStruct((size, STRIP), F32),
            jax.ShapeDtypeStruct((size + META, STRIP), F32),
        ],
    )


def combine(chips, place, first, keep, decay, log):
    out_specs, out_shape = halves(keep.shape[0] // 2)
    return pl.pallas_call(
        lambda *refs: combine_kernel(chips, *refs),
        in_specs=[SCALARS] + [whole(*value.shape) for value in (first, keep, decay, log)],
        out_specs=out_specs,
        out_shape=out_shape,
        compiler_params=pltpu.CompilerParams(vmem_limit_bytes=SMALL_VMEM),
        cost_estimate=LITTLE,
        name="combine",
    )(place, first, keep, decay, log)


def is_ahead(place, level):
    return ((place[1] >> level) & 1) == place[0]


def tail_block(value):
    return pl.BlockSpec((META, STRIP), lambda c: (value.shape[0] // META - 1, 0))


def up_kernel(level, last, part, offset, strips, head_size, place, mine_ref, log_ref, got_ref, *outs):
    size = mine_ref.shape[0]
    ahead = is_ahead(place, level)
    mine_log, got_log = log_ref[0:1, :], got_ref[size : size + 1, :]
    mine_wide, got_wide = spread_rows(
        [jnp.where(ahead, 1.0, jnp.exp(got_log)), jnp.where(ahead, jnp.exp(mine_log), 1.0)],
        offset,
        strips,
        head_size,
    )
    bit = (place[1] >> (level + 1)) & 1
    half = size if last else size // 2
    targets = ((0, outs[0]),) if last else ((bit * half, outs[0]), ((1 - bit) * half, outs[1]))
    for base, out_ref in targets:
        for strip in range(strips):
            one = slice(strip, strip + 1)
            for at in range(strip * part, half, strips * part):
                rows = slice(at, at + part)
                if not last:
                    rows = pl.ds(pl.multiple_of(base + at, part), part)
                out_ref[at : at + part, :] = (
                    mine_ref[rows, :] * mine_wide[one, :] + got_ref[rows, :] * got_wide[one, :]
                )
    outs[-1][half:, :] = jnp.broadcast_to(mine_log + got_log, (META, STRIP))


def up(level, chips, half, strips, head_size, place, mine, send, got):
    size = mine.shape[0]
    last = 2 << level == chips
    out_specs, out_shape = halves(size if last else size // 2)
    if last:
        out_specs, out_shape = out_specs[1:], out_shape[1:]
    return pl.pallas_call(
        lambda *refs: up_kernel(
            level, last, STATE // chips, half * strips, strips, head_size, *refs
        ),
        grid=(1,),
        in_specs=[SCALARS, whole(size, STRIP), tail_block(send), whole(size + META, STRIP)],
        out_specs=out_specs,
        out_shape=out_shape,
        compiler_params=pltpu.CompilerParams(vmem_limit_bytes=SMALL_VMEM),
        cost_estimate=LITTLE,
        name="up",
    )(place, mine, send, got)


def down_kernel(level, top, part, offset, strips, head_size, place, mine_ref, log_ref, got_ref, *refs):
    sources, (here_ref, there_ref) = refs[:-2], refs[-2:]
    size = mine_ref.shape[0]
    ahead = is_ahead(place, level)
    rows_of = [
        jnp.where(ahead, jnp.exp(got_ref[size : size + 1, :]), 1.0),
        jnp.where(ahead, 1.0, jnp.exp(log_ref[0:1, :])),
    ]
    if top:
        passed = jnp.zeros_like(rows_of[0])
        for ref in sources:
            rows_of.append(jnp.exp(passed))
            passed = passed + ref[size : size + 1, :]
        bases, length = (0,), size
    else:
        length = size // 2
        bit = (place[1] >> (level + 1)) & 1
        bases = (bit * length, (1 - bit) * length)
    here_wide, there_wide, *group_wide = spread_rows(rows_of, offset, strips, head_size)
    for index, base in enumerate(bases):
        for strip in range(strips):
            one = slice(strip, strip + 1)
            for at in range(strip * part, length, strips * part):
                rows = slice(at, at + part)
                if top:
                    entering = sources[0][rows, :] * group_wide[0][one, :]
                    for ref, wide in zip(sources[1:], group_wide[1:]):
                        entering = entering + ref[rows, :] * wide[one, :]
                else:
                    entering = sources[index][rows, :]
                    rows = pl.ds(pl.multiple_of(base + at, part), part)
                got = jnp.where(ahead, got_ref[rows, :], 0.0)
                mine = jnp.where(ahead, 0.0, mine_ref[rows, :])
                here_ref[rows, :] = entering * here_wide[one, :] + got
                there_ref[rows, :] = entering * there_wide[one, :] + mine


def down(level, chips, half, strips, head_size, place, mine, send, got, sources):
    size = mine.shape[0]
    top = 2 << level == chips
    return pl.pallas_call(
        lambda *refs: down_kernel(
            level, top, STATE // chips, half * strips, strips, head_size, *refs
        ),
        grid=(1,),
        in_specs=[SCALARS, whole(size, STRIP), tail_block(send), whole(size + META, STRIP)]
        + [whole(*value.shape) for value in sources],
        out_specs=[whole(size, STRIP)] * 2,
        out_shape=[jax.ShapeDtypeStruct((size, STRIP), F32)] * 2,
        compiler_params=pltpu.CompilerParams(vmem_limit_bytes=SMALL_VMEM),
        cost_estimate=LITTLE,
        name="down",
    )(place, mine, send, got, *sources)


def intra_kernel(
    heads, head_size, start, last,
    after_ref, x_ref, g_ref, write_ref, read_ref, rates_ref, column_ref, tail_ref, lead_ref, *refs,
):
    dx_ref, state_ref, back_ref, change_ref, *sums, row_ref, scores_ref, mask_ref, pairs_ref, \
        write_t, read_t = refs[5 if start else 0 :]
    step = pl.program_id(0)
    chunk = start + step
    lanes = x_ref.shape[1]
    per_chunk = lanes // head_size

    @pl.when(step == 0)
    def _():
        rates = rates_ref[...]
        triangle = lower(STRETCH)
        row_ref[...] = dot(rates, triangle, 1, 1, HIGHEST)
        mask_ref[...] = triangle
        scores_ref[...] = dot(read_ref[...], write_ref[...], 1, 1)
        pairs_ref[...] = refs[4][...] if start else jnp.zeros_like(pairs_ref)
        change_ref[...] = refs[3][...] if start else jnp.zeros_like(change_ref)
        write_t[...] = write_ref[...].astype(F32).T.astype(BF16)
        read_t[...] = read_ref[...].astype(F32).T.astype(BF16)

    columns = pltpu.roll(column_ref[...], STATE - chunk * per_chunk, 1)
    rows = row_ref[pl.ds(pl.multiple_of(chunk * per_chunk, per_chunk), per_chunk), :]
    causal = mask_ref[...] > 0.5
    scores = scores_ref[...]
    pairs = pairs_ref[...]
    low_half = iota((STRETCH, 2 * head_size), 1) < head_size
    adder = head_adder(chunk, head_size, lanes)
    spread = spreader(chunk, heads, head_size, lanes)
    high, low = term_pair(x_ref[...].astype(F32) * dot(tail_ref[...], spread, 1, 0))
    state_ref[...] = dot(write_t[...], high, 1, 0) + dot(write_t[...], low, 1, 0)
    high, low = term_pair(g_ref[...].astype(F32) * dot(lead_ref[...], spread, 1, 0))
    back_ref[...] = dot(read_t[...], high, 1, 0) + dot(read_t[...], low, 1, 0)
    for pair in range(per_chunk // 2):
        strip = slice(pair * 2 * head_size, (pair + 1) * 2 * head_size)
        x = x_ref[:, strip]
        g = g_ref[:, strip]
        ys, dxs = [], []
        for half in range(2):
            head = 2 * pair + half
            gap = columns[:, head : head + 1] - rows[head : head + 1, :]
            decay = jnp.where(causal, jnp.exp(gap), 0.0)
            mixing = (scores * decay).astype(BF16)
            ys.append(dot(mixing, x, 1, 0))
            dxs.append(dot(mixing, g, 0, 0))
            mine = low_half if half == 0 else jnp.logical_not(low_half)
            pairs = pairs + dot(jnp.where(mine, g, jnp.zeros_like(g)), x, 1, 1) * decay
        y = jnp.where(low_half, ys[0], ys[1])
        dx = jnp.where(low_half, dxs[0], dxs[1])
        dx_ref[:, strip] = dx
        change_ref[...] += head_sums(
            g.astype(F32) * y - x.astype(F32) * dx, adder[strip, :]
        )
    pairs_ref[...] = pairs

    @pl.when(step == pl.num_programs(0) - 1)
    def _():
        if last:
            summed = pairs_ref[...].astype(BF16)
            sums[0][...] = dot(summed, read_ref[...], 0, 0)
            sums[1][...] = dot(summed, write_ref[...], 1, 0)
        else:
            sums[0][...] = pairs_ref[...]


def intra(start, steps, after, x, g, write_map, read_map, rates, shared, earlier):
    tokens, wide = x.shape
    heads = rates.shape[0]
    last = (start + steps) * LANES == wide
    lanes = lambda rows: pl.BlockSpec((rows, LANES), lambda c: (0, start + c))
    anywhere = pl.BlockSpec(memory_space=pl.ANY)
    sums = [(tokens, STATE)] * 2 if last else [(tokens, tokens)]
    return pl.pallas_call(
        lambda *refs: intra_kernel(heads, wide // heads, start, last, *refs),
        grid=(steps,),
        in_specs=[
            whole(META, STRIP),
            lanes(tokens),
            lanes(tokens),
            whole(tokens, STATE),
            whole(tokens, STATE),
            whole(heads, tokens),
        ]
        + [whole(tokens, STRIP)] * 3
        + ([anywhere] * 3 + [whole(tokens, STATE), whole(tokens, tokens)] if earlier else []),
        out_specs=[lanes(tokens), lanes(STATE), lanes(STATE), whole(tokens, STATE)]
        + [whole(*shape) for shape in sums],
        out_shape=[
            jax.ShapeDtypeStruct((tokens, wide), F32),
            jax.ShapeDtypeStruct((STATE, wide), F32),
            jax.ShapeDtypeStruct((STATE, wide), F32),
            jax.ShapeDtypeStruct((tokens, STATE), F32),
        ]
        + [jax.ShapeDtypeStruct(shape, F32) for shape in sums],
        scratch_shapes=[
            pltpu.VMEM((heads, tokens), F32),
            pltpu.VMEM((tokens, tokens), F32),
            pltpu.VMEM((tokens, tokens), F32),
            pltpu.VMEM((tokens, tokens), F32),
            pltpu.VMEM((STATE, tokens), BF16),
            pltpu.VMEM((STATE, tokens), BF16),
        ],
        input_output_aliases={9: 0, 10: 1, 11: 2} if earlier else {},
        compiler_params=pltpu.CompilerParams(vmem_limit_bytes=SMALL_VMEM),
        cost_estimate=LITTLE,
        name="intra",
    )(after, x, g, write_map, read_map, rates, *shared[1:], *earlier)


def order_kernel(place, after_ref, here_ref, got_ref, out_ref):
    size = here_ref.shape[0]
    bit = place[1] & 1
    out_ref[pl.ds(pl.multiple_of(bit * size, size), size), :] = here_ref[...]
    out_ref[pl.ds(pl.multiple_of((1 - bit) * size, size), size), :] = got_ref[...]


def order(place, after, here, got):
    shape = (2 * here.shape[0], STRIP)
    return pl.pallas_call(
        order_kernel,
        in_specs=[SCALARS, whole(META, STRIP), whole(*here.shape), whole(*got.shape)],
        out_specs=whole(*shape),
        out_shape=jax.ShapeDtypeStruct(shape, F32),
        compiler_params=pltpu.CompilerParams(vmem_limit_bytes=SMALL_VMEM),
        cost_estimate=LITTLE,
        name="order",
    )(place, after, here, got)


def assemble_kernel(
    heads, chips, half, head_size, place, after_ref, first_ref, state_own, back_own, own_ref, far_ref,
    state_ref, back_ref, total_ref,
):
    lanes = state_ref.shape[1]
    strips = lanes // STRIP
    part = STATE // chips
    size = strips * part
    log = first_ref[chips * size : chips * size + 1, :]
    decay = spread_rows([jnp.exp(log)], half * strips, strips, head_size)[0]
    is_first = place[0] == 0
    sums = [None] * strips
    for quarter in range(chips):
        rows = slice(quarter * part, (quarter + 1) * part)
        for strip in range(strips):
            wide = slice(strip * STRIP, (strip + 1) * STRIP)
            here = slice(quarter * size + strip * part, quarter * size + (strip + 1) * part)
            own = own_ref[here, :] * decay[strip : strip + 1, :] + first_ref[here, :]
            far = far_ref[here, :]
            state = jnp.where(is_first, far, own).astype(BF16)
            back = jnp.where(is_first, own, far).astype(BF16)
            state_ref[rows, wide] = state
            back_ref[rows, wide] = back
            gain = state.astype(F32) * back_own[rows, wide]
            gain = gain - back.astype(F32) * state_own[rows, wide]
            sums[strip] = gain if sums[strip] is None else sums[strip] + gain
    row_sum = [
        jnp.broadcast_to(jnp.sum(value, axis=0, keepdims=True), (META, STRIP)) for value in sums
    ]
    total = head_sums(jnp.concatenate(row_sum, axis=1), head_adder(half, head_size, lanes))
    total_ref[...] = total + after_ref[...] if half else total


def assemble(heads, chips, half, place, after, first, state_own, back_own, own, far):
    wide = state_own.shape[1]
    lanes = wide // HALVES
    mine = pl.BlockSpec((STATE, lanes), lambda c: (0, half))
    return pl.pallas_call(
        lambda *refs: assemble_kernel(heads, chips, half, wide // heads, *refs),
        grid=(1,),
        in_specs=[SCALARS, whole(META, STRIP), whole(*first.shape), mine, mine]
        + [whole(*own.shape), whole(*far.shape)],
        out_specs=[whole(STATE, lanes), whole(STATE, lanes), whole(META, STRIP)],
        out_shape=[
            jax.ShapeDtypeStruct((STATE, lanes), BF16),
            jax.ShapeDtypeStruct((STATE, lanes), BF16),
            jax.ShapeDtypeStruct((META, STRIP), F32),
        ],
        compiler_params=pltpu.CompilerParams(vmem_limit_bytes=SMALL_VMEM),
        cost_estimate=LITTLE,
        name="assemble",
    )(place, after, first, state_own, back_own, own, far)


def finish_kernel(
    heads, start, steps, last, x_ref, g_ref, write_ref, read_ref, tail_ref, lead_ref,
    dx_ref, db_ref, dc_ref, change_ref, state_ref, back_ref, *refs,
):
    grad_ref, db_out, dc_out, change_out, token_ref, db_sum, dc_sum, sum_out = refs[-8:]
    chunk = pl.program_id(0)
    lanes = x_ref.shape[1]
    head_size = lanes * STEPS * HALVES // heads
    wide = start + chunk

    @pl.when(chunk == 0)
    def _():
        sum_out[...] = change_ref[...]
        db_sum[...] = db_ref[...]
        dc_sum[...] = dc_ref[...]

    state = state_ref[...]
    back = back_ref[...]
    spread = spreader(wide, heads, head_size, lanes)
    tail = dot(tail_ref[...], spread, 1, 0)
    lead = dot(lead_ref[...], spread, 1, 0)
    x = x_ref[...].astype(F32)
    g = g_ref[...].astype(F32)
    y = dot(read_ref[...], state, 1, 0) * lead
    dx = dot(write_ref[...], back, 1, 0) * tail
    grad_ref[...] = (dx_ref[...] + dx).astype(BF16)
    adder = head_adder(wide, head_size, lanes)
    sum_out[...] += head_sums(g * y - x * dx, adder)
    db_sum[...] += dot((x * tail).astype(BF16), back, 1, 1)
    dc_sum[...] += dot((g * lead).astype(BF16), state, 1, 1)

    @pl.when(chunk == steps - 1)
    def _():
        token_ref[...] = jnp.zeros_like(token_ref)
        db_out[...] = db_sum[...].astype(db_out.dtype)
        dc_out[...] = dc_sum[...].astype(dc_out.dtype)
        if last:
            change_out[...] = dot(sum_out[...], lower(STRETCH), 0, 0, HIGHEST)[:heads, :]
        else:
            change_out[...] = sum_out[...]


def finish(heads, start, steps, after, x, g, write_map, read_map, shared, dx, sums, state, back, grad):
    tokens, wide = x.shape
    lanes = wide // (STEPS * HALVES)
    strip = pl.BlockSpec((tokens, lanes), lambda c: (0, start + c))
    own = pl.BlockSpec((STATE, lanes), lambda c: (0, start % STEPS + c))
    last = start + steps == STEPS * HALVES
    kind = BF16 if last else F32
    change = (heads, tokens) if last else (tokens, STATE)
    earlier = [] if grad is None else [grad]
    return pl.pallas_call(
        lambda *refs: finish_kernel(heads, start, steps, last, *refs),
        grid=(steps,),
        in_specs=[strip, strip]
        + [whole(tokens, STATE)] * 4
        + [strip]
        + [whole(tokens, STATE)] * 3
        + [own, own]
        + [pl.BlockSpec(memory_space=pl.ANY)] * len(earlier)
        + [whole(META, STRIP)],
        out_specs=[strip] + [whole(tokens, STATE)] * 2 + [whole(*change), whole(META, STRIP)],
        out_shape=[
            jax.ShapeDtypeStruct((tokens, wide), BF16),
            jax.ShapeDtypeStruct((tokens, STATE), kind),
            jax.ShapeDtypeStruct((tokens, STATE), kind),
            jax.ShapeDtypeStruct(change, F32),
            jax.ShapeDtypeStruct((META, STRIP), F32),
        ],
        scratch_shapes=[pltpu.VMEM((tokens, STATE), F32)] * 3,
        input_output_aliases={12: 0} if earlier else {},
        compiler_params=pltpu.CompilerParams(vmem_limit_bytes=SMALL_VMEM),
        cost_estimate=LITTLE,
        name="finish",
    )(x, g, write_map, read_map, *shared[2:], dx, *sums, state, back, *earlier, after)


def count_kernel(place, later_ref, total_ref, after_ref, *refs):
    got_refs, (later_out, total_out) = refs[:-2], refs[-2:]
    later, total = later_ref[...], total_ref[...] + after_ref[...]
    for step, ref in enumerate(got_refs, 1):
        later = later + jnp.where((place[1] ^ step) > place[1], ref[...], 0.0)
        total = total + ref[...]
    later_out[...] = later
    total_out[...] = total


def core_kernel(place, total_ref, after_ref, got_ref, later_out, total_out):
    later_out[...] = jnp.where(place[0] == 0, got_ref[...], 0.0)
    total_out[...] = total_ref[...] + got_ref[...] + after_ref[...]


def tiles(kernel, name, place, *values):
    return pl.pallas_call(
        kernel,
        in_specs=[SCALARS] + [whole(META, STRIP)] * len(values),
        out_specs=[whole(META, STRIP)] * 2,
        out_shape=[jax.ShapeDtypeStruct((META, STRIP), F32)] * 2,
        compiler_params=pltpu.CompilerParams(vmem_limit_bytes=SMALL_VMEM),
        cost_estimate=LITTLE,
        name=name,
    )(place, *values)


def add_later_kernel(suffix_ref, *refs):
    out_ref = refs[-1]
    heads = out_ref.shape[0]
    later = refs[0][...]
    for ref in refs[1:-1]:
        later = later + ref[...]
    out_ref[...] = suffix_ref[...] + later.T[:heads, 0:1]


def add_later(suffix, *parts):
    return pl.pallas_call(
        add_later_kernel,
        in_specs=[whole(*value.shape) for value in (suffix, *parts)],
        out_specs=whole(*suffix.shape),
        out_shape=jax.ShapeDtypeStruct(suffix.shape, F32),
        compiler_params=pltpu.CompilerParams(vmem_limit_bytes=SMALL_VMEM),
        cost_estimate=LITTLE,
        name="add_later",
    )(suffix, *parts)


def per_device(inputs, out_grad, input_map, output_map, log_decay):
    heads = log_decay.shape[0]
    head_size = inputs.shape[1] // heads
    groups, shards = lax.axis_size("grp"), lax.axis_size("seq")
    chips = shards // 2
    shard, group = lax.axis_index("seq"), lax.axis_index("grp")
    chip, core = shard >> 1, shard & 1
    place = jnp.stack([core, chip, group]).astype(jnp.int32)
    strips = inputs.shape[1] // STRIP // HALVES
    everyone = [(a, z, c) for a in range(groups) for z in range(chips) for c in range(2)]

    def move(value, target):
        pairs = []
        for a, z, c in everyone:
            to = target(a, z, c)
            if to is not None:
                pairs.append((a * shards + 2 * z + c, to[0] * shards + 2 * to[1] + to[2]))
        return lax.ppermute(value, ("grp", "seq"), pairs)

    def to_core(value):
        return move(value, lambda a, z, c: (a, z, 1 - c))

    def to_chip(value, step):
        return move(value, lambda a, z, c: (a, z ^ step, c)) if step else value

    def to_earlier(value, step):
        return move(value, lambda a, z, c: (a - step, z, c) if a >= step else None)

    def to_later(value, step):
        def target(a, z, c):
            to = a + step if c == 1 else a - step
            return (to, z, c) if 0 <= to < groups else None

        return move(value, target)

    maps = (inputs, out_grad, input_map, output_map)
    send, keep, decay, *shared = summary(chips, 0, place, *maps, log_decay, None)
    first = [to_core(send)]
    kept, decays = [keep], [decay]
    send, keep, decay = summary(chips, 1, place, *maps, log_decay, shared)
    first.append(to_core(send))
    kept.append(keep)
    decays.append(decay)

    levels = chips.bit_length() - 1
    held = [[], []]
    waiting = [None, None]

    def advance(half, step, after=None):
        fixed = (chips, half, strips, head_size, place)
        if step == 0:
            mine, send = combine(
                chips, place, first[half], kept[half], decays[half], shared[0]
            )
        elif step < levels:
            held[half][-1] += (waiting[half],)
            mine, send = up(step - 1, *fixed, *held[half][-1])
        elif step == levels:
            held[half][-1] += (waiting[half],)
            (send,) = up(step - 1, *fixed, *held[half][-1])
            waiting[half] = [to_later(send, far) for far in range(1, groups)]
            return send
        elif step <= 2 * levels:
            level = 2 * levels - step
            if level < levels - 1:
                waiting[half] = (held[half][level + 1], waiting[half])
            mine, send = down(level, *fixed, *held[half][level], waiting[half])
            held[half][level] = mine
            waiting[half] = to_chip(send, 1 << level)
            return send
        else:
            send = order(place, after, held[half][0], waiting[half])
            held[half] = send
            waiting[half] = to_core(send)
            return send
        held[half].append((mine, send))
        waiting[half] = to_chip(send, 1 << step)
        return send

    def entering(half, token):
        return assemble(
            heads, chips, half, place, token, first[half], state_own, back_own,
            held[half], waiting[half],
        )

    chunks = inputs.shape[1] // LANES
    rounds = 2 * levels + 2
    block, ready = (), 0
    for step in range(rounds):
        token = advance(0, step, shared[0])
        if step:
            advance(1, step - 1)
        if step < 3:
            more = pl.cdiv(chunks - ready, 3 - step)
            block = intra(ready, more, token, *maps, log_decay, shared, block)
            ready += more
            waiting[0], waiting[1], first[1], block = lax.optimization_barrier(
                (waiting[0], waiting[1], first[1], block)
            )
        elif step < rounds - 1:
            waiting[0], waiting[1] = lax.optimization_barrier((waiting[0], waiting[1]))
    dx, state_own, back_own, change, db, dc = block
    state, back, counted = entering(0, change)
    grad, *sums, token = finish(
        heads, 0, STEPS, counted, *maps, shared, dx, (db, dc, change), state, back, None
    )
    advance(1, rounds - 1, token)
    state, back, counted = entering(1, counted)

    got = to_core(counted)
    grad, *sums, token = finish(
        heads, STEPS, 1, counted, *maps, shared, dx, sums, state, back, grad
    )
    later, counted = tiles(core_kernel, "core_sum", place, counted, token, got)
    got = [to_chip(counted, step) for step in range(1, chips)]
    grad, *sums, token = finish(
        heads, STEPS + 1, 1, counted, *maps, shared, dx, sums, state, back, grad
    )
    later, counted = tiles(count_kernel, "chip_sum", place, later, counted, token, *got)
    got = [to_earlier(counted, step) for step in range(1, groups)]
    return (grad, sums[0], sums[1], add_later(sums[2], later, *got))


def solution(mesh):
    tokens = P(("grp", "seq"), None)
    in_specs = (tokens, tokens, tokens, tokens, P(None, ("grp", "seq")))
    out_specs = (tokens, tokens, tokens, P(None, ("grp", "seq")))
    return jax.shard_map(
        per_device, mesh=mesh, in_specs=in_specs, out_specs=out_specs, check_vma=False
    )
```

```python
import jax
import jax.numpy as jnp
from jax import lax
from jax.experimental import pallas as pl
from jax.experimental.pallas import tpu as pltpu
from jax.sharding import PartitionSpec as P

STATE = 128
STRETCH = 256
LANES = 512
HALVES = 2
STRIP = 128
META = 8
PAD = 2 * META
BIG_VMEM = 56 << 20
SMALL_VMEM = 24 << 20
F32 = jnp.float32
BF16 = jnp.bfloat16
HIGHEST = lax.Precision.HIGHEST


def dot(left, right, left_dim, right_dim, precision=None):
    return lax.dot_general(
        left,
        right,
        (((left_dim,), (right_dim,)), ((), ())),
        precision=precision,
        preferred_element_type=F32,
    )


def iota(shape, dim):
    return lax.broadcasted_iota(jnp.int32, shape, dim)


def lower(length):
    return (iota((length, length), 0) >= iota((length, length), 1)).astype(F32)


def thrice(rates):
    heads, length = rates.shape
    spare = jnp.zeros((STATE - 3 * heads, length), F32)
    return jnp.concatenate([rates, rates, rates, spare], axis=0)


def three_terms(value, heads):
    lane = iota(value.shape, 1)
    first = value.astype(BF16)
    rest = value - first.astype(F32)
    second = rest.astype(BF16)
    third = (rest - second.astype(F32)).astype(BF16)
    return jnp.where(lane < heads, first, jnp.where(lane < 2 * heads, second, third))


def spreader(chunk, heads, head_size, lanes):
    row = iota((STATE, lanes), 0)
    head = (iota((STATE, lanes), 1) + chunk * lanes) // head_size
    hit = (row == head) | (row == head + heads) | (row == head + 2 * heads)
    return hit.astype(F32).astype(BF16)


def head_adder(chunk, head_size, lanes):
    head = (iota((lanes, STATE), 0) + chunk * lanes) // head_size
    return (iota((lanes, STATE), 1) == head).astype(F32).astype(BF16)


def head_sums(value, adder):
    first = value.astype(BF16)
    second = (value - first.astype(F32)).astype(BF16)
    return dot(first, adder, 1, 0) + dot(second, adder, 1, 0)


def decay_terms(rates, heads):
    length = rates.shape[1]
    running = dot(lower(length), thrice(rates), 1, 1, HIGHEST)
    last = running[length - 1 : length, :]
    return (
        running,
        three_terms(jnp.exp(last - running), heads),
        three_terms(jnp.exp(running), heads),
    )


def term_pair(value):
    first = value.astype(BF16)
    return first, (value - first.astype(F32)).astype(BF16)


def lane_spread(per_strip, head_size):
    head = iota((STRIP, STRIP), 0) % per_strip
    return (iota((STRIP, STRIP), 1) // head_size == head).astype(F32)


def spread_rows(rows, offset, strips, head_size):
    per_strip = STRIP // head_size
    lane = iota((strips, STRIP), 1)
    row = iota((strips, STRIP), 0) + offset
    picked = [jnp.where(lane // per_strip == row, value, 0.0) for value in rows]
    stacked = jnp.concatenate(picked, axis=0) if len(picked) > 1 else picked[0]
    wide = dot(stacked, lane_spread(per_strip, head_size), 1, 0, HIGHEST)
    return [wide[i * strips : (i + 1) * strips, :] for i in range(len(rows))]


def whole(*shape):
    return pl.BlockSpec(shape, lambda *_: (0,) * len(shape))


def lanes_of(rows):
    return pl.BlockSpec((rows, LANES), lambda c: (0, c))


def half_lanes(rows, lanes, half, steps):
    return pl.BlockSpec((rows, lanes), lambda c: (0, half * steps + c))


LITTLE = pl.CostEstimate(flops=1, bytes_accessed=1, transcendentals=0)
SCALARS = pl.BlockSpec(memory_space=pltpu.SMEM)
STEPS = 2


def summary_kernel(heads, chips, half, place, x_ref, g_ref, write_ref, read_ref, *refs):
    chunk = pl.program_id(0)
    lanes = x_ref.shape[1]
    strips = lanes // STRIP
    half_strips = strips * STEPS
    head_size = lanes * STEPS * HALVES // heads
    part = STATE // chips
    if half == 0:
        rates_ref, send_ref, keep_ref, decay_ref, log_ref, run_ref, tail_ref, lead_ref = refs[:8]
    else:
        log_ref, tail_ref, lead_ref, send_ref, keep_ref, decay_ref = refs[:6]
    write_t, read_t = refs[-2:]

    @pl.when(chunk == 0)
    def _():
        if half == 0:
            running, tail, lead = decay_terms(rates_ref[...], heads)
            run_ref[...] = running
            tail_ref[...] = tail
            lead_ref[...] = lead
            log_ref[...] = jnp.broadcast_to(running[STRETCH - 1 :, :], (META, STRIP))
        send_ref[pl.ds(half_strips * STATE, META), :] = log_ref[...]
        write_t[...] = write_ref[...].astype(F32).T.astype(BF16)
        read_t[...] = read_ref[...].astype(F32).T.astype(BF16)

    spread = spreader(half * STEPS + chunk, heads, head_size, lanes)
    tail = dot(tail_ref[...], spread, 1, 0)
    lead = dot(lead_ref[...], spread, 1, 0)
    inputs_tail = (x_ref[...].astype(F32) * tail).astype(BF16)
    grads_lead = (g_ref[...].astype(F32) * lead).astype(BF16)
    state = dot(write_t[...], inputs_tail, 1, 0)
    back = dot(read_t[...], grads_lead, 1, 0)
    first = place[0] == 0
    send = jnp.where(first, state, back)
    keep = jnp.where(first, back, state)
    for strip in range(strips):
        at = chunk * strips + strip
        wide = slice(strip * STRIP, (strip + 1) * STRIP)
        decay_ref[pl.ds(at, 1), :] = lead[STRETCH - 1 :, wide]
        for quarter in range(chips):
            rows = pl.ds(pl.multiple_of((quarter * half_strips + at) * part, part), part)
            mine = slice(quarter * part, (quarter + 1) * part)
            send_ref[rows, :] = send[mine, wide]
            keep_ref[rows, :] = keep[mine, wide]


def summary(chips, half, place, x, g, write_map, read_map, rates, shared):
    tokens, wide = x.shape
    heads = rates.shape[0]
    lanes = wide // (STEPS * HALVES)
    strips = wide // STRIP // HALVES
    terms = [
        jax.ShapeDtypeStruct((META, STRIP), F32),
        jax.ShapeDtypeStruct((tokens, STRIP), F32),
        jax.ShapeDtypeStruct((tokens, STRIP), BF16),
        jax.ShapeDtypeStruct((tokens, STRIP), BF16),
    ]
    out_shape = [
        jax.ShapeDtypeStruct((strips * STATE + META, STRIP), F32),
        jax.ShapeDtypeStruct((strips * STATE, STRIP), F32),
        jax.ShapeDtypeStruct((strips, STRIP), F32),
    ]
    if half == 0:
        extra = [rates]
        out_shape = out_shape + terms
    else:
        extra = [shared[0], shared[2], shared[3]]
    return pl.pallas_call(
        lambda *refs: summary_kernel(heads, chips, half, *refs),
        grid=(STEPS,),
        in_specs=[
            SCALARS,
            half_lanes(tokens, lanes, half, STEPS),
            half_lanes(tokens, lanes, half, STEPS),
            whole(tokens, STATE),
            whole(tokens, STATE),
        ]
        + [whole(*value.shape) for value in extra],
        out_specs=[whole(*out.shape) for out in out_shape],
        out_shape=out_shape,
        scratch_shapes=[
            pltpu.VMEM((STATE, tokens), BF16),
            pltpu.VMEM((STATE, tokens), BF16),
        ],
        compiler_params=pltpu.CompilerParams(vmem_limit_bytes=BIG_VMEM),
        cost_estimate=LITTLE,
        name="summary",
    )(place, x, g, write_map, read_map, *extra)


def combine_kernel(chips, place, first_ref, keep_ref, decay_ref, log_ref, mine_ref, send_ref):
    strips = decay_ref.shape[0]
    part = STATE // chips
    size = mine_ref.shape[0]
    bit = place[1] & 1
    for base, out_ref in ((bit * size, mine_ref), ((1 - bit) * size, send_ref)):
        for strip in range(strips):
            decay = decay_ref[strip : strip + 1, :]
            for at in range(strip * part, size, strips * part):
                rows = pl.ds(pl.multiple_of(base + at, part), part)
                out_ref[at : at + part, :] = first_ref[rows, :] * decay + keep_ref[rows, :]
    meta = first_ref[2 * size :, :] + log_ref[...]
    send_ref[size : size + META, :] = meta
    send_ref[size + META :, :] = meta


def halves(size):
    return (
        [whole(size, STRIP), whole(size + PAD, STRIP)],
        [
            jax.ShapeDtypeStruct((size, STRIP), F32),
            jax.ShapeDtypeStruct((size + PAD, STRIP), F32),
        ],
    )


def combine(chips, place, first, keep, decay, log):
    out_specs, out_shape = halves(keep.shape[0] // 2)
    return pl.pallas_call(
        lambda *refs: combine_kernel(chips, *refs),
        in_specs=[SCALARS] + [whole(*value.shape) for value in (first, keep, decay, log)],
        out_specs=out_specs,
        out_shape=out_shape,
        compiler_params=pltpu.CompilerParams(vmem_limit_bytes=SMALL_VMEM),
        cost_estimate=LITTLE,
        name="combine",
    )(place, first, keep, decay, log)


def is_ahead(place, level):
    return ((place[1] >> level) & 1) == place[0]


def tail_block(value):
    return pl.BlockSpec((META, STRIP), lambda c: (value.shape[0] // META - 1, 0))


def up_kernel(level, last, part, offset, strips, head_size, place, mine_ref, log_ref, got_ref, *outs):
    size = mine_ref.shape[0]
    ahead = is_ahead(place, level)
    mine_log, got_log = log_ref[0:1, :], got_ref[size : size + 1, :]
    mine_wide, got_wide = spread_rows(
        [jnp.where(ahead, 1.0, jnp.exp(got_log)), jnp.where(ahead, jnp.exp(mine_log), 1.0)],
        offset,
        strips,
        head_size,
    )
    bit = (place[1] >> (level + 1)) & 1
    half = size if last else size // 2
    targets = ((0, outs[0]),) if last else ((bit * half, outs[0]), ((1 - bit) * half, outs[1]))
    for base, out_ref in targets:
        for strip in range(strips):
            one = slice(strip, strip + 1)
            for at in range(strip * part, half, strips * part):
                rows = slice(at, at + part)
                if not last:
                    rows = pl.ds(pl.multiple_of(base + at, part), part)
                out_ref[at : at + part, :] = (
                    mine_ref[rows, :] * mine_wide[one, :] + got_ref[rows, :] * got_wide[one, :]
                )
    outs[-1][half:, :] = jnp.broadcast_to(mine_log + got_log, (META if last else PAD, STRIP))


def up(level, chips, half, strips, head_size, place, mine, send, got):
    size = mine.shape[0]
    last = 2 << level == chips
    out_specs, out_shape = halves(size if last else size // 2)
    if last:
        out_specs = [whole(size + META, STRIP)]
        out_shape = [jax.ShapeDtypeStruct((size + META, STRIP), F32)]
    return pl.pallas_call(
        lambda *refs: up_kernel(
            level, last, STATE // chips, half * strips, strips, head_size, *refs
        ),
        grid=(1,),
        in_specs=[SCALARS, whole(size, STRIP), tail_block(send), whole(size + PAD, STRIP)],
        out_specs=out_specs,
        out_shape=out_shape,
        compiler_params=pltpu.CompilerParams(vmem_limit_bytes=SMALL_VMEM),
        cost_estimate=LITTLE,
        name="up",
    )(place, mine, send, got)


def down_kernel(level, top, part, offset, strips, head_size, place, mine_ref, log_ref, got_ref, *refs):
    sources, (here_ref, there_ref) = refs[:-2], refs[-2:]
    size = mine_ref.shape[0]
    ahead = is_ahead(place, level)
    rows_of = [
        jnp.where(ahead, jnp.exp(got_ref[size : size + 1, :]), 1.0),
        jnp.where(ahead, 1.0, jnp.exp(log_ref[0:1, :])),
    ]
    if top:
        passed = jnp.zeros_like(rows_of[0])
        for ref in sources:
            rows_of.append(jnp.exp(passed))
            passed = passed + ref[size : size + 1, :]
        bases, length = (0,), size
    else:
        length = size // 2
        bit = (place[1] >> (level + 1)) & 1
        bases = (bit * length, (1 - bit) * length)
    here_wide, there_wide, *group_wide = spread_rows(rows_of, offset, strips, head_size)
    for index, base in enumerate(bases):
        for strip in range(strips):
            one = slice(strip, strip + 1)
            for at in range(strip * part, length, strips * part):
                rows = slice(at, at + part)
                if top:
                    entering = sources[0][rows, :] * group_wide[0][one, :]
                    for ref, wide in zip(sources[1:], group_wide[1:]):
                        entering = entering + ref[rows, :] * wide[one, :]
                else:
                    entering = sources[index][rows, :]
                    rows = pl.ds(pl.multiple_of(base + at, part), part)
                got = jnp.where(ahead, got_ref[rows, :], 0.0)
                mine = jnp.where(ahead, 0.0, mine_ref[rows, :])
                here_ref[rows, :] = entering * here_wide[one, :] + got
                there_ref[rows, :] = entering * there_wide[one, :] + mine
    there_ref[size:, :] = jnp.zeros((PAD, STRIP), F32)


def down(level, chips, half, strips, head_size, place, mine, send, got, sources):
    size = mine.shape[0]
    top = 2 << level == chips
    return pl.pallas_call(
        lambda *refs: down_kernel(
            level, top, STATE // chips, half * strips, strips, head_size, *refs
        ),
        grid=(1,),
        in_specs=[SCALARS, whole(size, STRIP), tail_block(send), whole(size + PAD, STRIP)]
        + [whole(*value.shape) for value in sources],
        out_specs=[whole(size, STRIP), whole(size + PAD, STRIP)],
        out_shape=[
            jax.ShapeDtypeStruct((size, STRIP), F32),
            jax.ShapeDtypeStruct((size + PAD, STRIP), F32),
        ],
        compiler_params=pltpu.CompilerParams(vmem_limit_bytes=SMALL_VMEM),
        cost_estimate=LITTLE,
        name="down",
    )(place, mine, send, got, *sources)


def intra_kernel(
    heads, head_size, start, last,
    after_ref, x_ref, g_ref, write_ref, read_ref, rates_ref, column_ref, tail_ref, lead_ref, *refs,
):
    dx_ref, state_ref, back_ref, change_ref, *sums, row_ref, scores_ref, mask_ref, pairs_ref, \
        write_t, read_t = refs[5 if start else 0 :]
    step = pl.program_id(0)
    chunk = start + step
    lanes = x_ref.shape[1]
    per_chunk = lanes // head_size

    @pl.when(step == 0)
    def _():
        rates = rates_ref[...]
        triangle = lower(STRETCH)
        row_ref[...] = dot(rates, triangle, 1, 1, HIGHEST)
        mask_ref[...] = triangle
        scores_ref[...] = dot(read_ref[...], write_ref[...], 1, 1)
        pairs_ref[...] = refs[4][...] if start else jnp.zeros_like(pairs_ref)
        change_ref[...] = refs[3][...] if start else jnp.zeros_like(change_ref)
        write_t[...] = write_ref[...].astype(F32).T.astype(BF16)
        read_t[...] = read_ref[...].astype(F32).T.astype(BF16)

    columns = pltpu.roll(column_ref[...], STATE - chunk * per_chunk, 1)
    rows = row_ref[pl.ds(pl.multiple_of(chunk * per_chunk, per_chunk), per_chunk), :]
    causal = mask_ref[...] > 0.5
    scores = scores_ref[...]
    pairs = pairs_ref[...]
    low_half = iota((STRETCH, 2 * head_size), 1) < head_size
    adder = head_adder(chunk, head_size, lanes)
    spread = spreader(chunk, heads, head_size, lanes)
    high, low = term_pair(x_ref[...].astype(F32) * dot(tail_ref[...], spread, 1, 0))
    state_ref[...] = dot(write_t[...], high, 1, 0) + dot(write_t[...], low, 1, 0)
    high, low = term_pair(g_ref[...].astype(F32) * dot(lead_ref[...], spread, 1, 0))
    back_ref[...] = dot(read_t[...], high, 1, 0) + dot(read_t[...], low, 1, 0)
    for pair in range(per_chunk // 2):
        strip = slice(pair * 2 * head_size, (pair + 1) * 2 * head_size)
        x = x_ref[:, strip]
        g = g_ref[:, strip]
        ys, dxs = [], []
        for half in range(2):
            head = 2 * pair + half
            gap = columns[:, head : head + 1] - rows[head : head + 1, :]
            decay = jnp.where(causal, jnp.exp(gap), 0.0)
            mixing = (scores * decay).astype(BF16)
            ys.append(dot(mixing, x, 1, 0))
            dxs.append(dot(mixing, g, 0, 0))
            mine = low_half if half == 0 else jnp.logical_not(low_half)
            pairs = pairs + dot(jnp.where(mine, g, jnp.zeros_like(g)), x, 1, 1) * decay
        y = jnp.where(low_half, ys[0], ys[1])
        dx = jnp.where(low_half, dxs[0], dxs[1])
        dx_ref[:, strip] = dx
        change_ref[...] += head_sums(
            g.astype(F32) * y - x.astype(F32) * dx, adder[strip, :]
        )
    pairs_ref[...] = pairs

    @pl.when(step == pl.num_programs(0) - 1)
    def _():
        if last:
            summed = pairs_ref[...].astype(BF16)
            sums[0][...] = dot(summed, read_ref[...], 0, 0)
            sums[1][...] = dot(summed, write_ref[...], 1, 0)
        else:
            sums[0][...] = pairs_ref[...]


def intra(start, steps, after, x, g, write_map, read_map, rates, shared, earlier):
    tokens, wide = x.shape
    heads = rates.shape[0]
    last = (start + steps) * LANES == wide
    lanes = lambda rows: pl.BlockSpec((rows, LANES), lambda c: (0, start + c))
    anywhere = pl.BlockSpec(memory_space=pl.ANY)
    sums = [(tokens, STATE)] * 2 if last else [(tokens, tokens)]
    return pl.pallas_call(
        lambda *refs: intra_kernel(heads, wide // heads, start, last, *refs),
        grid=(steps,),
        in_specs=[
            whole(META, STRIP),
            lanes(tokens),
            lanes(tokens),
            whole(tokens, STATE),
            whole(tokens, STATE),
            whole(heads, tokens),
        ]
        + [whole(tokens, STRIP)] * 3
        + ([anywhere] * 3 + [whole(tokens, STATE), whole(tokens, tokens)] if earlier else []),
        out_specs=[lanes(tokens), lanes(STATE), lanes(STATE), whole(tokens, STATE)]
        + [whole(*shape) for shape in sums],
        out_shape=[
            jax.ShapeDtypeStruct((tokens, wide), F32),
            jax.ShapeDtypeStruct((STATE, wide), F32),
            jax.ShapeDtypeStruct((STATE, wide), F32),
            jax.ShapeDtypeStruct((tokens, STATE), F32),
        ]
        + [jax.ShapeDtypeStruct(shape, F32) for shape in sums],
        scratch_shapes=[
            pltpu.VMEM((heads, tokens), F32),
            pltpu.VMEM((tokens, tokens), F32),
            pltpu.VMEM((tokens, tokens), F32),
            pltpu.VMEM((tokens, tokens), F32),
            pltpu.VMEM((STATE, tokens), BF16),
            pltpu.VMEM((STATE, tokens), BF16),
        ],
        input_output_aliases={9: 0, 10: 1, 11: 2} if earlier else {},
        compiler_params=pltpu.CompilerParams(vmem_limit_bytes=SMALL_VMEM),
        cost_estimate=LITTLE,
        name="intra",
    )(after, x, g, write_map, read_map, rates, *shared[1:], *earlier)


def order_kernel(place, after_ref, here_ref, got_ref, *outs):
    size = here_ref.shape[0]
    bit = place[1] & 1
    if len(outs) == 1:
        outs[0][pl.ds(pl.multiple_of(bit * size, size), size), :] = here_ref[...]
        outs[0][pl.ds(pl.multiple_of((1 - bit) * size, size), size), :] = got_ref[:size, :]
    else:
        here, got = here_ref[...], got_ref[:size, :]
        outs[0][...] = jnp.where(bit == 0, here, got)
        outs[1][...] = jnp.where(bit == 0, got, here)


def order(pieces, place, after, here, got):
    shape = (2 * here.shape[0] // pieces, STRIP)
    return pl.pallas_call(
        order_kernel,
        grid=(1,),
        in_specs=[SCALARS, whole(META, STRIP), whole(*here.shape), whole(*got.shape)],
        out_specs=[whole(*shape)] * pieces,
        out_shape=[jax.ShapeDtypeStruct(shape, F32)] * pieces,
        compiler_params=pltpu.CompilerParams(vmem_limit_bytes=SMALL_VMEM),
        cost_estimate=LITTLE,
        name="order",
    )(place, after, here, got)


def assemble_kernel(
    heads, chips, half, head_size, place, after_ref, first_ref, state_own, back_own, *refs,
):
    state_ref, back_ref, total_ref = refs[-3:]
    pieces = (len(refs) - 3) // 2
    own_refs, far_refs = refs[:pieces], refs[pieces : 2 * pieces]
    lanes = state_ref.shape[1]
    strips = lanes // STRIP
    part = STATE // chips
    size = strips * part
    log = first_ref[chips * size : chips * size + 1, :]
    decay = spread_rows([jnp.exp(log)], half * strips, strips, head_size)[0]
    is_first = place[0] == 0
    sums = [None] * strips
    for quarter in range(chips):
        rows = slice(quarter * part, (quarter + 1) * part)
        for strip in range(strips):
            wide = slice(strip * STRIP, (strip + 1) * STRIP)
            here = slice(quarter * size + strip * part, quarter * size + (strip + 1) * part)
            piece, at = divmod(here.start, own_refs[0].shape[0])
            there = slice(at, at + part)
            own = own_refs[piece][there, :] * decay[strip : strip + 1, :] + first_ref[here, :]
            far = far_refs[piece][there, :]
            state = jnp.where(is_first, far, own).astype(BF16)
            back = jnp.where(is_first, own, far).astype(BF16)
            state_ref[rows, wide] = state
            back_ref[rows, wide] = back
            gain = state.astype(F32) * back_own[rows, wide]
            gain = gain - back.astype(F32) * state_own[rows, wide]
            sums[strip] = gain if sums[strip] is None else sums[strip] + gain
    row_sum = [
        jnp.broadcast_to(jnp.sum(value, axis=0, keepdims=True), (META, STRIP)) for value in sums
    ]
    total = head_sums(jnp.concatenate(row_sum, axis=1), head_adder(half, head_size, lanes))
    total_ref[...] = total + after_ref[...] if half else total


def assemble(heads, chips, half, place, after, first, state_own, back_own, own, far):
    wide = state_own.shape[1]
    lanes = wide // HALVES
    mine = pl.BlockSpec((STATE, lanes), lambda c: (0, half))
    return pl.pallas_call(
        lambda *refs: assemble_kernel(heads, chips, half, wide // heads, *refs),
        grid=(1,),
        in_specs=[SCALARS, whole(META, STRIP), whole(*first.shape), mine, mine]
        + [whole(*value.shape) for value in (*own, *far)],
        out_specs=[whole(STATE, lanes), whole(STATE, lanes), whole(META, STRIP)],
        out_shape=[
            jax.ShapeDtypeStruct((STATE, lanes), BF16),
            jax.ShapeDtypeStruct((STATE, lanes), BF16),
            jax.ShapeDtypeStruct((META, STRIP), F32),
        ],
        compiler_params=pltpu.CompilerParams(vmem_limit_bytes=SMALL_VMEM),
        cost_estimate=LITTLE,
        name="assemble",
    )(place, after, first, state_own, back_own, *own, *far)


def finish_kernel(
    heads, start, steps, last, x_ref, g_ref, write_ref, read_ref, tail_ref, lead_ref,
    dx_ref, db_ref, dc_ref, change_ref, state_ref, back_ref, *refs,
):
    grad_ref, db_out, dc_out, change_out, token_ref, db_sum, dc_sum, sum_out = refs[-8:]
    chunk = pl.program_id(0)
    lanes = x_ref.shape[1]
    head_size = lanes * STEPS * HALVES // heads
    wide = start + chunk

    @pl.when(chunk == 0)
    def _():
        sum_out[...] = change_ref[...]
        db_sum[...] = db_ref[...]
        dc_sum[...] = dc_ref[...]

    state = state_ref[...]
    back = back_ref[...]
    spread = spreader(wide, heads, head_size, lanes)
    tail = dot(tail_ref[...], spread, 1, 0)
    lead = dot(lead_ref[...], spread, 1, 0)
    x = x_ref[...].astype(F32)
    g = g_ref[...].astype(F32)
    y = dot(read_ref[...], state, 1, 0) * lead
    dx = dot(write_ref[...], back, 1, 0) * tail
    grad_ref[...] = (dx_ref[...] + dx).astype(BF16)
    adder = head_adder(wide, head_size, lanes)
    sum_out[...] += head_sums(g * y - x * dx, adder)
    db_sum[...] += dot((x * tail).astype(BF16), back, 1, 1)
    dc_sum[...] += dot((g * lead).astype(BF16), state, 1, 1)

    @pl.when(chunk == steps - 1)
    def _():
        token_ref[...] = jnp.zeros_like(token_ref)
        db_out[...] = db_sum[...].astype(db_out.dtype)
        dc_out[...] = dc_sum[...].astype(dc_out.dtype)
        if last:
            change_out[...] = dot(sum_out[...], lower(STRETCH), 0, 0, HIGHEST)[:heads, :]
        else:
            change_out[...] = sum_out[...]


def finish(heads, start, steps, after, x, g, write_map, read_map, shared, dx, sums, state, back, grad):
    tokens, wide = x.shape
    lanes = wide // (STEPS * HALVES)
    strip = pl.BlockSpec((tokens, lanes), lambda c: (0, start + c))
    own = pl.BlockSpec((STATE, lanes), lambda c: (0, start % STEPS + c))
    last = start + steps == STEPS * HALVES
    kind = BF16 if last else F32
    change = (heads, tokens) if last else (tokens, STATE)
    earlier = [] if grad is None else [grad]
    return pl.pallas_call(
        lambda *refs: finish_kernel(heads, start, steps, last, *refs),
        grid=(steps,),
        in_specs=[strip, strip]
        + [whole(tokens, STATE)] * 4
        + [strip]
        + [whole(tokens, STATE)] * 3
        + [own, own]
        + [pl.BlockSpec(memory_space=pl.ANY)] * len(earlier)
        + [whole(META, STRIP)],
        out_specs=[strip] + [whole(tokens, STATE)] * 2 + [whole(*change), whole(META, STRIP)],
        out_shape=[
            jax.ShapeDtypeStruct((tokens, wide), BF16),
            jax.ShapeDtypeStruct((tokens, STATE), kind),
            jax.ShapeDtypeStruct((tokens, STATE), kind),
            jax.ShapeDtypeStruct(change, F32),
            jax.ShapeDtypeStruct((META, STRIP), F32),
        ],
        scratch_shapes=[pltpu.VMEM((tokens, STATE), F32)] * 3,
        input_output_aliases={12: 0} if earlier else {},
        compiler_params=pltpu.CompilerParams(vmem_limit_bytes=SMALL_VMEM),
        cost_estimate=LITTLE,
        name="finish",
    )(x, g, write_map, read_map, *shared[2:], dx, *sums, state, back, *earlier, after)


def count_kernel(place, later_ref, total_ref, after_ref, *refs):
    got_refs, (later_out, total_out) = refs[:-2], refs[-2:]
    later, total = later_ref[...], total_ref[...] + after_ref[...]
    for step, ref in enumerate(got_refs, 1):
        later = later + jnp.where((place[1] ^ step) > place[1], ref[...], 0.0)
        total = total + ref[...]
    later_out[...] = later
    total_out[...] = total


def core_kernel(place, total_ref, after_ref, got_ref, later_out, total_out):
    later_out[...] = jnp.where(place[0] == 0, got_ref[...], 0.0)
    total_out[...] = total_ref[...] + got_ref[...] + after_ref[...]


def tiles(kernel, name, place, *values):
    return pl.pallas_call(
        kernel,
        in_specs=[SCALARS] + [whole(META, STRIP)] * len(values),
        out_specs=[whole(META, STRIP)] * 2,
        out_shape=[jax.ShapeDtypeStruct((META, STRIP), F32)] * 2,
        compiler_params=pltpu.CompilerParams(vmem_limit_bytes=SMALL_VMEM),
        cost_estimate=LITTLE,
        name=name,
    )(place, *values)


def add_later_kernel(suffix_ref, *refs):
    out_ref = refs[-1]
    heads = out_ref.shape[0]
    later = refs[0][...]
    for ref in refs[1:-1]:
        later = later + ref[...]
    out_ref[...] = suffix_ref[...] + later.T[:heads, 0:1]


def add_later(suffix, *parts):
    return pl.pallas_call(
        add_later_kernel,
        in_specs=[whole(*value.shape) for value in (suffix, *parts)],
        out_specs=whole(*suffix.shape),
        out_shape=jax.ShapeDtypeStruct(suffix.shape, F32),
        compiler_params=pltpu.CompilerParams(vmem_limit_bytes=SMALL_VMEM),
        cost_estimate=LITTLE,
        name="add_later",
    )(suffix, *parts)


def per_device(inputs, out_grad, input_map, output_map, log_decay):
    heads = log_decay.shape[0]
    head_size = inputs.shape[1] // heads
    groups, shards = lax.axis_size("grp"), lax.axis_size("seq")
    chips = shards // 2
    shard, group = lax.axis_index("seq"), lax.axis_index("grp")
    chip, core = shard >> 1, shard & 1
    place = jnp.stack([core, chip, group]).astype(jnp.int32)
    strips = inputs.shape[1] // STRIP // HALVES
    everyone = [(a, z, c) for a in range(groups) for z in range(chips) for c in range(2)]

    def move(value, target):
        pairs = []
        for a, z, c in everyone:
            to = target(a, z, c)
            if to is not None:
                pairs.append((a * shards + 2 * z + c, to[0] * shards + 2 * to[1] + to[2]))
        return lax.ppermute(value, ("grp", "seq"), pairs)

    def to_core(value):
        return move(value, lambda a, z, c: (a, z, 1 - c))

    def to_chip(value, step):
        return move(value, lambda a, z, c: (a, z ^ step, c)) if step else value

    def to_earlier(value, step):
        return move(value, lambda a, z, c: (a - step, z, c) if a >= step else None)

    def to_later(value, step):
        def target(a, z, c):
            to = a + step if c == 1 else a - step
            return (to, z, c) if 0 <= to < groups else None

        return move(value, target)

    maps = (inputs, out_grad, input_map, output_map)
    send, keep, decay, *shared = summary(chips, 0, place, *maps, log_decay, None)
    first = [to_core(send)]
    kept, decays = [keep], [decay]
    send, keep, decay = summary(chips, 1, place, *maps, log_decay, shared)
    first.append(to_core(send))
    kept.append(keep)
    decays.append(decay)

    levels = chips.bit_length() - 1
    held = [[], []]
    waiting = [None, None]

    def advance(half, step, after=None):
        fixed = (chips, half, strips, head_size, place)
        if step == 0:
            mine, send = combine(
                chips, place, first[half], kept[half], decays[half], shared[0]
            )
        elif step < levels:
            held[half][-1] += (waiting[half],)
            mine, send = up(step - 1, *fixed, *held[half][-1])
        elif step == levels:
            held[half][-1] += (waiting[half],)
            (send,) = up(step - 1, *fixed, *held[half][-1])
            waiting[half] = [to_later(send, far) for far in range(1, groups)]
            return send
        elif step <= 2 * levels:
            level = 2 * levels - step
            if level < levels - 1:
                waiting[half] = (held[half][level + 1], waiting[half])
            mine, send = down(level, *fixed, *held[half][level], waiting[half])
            held[half][level] = mine
            waiting[half] = to_chip(send, 1 << level)
            return send
        else:
            held[half] = order(2 - half, place, after, held[half][0], waiting[half])
            waiting[half] = [to_core(value) for value in held[half]]
            return held[half][0]
        held[half].append((mine, send))
        waiting[half] = to_chip(send, 1 << step)
        return send

    def entering(half, token):
        return assemble(
            heads, chips, half, place, token, first[half], state_own, back_own,
            held[half], waiting[half],
        )

    chunks = inputs.shape[1] // LANES
    rounds = 2 * levels + 2
    block, ready = (), 0
    for step in range(rounds):
        token = advance(0, step, shared[0])
        if step:
            advance(1, step - 1)
        if step < 3:
            more = pl.cdiv(chunks - ready, 3 - step)
            block = intra(ready, more, token, *maps, log_decay, shared, block)
            ready += more
            waiting[0], waiting[1], first[1], block = lax.optimization_barrier(
                (waiting[0], waiting[1], first[1], block)
            )
        elif step < rounds - 1:
            waiting[0], waiting[1] = lax.optimization_barrier((waiting[0], waiting[1]))
    dx, state_own, back_own, change, db, dc = block
    state, back, counted = entering(0, change)
    grad, *sums, token = finish(
        heads, 0, STEPS, counted, *maps, shared, dx, (db, dc, change), state, back, None
    )
    advance(1, rounds - 1, token)
    state, back, counted = entering(1, counted)

    got = to_core(counted)
    grad, *sums, token = finish(
        heads, STEPS, 1, counted, *maps, shared, dx, sums, state, back, grad
    )
    later, counted = tiles(core_kernel, "core_sum", place, counted, token, got)
    got = [to_chip(counted, step) for step in range(1, chips)]
    grad, *sums, token = finish(
        heads, STEPS + 1, 1, counted, *maps, shared, dx, sums, state, back, grad
    )
    later, counted = tiles(count_kernel, "chip_sum", place, later, counted, token, *got)
    got = [to_earlier(counted, step) for step in range(1, groups)]
    return (grad, sums[0], sums[1], add_later(sums[2], later, *got))


def solution(mesh):
    tokens = P(("grp", "seq"), None)
    in_specs = (tokens, tokens, tokens, tokens, P(None, ("grp", "seq")))
    out_specs = (tokens, tokens, tokens, P(None, ("grp", "seq")))
    return jax.shard_map(
        per_device, mesh=mesh, in_specs=in_specs, out_specs=out_specs, check_vma=False
    )
```

```python
import jax
import jax.numpy as jnp
from jax import lax
from jax.experimental import pallas as pl
from jax.experimental.pallas import tpu as pltpu
from jax.sharding import PartitionSpec as P

STATE = 128
STRETCH = 256
LANES = 512
HALVES = 2
STRIP = 128
META = 8
PAD = 2 * META
BIG_VMEM = 56 << 20
SMALL_VMEM = 24 << 20
F32 = jnp.float32
BF16 = jnp.bfloat16
HIGHEST = lax.Precision.HIGHEST


def dot(left, right, left_dim, right_dim, precision=None):
    return lax.dot_general(
        left,
        right,
        (((left_dim,), (right_dim,)), ((), ())),
        precision=precision,
        preferred_element_type=F32,
    )


def iota(shape, dim):
    return lax.broadcasted_iota(jnp.int32, shape, dim)


def lower(length):
    return (iota((length, length), 0) >= iota((length, length), 1)).astype(F32)


def thrice(rates):
    heads, length = rates.shape
    spare = jnp.zeros((STATE - 3 * heads, length), F32)
    return jnp.concatenate([rates, rates, rates, spare], axis=0)


def three_terms(value, heads):
    lane = iota(value.shape, 1)
    first = value.astype(BF16)
    rest = value - first.astype(F32)
    second = rest.astype(BF16)
    third = (rest - second.astype(F32)).astype(BF16)
    return jnp.where(lane < heads, first, jnp.where(lane < 2 * heads, second, third))


def spreader(chunk, heads, head_size, lanes):
    row = iota((STATE, lanes), 0)
    head = (iota((STATE, lanes), 1) + chunk * lanes) // head_size
    hit = (row == head) | (row == head + heads) | (row == head + 2 * heads)
    return hit.astype(F32).astype(BF16)


def head_adder(chunk, head_size, lanes):
    head = (iota((lanes, STATE), 0) + chunk * lanes) // head_size
    return (iota((lanes, STATE), 1) == head).astype(F32).astype(BF16)


def head_sums(value, adder):
    first = value.astype(BF16)
    second = (value - first.astype(F32)).astype(BF16)
    return dot(first, adder, 1, 0) + dot(second, adder, 1, 0)


def decay_terms(rates, heads):
    length = rates.shape[1]
    running = dot(lower(length), thrice(rates), 1, 1, HIGHEST)
    last = running[length - 1 : length, :]
    return (
        running,
        three_terms(jnp.exp(last - running), heads),
        three_terms(jnp.exp(running), heads),
    )


def term_pair(value):
    first = value.astype(BF16)
    return first, (value - first.astype(F32)).astype(BF16)


def lane_spread(per_strip, head_size):
    head = iota((STRIP, STRIP), 0) % per_strip
    return (iota((STRIP, STRIP), 1) // head_size == head).astype(F32)


def spread_rows(rows, offset, strips, head_size):
    per_strip = STRIP // head_size
    lane = iota((strips, STRIP), 1)
    row = iota((strips, STRIP), 0) + offset
    picked = [jnp.where(lane // per_strip == row, value, 0.0) for value in rows]
    stacked = jnp.concatenate(picked, axis=0) if len(picked) > 1 else picked[0]
    wide = dot(stacked, lane_spread(per_strip, head_size), 1, 0, HIGHEST)
    return [wide[i * strips : (i + 1) * strips, :] for i in range(len(rows))]


def whole(*shape):
    return pl.BlockSpec(shape, lambda *_: (0,) * len(shape))


def lanes_of(rows):
    return pl.BlockSpec((rows, LANES), lambda c: (0, c))


def half_lanes(rows, lanes, half, steps):
    return pl.BlockSpec((rows, lanes), lambda c: (0, half * steps + c))


LITTLE = pl.CostEstimate(flops=1, bytes_accessed=1, transcendentals=0)
SCALARS = pl.BlockSpec(memory_space=pltpu.SMEM)
STEPS = 2


def summary_kernel(heads, chips, half, place, x_ref, g_ref, write_ref, read_ref, *refs):
    chunk = pl.program_id(0)
    lanes = x_ref.shape[1]
    strips = lanes // STRIP
    half_strips = strips * STEPS
    head_size = lanes * STEPS * HALVES // heads
    part = STATE // chips
    if half == 0:
        rates_ref, send_ref, keep_ref, decay_ref, log_ref, run_ref, tail_ref, lead_ref = refs[:8]
    else:
        log_ref, tail_ref, lead_ref, send_ref, keep_ref, decay_ref = refs[:6]
    write_t, read_t = refs[-2:]

    @pl.when(chunk == 0)
    def _():
        if half == 0:
            running, tail, lead = decay_terms(rates_ref[...], heads)
            run_ref[...] = running
            tail_ref[...] = tail
            lead_ref[...] = lead
            log_ref[...] = jnp.broadcast_to(running[STRETCH - 1 :, :], (META, STRIP))
        send_ref[pl.ds(half_strips * STATE, META), :] = log_ref[...]
        write_t[...] = write_ref[...].astype(F32).T.astype(BF16)
        read_t[...] = read_ref[...].astype(F32).T.astype(BF16)

    spread = spreader(half * STEPS + chunk, heads, head_size, lanes)
    tail = dot(tail_ref[...], spread, 1, 0)
    lead = dot(lead_ref[...], spread, 1, 0)
    inputs_tail = (x_ref[...].astype(F32) * tail).astype(BF16)
    grads_lead = (g_ref[...].astype(F32) * lead).astype(BF16)
    state = dot(write_t[...], inputs_tail, 1, 0)
    back = dot(read_t[...], grads_lead, 1, 0)
    first = place[0] == 0
    send = jnp.where(first, state, back)
    keep = jnp.where(first, back, state)
    for strip in range(strips):
        at = chunk * strips + strip
        wide = slice(strip * STRIP, (strip + 1) * STRIP)
        decay_ref[pl.ds(at, 1), :] = lead[STRETCH - 1 :, wide]
        for quarter in range(chips):
            rows = pl.ds(pl.multiple_of((quarter * half_strips + at) * part, part), part)
            mine = slice(quarter * part, (quarter + 1) * part)
            send_ref[rows, :] = send[mine, wide]
            keep_ref[rows, :] = keep[mine, wide]


def summary(chips, half, place, x, g, write_map, read_map, rates, shared):
    tokens, wide = x.shape
    heads = rates.shape[0]
    lanes = wide // (STEPS * HALVES)
    strips = wide // STRIP // HALVES
    terms = [
        jax.ShapeDtypeStruct((META, STRIP), F32),
        jax.ShapeDtypeStruct((tokens, STRIP), F32),
        jax.ShapeDtypeStruct((tokens, STRIP), BF16),
        jax.ShapeDtypeStruct((tokens, STRIP), BF16),
    ]
    out_shape = [
        jax.ShapeDtypeStruct((strips * STATE + META, STRIP), F32),
        jax.ShapeDtypeStruct((strips * STATE, STRIP), F32),
        jax.ShapeDtypeStruct((strips, STRIP), F32),
    ]
    if half == 0:
        extra = [rates]
        out_shape = out_shape + terms
    else:
        extra = [shared[0], shared[2], shared[3]]
    return pl.pallas_call(
        lambda *refs: summary_kernel(heads, chips, half, *refs),
        grid=(STEPS,),
        in_specs=[
            SCALARS,
            half_lanes(tokens, lanes, half, STEPS),
            half_lanes(tokens, lanes, half, STEPS),
            whole(tokens, STATE),
            whole(tokens, STATE),
        ]
        + [whole(*value.shape) for value in extra],
        out_specs=[whole(*out.shape) for out in out_shape],
        out_shape=out_shape,
        scratch_shapes=[
            pltpu.VMEM((STATE, tokens), BF16),
            pltpu.VMEM((STATE, tokens), BF16),
        ],
        compiler_params=pltpu.CompilerParams(vmem_limit_bytes=BIG_VMEM),
        cost_estimate=LITTLE,
        name="summary",
    )(place, x, g, write_map, read_map, *extra)


def combine_kernel(chips, place, first_ref, keep_ref, decay_ref, log_ref, mine_ref, send_ref):
    strips = decay_ref.shape[0]
    part = STATE // chips
    size = mine_ref.shape[0]
    bit = place[1] & 1
    for base, out_ref in ((bit * size, mine_ref), ((1 - bit) * size, send_ref)):
        for strip in range(strips):
            decay = decay_ref[strip : strip + 1, :]
            for at in range(strip * part, size, strips * part):
                rows = pl.ds(pl.multiple_of(base + at, part), part)
                out_ref[at : at + part, :] = first_ref[rows, :] * decay + keep_ref[rows, :]
    meta = first_ref[2 * size :, :] + log_ref[...]
    send_ref[size : size + META, :] = meta
    send_ref[size + META :, :] = meta


def halves(size):
    return (
        [whole(size, STRIP), whole(size + PAD, STRIP)],
        [
            jax.ShapeDtypeStruct((size, STRIP), F32),
            jax.ShapeDtypeStruct((size + PAD, STRIP), F32),
        ],
    )


def combine(chips, place, first, keep, decay, log):
    out_specs, out_shape = halves(keep.shape[0] // 2)
    return pl.pallas_call(
        lambda *refs: combine_kernel(chips, *refs),
        in_specs=[SCALARS] + [whole(*value.shape) for value in (first, keep, decay, log)],
        out_specs=out_specs,
        out_shape=out_shape,
        compiler_params=pltpu.CompilerParams(vmem_limit_bytes=SMALL_VMEM),
        cost_estimate=LITTLE,
        name="combine",
    )(place, first, keep, decay, log)


def is_ahead(place, level):
    return ((place[1] >> level) & 1) == place[0]


def tail_block(value):
    return pl.BlockSpec((META, STRIP), lambda c: (value.shape[0] // META - 1, 0))


def up_kernel(level, last, part, offset, strips, head_size, place, mine_ref, log_ref, got_ref, *outs):
    size = mine_ref.shape[0]
    ahead = is_ahead(place, level)
    mine_log, got_log = log_ref[0:1, :], got_ref[size : size + 1, :]
    mine_wide, got_wide = spread_rows(
        [jnp.where(ahead, 1.0, jnp.exp(got_log)), jnp.where(ahead, jnp.exp(mine_log), 1.0)],
        offset,
        strips,
        head_size,
    )
    bit = (place[1] >> (level + 1)) & 1
    half = size if last else size // 2
    targets = ((0, outs[0]),) if last else ((bit * half, outs[0]), ((1 - bit) * half, outs[1]))
    for base, out_ref in targets:
        for strip in range(strips):
            one = slice(strip, strip + 1)
            for at in range(strip * part, half, strips * part):
                rows = slice(at, at + part)
                if not last:
                    rows = pl.ds(pl.multiple_of(base + at, part), part)
                out_ref[at : at + part, :] = (
                    mine_ref[rows, :] * mine_wide[one, :] + got_ref[rows, :] * got_wide[one, :]
                )
    outs[-1][half:, :] = jnp.broadcast_to(mine_log + got_log, (META if last else PAD, STRIP))


def up(level, chips, half, strips, head_size, place, mine, send, got):
    size = mine.shape[0]
    last = 2 << level == chips
    out_specs, out_shape = halves(size if last else size // 2)
    if last:
        out_specs = [whole(size + META, STRIP)]
        out_shape = [jax.ShapeDtypeStruct((size + META, STRIP), F32)]
    return pl.pallas_call(
        lambda *refs: up_kernel(
            level, last, STATE // chips, half * strips, strips, head_size, *refs
        ),
        grid=(1,),
        in_specs=[SCALARS, whole(size, STRIP), tail_block(send), whole(size + PAD, STRIP)],
        out_specs=out_specs,
        out_shape=out_shape,
        compiler_params=pltpu.CompilerParams(vmem_limit_bytes=SMALL_VMEM),
        cost_estimate=LITTLE,
        name="up",
    )(place, mine, send, got)


def down_kernel(level, top, part, offset, strips, head_size, place, mine_ref, log_ref, got_ref, *refs):
    sources, (here_ref, there_ref) = refs[:-2], refs[-2:]
    size = mine_ref.shape[0]
    ahead = is_ahead(place, level)
    rows_of = [
        jnp.where(ahead, jnp.exp(got_ref[size : size + 1, :]), 1.0),
        jnp.where(ahead, 1.0, jnp.exp(log_ref[0:1, :])),
    ]
    if top:
        passed = jnp.zeros_like(rows_of[0])
        for ref in sources:
            rows_of.append(jnp.exp(passed))
            passed = passed + ref[size : size + 1, :]
        bases, length = (0,), size
    else:
        length = size // 2
        bit = (place[1] >> (level + 1)) & 1
        bases = (bit * length, (1 - bit) * length)
    here_wide, there_wide, *group_wide = spread_rows(rows_of, offset, strips, head_size)
    for index, base in enumerate(bases):
        for strip in range(strips):
            one = slice(strip, strip + 1)
            for at in range(strip * part, length, strips * part):
                rows = slice(at, at + part)
                if top:
                    entering = sources[0][rows, :] * group_wide[0][one, :]
                    for ref, wide in zip(sources[1:], group_wide[1:]):
                        entering = entering + ref[rows, :] * wide[one, :]
                else:
                    entering = sources[index][rows, :]
                    rows = pl.ds(pl.multiple_of(base + at, part), part)
                got = jnp.where(ahead, got_ref[rows, :], 0.0)
                mine = jnp.where(ahead, 0.0, mine_ref[rows, :])
                here_ref[rows, :] = entering * here_wide[one, :] + got
                there_ref[rows, :] = entering * there_wide[one, :] + mine
    there_ref[size:, :] = jnp.zeros((PAD, STRIP), F32)


def down(level, chips, half, strips, head_size, place, mine, send, got, sources):
    size = mine.shape[0]
    top = 2 << level == chips
    return pl.pallas_call(
        lambda *refs: down_kernel(
            level, top, STATE // chips, half * strips, strips, head_size, *refs
        ),
        grid=(1,),
        in_specs=[SCALARS, whole(size, STRIP), tail_block(send), whole(size + PAD, STRIP)]
        + [whole(*value.shape) for value in sources],
        out_specs=[whole(size, STRIP), whole(size + PAD, STRIP)],
        out_shape=[
            jax.ShapeDtypeStruct((size, STRIP), F32),
            jax.ShapeDtypeStruct((size + PAD, STRIP), F32),
        ],
        compiler_params=pltpu.CompilerParams(vmem_limit_bytes=SMALL_VMEM),
        cost_estimate=LITTLE,
        name="down",
    )(place, mine, send, got, *sources)


def intra_kernel(
    heads, head_size, start, last,
    after_ref, x_ref, g_ref, write_ref, read_ref, rates_ref, column_ref, tail_ref, lead_ref, *refs,
):
    dx_ref, state_ref, back_ref, change_ref, *sums, row_ref, scores_ref, mask_ref, pairs_ref, \
        write_t, read_t = refs[5 if start else 0 :]
    step = pl.program_id(0)
    chunk = start + step
    lanes = x_ref.shape[1]
    per_chunk = lanes // head_size

    @pl.when(step == 0)
    def _():
        rates = rates_ref[...]
        triangle = lower(STRETCH)
        row_ref[...] = dot(rates, triangle, 1, 1, HIGHEST)
        mask_ref[...] = triangle
        scores_ref[...] = dot(read_ref[...], write_ref[...], 1, 1)
        pairs_ref[...] = refs[4][...] if start else jnp.zeros_like(pairs_ref)
        change_ref[...] = refs[3][...] if start else jnp.zeros_like(change_ref)
        write_t[...] = write_ref[...].astype(F32).T.astype(BF16)
        read_t[...] = read_ref[...].astype(F32).T.astype(BF16)

    columns = pltpu.roll(column_ref[...], STATE - chunk * per_chunk, 1)
    rows = row_ref[pl.ds(pl.multiple_of(chunk * per_chunk, per_chunk), per_chunk), :]
    causal = mask_ref[...] > 0.5
    scores = scores_ref[...]
    pairs = pairs_ref[...]
    low_half = iota((STRETCH, 2 * head_size), 1) < head_size
    adder = head_adder(chunk, head_size, lanes)
    spread = spreader(chunk, heads, head_size, lanes)
    high, low = term_pair(x_ref[...].astype(F32) * dot(tail_ref[...], spread, 1, 0))
    state_ref[...] = dot(write_t[...], high, 1, 0) + dot(write_t[...], low, 1, 0)
    high, low = term_pair(g_ref[...].astype(F32) * dot(lead_ref[...], spread, 1, 0))
    back_ref[...] = dot(read_t[...], high, 1, 0) + dot(read_t[...], low, 1, 0)
    for pair in range(per_chunk // 2):
        strip = slice(pair * 2 * head_size, (pair + 1) * 2 * head_size)
        x = x_ref[:, strip]
        g = g_ref[:, strip]
        ys, dxs = [], []
        for half in range(2):
            head = 2 * pair + half
            gap = columns[:, head : head + 1] - rows[head : head + 1, :]
            decay = jnp.where(causal, jnp.exp(gap), 0.0)
            mixing = (scores * decay).astype(BF16)
            ys.append(dot(mixing, x, 1, 0))
            dxs.append(dot(mixing, g, 0, 0))
            mine = low_half if half == 0 else jnp.logical_not(low_half)
            pairs = pairs + dot(jnp.where(mine, g, jnp.zeros_like(g)), x, 1, 1) * decay
        y = jnp.where(low_half, ys[0], ys[1])
        dx = jnp.where(low_half, dxs[0], dxs[1])
        dx_ref[:, strip] = dx
        change_ref[...] += head_sums(
            g.astype(F32) * y - x.astype(F32) * dx, adder[strip, :]
        )
    pairs_ref[...] = pairs

    @pl.when(step == pl.num_programs(0) - 1)
    def _():
        if last:
            summed = pairs_ref[...].astype(BF16)
            sums[0][...] = dot(summed, read_ref[...], 0, 0)
            sums[1][...] = dot(summed, write_ref[...], 1, 0)
        else:
            sums[0][...] = pairs_ref[...]


def intra(start, steps, after, x, g, write_map, read_map, rates, shared, earlier):
    tokens, wide = x.shape
    heads = rates.shape[0]
    last = (start + steps) * LANES == wide
    lanes = lambda rows: pl.BlockSpec((rows, LANES), lambda c: (0, start + c))
    anywhere = pl.BlockSpec(memory_space=pl.ANY)
    sums = [(tokens, STATE)] * 2 if last else [(tokens, tokens)]
    return pl.pallas_call(
        lambda *refs: intra_kernel(heads, wide // heads, start, last, *refs),
        grid=(steps,),
        in_specs=[
            whole(META, STRIP),
            lanes(tokens),
            lanes(tokens),
            whole(tokens, STATE),
            whole(tokens, STATE),
            whole(heads, tokens),
        ]
        + [whole(tokens, STRIP)] * 3
        + ([anywhere] * 3 + [whole(tokens, STATE), whole(tokens, tokens)] if earlier else []),
        out_specs=[lanes(tokens), lanes(STATE), lanes(STATE), whole(tokens, STATE)]
        + [whole(*shape) for shape in sums],
        out_shape=[
            jax.ShapeDtypeStruct((tokens, wide), F32),
            jax.ShapeDtypeStruct((STATE, wide), F32),
            jax.ShapeDtypeStruct((STATE, wide), F32),
            jax.ShapeDtypeStruct((tokens, STATE), F32),
        ]
        + [jax.ShapeDtypeStruct(shape, F32) for shape in sums],
        scratch_shapes=[
            pltpu.VMEM((heads, tokens), F32),
            pltpu.VMEM((tokens, tokens), F32),
            pltpu.VMEM((tokens, tokens), F32),
            pltpu.VMEM((tokens, tokens), F32),
            pltpu.VMEM((STATE, tokens), BF16),
            pltpu.VMEM((STATE, tokens), BF16),
        ],
        input_output_aliases={9: 0, 10: 1, 11: 2} if earlier else {},
        compiler_params=pltpu.CompilerParams(vmem_limit_bytes=SMALL_VMEM),
        cost_estimate=LITTLE,
        name="intra",
    )(after, x, g, write_map, read_map, rates, *shared[1:], *earlier)


def order_kernel(place, here_ref, got_ref, low_ref, high_ref):
    bit = place[1] & 1
    here, got = here_ref[...], got_ref[: here_ref.shape[0], :]
    low_ref[...] = jnp.where(bit == 0, here, got)
    high_ref[...] = jnp.where(bit == 0, got, here)


def order(place, here, got):
    return pl.pallas_call(
        order_kernel,
        in_specs=[SCALARS, whole(*here.shape), whole(*got.shape)],
        out_specs=[whole(*here.shape)] * 2,
        out_shape=[jax.ShapeDtypeStruct(here.shape, F32)] * 2,
        compiler_params=pltpu.CompilerParams(vmem_limit_bytes=SMALL_VMEM),
        cost_estimate=LITTLE,
        name="order",
    )(place, here, got)


def assemble_kernel(
    heads, chips, half, head_size, ordered,
    place, after_ref, first_ref, state_own, back_own, *refs,
):
    own_refs, far_refs, (state_ref, back_ref, total_ref) = refs[:2], refs[2:4], refs[4:]
    bit = 0 if ordered else place[1] & 1
    lanes = state_ref.shape[1]
    strips = lanes // STRIP
    part = STATE // chips
    size = strips * part
    log = first_ref[chips * size : chips * size + 1, :]
    decay = spread_rows([jnp.exp(log)], half * strips, strips, head_size)[0]
    is_first = place[0] == 0
    sums = [None] * strips
    for quarter in range(chips):
        rows = slice(quarter * part, (quarter + 1) * part)
        for strip in range(strips):
            wide = slice(strip * STRIP, (strip + 1) * STRIP)
            here = slice(quarter * size + strip * part, quarter * size + (strip + 1) * part)
            piece, at = divmod(here.start, chips // 2 * size)
            there = slice(at, at + part)
            own, far = own_refs[piece][there, :], far_refs[piece][there, :]
            if not ordered:
                own = jnp.where(bit == 0, own, own_refs[1 - piece][there, :])
                far = jnp.where(bit == 0, far, far_refs[1 - piece][there, :])
            own = own * decay[strip : strip + 1, :] + first_ref[here, :]
            state = jnp.where(is_first, far, own).astype(BF16)
            back = jnp.where(is_first, own, far).astype(BF16)
            state_ref[rows, wide] = state
            back_ref[rows, wide] = back
            gain = state.astype(F32) * back_own[rows, wide]
            gain = gain - back.astype(F32) * state_own[rows, wide]
            sums[strip] = gain if sums[strip] is None else sums[strip] + gain
    row_sum = [
        jnp.broadcast_to(jnp.sum(value, axis=0, keepdims=True), (META, STRIP)) for value in sums
    ]
    total = head_sums(jnp.concatenate(row_sum, axis=1), head_adder(half, head_size, lanes))
    total_ref[...] = total + after_ref[...] if half else total


def assemble(heads, chips, half, ordered, place, after, first, state_own, back_own, own, far):
    wide = state_own.shape[1]
    lanes = wide // HALVES
    mine = pl.BlockSpec((STATE, lanes), lambda c: (0, half))
    return pl.pallas_call(
        lambda *refs: assemble_kernel(heads, chips, half, wide // heads, ordered, *refs),
        grid=(1,),
        in_specs=[SCALARS, whole(META, STRIP), whole(*first.shape), mine, mine]
        + [whole(*value.shape) for value in (*own, *far)],
        out_specs=[whole(STATE, lanes), whole(STATE, lanes), whole(META, STRIP)],
        out_shape=[
            jax.ShapeDtypeStruct((STATE, lanes), BF16),
            jax.ShapeDtypeStruct((STATE, lanes), BF16),
            jax.ShapeDtypeStruct((META, STRIP), F32),
        ],
        compiler_params=pltpu.CompilerParams(vmem_limit_bytes=SMALL_VMEM),
        cost_estimate=LITTLE,
        name="assemble",
    )(place, after, first, state_own, back_own, *own, *far)


def finish_kernel(
    heads, start, steps, last, x_ref, g_ref, write_ref, read_ref, tail_ref, lead_ref,
    dx_ref, db_ref, dc_ref, change_ref, state_ref, back_ref, *refs,
):
    grad_ref, db_out, dc_out, change_out, token_ref, db_sum, dc_sum, sum_out = refs[-8:]
    chunk = pl.program_id(0)
    lanes = x_ref.shape[1]
    head_size = lanes * STEPS * HALVES // heads
    wide = start + chunk

    @pl.when(chunk == 0)
    def _():
        sum_out[...] = change_ref[...]
        db_sum[...] = db_ref[...]
        dc_sum[...] = dc_ref[...]

    state = state_ref[...]
    back = back_ref[...]
    spread = spreader(wide, heads, head_size, lanes)
    tail = dot(tail_ref[...], spread, 1, 0)
    lead = dot(lead_ref[...], spread, 1, 0)
    x = x_ref[...].astype(F32)
    g = g_ref[...].astype(F32)
    y = dot(read_ref[...], state, 1, 0) * lead
    dx = dot(write_ref[...], back, 1, 0) * tail
    grad_ref[...] = (dx_ref[...] + dx).astype(BF16)
    adder = head_adder(wide, head_size, lanes)
    sum_out[...] += head_sums(g * y - x * dx, adder)
    db_sum[...] += dot((x * tail).astype(BF16), back, 1, 1)
    dc_sum[...] += dot((g * lead).astype(BF16), state, 1, 1)

    @pl.when(chunk == steps - 1)
    def _():
        token_ref[...] = refs[-9][...]
        db_out[...] = db_sum[...].astype(db_out.dtype)
        dc_out[...] = dc_sum[...].astype(dc_out.dtype)
        if last:
            change_out[...] = dot(sum_out[...], lower(STRETCH), 0, 0, HIGHEST)[:heads, :]
        else:
            change_out[...] = sum_out[...]


def finish(heads, start, steps, after, x, g, write_map, read_map, shared, dx, sums, state, back, grad):
    tokens, wide = x.shape
    lanes = wide // (STEPS * HALVES)
    strip = pl.BlockSpec((tokens, lanes), lambda c: (0, start + c))
    own = pl.BlockSpec((STATE, lanes), lambda c: (0, start % STEPS + c))
    last = start + steps == STEPS * HALVES
    kind = BF16 if last else F32
    change = (heads, tokens) if last else (tokens, STATE)
    earlier = [] if grad is None else [grad]
    return pl.pallas_call(
        lambda *refs: finish_kernel(heads, start, steps, last, *refs),
        grid=(steps,),
        in_specs=[strip, strip]
        + [whole(tokens, STATE)] * 4
        + [strip]
        + [whole(tokens, STATE)] * 3
        + [own, own]
        + [pl.BlockSpec(memory_space=pl.ANY)] * len(earlier)
        + [whole(META, STRIP)],
        out_specs=[strip] + [whole(tokens, STATE)] * 2 + [whole(*change), whole(META, STRIP)],
        out_shape=[
            jax.ShapeDtypeStruct((tokens, wide), BF16),
            jax.ShapeDtypeStruct((tokens, STATE), kind),
            jax.ShapeDtypeStruct((tokens, STATE), kind),
            jax.ShapeDtypeStruct(change, F32),
            jax.ShapeDtypeStruct((META, STRIP), F32),
        ],
        scratch_shapes=[pltpu.VMEM((tokens, STATE), F32)] * 3,
        input_output_aliases={12: 0} if earlier else {},
        compiler_params=pltpu.CompilerParams(vmem_limit_bytes=SMALL_VMEM),
        cost_estimate=LITTLE,
        name="finish",
    )(x, g, write_map, read_map, *shared[2:], dx, *sums, state, back, *earlier, after)


def count_kernel(place, after_ref, later_ref, total_ref, *refs):
    got_refs, (later_out, total_out) = refs[:-2], refs[-2:]
    later, total = later_ref[...], total_ref[...]
    for step, ref in enumerate(got_refs, 1):
        later = later + jnp.where((place[1] ^ step) > place[1], ref[...], 0.0)
        total = total + ref[...]
    later_out[...] = later
    total_out[...] = total


def core_kernel(place, total_ref, got_ref, later_out, total_out):
    later_out[...] = jnp.where(place[0] == 0, got_ref[...], 0.0)
    total_out[...] = total_ref[...] + got_ref[...]


def tiles(kernel, name, place, *values):
    return pl.pallas_call(
        kernel,
        in_specs=[SCALARS] + [whole(META, STRIP)] * len(values),
        out_specs=[whole(META, STRIP)] * 2,
        out_shape=[jax.ShapeDtypeStruct((META, STRIP), F32)] * 2,
        compiler_params=pltpu.CompilerParams(vmem_limit_bytes=SMALL_VMEM),
        cost_estimate=LITTLE,
        name=name,
    )(place, *values)


def add_later_kernel(suffix_ref, *refs):
    out_ref = refs[-1]
    heads = out_ref.shape[0]
    later = refs[0][...]
    for ref in refs[1:-1]:
        later = later + ref[...]
    out_ref[...] = suffix_ref[...] + later.T[:heads, 0:1]


def add_later(suffix, *parts):
    return pl.pallas_call(
        add_later_kernel,
        in_specs=[whole(*value.shape) for value in (suffix, *parts)],
        out_specs=whole(*suffix.shape),
        out_shape=jax.ShapeDtypeStruct(suffix.shape, F32),
        compiler_params=pltpu.CompilerParams(vmem_limit_bytes=SMALL_VMEM),
        cost_estimate=LITTLE,
        name="add_later",
    )(suffix, *parts)


def per_device(inputs, out_grad, input_map, output_map, log_decay):
    heads = log_decay.shape[0]
    head_size = inputs.shape[1] // heads
    groups, shards = lax.axis_size("grp"), lax.axis_size("seq")
    chips = shards // 2
    shard, group = lax.axis_index("seq"), lax.axis_index("grp")
    chip, core = shard >> 1, shard & 1
    place = jnp.stack([core, chip, group]).astype(jnp.int32)
    strips = inputs.shape[1] // STRIP // HALVES
    everyone = [(a, z, c) for a in range(groups) for z in range(chips) for c in range(2)]

    def move(value, target):
        pairs = []
        for a, z, c in everyone:
            to = target(a, z, c)
            if to is not None:
                pairs.append((a * shards + 2 * z + c, to[0] * shards + 2 * to[1] + to[2]))
        return lax.ppermute(value, ("grp", "seq"), pairs)

    def to_core(value):
        return move(value, lambda a, z, c: (a, z, 1 - c))

    def to_chip(value, step):
        return move(value, lambda a, z, c: (a, z ^ step, c)) if step else value

    def to_earlier(value, step):
        return move(value, lambda a, z, c: (a - step, z, c) if a >= step else None)

    def to_later(value, step):
        def target(a, z, c):
            to = a + step if c == 1 else a - step
            return (to, z, c) if 0 <= to < groups else None

        return move(value, target)

    maps = (inputs, out_grad, input_map, output_map)
    send, keep, decay, *shared = summary(chips, 0, place, *maps, log_decay, None)
    first = [to_core(send)]
    kept, decays = [keep], [decay]
    send, keep, decay = summary(chips, 1, place, *maps, log_decay, shared)
    first.append(to_core(send))
    kept.append(keep)
    decays.append(decay)

    levels = chips.bit_length() - 1
    held = [[], []]
    waiting = [None, None]

    def advance(half, step):
        fixed = (chips, half, strips, head_size, place)
        if step == 0:
            mine, send = combine(
                chips, place, first[half], kept[half], decays[half], shared[0]
            )
        elif step < levels:
            held[half][-1] += (waiting[half],)
            mine, send = up(step - 1, *fixed, *held[half][-1])
        elif step == levels:
            held[half][-1] += (waiting[half],)
            (send,) = up(step - 1, *fixed, *held[half][-1])
            waiting[half] = [to_later(send, far) for far in range(1, groups)]
            return send
        elif step <= 2 * levels:
            level = 2 * levels - step
            if level < levels - 1:
                waiting[half] = (held[half][level + 1], waiting[half])
            mine, send = down(level, *fixed, *held[half][level], waiting[half])
            held[half][level] = mine
            waiting[half] = to_chip(send, 1 << level)
            return send
        else:
            held[half] = order(place, held[half][0], waiting[half])
            waiting[half] = [to_core(value) for value in held[half]]
            return held[half][0]
        held[half].append((mine, send))
        waiting[half] = to_chip(send, 1 << step)
        return send

    chunks = inputs.shape[1] // LANES
    rounds = 2 * levels + 2
    block, ready = (), 0
    for step in range(rounds):
        token = advance(0, step)
        if step:
            advance(1, step - 1)
        if step < 3:
            more = pl.cdiv(chunks - ready, 3 - step)
            block = intra(ready, more, token, *maps, log_decay, shared, block)
            ready += more
            waiting[0], waiting[1], first[1], block = lax.optimization_barrier(
                (waiting[0], waiting[1], first[1], block)
            )
        elif step < rounds - 1:
            waiting[0], waiting[1] = lax.optimization_barrier((waiting[0], waiting[1]))
    dx, state_own, back_own, change, db, dc = block
    own_b = held[1][0]
    far_b = to_core(own_b)
    state, back, counted = assemble(
        heads, chips, 0, True, place, change, first[0], state_own, back_own, held[0], waiting[0]
    )
    grad, *sums, counted = finish(
        heads, 0, STEPS, counted, *maps, shared, dx, (db, dc, change), state, back, None
    )
    got, far_b, counted = lax.optimization_barrier((waiting[1], far_b, counted))
    own_b, far_b = (own_b, got), (far_b, to_core(got))
    state, back, counted = assemble(
        heads, chips, 1, False, place, counted, first[1], state_own, back_own, own_b, far_b
    )

    later, counted = tiles(core_kernel, "core_sum", place, counted, to_core(counted))
    got = [to_chip(counted, step) for step in range(1, chips)]
    grad, *sums, token = finish(
        heads, STEPS, 1, counted, *maps, shared, dx, sums, state, back, grad
    )
    later, counted = tiles(count_kernel, "chip_sum", place, token, later, counted, *got)
    got = [to_earlier(counted, step) for step in range(1, groups)]
    grad, *sums, _ = finish(
        heads, STEPS + 1, 1, counted, *maps, shared, dx, sums, state, back, grad
    )
    return (grad, sums[0], sums[1], add_later(sums[2], later, *got))


def solution(mesh):
    tokens = P(("grp", "seq"), None)
    in_specs = (tokens, tokens, tokens, tokens, P(None, ("grp", "seq")))
    out_specs = (tokens, tokens, tokens, P(None, ("grp", "seq")))
    return jax.shard_map(
        per_device, mesh=mesh, in_specs=in_specs, out_specs=out_specs, check_vma=False
    )
```

```python
import jax
import jax.numpy as jnp
from jax import lax
from jax.experimental import pallas as pl
from jax.experimental.pallas import tpu as pltpu
from jax.sharding import PartitionSpec as P

STATE = 128
STRETCH = 256
LANES = 512
HALVES = 2
STRIP = 128
META = 8
PAD = 2 * META
BIG_VMEM = 56 << 20
SMALL_VMEM = 24 << 20
F32 = jnp.float32
BF16 = jnp.bfloat16
HIGHEST = lax.Precision.HIGHEST


def dot(left, right, left_dim, right_dim, precision=None):
    return lax.dot_general(
        left,
        right,
        (((left_dim,), (right_dim,)), ((), ())),
        precision=precision,
        preferred_element_type=F32,
    )


def iota(shape, dim):
    return lax.broadcasted_iota(jnp.int32, shape, dim)


def lower(length):
    return (iota((length, length), 0) >= iota((length, length), 1)).astype(F32)


def thrice(rates):
    heads, length = rates.shape
    spare = jnp.zeros((STATE - 3 * heads, length), F32)
    return jnp.concatenate([rates, rates, rates, spare], axis=0)


def three_terms(value, heads):
    lane = iota(value.shape, 1)
    first = value.astype(BF16)
    rest = value - first.astype(F32)
    second = rest.astype(BF16)
    third = (rest - second.astype(F32)).astype(BF16)
    return jnp.where(lane < heads, first, jnp.where(lane < 2 * heads, second, third))


def spreader(chunk, heads, head_size, lanes):
    row = iota((STATE, lanes), 0)
    head = (iota((STATE, lanes), 1) + chunk * lanes) // head_size
    hit = (row == head) | (row == head + heads) | (row == head + 2 * heads)
    return hit.astype(F32).astype(BF16)


def head_adder(chunk, head_size, lanes):
    head = (iota((lanes, STATE), 0) + chunk * lanes) // head_size
    return (iota((lanes, STATE), 1) == head).astype(F32).astype(BF16)


def head_sums(value, adder):
    first = value.astype(BF16)
    second = (value - first.astype(F32)).astype(BF16)
    return dot(first, adder, 1, 0) + dot(second, adder, 1, 0)


def decay_terms(rates, heads):
    length = rates.shape[1]
    running = dot(lower(length), thrice(rates), 1, 1, HIGHEST)
    last = running[length - 1 : length, :]
    return (
        running,
        three_terms(jnp.exp(last - running), heads),
        three_terms(jnp.exp(running), heads),
    )


def term_pair(value):
    first = value.astype(BF16)
    return first, (value - first.astype(F32)).astype(BF16)


def lane_spread(per_strip, head_size):
    head = iota((STRIP, STRIP), 0) % per_strip
    return (iota((STRIP, STRIP), 1) // head_size == head).astype(F32)


def spread_rows(rows, offset, strips, head_size):
    per_strip = STRIP // head_size
    lane = iota((strips, STRIP), 1)
    row = iota((strips, STRIP), 0) + offset
    picked = [jnp.where(lane // per_strip == row, value, 0.0) for value in rows]
    stacked = jnp.concatenate(picked, axis=0) if len(picked) > 1 else picked[0]
    wide = dot(stacked, lane_spread(per_strip, head_size), 1, 0, HIGHEST)
    return [wide[i * strips : (i + 1) * strips, :] for i in range(len(rows))]


def whole(*shape):
    return pl.BlockSpec(shape, lambda *_: (0,) * len(shape))


def lanes_of(rows):
    return pl.BlockSpec((rows, LANES), lambda c: (0, c))


def half_lanes(rows, lanes, half, steps):
    return pl.BlockSpec((rows, lanes), lambda c: (0, half * steps + c))


LITTLE = pl.CostEstimate(flops=1, bytes_accessed=1, transcendentals=0)


def position():
    shard = lax.axis_index("seq")
    return shard & 1, shard >> 1


STEPS = 2


def summary_kernel(heads, chips, half, x_ref, g_ref, write_ref, read_ref, *refs):
    place = position()
    chunk = pl.program_id(0)
    lanes = x_ref.shape[1]
    strips = lanes // STRIP
    half_strips = strips * STEPS
    head_size = lanes * STEPS * HALVES // heads
    part = STATE // chips
    if half == 0:
        rates_ref, send_ref, keep_ref, decay_ref, log_ref, run_ref, tail_ref, lead_ref = refs[:8]
    else:
        log_ref, tail_ref, lead_ref, send_ref, keep_ref, decay_ref = refs[:6]
    write_t, read_t = refs[-2:]

    @pl.when(chunk == 0)
    def _():
        if half == 0:
            running, tail, lead = decay_terms(rates_ref[...], heads)
            run_ref[...] = running
            tail_ref[...] = tail
            lead_ref[...] = lead
            log_ref[...] = jnp.broadcast_to(running[STRETCH - 1 :, :], (META, STRIP))
        send_ref[pl.ds(half_strips * STATE, META), :] = log_ref[...]
        write_t[...] = write_ref[...].astype(F32).T.astype(BF16)
        read_t[...] = read_ref[...].astype(F32).T.astype(BF16)

    spread = spreader(half * STEPS + chunk, heads, head_size, lanes)
    tail = dot(tail_ref[...], spread, 1, 0)
    lead = dot(lead_ref[...], spread, 1, 0)
    inputs_tail = (x_ref[...].astype(F32) * tail).astype(BF16)
    grads_lead = (g_ref[...].astype(F32) * lead).astype(BF16)
    state = dot(write_t[...], inputs_tail, 1, 0)
    back = dot(read_t[...], grads_lead, 1, 0)
    first = place[0] == 0
    send = jnp.where(first, state, back)
    keep = jnp.where(first, back, state)
    for strip in range(strips):
        at = chunk * strips + strip
        wide = slice(strip * STRIP, (strip + 1) * STRIP)
        decay_ref[pl.ds(at, 1), :] = lead[STRETCH - 1 :, wide]
        for quarter in range(chips):
            rows = pl.ds(pl.multiple_of((quarter * half_strips + at) * part, part), part)
            mine = slice(quarter * part, (quarter + 1) * part)
            send_ref[rows, :] = send[mine, wide]
            keep_ref[rows, :] = keep[mine, wide]


def summary(chips, half, x, g, write_map, read_map, rates, shared):
    tokens, wide = x.shape
    heads = rates.shape[0]
    lanes = wide // (STEPS * HALVES)
    strips = wide // STRIP // HALVES
    terms = [
        jax.ShapeDtypeStruct((META, STRIP), F32),
        jax.ShapeDtypeStruct((tokens, STRIP), F32),
        jax.ShapeDtypeStruct((tokens, STRIP), BF16),
        jax.ShapeDtypeStruct((tokens, STRIP), BF16),
    ]
    out_shape = [
        jax.ShapeDtypeStruct((strips * STATE + META, STRIP), F32),
        jax.ShapeDtypeStruct((strips * STATE, STRIP), F32),
        jax.ShapeDtypeStruct((strips, STRIP), F32),
    ]
    if half == 0:
        extra = [rates]
        out_shape = out_shape + terms
    else:
        extra = [shared[0], shared[2], shared[3]]
    return pl.pallas_call(
        lambda *refs: summary_kernel(heads, chips, half, *refs),
        grid=(STEPS,),
        in_specs=[
            half_lanes(tokens, lanes, half, STEPS),
            half_lanes(tokens, lanes, half, STEPS),
            whole(tokens, STATE),
            whole(tokens, STATE),
        ]
        + [whole(*value.shape) for value in extra],
        out_specs=[whole(*out.shape) for out in out_shape],
        out_shape=out_shape,
        scratch_shapes=[
            pltpu.VMEM((STATE, tokens), BF16),
            pltpu.VMEM((STATE, tokens), BF16),
        ],
        compiler_params=pltpu.CompilerParams(vmem_limit_bytes=BIG_VMEM),
        cost_estimate=LITTLE,
        name="summary",
    )(x, g, write_map, read_map, *extra)


def combine_kernel(chips, first_ref, keep_ref, decay_ref, log_ref, mine_ref, send_ref):
    place = position()
    strips = decay_ref.shape[0]
    part = STATE // chips
    size = mine_ref.shape[0]
    bit = place[1] & 1
    for base, out_ref in ((bit * size, mine_ref), ((1 - bit) * size, send_ref)):
        for strip in range(strips):
            decay = decay_ref[strip : strip + 1, :]
            for at in range(strip * part, size, strips * part):
                rows = pl.ds(pl.multiple_of(base + at, part), part)
                out_ref[at : at + part, :] = first_ref[rows, :] * decay + keep_ref[rows, :]
    meta = first_ref[2 * size :, :] + log_ref[...]
    send_ref[size : size + META, :] = meta
    send_ref[size + META :, :] = meta


def halves(size):
    return (
        [whole(size, STRIP), whole(size + PAD, STRIP)],
        [
            jax.ShapeDtypeStruct((size, STRIP), F32),
            jax.ShapeDtypeStruct((size + PAD, STRIP), F32),
        ],
    )


def combine(chips, first, keep, decay, log):
    out_specs, out_shape = halves(keep.shape[0] // 2)
    return pl.pallas_call(
        lambda *refs: combine_kernel(chips, *refs),
        in_specs=[whole(*value.shape) for value in (first, keep, decay, log)],
        out_specs=out_specs,
        out_shape=out_shape,
        compiler_params=pltpu.CompilerParams(vmem_limit_bytes=SMALL_VMEM),
        cost_estimate=LITTLE,
        name="combine",
    )(first, keep, decay, log)


def is_ahead(place, level):
    return ((place[1] >> level) & 1) == place[0]


def up_kernel(level, last, part, offset, strips, head_size, mine_ref, log_ref, got_ref, *outs):
    place = position()
    size = mine_ref.shape[0]
    ahead = is_ahead(place, level)
    mine_log, got_log = log_ref[size : size + 1, :], got_ref[size : size + 1, :]
    mine_wide, got_wide = spread_rows(
        [jnp.where(ahead, 1.0, jnp.exp(got_log)), jnp.where(ahead, jnp.exp(mine_log), 1.0)],
        offset,
        strips,
        head_size,
    )
    bit = (place[1] >> (level + 1)) & 1
    half = size if last else size // 2
    targets = ((0, outs[0]),) if last else ((bit * half, outs[0]), ((1 - bit) * half, outs[1]))
    for base, out_ref in targets:
        for strip in range(strips):
            one = slice(strip, strip + 1)
            for at in range(strip * part, half, strips * part):
                rows = slice(at, at + part)
                if not last:
                    rows = pl.ds(pl.multiple_of(base + at, part), part)
                out_ref[at : at + part, :] = (
                    mine_ref[rows, :] * mine_wide[one, :] + got_ref[rows, :] * got_wide[one, :]
                )
    outs[-1][half:, :] = jnp.broadcast_to(mine_log + got_log, (META if last else PAD, STRIP))


def up(level, chips, half, strips, head_size, mine, send, got):
    size = mine.shape[0]
    last = 2 << level == chips
    out_specs, out_shape = halves(size if last else size // 2)
    if last:
        out_specs = [whole(size + META, STRIP)]
        out_shape = [jax.ShapeDtypeStruct((size + META, STRIP), F32)]
    return pl.pallas_call(
        lambda *refs: up_kernel(
            level, last, STATE // chips, half * strips, strips, head_size, *refs
        ),
        in_specs=[whole(size, STRIP), whole(*send.shape), whole(size + PAD, STRIP)],
        out_specs=out_specs,
        out_shape=out_shape,
        compiler_params=pltpu.CompilerParams(vmem_limit_bytes=SMALL_VMEM),
        cost_estimate=LITTLE,
        name="up",
    )(mine, send, got)


def down_kernel(level, top, part, offset, strips, head_size, mine_ref, log_ref, got_ref, *refs):
    place = position()
    sources, (here_ref, there_ref) = refs[:-2], refs[-2:]
    size = mine_ref.shape[0]
    ahead = is_ahead(place, level)
    rows_of = [
        jnp.where(ahead, jnp.exp(got_ref[size : size + 1, :]), 1.0),
        jnp.where(ahead, 1.0, jnp.exp(log_ref[size : size + 1, :])),
    ]
    if top:
        passed = jnp.zeros_like(rows_of[0])
        for ref in sources:
            rows_of.append(jnp.exp(passed))
            passed = passed + ref[size : size + 1, :]
        bases, length = (0,), size
    else:
        length = size // 2
        bit = (place[1] >> (level + 1)) & 1
        bases = (bit * length, (1 - bit) * length)
    here_wide, there_wide, *group_wide = spread_rows(rows_of, offset, strips, head_size)
    for index, base in enumerate(bases):
        for strip in range(strips):
            one = slice(strip, strip + 1)
            for at in range(strip * part, length, strips * part):
                rows = slice(at, at + part)
                if top:
                    entering = sources[0][rows, :] * group_wide[0][one, :]
                    for ref, wide in zip(sources[1:], group_wide[1:]):
                        entering = entering + ref[rows, :] * wide[one, :]
                else:
                    entering = sources[index][rows, :]
                    rows = pl.ds(pl.multiple_of(base + at, part), part)
                got = jnp.where(ahead, got_ref[rows, :], 0.0)
                mine = jnp.where(ahead, 0.0, mine_ref[rows, :])
                here_ref[rows, :] = entering * here_wide[one, :] + got
                there_ref[rows, :] = entering * there_wide[one, :] + mine
    there_ref[size:, :] = jnp.zeros((PAD, STRIP), F32)


def down(level, chips, half, strips, head_size, mine, send, got, sources):
    size = mine.shape[0]
    top = 2 << level == chips
    return pl.pallas_call(
        lambda *refs: down_kernel(
            level, top, STATE // chips, half * strips, strips, head_size, *refs
        ),
        in_specs=[whole(size, STRIP), whole(*send.shape), whole(size + PAD, STRIP)]
        + [whole(*value.shape) for value in sources],
        out_specs=[whole(size, STRIP), whole(size + PAD, STRIP)],
        out_shape=[
            jax.ShapeDtypeStruct((size, STRIP), F32),
            jax.ShapeDtypeStruct((size + PAD, STRIP), F32),
        ],
        compiler_params=pltpu.CompilerParams(vmem_limit_bytes=SMALL_VMEM),
        cost_estimate=LITTLE,
        name="down",
    )(mine, send, got, *sources)


def intra_kernel(
    heads, head_size, start, last,
    after_ref, x_ref, g_ref, write_ref, read_ref, rates_ref, column_ref, tail_ref, lead_ref, *refs,
):
    dx_ref, state_ref, back_ref, change_ref, *sums, row_ref, scores_ref, mask_ref, pairs_ref, \
        write_t, read_t = refs[5 if start else 0 :]
    step = pl.program_id(0)
    chunk = start + step
    lanes = x_ref.shape[1]
    per_chunk = lanes // head_size

    @pl.when(step == 0)
    def _():
        rates = rates_ref[...]
        triangle = lower(STRETCH)
        row_ref[...] = dot(rates, triangle, 1, 1, HIGHEST)
        mask_ref[...] = triangle
        scores_ref[...] = dot(read_ref[...], write_ref[...], 1, 1)
        pairs_ref[...] = refs[4][...] if start else jnp.zeros_like(pairs_ref)
        change_ref[...] = refs[3][...] if start else jnp.zeros_like(change_ref)
        write_t[...] = write_ref[...].astype(F32).T.astype(BF16)
        read_t[...] = read_ref[...].astype(F32).T.astype(BF16)

    columns = pltpu.roll(column_ref[...], STATE - chunk * per_chunk, 1)
    rows = row_ref[pl.ds(pl.multiple_of(chunk * per_chunk, per_chunk), per_chunk), :]
    causal = mask_ref[...] > 0.5
    scores = scores_ref[...]
    pairs = pairs_ref[...]
    low_half = iota((STRETCH, 2 * head_size), 1) < head_size
    adder = head_adder(chunk, head_size, lanes)
    spread = spreader(chunk, heads, head_size, lanes)
    high, low = term_pair(x_ref[...].astype(F32) * dot(tail_ref[...], spread, 1, 0))
    state_ref[...] = dot(write_t[...], high, 1, 0) + dot(write_t[...], low, 1, 0)
    high, low = term_pair(g_ref[...].astype(F32) * dot(lead_ref[...], spread, 1, 0))
    back_ref[...] = dot(read_t[...], high, 1, 0) + dot(read_t[...], low, 1, 0)
    for pair in range(per_chunk // 2):
        strip = slice(pair * 2 * head_size, (pair + 1) * 2 * head_size)
        x = x_ref[:, strip]
        g = g_ref[:, strip]
        ys, dxs = [], []
        for half in range(2):
            head = 2 * pair + half
            gap = columns[:, head : head + 1] - rows[head : head + 1, :]
            decay = jnp.where(causal, jnp.exp(gap), 0.0)
            mixing = (scores * decay).astype(BF16)
            ys.append(dot(mixing, x, 1, 0))
            dxs.append(dot(mixing, g, 0, 0))
            mine = low_half if half == 0 else jnp.logical_not(low_half)
            pairs = pairs + dot(jnp.where(mine, g, jnp.zeros_like(g)), x, 1, 1) * decay
        y = jnp.where(low_half, ys[0], ys[1])
        dx = jnp.where(low_half, dxs[0], dxs[1])
        dx_ref[:, strip] = dx
        change_ref[...] += head_sums(
            g.astype(F32) * y - x.astype(F32) * dx, adder[strip, :]
        )
    pairs_ref[...] = pairs

    @pl.when(step == pl.num_programs(0) - 1)
    def _():
        if last:
            summed = pairs_ref[...].astype(BF16)
            sums[0][...] = dot(summed, read_ref[...], 0, 0)
            sums[1][...] = dot(summed, write_ref[...], 1, 0)
        else:
            sums[0][...] = pairs_ref[...]


def intra(start, steps, after, x, g, write_map, read_map, rates, shared, earlier):
    tokens, wide = x.shape
    heads = rates.shape[0]
    last = (start + steps) * LANES == wide
    lanes = lambda rows: pl.BlockSpec((rows, LANES), lambda c: (0, start + c))
    anywhere = pl.BlockSpec(memory_space=pl.ANY)
    sums = [(tokens, STATE)] * 2 if last else [(tokens, tokens)]
    return pl.pallas_call(
        lambda *refs: intra_kernel(heads, wide // heads, start, last, *refs),
        grid=(steps,),
        in_specs=[
            whole(META, STRIP),
            lanes(tokens),
            lanes(tokens),
            whole(tokens, STATE),
            whole(tokens, STATE),
            whole(heads, tokens),
        ]
        + [whole(tokens, STRIP)] * 3
        + ([anywhere] * 3 + [whole(tokens, STATE), whole(tokens, tokens)] if earlier else []),
        out_specs=[lanes(tokens), lanes(STATE), lanes(STATE), whole(tokens, STATE)]
        + [whole(*shape) for shape in sums],
        out_shape=[
            jax.ShapeDtypeStruct((tokens, wide), F32),
            jax.ShapeDtypeStruct((STATE, wide), F32),
            jax.ShapeDtypeStruct((STATE, wide), F32),
            jax.ShapeDtypeStruct((tokens, STATE), F32),
        ]
        + [jax.ShapeDtypeStruct(shape, F32) for shape in sums],
        scratch_shapes=[
            pltpu.VMEM((heads, tokens), F32),
            pltpu.VMEM((tokens, tokens), F32),
            pltpu.VMEM((tokens, tokens), F32),
            pltpu.VMEM((tokens, tokens), F32),
            pltpu.VMEM((STATE, tokens), BF16),
            pltpu.VMEM((STATE, tokens), BF16),
        ],
        input_output_aliases={9: 0, 10: 1, 11: 2} if earlier else {},
        compiler_params=pltpu.CompilerParams(vmem_limit_bytes=SMALL_VMEM),
        cost_estimate=LITTLE,
        name="intra",
    )(after, x, g, write_map, read_map, rates, *shared[1:], *earlier)


def order_kernel(here_ref, got_ref, low_ref, high_ref):
    place = position()
    bit = place[1] & 1
    here, got = here_ref[...], got_ref[: here_ref.shape[0], :]
    low_ref[...] = jnp.where(bit == 0, here, got)
    high_ref[...] = jnp.where(bit == 0, got, here)


def order(here, got):
    return pl.pallas_call(
        order_kernel,
        in_specs=[whole(*here.shape), whole(*got.shape)],
        out_specs=[whole(*here.shape)] * 2,
        out_shape=[jax.ShapeDtypeStruct(here.shape, F32)] * 2,
        compiler_params=pltpu.CompilerParams(vmem_limit_bytes=SMALL_VMEM),
        cost_estimate=LITTLE,
        name="order",
    )(here, got)


def assemble_kernel(
    heads, chips, half, head_size, ordered,
    after_ref, first_ref, state_own, back_own, *refs,
):
    place = position()
    own_refs, far_refs, (state_ref, back_ref, total_ref) = refs[:2], refs[2:4], refs[4:]
    bit = 0 if ordered else place[1] & 1
    lanes = state_ref.shape[1]
    strips = lanes // STRIP
    part = STATE // chips
    size = strips * part
    log = first_ref[chips * size : chips * size + 1, :]
    decay = spread_rows([jnp.exp(log)], half * strips, strips, head_size)[0]
    is_first = place[0] == 0
    sums = [None] * strips
    for quarter in range(chips):
        rows = slice(quarter * part, (quarter + 1) * part)
        for strip in range(strips):
            wide = slice(strip * STRIP, (strip + 1) * STRIP)
            here = slice(quarter * size + strip * part, quarter * size + (strip + 1) * part)
            piece, at = divmod(here.start, chips // 2 * size)
            there = slice(at, at + part)
            own, far = own_refs[piece][there, :], far_refs[piece][there, :]
            if not ordered:
                own = jnp.where(bit == 0, own, own_refs[1 - piece][there, :])
                far = jnp.where(bit == 0, far, far_refs[1 - piece][there, :])
            own = own * decay[strip : strip + 1, :] + first_ref[here, :]
            state = jnp.where(is_first, far, own).astype(BF16)
            back = jnp.where(is_first, own, far).astype(BF16)
            state_ref[rows, wide] = state
            back_ref[rows, wide] = back
            gain = state.astype(F32) * back_own[rows, wide]
            gain = gain - back.astype(F32) * state_own[rows, wide]
            sums[strip] = gain if sums[strip] is None else sums[strip] + gain
    row_sum = [
        jnp.broadcast_to(jnp.sum(value, axis=0, keepdims=True), (META, STRIP)) for value in sums
    ]
    total = head_sums(jnp.concatenate(row_sum, axis=1), head_adder(half, head_size, lanes))
    total_ref[...] = total + after_ref[...] if half else total


def assemble(heads, chips, half, ordered, after, first, state_own, back_own, own, far):
    wide = state_own.shape[1]
    lanes = wide // HALVES
    mine = pl.BlockSpec((STATE, lanes), lambda c: (0, half))
    return pl.pallas_call(
        lambda *refs: assemble_kernel(heads, chips, half, wide // heads, ordered, *refs),
        grid=(1,),
        in_specs=[whole(META, STRIP), whole(*first.shape), mine, mine]
        + [whole(*value.shape) for value in (*own, *far)],
        out_specs=[whole(STATE, lanes), whole(STATE, lanes), whole(META, STRIP)],
        out_shape=[
            jax.ShapeDtypeStruct((STATE, lanes), BF16),
            jax.ShapeDtypeStruct((STATE, lanes), BF16),
            jax.ShapeDtypeStruct((META, STRIP), F32),
        ],
        compiler_params=pltpu.CompilerParams(vmem_limit_bytes=SMALL_VMEM),
        cost_estimate=LITTLE,
        name="assemble",
    )(after, first, state_own, back_own, *own, *far)


def finish_kernel(
    heads, start, steps, last, x_ref, g_ref, write_ref, read_ref, tail_ref, lead_ref,
    dx_ref, db_ref, dc_ref, change_ref, state_ref, back_ref, *refs,
):
    grad_ref, db_out, dc_out, change_out, token_ref, db_sum, dc_sum, sum_out = refs[-8:]
    chunk = pl.program_id(0)
    lanes = x_ref.shape[1]
    head_size = lanes * STEPS * HALVES // heads
    wide = start + chunk

    @pl.when(chunk == 0)
    def _():
        sum_out[...] = change_ref[...]
        db_sum[...] = db_ref[...]
        dc_sum[...] = dc_ref[...]

    state = state_ref[...]
    back = back_ref[...]
    spread = spreader(wide, heads, head_size, lanes)
    tail = dot(tail_ref[...], spread, 1, 0)
    lead = dot(lead_ref[...], spread, 1, 0)
    x = x_ref[...].astype(F32)
    g = g_ref[...].astype(F32)
    y = dot(read_ref[...], state, 1, 0) * lead
    dx = dot(write_ref[...], back, 1, 0) * tail
    grad_ref[...] = (dx_ref[...] + dx).astype(BF16)
    adder = head_adder(wide, head_size, lanes)
    sum_out[...] += head_sums(g * y - x * dx, adder)
    db_sum[...] += dot((x * tail).astype(BF16), back, 1, 1)
    dc_sum[...] += dot((g * lead).astype(BF16), state, 1, 1)

    @pl.when(chunk == steps - 1)
    def _():
        token_ref[...] = refs[-9][...]
        db_out[...] = db_sum[...].astype(db_out.dtype)
        dc_out[...] = dc_sum[...].astype(dc_out.dtype)
        if last:
            change_out[...] = dot(sum_out[...], lower(STRETCH), 0, 0, HIGHEST)[:heads, :]
        else:
            change_out[...] = sum_out[...]


def finish(heads, start, steps, after, x, g, write_map, read_map, shared, dx, sums, state, back, grad):
    tokens, wide = x.shape
    lanes = wide // (STEPS * HALVES)
    strip = pl.BlockSpec((tokens, lanes), lambda c: (0, start + c))
    own = pl.BlockSpec((STATE, lanes), lambda c: (0, start % STEPS + c))
    last = start + steps == STEPS * HALVES
    kind = BF16 if last else F32
    change = (heads, tokens) if last else (tokens, STATE)
    earlier = [] if grad is None else [grad]
    return pl.pallas_call(
        lambda *refs: finish_kernel(heads, start, steps, last, *refs),
        grid=(steps,),
        in_specs=[strip, strip]
        + [whole(tokens, STATE)] * 4
        + [strip]
        + [whole(tokens, STATE)] * 3
        + [own, own]
        + [pl.BlockSpec(memory_space=pl.ANY)] * len(earlier)
        + [whole(META, STRIP)],
        out_specs=[strip] + [whole(tokens, STATE)] * 2 + [whole(*change), whole(META, STRIP)],
        out_shape=[
            jax.ShapeDtypeStruct((tokens, wide), BF16),
            jax.ShapeDtypeStruct((tokens, STATE), kind),
            jax.ShapeDtypeStruct((tokens, STATE), kind),
            jax.ShapeDtypeStruct(change, F32),
            jax.ShapeDtypeStruct((META, STRIP), F32),
        ],
        scratch_shapes=[pltpu.VMEM((tokens, STATE), F32)] * 3,
        input_output_aliases={12: 0} if earlier else {},
        compiler_params=pltpu.CompilerParams(vmem_limit_bytes=SMALL_VMEM),
        cost_estimate=LITTLE,
        name="finish",
    )(x, g, write_map, read_map, *shared[2:], dx, *sums, state, back, *earlier, after)


def count_kernel(after_ref, later_ref, total_ref, *refs):
    place = position()
    got_refs, (later_out, total_out) = refs[:-2], refs[-2:]
    later, total = later_ref[...], total_ref[...]
    for step, ref in enumerate(got_refs, 1):
        later = later + jnp.where((place[1] ^ step) > place[1], ref[...], 0.0)
        total = total + ref[...]
    later_out[...] = later
    total_out[...] = total


def core_kernel(total_ref, got_ref, later_out, total_out):
    place = position()
    later_out[...] = jnp.where(place[0] == 0, got_ref[...], 0.0)
    total_out[...] = total_ref[...] + got_ref[...]


def tiles(kernel, name, *values):
    return pl.pallas_call(
        kernel,
        in_specs=[whole(META, STRIP)] * len(values),
        out_specs=[whole(META, STRIP)] * 2,
        out_shape=[jax.ShapeDtypeStruct((META, STRIP), F32)] * 2,
        compiler_params=pltpu.CompilerParams(vmem_limit_bytes=SMALL_VMEM),
        cost_estimate=LITTLE,
        name=name,
    )(*values)


def add_later_kernel(suffix_ref, *refs):
    out_ref = refs[-1]
    heads = out_ref.shape[0]
    later = refs[0][...]
    for ref in refs[1:-1]:
        later = later + ref[...]
    out_ref[...] = suffix_ref[...] + later.T[:heads, 0:1]


def add_later(suffix, *parts):
    return pl.pallas_call(
        add_later_kernel,
        in_specs=[whole(*value.shape) for value in (suffix, *parts)],
        out_specs=whole(*suffix.shape),
        out_shape=jax.ShapeDtypeStruct(suffix.shape, F32),
        compiler_params=pltpu.CompilerParams(vmem_limit_bytes=SMALL_VMEM),
        cost_estimate=LITTLE,
        name="add_later",
    )(suffix, *parts)


def per_device(inputs, out_grad, input_map, output_map, log_decay):
    heads = log_decay.shape[0]
    head_size = inputs.shape[1] // heads
    groups, shards = lax.axis_size("grp"), lax.axis_size("seq")
    chips = shards // 2
    strips = inputs.shape[1] // STRIP // HALVES
    everyone = [(a, z, c) for a in range(groups) for z in range(chips) for c in range(2)]

    def move(value, target):
        pairs = []
        for a, z, c in everyone:
            to = target(a, z, c)
            if to is not None:
                pairs.append((a * shards + 2 * z + c, to[0] * shards + 2 * to[1] + to[2]))
        return lax.ppermute(value, ("grp", "seq"), pairs)

    def to_core(value):
        return move(value, lambda a, z, c: (a, z, 1 - c))

    def to_chip(value, step):
        return move(value, lambda a, z, c: (a, z ^ step, c)) if step else value

    def to_earlier(value, step):
        return move(value, lambda a, z, c: (a - step, z, c) if a >= step else None)

    def to_later(value, step):
        def target(a, z, c):
            to = a + step if c == 1 else a - step
            return (to, z, c) if 0 <= to < groups else None

        return move(value, target)

    maps = (inputs, out_grad, input_map, output_map)
    send, keep, decay, *shared = summary(chips, 0, *maps, log_decay, None)
    first = [to_core(send)]
    kept, decays = [keep], [decay]
    send, keep, decay = summary(chips, 1, *maps, log_decay, shared)
    first.append(to_core(send))
    kept.append(keep)
    decays.append(decay)

    levels = chips.bit_length() - 1
    held = [[], []]
    waiting = [None, None]

    def advance(half, step):
        fixed = (chips, half, strips, head_size)
        if step == 0:
            mine, send = combine(
                chips, first[half], kept[half], decays[half], shared[0]
            )
        elif step < levels:
            held[half][-1] += (waiting[half],)
            mine, send = up(step - 1, *fixed, *held[half][-1])
        elif step == levels:
            held[half][-1] += (waiting[half],)
            (send,) = up(step - 1, *fixed, *held[half][-1])
            waiting[half] = [to_later(send, far) for far in range(1, groups)]
            return send
        elif step <= 2 * levels:
            level = 2 * levels - step
            if level < levels - 1:
                waiting[half] = (held[half][level + 1], waiting[half])
            mine, send = down(level, *fixed, *held[half][level], waiting[half])
            held[half][level] = mine
            waiting[half] = to_chip(send, 1 << level)
            return send
        else:
            held[half] = order(held[half][0], waiting[half])
            waiting[half] = [to_core(value) for value in held[half]]
            return held[half][0]
        held[half].append((mine, send))
        waiting[half] = to_chip(send, 1 << step)
        return send

    chunks = inputs.shape[1] // LANES
    rounds = 2 * levels + 2
    block, ready = (), 0
    for step in range(rounds):
        token = advance(0, step)
        if step:
            advance(1, step - 1)
        if step < 3:
            more = pl.cdiv(chunks - ready, 3 - step)
            block = intra(ready, more, token, *maps, log_decay, shared, block)
            ready += more
            waiting[0], waiting[1], first[1], block = lax.optimization_barrier(
                (waiting[0], waiting[1], first[1], block)
            )
        elif step < rounds - 1:
            waiting[0], waiting[1] = lax.optimization_barrier((waiting[0], waiting[1]))
    dx, state_own, back_own, change, db, dc = block
    own_b = held[1][0]
    far_b = to_core(own_b)
    state, back, counted = assemble(
        heads, chips, 0, True, change, first[0], state_own, back_own, held[0], waiting[0]
    )
    grad, *sums, counted = finish(
        heads, 0, STEPS, counted, *maps, shared, dx, (db, dc, change), state, back, None
    )
    got, far_b, counted = lax.optimization_barrier((waiting[1], far_b, counted))
    own_b, far_b = (own_b, got), (far_b, to_core(got))
    state, back, counted = assemble(
        heads, chips, 1, False, counted, first[1], state_own, back_own, own_b, far_b
    )

    later, counted = tiles(core_kernel, "core_sum", counted, to_core(counted))
    got = [to_chip(counted, step) for step in range(1, chips)]
    grad, *sums, token = finish(
        heads, STEPS, 1, counted, *maps, shared, dx, sums, state, back, grad
    )
    later, counted = tiles(count_kernel, "chip_sum", token, later, counted, *got)
    got = [to_earlier(counted, step) for step in range(1, groups)]
    grad, *sums, _ = finish(
        heads, STEPS + 1, 1, counted, *maps, shared, dx, sums, state, back, grad
    )
    return (grad, sums[0], sums[1], add_later(sums[2], later, *got))


def solution(mesh):
    tokens = P(("grp", "seq"), None)
    in_specs = (tokens, tokens, tokens, tokens, P(None, ("grp", "seq")))
    out_specs = (tokens, tokens, tokens, P(None, ("grp", "seq")))
    return jax.shard_map(
        per_device, mesh=mesh, in_specs=in_specs, out_specs=out_specs, check_vma=False
    )
```

```python
import jax
import jax.numpy as jnp
from jax import lax
from jax.experimental import pallas as pl
from jax.experimental.pallas import tpu as pltpu
from jax.sharding import PartitionSpec as P

STATE = 128
STRETCH = 256
LANES = 512
HALVES = 2
STRIP = 128
META = 8
PAD = 2 * META
BIG_VMEM = 56 << 20
SMALL_VMEM = 24 << 20
F32 = jnp.float32
BF16 = jnp.bfloat16
HIGHEST = lax.Precision.HIGHEST


def dot(left, right, left_dim, right_dim, precision=None):
    return lax.dot_general(
        left,
        right,
        (((left_dim,), (right_dim,)), ((), ())),
        precision=precision,
        preferred_element_type=F32,
    )


def iota(shape, dim):
    return lax.broadcasted_iota(jnp.int32, shape, dim)


def lower(length):
    return (iota((length, length), 0) >= iota((length, length), 1)).astype(F32)


def thrice(rates):
    heads, length = rates.shape
    spare = jnp.zeros((STATE - 3 * heads, length), F32)
    return jnp.concatenate([rates, rates, rates, spare], axis=0)


def three_terms(value, heads):
    lane = iota(value.shape, 1)
    first = value.astype(BF16)
    rest = value - first.astype(F32)
    second = rest.astype(BF16)
    third = (rest - second.astype(F32)).astype(BF16)
    return jnp.where(lane < heads, first, jnp.where(lane < 2 * heads, second, third))


def spreader(chunk, heads, head_size, lanes):
    row = iota((STATE, lanes), 0)
    head = (iota((STATE, lanes), 1) + chunk * lanes) // head_size
    hit = (row == head) | (row == head + heads) | (row == head + 2 * heads)
    return hit.astype(F32).astype(BF16)


def head_adder(chunk, head_size, lanes):
    head = (iota((lanes, STATE), 0) + chunk * lanes) // head_size
    return (iota((lanes, STATE), 1) == head).astype(F32).astype(BF16)


def head_sums(value, adder):
    first = value.astype(BF16)
    second = (value - first.astype(F32)).astype(BF16)
    return dot(first, adder, 1, 0) + dot(second, adder, 1, 0)


def decay_terms(rates, heads):
    length = rates.shape[1]
    running = dot(lower(length), thrice(rates), 1, 1, HIGHEST)
    last = running[length - 1 : length, :]
    return (
        running,
        three_terms(jnp.exp(last - running), heads),
        three_terms(jnp.exp(running), heads),
    )


def term_pair(value):
    first = value.astype(BF16)
    return first, (value - first.astype(F32)).astype(BF16)


def lane_spread(per_strip, head_size):
    head = iota((STRIP, STRIP), 0) % per_strip
    return (iota((STRIP, STRIP), 1) // head_size == head).astype(F32)


def spread_rows(rows, offset, strips, head_size):
    per_strip = STRIP // head_size
    lane = iota((strips, STRIP), 1)
    row = iota((strips, STRIP), 0) + offset
    picked = [jnp.where(lane // per_strip == row, value, 0.0) for value in rows]
    stacked = jnp.concatenate(picked, axis=0) if len(picked) > 1 else picked[0]
    wide = dot(stacked, lane_spread(per_strip, head_size), 1, 0, HIGHEST)
    return [wide[i * strips : (i + 1) * strips, :] for i in range(len(rows))]


def whole(*shape):
    return pl.BlockSpec(shape, lambda *_: (0,) * len(shape))


def lanes_of(rows):
    return pl.BlockSpec((rows, LANES), lambda c: (0, c))


def half_lanes(rows, lanes, half, steps):
    return pl.BlockSpec((rows, lanes), lambda c: (0, half * steps + c))


LITTLE = pl.CostEstimate(flops=1, bytes_accessed=1, transcendentals=0)


def position():
    shard = lax.axis_index("seq")
    return shard & 1, shard >> 1


STEPS = 2


def summary_kernel(heads, chips, half, x_ref, g_ref, write_ref, read_ref, *refs):
    place = position()
    chunk = pl.program_id(0)
    lanes = x_ref.shape[1]
    strips = lanes // STRIP
    half_strips = strips * STEPS
    head_size = lanes * STEPS * HALVES // heads
    part = STATE // chips
    if half == 0:
        rates_ref, send_ref, keep_ref, decay_ref, log_ref, run_ref, tail_ref, lead_ref = refs[:8]
    else:
        log_ref, tail_ref, lead_ref, send_ref, keep_ref, decay_ref = refs[:6]
    write_t, read_t = refs[-2:]

    @pl.when(chunk == 0)
    def _():
        if half == 0:
            running, tail, lead = decay_terms(rates_ref[...], heads)
            run_ref[...] = running
            tail_ref[...] = tail
            lead_ref[...] = lead
            log_ref[...] = jnp.broadcast_to(running[STRETCH - 1 :, :], (META, STRIP))
        send_ref[pl.ds(half_strips * STATE, META), :] = log_ref[...]
        write_t[...] = write_ref[...].astype(F32).T.astype(BF16)
        read_t[...] = read_ref[...].astype(F32).T.astype(BF16)

    spread = spreader(half * STEPS + chunk, heads, head_size, lanes)
    tail = dot(tail_ref[...], spread, 1, 0)
    lead = dot(lead_ref[...], spread, 1, 0)
    inputs_tail = (x_ref[...].astype(F32) * tail).astype(BF16)
    grads_lead = (g_ref[...].astype(F32) * lead).astype(BF16)
    state = dot(write_t[...], inputs_tail, 1, 0)
    back = dot(read_t[...], grads_lead, 1, 0)
    first = place[0] == 0
    send = jnp.where(first, state, back)
    keep = jnp.where(first, back, state)
    for strip in range(strips):
        at = chunk * strips + strip
        wide = slice(strip * STRIP, (strip + 1) * STRIP)
        decay_ref[pl.ds(at, 1), :] = lead[STRETCH - 1 :, wide]
        for quarter in range(chips):
            rows = pl.ds(pl.multiple_of((quarter * half_strips + at) * part, part), part)
            mine = slice(quarter * part, (quarter + 1) * part)
            send_ref[rows, :] = send[mine, wide]
            keep_ref[rows, :] = keep[mine, wide]


def summary(chips, half, x, g, write_map, read_map, rates, shared):
    tokens, wide = x.shape
    heads = rates.shape[0]
    lanes = wide // (STEPS * HALVES)
    strips = wide // STRIP // HALVES
    terms = [
        jax.ShapeDtypeStruct((META, STRIP), F32),
        jax.ShapeDtypeStruct((tokens, STRIP), F32),
        jax.ShapeDtypeStruct((tokens, STRIP), BF16),
        jax.ShapeDtypeStruct((tokens, STRIP), BF16),
    ]
    out_shape = [
        jax.ShapeDtypeStruct((strips * STATE + META, STRIP), F32),
        jax.ShapeDtypeStruct((strips * STATE, STRIP), F32),
        jax.ShapeDtypeStruct((strips, STRIP), F32),
    ]
    if half == 0:
        extra = [rates]
        out_shape = out_shape + terms
    else:
        extra = [shared[0], shared[2], shared[3]]
    return pl.pallas_call(
        lambda *refs: summary_kernel(heads, chips, half, *refs),
        grid=(STEPS,),
        in_specs=[
            half_lanes(tokens, lanes, half, STEPS),
            half_lanes(tokens, lanes, half, STEPS),
            whole(tokens, STATE),
            whole(tokens, STATE),
        ]
        + [whole(*value.shape) for value in extra],
        out_specs=[whole(*out.shape) for out in out_shape],
        out_shape=out_shape,
        scratch_shapes=[
            pltpu.VMEM((STATE, tokens), BF16),
            pltpu.VMEM((STATE, tokens), BF16),
        ],
        compiler_params=pltpu.CompilerParams(vmem_limit_bytes=BIG_VMEM),
        cost_estimate=LITTLE,
        name="summary",
    )(x, g, write_map, read_map, *extra)


def combine_kernel(chips, first_ref, keep_ref, decay_ref, log_ref, mine_ref, send_ref):
    place = position()
    strips = decay_ref.shape[0]
    part = STATE // chips
    size = mine_ref.shape[0]
    bit = place[1] & 1
    for base, out_ref in ((bit * size, mine_ref), ((1 - bit) * size, send_ref)):
        for strip in range(strips):
            decay = decay_ref[strip : strip + 1, :]
            for at in range(strip * part, size, strips * part):
                rows = pl.ds(pl.multiple_of(base + at, part), part)
                out_ref[at : at + part, :] = first_ref[rows, :] * decay + keep_ref[rows, :]
    meta = first_ref[2 * size :, :] + log_ref[...]
    send_ref[size : size + META, :] = meta
    send_ref[size + META :, :] = meta


def halves(size):
    return (
        [whole(size, STRIP), whole(size + PAD, STRIP)],
        [
            jax.ShapeDtypeStruct((size, STRIP), F32),
            jax.ShapeDtypeStruct((size + PAD, STRIP), F32),
        ],
    )


def combine(chips, first, keep, decay, log):
    out_specs, out_shape = halves(keep.shape[0] // 2)
    return pl.pallas_call(
        lambda *refs: combine_kernel(chips, *refs),
        in_specs=[whole(*value.shape) for value in (first, keep, decay, log)],
        out_specs=out_specs,
        out_shape=out_shape,
        compiler_params=pltpu.CompilerParams(vmem_limit_bytes=SMALL_VMEM),
        cost_estimate=LITTLE,
        name="combine",
    )(first, keep, decay, log)


def is_ahead(place, level):
    return ((place[1] >> level) & 1) == place[0]


def up_kernel(level, last, part, offset, strips, head_size, mine_ref, log_ref, got_ref, *outs):
    place = position()
    size = mine_ref.shape[0]
    ahead = is_ahead(place, level)
    mine_log, got_log = log_ref[size : size + 1, :], got_ref[size : size + 1, :]
    mine_wide, got_wide = spread_rows(
        [jnp.where(ahead, 1.0, jnp.exp(got_log)), jnp.where(ahead, jnp.exp(mine_log), 1.0)],
        offset,
        strips,
        head_size,
    )
    bit = (place[1] >> (level + 1)) & 1
    half = size if last else size // 2
    targets = ((0, outs[0]),) if last else ((bit * half, outs[0]), ((1 - bit) * half, outs[1]))
    for base, out_ref in targets:
        for strip in range(strips):
            one = slice(strip, strip + 1)
            for at in range(strip * part, half, strips * part):
                rows = slice(at, at + part)
                if not last:
                    rows = pl.ds(pl.multiple_of(base + at, part), part)
                out_ref[at : at + part, :] = (
                    mine_ref[rows, :] * mine_wide[one, :] + got_ref[rows, :] * got_wide[one, :]
                )
    outs[-1][half:, :] = jnp.broadcast_to(mine_log + got_log, (META if last else PAD, STRIP))


def up(level, chips, half, strips, head_size, mine, send, got):
    size = mine.shape[0]
    last = 2 << level == chips
    out_specs, out_shape = halves(size if last else size // 2)
    if last:
        out_specs = [whole(size + META, STRIP)]
        out_shape = [jax.ShapeDtypeStruct((size + META, STRIP), F32)]
    return pl.pallas_call(
        lambda *refs: up_kernel(
            level, last, STATE // chips, half * strips, strips, head_size, *refs
        ),
        in_specs=[whole(size, STRIP), whole(*send.shape), whole(size + PAD, STRIP)],
        out_specs=out_specs,
        out_shape=out_shape,
        compiler_params=pltpu.CompilerParams(vmem_limit_bytes=SMALL_VMEM),
        cost_estimate=LITTLE,
        name="up",
    )(mine, send, got)


def down_kernel(level, top, part, offset, strips, head_size, mine_ref, log_ref, got_ref, *refs):
    place = position()
    sources, (here_ref, there_ref) = refs[:-2], refs[-2:]
    size = mine_ref.shape[0]
    ahead = is_ahead(place, level)
    rows_of = [
        jnp.where(ahead, jnp.exp(got_ref[size : size + 1, :]), 1.0),
        jnp.where(ahead, 1.0, jnp.exp(log_ref[size : size + 1, :])),
    ]
    if top:
        passed = jnp.zeros_like(rows_of[0])
        for ref in sources:
            rows_of.append(jnp.exp(passed))
            passed = passed + ref[size : size + 1, :]
        bases, length = (0,), size
    else:
        length = size // 2
        bit = (place[1] >> (level + 1)) & 1
        bases = (bit * length, (1 - bit) * length)
    here_wide, there_wide, *group_wide = spread_rows(rows_of, offset, strips, head_size)
    for index, base in enumerate(bases):
        for strip in range(strips):
            one = slice(strip, strip + 1)
            for at in range(strip * part, length, strips * part):
                rows = slice(at, at + part)
                if top:
                    entering = sources[0][rows, :] * group_wide[0][one, :]
                    for ref, wide in zip(sources[1:], group_wide[1:]):
                        entering = entering + ref[rows, :] * wide[one, :]
                else:
                    entering = sources[index][rows, :]
                    rows = pl.ds(pl.multiple_of(base + at, part), part)
                got = jnp.where(ahead, got_ref[rows, :], 0.0)
                mine = jnp.where(ahead, 0.0, mine_ref[rows, :])
                here_ref[rows, :] = entering * here_wide[one, :] + got
                there_ref[rows, :] = entering * there_wide[one, :] + mine
    there_ref[size:, :] = jnp.zeros((PAD, STRIP), F32)


def down(level, chips, half, strips, head_size, mine, send, got, sources):
    size = mine.shape[0]
    top = 2 << level == chips
    return pl.pallas_call(
        lambda *refs: down_kernel(
            level, top, STATE // chips, half * strips, strips, head_size, *refs
        ),
        in_specs=[whole(size, STRIP), whole(*send.shape), whole(size + PAD, STRIP)]
        + [whole(*value.shape) for value in sources],
        out_specs=[whole(size, STRIP), whole(size + PAD, STRIP)],
        out_shape=[
            jax.ShapeDtypeStruct((size, STRIP), F32),
            jax.ShapeDtypeStruct((size + PAD, STRIP), F32),
        ],
        compiler_params=pltpu.CompilerParams(vmem_limit_bytes=SMALL_VMEM),
        cost_estimate=LITTLE,
        name="down",
    )(mine, send, got, *sources)


def intra_kernel(
    heads, head_size, start, last,
    after_ref, x_ref, g_ref, write_ref, read_ref, rates_ref, column_ref, tail_ref, lead_ref, *refs,
):
    dx_ref, state_ref, back_ref, change_ref, *sums, row_ref, scores_ref, mask_ref, pairs_ref, \
        write_t, read_t = refs[5 if start else 0 :]
    step = pl.program_id(0)
    chunk = start + step
    lanes = x_ref.shape[1]
    per_chunk = lanes // head_size

    @pl.when(step == 0)
    def _():
        rates = rates_ref[...]
        triangle = lower(STRETCH)
        row_ref[...] = dot(rates, triangle, 1, 1, HIGHEST)
        mask_ref[...] = triangle
        scores_ref[...] = dot(read_ref[...], write_ref[...], 1, 1)
        pairs_ref[...] = refs[4][...] if start else jnp.zeros_like(pairs_ref)
        change_ref[...] = refs[3][...] if start else jnp.zeros_like(change_ref)
        write_t[...] = write_ref[...].astype(F32).T.astype(BF16)
        read_t[...] = read_ref[...].astype(F32).T.astype(BF16)

    columns = pltpu.roll(column_ref[...], STATE - chunk * per_chunk, 1)
    rows = row_ref[pl.ds(pl.multiple_of(chunk * per_chunk, per_chunk), per_chunk), :]
    causal = mask_ref[...] > 0.5
    scores = scores_ref[...]
    pairs = pairs_ref[...]
    low_half = iota((STRETCH, 2 * head_size), 1) < head_size
    adder = head_adder(chunk, head_size, lanes)
    spread = spreader(chunk, heads, head_size, lanes)
    high, low = term_pair(x_ref[...].astype(F32) * dot(tail_ref[...], spread, 1, 0))
    state_ref[...] = dot(write_t[...], high, 1, 0) + dot(write_t[...], low, 1, 0)
    high, low = term_pair(g_ref[...].astype(F32) * dot(lead_ref[...], spread, 1, 0))
    back_ref[...] = dot(read_t[...], high, 1, 0) + dot(read_t[...], low, 1, 0)
    for pair in range(per_chunk // 2):
        strip = slice(pair * 2 * head_size, (pair + 1) * 2 * head_size)
        x = x_ref[:, strip]
        g = g_ref[:, strip]
        ys, dxs = [], []
        for half in range(2):
            head = 2 * pair + half
            gap = columns[:, head : head + 1] - rows[head : head + 1, :]
            decay = jnp.where(causal, jnp.exp(gap), 0.0)
            mixing = (scores * decay).astype(BF16)
            ys.append(dot(mixing, x, 1, 0))
            dxs.append(dot(mixing, g, 0, 0))
            mine = low_half if half == 0 else jnp.logical_not(low_half)
            pairs = pairs + dot(jnp.where(mine, g, jnp.zeros_like(g)), x, 1, 1) * decay
        y = jnp.where(low_half, ys[0], ys[1])
        dx = jnp.where(low_half, dxs[0], dxs[1])
        dx_ref[:, strip] = dx
        change_ref[...] += head_sums(
            g.astype(F32) * y - x.astype(F32) * dx, adder[strip, :]
        )
    pairs_ref[...] = pairs

    @pl.when(step == pl.num_programs(0) - 1)
    def _():
        if last:
            summed = pairs_ref[...].astype(BF16)
            sums[0][...] = dot(summed, read_ref[...], 0, 0)
            sums[1][...] = dot(summed, write_ref[...], 1, 0)
        else:
            sums[0][...] = pairs_ref[...]


def intra(start, steps, after, x, g, write_map, read_map, rates, shared, earlier):
    tokens, wide = x.shape
    heads = rates.shape[0]
    last = (start + steps) * LANES == wide
    lanes = lambda rows: pl.BlockSpec((rows, LANES), lambda c: (0, start + c))
    anywhere = pl.BlockSpec(memory_space=pl.ANY)
    sums = [(tokens, STATE)] * 2 if last else [(tokens, tokens)]
    return pl.pallas_call(
        lambda *refs: intra_kernel(heads, wide // heads, start, last, *refs),
        grid=(steps,),
        in_specs=[
            whole(META, STRIP),
            lanes(tokens),
            lanes(tokens),
            whole(tokens, STATE),
            whole(tokens, STATE),
            whole(heads, tokens),
        ]
        + [whole(tokens, STRIP)] * 3
        + ([anywhere] * 3 + [whole(tokens, STATE), whole(tokens, tokens)] if earlier else []),
        out_specs=[lanes(tokens), lanes(STATE), lanes(STATE), whole(tokens, STATE)]
        + [whole(*shape) for shape in sums],
        out_shape=[
            jax.ShapeDtypeStruct((tokens, wide), F32),
            jax.ShapeDtypeStruct((STATE, wide), F32),
            jax.ShapeDtypeStruct((STATE, wide), F32),
            jax.ShapeDtypeStruct((tokens, STATE), F32),
        ]
        + [jax.ShapeDtypeStruct(shape, F32) for shape in sums],
        scratch_shapes=[
            pltpu.VMEM((heads, tokens), F32),
            pltpu.VMEM((tokens, tokens), F32),
            pltpu.VMEM((tokens, tokens), F32),
            pltpu.VMEM((tokens, tokens), F32),
            pltpu.VMEM((STATE, tokens), BF16),
            pltpu.VMEM((STATE, tokens), BF16),
        ],
        input_output_aliases={9: 0, 10: 1, 11: 2} if earlier else {},
        compiler_params=pltpu.CompilerParams(vmem_limit_bytes=SMALL_VMEM),
        cost_estimate=LITTLE,
        name="intra",
    )(after, x, g, write_map, read_map, rates, *shared[1:], *earlier)


def order_kernel(here_ref, got_ref, low_ref, high_ref):
    place = position()
    bit = place[1] & 1
    here, got = here_ref[...], got_ref[: here_ref.shape[0], :]
    low_ref[...] = jnp.where(bit == 0, here, got)
    high_ref[...] = jnp.where(bit == 0, got, here)


def order(here, got):
    return pl.pallas_call(
        order_kernel,
        in_specs=[whole(*here.shape), whole(*got.shape)],
        out_specs=[whole(*here.shape)] * 2,
        out_shape=[jax.ShapeDtypeStruct(here.shape, F32)] * 2,
        compiler_params=pltpu.CompilerParams(vmem_limit_bytes=SMALL_VMEM),
        cost_estimate=LITTLE,
        name="order",
    )(here, got)


def assemble_kernel(
    heads, chips, half, head_size, ordered,
    after_ref, first_ref, state_own, back_own, *refs,
):
    place = position()
    own_refs, far_refs, (state_ref, back_ref, total_ref) = refs[:2], refs[2:4], refs[4:]
    bit = 0 if ordered else place[1] & 1
    lanes = state_ref.shape[1]
    strips = lanes // STRIP
    part = STATE // chips
    size = strips * part
    log = first_ref[chips * size : chips * size + 1, :]
    decay = spread_rows([jnp.exp(log)], half * strips, strips, head_size)[0]
    is_first = place[0] == 0
    sums = [None] * strips
    for quarter in range(chips):
        rows = slice(quarter * part, (quarter + 1) * part)
        for strip in range(strips):
            wide = slice(strip * STRIP, (strip + 1) * STRIP)
            here = slice(quarter * size + strip * part, quarter * size + (strip + 1) * part)
            piece, at = divmod(here.start, chips // 2 * size)
            there = slice(at, at + part)
            own, far = own_refs[piece][there, :], far_refs[piece][there, :]
            if not ordered:
                own = jnp.where(bit == 0, own, own_refs[1 - piece][there, :])
                far = jnp.where(bit == 0, far, far_refs[1 - piece][there, :])
            own = own * decay[strip : strip + 1, :] + first_ref[here, :]
            state = jnp.where(is_first, far, own).astype(BF16)
            back = jnp.where(is_first, own, far).astype(BF16)
            state_ref[rows, wide] = state
            back_ref[rows, wide] = back
            gain = state.astype(F32) * back_own[rows, wide]
            gain = gain - back.astype(F32) * state_own[rows, wide]
            sums[strip] = gain if sums[strip] is None else sums[strip] + gain
    row_sum = [
        jnp.broadcast_to(jnp.sum(value, axis=0, keepdims=True), (META, STRIP)) for value in sums
    ]
    total = head_sums(jnp.concatenate(row_sum, axis=1), head_adder(half, head_size, lanes))
    total_ref[...] = total + after_ref[...] if half else total


def assemble(heads, chips, half, ordered, after, first, state_own, back_own, own, far):
    wide = state_own.shape[1]
    lanes = wide // HALVES
    mine = pl.BlockSpec((STATE, lanes), lambda c: (0, half))
    return pl.pallas_call(
        lambda *refs: assemble_kernel(heads, chips, half, wide // heads, ordered, *refs),
        grid=(1,),
        in_specs=[whole(META, STRIP), whole(*first.shape), mine, mine]
        + [whole(*value.shape) for value in (*own, *far)],
        out_specs=[whole(STATE, lanes), whole(STATE, lanes), whole(META, STRIP)],
        out_shape=[
            jax.ShapeDtypeStruct((STATE, lanes), BF16),
            jax.ShapeDtypeStruct((STATE, lanes), BF16),
            jax.ShapeDtypeStruct((META, STRIP), F32),
        ],
        compiler_params=pltpu.CompilerParams(vmem_limit_bytes=SMALL_VMEM),
        cost_estimate=LITTLE,
        name="assemble",
    )(after, first, state_own, back_own, *own, *far)


def finish_kernel(
    heads, start, steps, last, x_ref, g_ref, write_ref, read_ref, tail_ref, lead_ref,
    dx_ref, db_ref, dc_ref, change_ref, state_ref, back_ref, *refs,
):
    grad_ref, db_out, dc_out, change_out, token_ref, db_sum, dc_sum, sum_out = refs[-8:]
    chunk = pl.program_id(0)
    lanes = x_ref.shape[1]
    head_size = lanes * STEPS * HALVES // heads
    wide = start + chunk

    @pl.when(chunk == 0)
    def _():
        sum_out[...] = change_ref[...]
        db_sum[...] = db_ref[...]
        dc_sum[...] = dc_ref[...]

    state = state_ref[...]
    back = back_ref[...]
    spread = spreader(wide, heads, head_size, lanes)
    tail = dot(tail_ref[...], spread, 1, 0)
    lead = dot(lead_ref[...], spread, 1, 0)
    x = x_ref[...].astype(F32)
    g = g_ref[...].astype(F32)
    y = dot(read_ref[...], state, 1, 0) * lead
    dx = dot(write_ref[...], back, 1, 0) * tail
    grad_ref[...] = (dx_ref[...] + dx).astype(BF16)
    adder = head_adder(wide, head_size, lanes)
    sum_out[...] += head_sums(g * y - x * dx, adder)
    db_sum[...] += dot((x * tail).astype(BF16), back, 1, 1)
    dc_sum[...] += dot((g * lead).astype(BF16), state, 1, 1)

    @pl.when(chunk == steps - 1)
    def _():
        token_ref[...] = refs[-9][...]
        db_out[...] = db_sum[...].astype(db_out.dtype)
        dc_out[...] = dc_sum[...].astype(dc_out.dtype)
        if last:
            change_out[...] = dot(sum_out[...], lower(STRETCH), 0, 0, HIGHEST)[:heads, :]
        else:
            change_out[...] = sum_out[...]


def finish(heads, start, steps, after, x, g, write_map, read_map, shared, dx, sums, state, back, grad):
    tokens, wide = x.shape
    lanes = wide // (STEPS * HALVES)
    strip = pl.BlockSpec((tokens, lanes), lambda c: (0, start + c))
    own = pl.BlockSpec((STATE, lanes), lambda c: (0, start % STEPS + c))
    last = start + steps == STEPS * HALVES
    kind = BF16 if last else F32
    change = (heads, tokens) if last else (tokens, STATE)
    earlier = [] if grad is None else [grad]
    return pl.pallas_call(
        lambda *refs: finish_kernel(heads, start, steps, last, *refs),
        grid=(steps,),
        in_specs=[strip, strip]
        + [whole(tokens, STATE)] * 4
        + [strip]
        + [whole(tokens, STATE)] * 3
        + [own, own]
        + [pl.BlockSpec(memory_space=pl.ANY)] * len(earlier)
        + [whole(META, STRIP)],
        out_specs=[strip] + [whole(tokens, STATE)] * 2 + [whole(*change), whole(META, STRIP)],
        out_shape=[
            jax.ShapeDtypeStruct((tokens, wide), BF16),
            jax.ShapeDtypeStruct((tokens, STATE), kind),
            jax.ShapeDtypeStruct((tokens, STATE), kind),
            jax.ShapeDtypeStruct(change, F32),
            jax.ShapeDtypeStruct((META, STRIP), F32),
        ],
        scratch_shapes=[pltpu.VMEM((tokens, STATE), F32)] * 3,
        input_output_aliases={12: 0} if earlier else {},
        compiler_params=pltpu.CompilerParams(vmem_limit_bytes=SMALL_VMEM),
        cost_estimate=LITTLE,
        name="finish",
    )(x, g, write_map, read_map, *shared[2:], dx, *sums, state, back, *earlier, after)


def count_kernel(after_ref, later_ref, total_ref, *refs):
    place = position()
    got_refs, (later_out, total_out) = refs[:-2], refs[-2:]
    later, total = later_ref[...], total_ref[...]
    for step, ref in enumerate(got_refs, 1):
        later = later + jnp.where((place[1] ^ step) > place[1], ref[...], 0.0)
        total = total + ref[...]
    later_out[...] = later
    total_out[...] = total


def core_kernel(total_ref, got_ref, later_out, total_out):
    place = position()
    later_out[...] = jnp.where(place[0] == 0, got_ref[...], 0.0)
    total_out[...] = total_ref[...] + got_ref[...]


def tiles(kernel, name, *values):
    return pl.pallas_call(
        kernel,
        in_specs=[whole(META, STRIP)] * len(values),
        out_specs=[whole(META, STRIP)] * 2,
        out_shape=[jax.ShapeDtypeStruct((META, STRIP), F32)] * 2,
        compiler_params=pltpu.CompilerParams(vmem_limit_bytes=SMALL_VMEM),
        cost_estimate=LITTLE,
        name=name,
    )(*values)


def add_later_kernel(suffix_ref, *refs):
    out_ref = refs[-1]
    heads = out_ref.shape[0]
    later = refs[0][...]
    for ref in refs[1:-1]:
        later = later + ref[...]
    out_ref[...] = suffix_ref[...] + later.T[:heads, 0:1]


def add_later(suffix, *parts):
    return pl.pallas_call(
        add_later_kernel,
        in_specs=[whole(*value.shape) for value in (suffix, *parts)],
        out_specs=whole(*suffix.shape),
        out_shape=jax.ShapeDtypeStruct(suffix.shape, F32),
        compiler_params=pltpu.CompilerParams(vmem_limit_bytes=SMALL_VMEM),
        cost_estimate=LITTLE,
        name="add_later",
    )(suffix, *parts)


def per_device(inputs, out_grad, input_map, output_map, log_decay):
    heads = log_decay.shape[0]
    head_size = inputs.shape[1] // heads
    groups, shards = lax.axis_size("grp"), lax.axis_size("seq")
    chips = shards // 2
    strips = inputs.shape[1] // STRIP // HALVES
    everyone = [(a, z, c) for a in range(groups) for z in range(chips) for c in range(2)]

    def move(value, target):
        pairs = []
        for a, z, c in everyone:
            to = target(a, z, c)
            if to is not None:
                pairs.append((a * shards + 2 * z + c, to[0] * shards + 2 * to[1] + to[2]))
        return lax.ppermute(value, ("grp", "seq"), pairs)

    def to_core(value):
        return move(value, lambda a, z, c: (a, z, 1 - c))

    def to_chip(value, step):
        return move(value, lambda a, z, c: (a, z ^ step, c)) if step else value

    def to_earlier(value, step):
        return move(value, lambda a, z, c: (a - step, z, c) if a >= step else None)

    def to_later(value, step):
        def target(a, z, c):
            to = a + step if c == 1 else a - step
            return (to, z, c) if 0 <= to < groups else None

        return move(value, target)

    maps = (inputs, out_grad, input_map, output_map)
    send, keep, decay, *shared = summary(chips, 0, *maps, log_decay, None)
    first = [to_core(send)]
    kept, decays = [keep], [decay]
    send, keep, decay = summary(chips, 1, *maps, log_decay, shared)
    first.append(to_core(send))
    kept.append(keep)
    decays.append(decay)

    levels = chips.bit_length() - 1
    held = [[], []]
    waiting = [None, None]

    def advance(half, step):
        fixed = (chips, half, strips, head_size)
        if step == 0:
            mine, send = combine(
                chips, first[half], kept[half], decays[half], shared[0]
            )
        elif step < levels:
            held[half][-1] += (waiting[half],)
            mine, send = up(step - 1, *fixed, *held[half][-1])
        elif step == levels:
            held[half][-1] += (waiting[half],)
            (send,) = up(step - 1, *fixed, *held[half][-1])
            waiting[half] = [to_later(send, far) for far in range(1, groups)]
            return send
        elif step <= 2 * levels:
            level = 2 * levels - step
            if level < levels - 1:
                waiting[half] = (held[half][level + 1], waiting[half])
            mine, send = down(level, *fixed, *held[half][level], waiting[half])
            held[half][level] = mine
            waiting[half] = to_chip(send, 1 << level)
            return send
        else:
            held[half] = order(held[half][0], waiting[half])
            waiting[half] = [to_core(value) for value in held[half]]
            return held[half][0]
        held[half].append((mine, send))
        waiting[half] = to_chip(send, 1 << step)
        return send

    chunks = inputs.shape[1] // LANES
    rounds = 2 * levels + 2
    block, ready = (), 0
    for step in range(rounds):
        token = advance(0, step)
        if step:
            advance(1, step - 1)
        if step < 3:
            more = pl.cdiv(chunks - ready, 3 - step)
            block = intra(ready, more, token, *maps, log_decay, shared, block)
            ready += more
            waiting[0], waiting[1], first[1], block = lax.optimization_barrier(
                (waiting[0], waiting[1], first[1], block)
            )
        elif levels + 1 < step < rounds - 1:
            waiting[0], waiting[1] = lax.optimization_barrier((waiting[0], waiting[1]))
    dx, state_own, back_own, change, db, dc = block
    own_b = held[1][0]
    far_b = to_core(own_b)
    state, back, counted = assemble(
        heads, chips, 0, True, change, first[0], state_own, back_own, held[0], waiting[0]
    )
    grad, *sums, counted = finish(
        heads, 0, STEPS, counted, *maps, shared, dx, (db, dc, change), state, back, None
    )
    got, far_b, counted = lax.optimization_barrier((waiting[1], far_b, counted))
    own_b, far_b = (own_b, got), (far_b, to_core(got))
    state, back, counted = assemble(
        heads, chips, 1, False, counted, first[1], state_own, back_own, own_b, far_b
    )

    later, counted = tiles(core_kernel, "core_sum", counted, to_core(counted))
    got = [to_chip(counted, step) for step in range(1, chips)]
    grad, *sums, token = finish(
        heads, STEPS, 1, counted, *maps, shared, dx, sums, state, back, grad
    )
    later, counted = tiles(count_kernel, "chip_sum", token, later, counted, *got)
    got = [to_earlier(counted, step) for step in range(1, groups)]
    grad, *sums, _ = finish(
        heads, STEPS + 1, 1, counted, *maps, shared, dx, sums, state, back, grad
    )
    return (grad, sums[0], sums[1], add_later(sums[2], later, *got))


def solution(mesh):
    tokens = P(("grp", "seq"), None)
    in_specs = (tokens, tokens, tokens, tokens, P(None, ("grp", "seq")))
    out_specs = (tokens, tokens, tokens, P(None, ("grp", "seq")))
    return jax.shard_map(
        per_device, mesh=mesh, in_specs=in_specs, out_specs=out_specs, check_vma=False
    )
```

```python
import jax
import jax.numpy as jnp
from jax import lax
from jax.experimental import pallas as pl
from jax.experimental.pallas import tpu as pltpu
from jax.sharding import PartitionSpec as P

STATE = 128
STRETCH = 256
LANES = 512
HALVES = 2
STRIP = 128
META = 8
PAD = 2 * META
BIG_VMEM = 56 << 20
SMALL_VMEM = 24 << 20
F32 = jnp.float32
BF16 = jnp.bfloat16
HIGHEST = lax.Precision.HIGHEST


def dot(left, right, left_dim, right_dim, precision=None):
    return lax.dot_general(
        left,
        right,
        (((left_dim,), (right_dim,)), ((), ())),
        precision=precision,
        preferred_element_type=F32,
    )


def iota(shape, dim):
    return lax.broadcasted_iota(jnp.int32, shape, dim)


def lower(length):
    return (iota((length, length), 0) >= iota((length, length), 1)).astype(F32)


def thrice(rates):
    heads, length = rates.shape
    spare = jnp.zeros((STATE - 3 * heads, length), F32)
    return jnp.concatenate([rates, rates, rates, spare], axis=0)


def three_terms(value, heads):
    lane = iota(value.shape, 1)
    first = value.astype(BF16)
    rest = value - first.astype(F32)
    second = rest.astype(BF16)
    third = (rest - second.astype(F32)).astype(BF16)
    return jnp.where(lane < heads, first, jnp.where(lane < 2 * heads, second, third))


def spreader(chunk, heads, head_size, lanes):
    row = iota((STATE, lanes), 0)
    head = (iota((STATE, lanes), 1) + chunk * lanes) // head_size
    hit = (row == head) | (row == head + heads) | (row == head + 2 * heads)
    return hit.astype(F32).astype(BF16)


def head_adder(chunk, head_size, lanes):
    head = (iota((lanes, STATE), 0) + chunk * lanes) // head_size
    return (iota((lanes, STATE), 1) == head).astype(F32).astype(BF16)


def head_sums(value, adder):
    first = value.astype(BF16)
    second = (value - first.astype(F32)).astype(BF16)
    return dot(first, adder, 1, 0) + dot(second, adder, 1, 0)


def decay_terms(rates, heads):
    length = rates.shape[1]
    running = dot(lower(length), thrice(rates), 1, 1, HIGHEST)
    last = running[length - 1 : length, :]
    return (
        running,
        three_terms(jnp.exp(last - running), heads),
        three_terms(jnp.exp(running), heads),
    )


def term_pair(value):
    first = value.astype(BF16)
    return first, (value - first.astype(F32)).astype(BF16)


def lane_spread(per_strip, head_size):
    head = iota((STRIP, STRIP), 0) % per_strip
    return (iota((STRIP, STRIP), 1) // head_size == head).astype(F32)


def spread_rows(rows, offset, strips, head_size):
    per_strip = STRIP // head_size
    lane = iota((strips, STRIP), 1)
    row = iota((strips, STRIP), 0) + offset
    picked = [jnp.where(lane // per_strip == row, value, 0.0) for value in rows]
    stacked = jnp.concatenate(picked, axis=0) if len(picked) > 1 else picked[0]
    wide = dot(stacked, lane_spread(per_strip, head_size), 1, 0, HIGHEST)
    return [wide[i * strips : (i + 1) * strips, :] for i in range(len(rows))]


def whole(*shape):
    return pl.BlockSpec(shape, lambda *_: (0,) * len(shape))


def lanes_of(rows):
    return pl.BlockSpec((rows, LANES), lambda c: (0, c))


def half_lanes(rows, lanes, half, steps):
    return pl.BlockSpec((rows, lanes), lambda c: (0, half * steps + c))


LITTLE = pl.CostEstimate(flops=1, bytes_accessed=1, transcendentals=0)


def position():
    shard = lax.axis_index("seq")
    return shard & 1, shard >> 1


STEPS = 2


def summary_kernel(heads, chips, half, x_ref, g_ref, write_ref, read_ref, *refs):
    place = position()
    chunk = pl.program_id(0)
    lanes = x_ref.shape[1]
    strips = lanes // STRIP
    half_strips = strips * STEPS
    head_size = lanes * STEPS * HALVES // heads
    part = STATE // chips
    if half == 0:
        rates_ref, send_ref, keep_ref, decay_ref, log_ref, run_ref, tail_ref, lead_ref = refs[:8]
    else:
        log_ref, tail_ref, lead_ref, send_ref, keep_ref, decay_ref = refs[:6]
    write_t, read_t = refs[-2:]

    @pl.when(chunk == 0)
    def _():
        if half == 0:
            running, tail, lead = decay_terms(rates_ref[...], heads)
            run_ref[...] = running
            tail_ref[...] = tail
            lead_ref[...] = lead
            log_ref[...] = jnp.broadcast_to(running[STRETCH - 1 :, :], (META, STRIP))
        send_ref[pl.ds(half_strips * STATE, META), :] = log_ref[...]
        write_t[...] = write_ref[...].astype(F32).T.astype(BF16)
        read_t[...] = read_ref[...].astype(F32).T.astype(BF16)

    spread = spreader(half * STEPS + chunk, heads, head_size, lanes)
    tail = dot(tail_ref[...], spread, 1, 0)
    lead = dot(lead_ref[...], spread, 1, 0)
    inputs_tail = (x_ref[...].astype(F32) * tail).astype(BF16)
    grads_lead = (g_ref[...].astype(F32) * lead).astype(BF16)
    state = dot(write_t[...], inputs_tail, 1, 0)
    back = dot(read_t[...], grads_lead, 1, 0)
    first = place[0] == 0
    send = jnp.where(first, state, back)
    keep = jnp.where(first, back, state)
    for strip in range(strips):
        at = chunk * strips + strip
        wide = slice(strip * STRIP, (strip + 1) * STRIP)
        decay_ref[pl.ds(at, 1), :] = lead[STRETCH - 1 :, wide]
        for quarter in range(chips):
            rows = pl.ds(pl.multiple_of((quarter * half_strips + at) * part, part), part)
            mine = slice(quarter * part, (quarter + 1) * part)
            send_ref[rows, :] = send[mine, wide]
            keep_ref[rows, :] = keep[mine, wide]


def summary(chips, half, x, g, write_map, read_map, rates, shared):
    tokens, wide = x.shape
    heads = rates.shape[0]
    lanes = wide // (STEPS * HALVES)
    strips = wide // STRIP // HALVES
    terms = [
        jax.ShapeDtypeStruct((META, STRIP), F32),
        jax.ShapeDtypeStruct((tokens, STRIP), F32),
        jax.ShapeDtypeStruct((tokens, STRIP), BF16),
        jax.ShapeDtypeStruct((tokens, STRIP), BF16),
    ]
    out_shape = [
        jax.ShapeDtypeStruct((strips * STATE + META, STRIP), F32),
        jax.ShapeDtypeStruct((strips * STATE, STRIP), F32),
        jax.ShapeDtypeStruct((strips, STRIP), F32),
    ]
    if half == 0:
        extra = [rates]
        out_shape = out_shape + terms
    else:
        extra = [shared[0], shared[2], shared[3]]
    return pl.pallas_call(
        lambda *refs: summary_kernel(heads, chips, half, *refs),
        grid=(STEPS,),
        in_specs=[
            half_lanes(tokens, lanes, half, STEPS),
            half_lanes(tokens, lanes, half, STEPS),
            whole(tokens, STATE),
            whole(tokens, STATE),
        ]
        + [whole(*value.shape) for value in extra],
        out_specs=[whole(*out.shape) for out in out_shape],
        out_shape=out_shape,
        scratch_shapes=[
            pltpu.VMEM((STATE, tokens), BF16),
            pltpu.VMEM((STATE, tokens), BF16),
        ],
        compiler_params=pltpu.CompilerParams(vmem_limit_bytes=BIG_VMEM),
        cost_estimate=LITTLE,
        name="summary",
    )(x, g, write_map, read_map, *extra)


def combine_kernel(chips, first_ref, keep_ref, decay_ref, log_ref, mine_ref, send_ref):
    place = position()
    strips = decay_ref.shape[0]
    part = STATE // chips
    size = mine_ref.shape[0]
    bit = place[1] & 1
    for base, out_ref in ((bit * size, mine_ref), ((1 - bit) * size, send_ref)):
        for strip in range(strips):
            decay = decay_ref[strip : strip + 1, :]
            for at in range(strip * part, size, strips * part):
                rows = pl.ds(pl.multiple_of(base + at, part), part)
                out_ref[at : at + part, :] = first_ref[rows, :] * decay + keep_ref[rows, :]
    meta = first_ref[2 * size :, :] + log_ref[...]
    send_ref[size : size + META, :] = meta
    send_ref[size + META :, :] = meta


def halves(size):
    return (
        [whole(size, STRIP), whole(size + PAD, STRIP)],
        [
            jax.ShapeDtypeStruct((size, STRIP), F32),
            jax.ShapeDtypeStruct((size + PAD, STRIP), F32),
        ],
    )


def combine(chips, first, keep, decay, log):
    out_specs, out_shape = halves(keep.shape[0] // 2)
    return pl.pallas_call(
        lambda *refs: combine_kernel(chips, *refs),
        in_specs=[whole(*value.shape) for value in (first, keep, decay, log)],
        out_specs=out_specs,
        out_shape=out_shape,
        compiler_params=pltpu.CompilerParams(vmem_limit_bytes=SMALL_VMEM),
        cost_estimate=LITTLE,
        name="combine",
    )(first, keep, decay, log)


def is_ahead(place, level):
    return ((place[1] >> level) & 1) == place[0]


def up_kernel(level, last, part, offset, strips, head_size, mine_ref, log_ref, got_ref, *outs):
    place = position()
    size = mine_ref.shape[0]
    ahead = is_ahead(place, level)
    mine_log, got_log = log_ref[size : size + 1, :], got_ref[size : size + 1, :]
    mine_wide, got_wide = spread_rows(
        [jnp.where(ahead, 1.0, jnp.exp(got_log)), jnp.where(ahead, jnp.exp(mine_log), 1.0)],
        offset,
        strips,
        head_size,
    )
    bit = (place[1] >> (level + 1)) & 1
    half = size if last else size // 2
    targets = ((0, outs[0]),) if last else ((bit * half, outs[0]), ((1 - bit) * half, outs[1]))
    for base, out_ref in targets:
        for strip in range(strips):
            one = slice(strip, strip + 1)
            for at in range(strip * part, half, strips * part):
                rows = slice(at, at + part)
                if not last:
                    rows = pl.ds(pl.multiple_of(base + at, part), part)
                out_ref[at : at + part, :] = (
                    mine_ref[rows, :] * mine_wide[one, :] + got_ref[rows, :] * got_wide[one, :]
                )
    outs[-1][half:, :] = jnp.broadcast_to(mine_log + got_log, (META if last else PAD, STRIP))


def up(level, chips, half, strips, head_size, mine, send, got):
    size = mine.shape[0]
    last = 2 << level == chips
    out_specs, out_shape = halves(size if last else size // 2)
    if last:
        out_specs = [whole(size + META, STRIP)]
        out_shape = [jax.ShapeDtypeStruct((size + META, STRIP), F32)]
    return pl.pallas_call(
        lambda *refs: up_kernel(
            level, last, STATE // chips, half * strips, strips, head_size, *refs
        ),
        in_specs=[whole(size, STRIP), whole(*send.shape), whole(size + PAD, STRIP)],
        out_specs=out_specs,
        out_shape=out_shape,
        compiler_params=pltpu.CompilerParams(vmem_limit_bytes=SMALL_VMEM),
        cost_estimate=LITTLE,
        name="up",
    )(mine, send, got)


def down_kernel(level, top, part, offset, strips, head_size, mine_ref, log_ref, got_ref, *refs):
    place = position()
    sources, (here_ref, there_ref) = refs[:-2], refs[-2:]
    size = mine_ref.shape[0]
    ahead = is_ahead(place, level)
    rows_of = [
        jnp.where(ahead, jnp.exp(got_ref[size : size + 1, :]), 1.0),
        jnp.where(ahead, 1.0, jnp.exp(log_ref[size : size + 1, :])),
    ]
    if top:
        passed = jnp.zeros_like(rows_of[0])
        for ref in sources:
            rows_of.append(jnp.exp(passed))
            passed = passed + ref[size : size + 1, :]
        bases, length = (0,), size
    else:
        length = size // 2
        bit = (place[1] >> (level + 1)) & 1
        bases = (bit * length, (1 - bit) * length)
    here_wide, there_wide, *group_wide = spread_rows(rows_of, offset, strips, head_size)
    for index, base in enumerate(bases):
        for strip in range(strips):
            one = slice(strip, strip + 1)
            for at in range(strip * part, length, strips * part):
                rows = slice(at, at + part)
                if top:
                    entering = sources[0][rows, :] * group_wide[0][one, :]
                    for ref, wide in zip(sources[1:], group_wide[1:]):
                        entering = entering + ref[rows, :] * wide[one, :]
                else:
                    entering = sources[index][rows, :]
                    rows = pl.ds(pl.multiple_of(base + at, part), part)
                got = jnp.where(ahead, got_ref[rows, :], 0.0)
                mine = jnp.where(ahead, 0.0, mine_ref[rows, :])
                here_ref[rows, :] = entering * here_wide[one, :] + got
                there_ref[rows, :] = entering * there_wide[one, :] + mine
    there_ref[size:, :] = jnp.zeros((PAD, STRIP), F32)


def down(level, chips, half, strips, head_size, mine, send, got, sources):
    size = mine.shape[0]
    top = 2 << level == chips
    return pl.pallas_call(
        lambda *refs: down_kernel(
            level, top, STATE // chips, half * strips, strips, head_size, *refs
        ),
        in_specs=[whole(size, STRIP), whole(*send.shape), whole(size + PAD, STRIP)]
        + [whole(*value.shape) for value in sources],
        out_specs=[whole(size, STRIP), whole(size + PAD, STRIP)],
        out_shape=[
            jax.ShapeDtypeStruct((size, STRIP), F32),
            jax.ShapeDtypeStruct((size + PAD, STRIP), F32),
        ],
        compiler_params=pltpu.CompilerParams(vmem_limit_bytes=SMALL_VMEM),
        cost_estimate=LITTLE,
        name="down",
    )(mine, send, got, *sources)


def intra_kernel(
    heads, head_size, start, last,
    after_ref, x_ref, g_ref, write_ref, read_ref, rates_ref, column_ref, tail_ref, lead_ref, *refs,
):
    dx_ref, state_ref, back_ref, change_ref, *sums, row_ref, scores_ref, mask_ref, pairs_ref, \
        write_t, read_t = refs[5 if start else 0 :]
    step = pl.program_id(0)
    chunk = start + step
    lanes = x_ref.shape[1]
    per_chunk = lanes // head_size

    @pl.when(step == 0)
    def _():
        rates = rates_ref[...]
        triangle = lower(STRETCH)
        row_ref[...] = dot(rates, triangle, 1, 1, HIGHEST)
        mask_ref[...] = triangle
        scores_ref[...] = dot(read_ref[...], write_ref[...], 1, 1)
        pairs_ref[...] = refs[4][...] if start else jnp.zeros_like(pairs_ref)
        change_ref[...] = refs[3][...] if start else jnp.zeros_like(change_ref)
        write_t[...] = write_ref[...].astype(F32).T.astype(BF16)
        read_t[...] = read_ref[...].astype(F32).T.astype(BF16)

    columns = pltpu.roll(column_ref[...], STATE - chunk * per_chunk, 1)
    rows = row_ref[pl.ds(pl.multiple_of(chunk * per_chunk, per_chunk), per_chunk), :]
    causal = mask_ref[...] > 0.5
    scores = scores_ref[...]
    pairs = pairs_ref[...]
    low_half = iota((STRETCH, 2 * head_size), 1) < head_size
    adder = head_adder(chunk, head_size, lanes)
    spread = spreader(chunk, heads, head_size, lanes)
    high, low = term_pair(x_ref[...].astype(F32) * dot(tail_ref[...], spread, 1, 0))
    state_ref[...] = dot(write_t[...], high, 1, 0) + dot(write_t[...], low, 1, 0)
    high, low = term_pair(g_ref[...].astype(F32) * dot(lead_ref[...], spread, 1, 0))
    back_ref[...] = dot(read_t[...], high, 1, 0) + dot(read_t[...], low, 1, 0)
    for pair in range(per_chunk // 2):
        strip = slice(pair * 2 * head_size, (pair + 1) * 2 * head_size)
        x = x_ref[:, strip]
        g = g_ref[:, strip]
        ys, dxs = [], []
        for half in range(2):
            head = 2 * pair + half
            gap = columns[:, head : head + 1] - rows[head : head + 1, :]
            decay = jnp.where(causal, jnp.exp(gap), 0.0)
            mixing = (scores * decay).astype(BF16)
            ys.append(dot(mixing, x, 1, 0))
            dxs.append(dot(mixing, g, 0, 0))
            mine = low_half if half == 0 else jnp.logical_not(low_half)
            pairs = pairs + dot(jnp.where(mine, g, jnp.zeros_like(g)), x, 1, 1) * decay
        y = jnp.where(low_half, ys[0], ys[1])
        dx = jnp.where(low_half, dxs[0], dxs[1])
        dx_ref[:, strip] = dx
        change_ref[...] += head_sums(
            g.astype(F32) * y - x.astype(F32) * dx, adder[strip, :]
        )
    pairs_ref[...] = pairs

    @pl.when(step == pl.num_programs(0) - 1)
    def _():
        if last:
            summed = pairs_ref[...].astype(BF16)
            sums[0][...] = dot(summed, read_ref[...], 0, 0)
            sums[1][...] = dot(summed, write_ref[...], 1, 0)
        else:
            sums[0][...] = pairs_ref[...]


def intra(start, steps, after, x, g, write_map, read_map, rates, shared, earlier):
    tokens, wide = x.shape
    heads = rates.shape[0]
    last = (start + steps) * LANES == wide
    lanes = lambda rows: pl.BlockSpec((rows, LANES), lambda c: (0, start + c))
    anywhere = pl.BlockSpec(memory_space=pl.ANY)
    sums = [(tokens, STATE)] * 2 if last else [(tokens, tokens)]
    return pl.pallas_call(
        lambda *refs: intra_kernel(heads, wide // heads, start, last, *refs),
        grid=(steps,),
        in_specs=[
            whole(META, STRIP),
            lanes(tokens),
            lanes(tokens),
            whole(tokens, STATE),
            whole(tokens, STATE),
            whole(heads, tokens),
        ]
        + [whole(tokens, STRIP)] * 3
        + ([anywhere] * 3 + [whole(tokens, STATE), whole(tokens, tokens)] if earlier else []),
        out_specs=[lanes(tokens), lanes(STATE), lanes(STATE), whole(tokens, STATE)]
        + [whole(*shape) for shape in sums],
        out_shape=[
            jax.ShapeDtypeStruct((tokens, wide), F32),
            jax.ShapeDtypeStruct((STATE, wide), F32),
            jax.ShapeDtypeStruct((STATE, wide), F32),
            jax.ShapeDtypeStruct((tokens, STATE), F32),
        ]
        + [jax.ShapeDtypeStruct(shape, F32) for shape in sums],
        scratch_shapes=[
            pltpu.VMEM((heads, tokens), F32),
            pltpu.VMEM((tokens, tokens), F32),
            pltpu.VMEM((tokens, tokens), F32),
            pltpu.VMEM((tokens, tokens), F32),
            pltpu.VMEM((STATE, tokens), BF16),
            pltpu.VMEM((STATE, tokens), BF16),
        ],
        input_output_aliases={9: 0, 10: 1, 11: 2} if earlier else {},
        compiler_params=pltpu.CompilerParams(vmem_limit_bytes=SMALL_VMEM),
        cost_estimate=LITTLE,
        name="intra",
    )(after, x, g, write_map, read_map, rates, *shared[1:], *earlier)


def order_kernel(here_ref, got_ref, low_ref, high_ref):
    place = position()
    bit = place[1] & 1
    here, got = here_ref[...], got_ref[: here_ref.shape[0], :]
    low_ref[...] = jnp.where(bit == 0, here, got)
    high_ref[...] = jnp.where(bit == 0, got, here)


def order(here, got):
    return pl.pallas_call(
        order_kernel,
        in_specs=[whole(*here.shape), whole(*got.shape)],
        out_specs=[whole(*here.shape)] * 2,
        out_shape=[jax.ShapeDtypeStruct(here.shape, F32)] * 2,
        compiler_params=pltpu.CompilerParams(vmem_limit_bytes=SMALL_VMEM),
        cost_estimate=LITTLE,
        name="order",
    )(here, got)


def assemble_kernel(
    heads, chips, half, head_size, ordered,
    after_ref, first_ref, state_own, back_own, *refs,
):
    place = position()
    own_refs, far_refs, (state_ref, back_ref, total_ref) = refs[:2], refs[2:4], refs[4:]
    bit = 0 if ordered else place[1] & 1
    lanes = state_ref.shape[1]
    strips = lanes // STRIP
    part = STATE // chips
    size = strips * part
    log = first_ref[chips * size : chips * size + 1, :]
    decay = spread_rows([jnp.exp(log)], half * strips, strips, head_size)[0]
    is_first = place[0] == 0
    sums = [None] * strips
    for quarter in range(chips):
        rows = slice(quarter * part, (quarter + 1) * part)
        for strip in range(strips):
            wide = slice(strip * STRIP, (strip + 1) * STRIP)
            here = slice(quarter * size + strip * part, quarter * size + (strip + 1) * part)
            piece, at = divmod(here.start, chips // 2 * size)
            there = slice(at, at + part)
            own, far = own_refs[piece][there, :], far_refs[piece][there, :]
            if not ordered:
                own = jnp.where(bit == 0, own, own_refs[1 - piece][there, :])
                far = jnp.where(bit == 0, far, far_refs[1 - piece][there, :])
            own = own * decay[strip : strip + 1, :] + first_ref[here, :]
            state = jnp.where(is_first, far, own).astype(BF16)
            back = jnp.where(is_first, own, far).astype(BF16)
            state_ref[rows, wide] = state
            back_ref[rows, wide] = back
            gain = state.astype(F32) * back_own[rows, wide]
            gain = gain - back.astype(F32) * state_own[rows, wide]
            sums[strip] = gain if sums[strip] is None else sums[strip] + gain
    row_sum = [
        jnp.broadcast_to(jnp.sum(value, axis=0, keepdims=True), (META, STRIP)) for value in sums
    ]
    total = head_sums(jnp.concatenate(row_sum, axis=1), head_adder(half, head_size, lanes))
    total_ref[...] = total + after_ref[...] if half else total


def assemble(heads, chips, half, ordered, after, first, state_own, back_own, own, far):
    wide = state_own.shape[1]
    lanes = wide // HALVES
    mine = pl.BlockSpec((STATE, lanes), lambda c: (0, half))
    return pl.pallas_call(
        lambda *refs: assemble_kernel(heads, chips, half, wide // heads, ordered, *refs),
        grid=(1,),
        in_specs=[whole(META, STRIP), whole(*first.shape), mine, mine]
        + [whole(*value.shape) for value in (*own, *far)],
        out_specs=[whole(STATE, lanes), whole(STATE, lanes), whole(META, STRIP)],
        out_shape=[
            jax.ShapeDtypeStruct((STATE, lanes), BF16),
            jax.ShapeDtypeStruct((STATE, lanes), BF16),
            jax.ShapeDtypeStruct((META, STRIP), F32),
        ],
        compiler_params=pltpu.CompilerParams(vmem_limit_bytes=SMALL_VMEM),
        cost_estimate=LITTLE,
        name="assemble",
    )(after, first, state_own, back_own, *own, *far)


def finish_kernel(
    heads, start, steps, last, x_ref, g_ref, write_ref, read_ref, tail_ref, lead_ref,
    dx_ref, db_ref, dc_ref, change_ref, state_ref, back_ref, *refs,
):
    grad_ref, db_out, dc_out, change_out, token_ref, db_sum, dc_sum, sum_out = refs[-8:]
    chunk = pl.program_id(0)
    lanes = x_ref.shape[1]
    head_size = lanes * STEPS * HALVES // heads
    wide = start + chunk

    @pl.when(chunk == 0)
    def _():
        sum_out[...] = change_ref[...]
        db_sum[...] = db_ref[...]
        dc_sum[...] = dc_ref[...]

    state = state_ref[...]
    back = back_ref[...]
    spread = spreader(wide, heads, head_size, lanes)
    tail = dot(tail_ref[...], spread, 1, 0)
    lead = dot(lead_ref[...], spread, 1, 0)
    x = x_ref[...].astype(F32)
    g = g_ref[...].astype(F32)
    y = dot(read_ref[...], state, 1, 0) * lead
    dx = dot(write_ref[...], back, 1, 0) * tail
    grad_ref[...] = (dx_ref[...] + dx).astype(BF16)
    adder = head_adder(wide, head_size, lanes)
    sum_out[...] += head_sums(g * y - x * dx, adder)
    db_sum[...] += dot((x * tail).astype(BF16), back, 1, 1)
    dc_sum[...] += dot((g * lead).astype(BF16), state, 1, 1)

    @pl.when(chunk == steps - 1)
    def _():
        token_ref[...] = refs[-9][...]
        db_out[...] = db_sum[...].astype(db_out.dtype)
        dc_out[...] = dc_sum[...].astype(dc_out.dtype)
        if last:
            change_out[...] = dot(sum_out[...], lower(STRETCH), 0, 0, HIGHEST)[:heads, :]
        else:
            change_out[...] = sum_out[...]


def finish(heads, start, steps, after, x, g, write_map, read_map, shared, dx, sums, state, back, grad):
    tokens, wide = x.shape
    lanes = wide // (STEPS * HALVES)
    strip = pl.BlockSpec((tokens, lanes), lambda c: (0, start + c))
    own = pl.BlockSpec((STATE, lanes), lambda c: (0, start % STEPS + c))
    last = start + steps == STEPS * HALVES
    kind = BF16 if last else F32
    change = (heads, tokens) if last else (tokens, STATE)
    earlier = [] if grad is None else [grad]
    return pl.pallas_call(
        lambda *refs: finish_kernel(heads, start, steps, last, *refs),
        grid=(steps,),
        in_specs=[strip, strip]
        + [whole(tokens, STATE)] * 4
        + [strip]
        + [whole(tokens, STATE)] * 3
        + [own, own]
        + [pl.BlockSpec(memory_space=pl.ANY)] * len(earlier)
        + [whole(META, STRIP)],
        out_specs=[strip] + [whole(tokens, STATE)] * 2 + [whole(*change), whole(META, STRIP)],
        out_shape=[
            jax.ShapeDtypeStruct((tokens, wide), BF16),
            jax.ShapeDtypeStruct((tokens, STATE), kind),
            jax.ShapeDtypeStruct((tokens, STATE), kind),
            jax.ShapeDtypeStruct(change, F32),
            jax.ShapeDtypeStruct((META, STRIP), F32),
        ],
        scratch_shapes=[pltpu.VMEM((tokens, STATE), F32)] * 3,
        input_output_aliases={12: 0} if earlier else {},
        compiler_params=pltpu.CompilerParams(vmem_limit_bytes=SMALL_VMEM),
        cost_estimate=LITTLE,
        name="finish",
    )(x, g, write_map, read_map, *shared[2:], dx, *sums, state, back, *earlier, after)


def count_kernel(after_ref, later_ref, total_ref, *refs):
    place = position()
    got_refs, (later_out, total_out) = refs[:-2], refs[-2:]
    later, total = later_ref[...], total_ref[...]
    for step, ref in enumerate(got_refs, 1):
        later = later + jnp.where((place[1] ^ step) > place[1], ref[...], 0.0)
        total = total + ref[...]
    later_out[...] = later
    total_out[...] = total


def core_kernel(total_ref, got_ref, later_out, total_out):
    place = position()
    later_out[...] = jnp.where(place[0] == 0, got_ref[...], 0.0)
    total_out[...] = total_ref[...] + got_ref[...]


def tiles(kernel, name, *values):
    return pl.pallas_call(
        kernel,
        in_specs=[whole(META, STRIP)] * len(values),
        out_specs=[whole(META, STRIP)] * 2,
        out_shape=[jax.ShapeDtypeStruct((META, STRIP), F32)] * 2,
        compiler_params=pltpu.CompilerParams(vmem_limit_bytes=SMALL_VMEM),
        cost_estimate=LITTLE,
        name=name,
    )(*values)


def add_later_kernel(suffix_ref, *refs):
    out_ref = refs[-1]
    heads = out_ref.shape[0]
    later = refs[0][...]
    for ref in refs[1:-1]:
        later = later + ref[...]
    out_ref[...] = suffix_ref[...] + later.T[:heads, 0:1]


def add_later(suffix, *parts):
    return pl.pallas_call(
        add_later_kernel,
        in_specs=[whole(*value.shape) for value in (suffix, *parts)],
        out_specs=whole(*suffix.shape),
        out_shape=jax.ShapeDtypeStruct(suffix.shape, F32),
        compiler_params=pltpu.CompilerParams(vmem_limit_bytes=SMALL_VMEM),
        cost_estimate=LITTLE,
        name="add_later",
    )(suffix, *parts)


def per_device(inputs, out_grad, input_map, output_map, log_decay):
    heads = log_decay.shape[0]
    head_size = inputs.shape[1] // heads
    groups, shards = lax.axis_size("grp"), lax.axis_size("seq")
    chips = shards // 2
    strips = inputs.shape[1] // STRIP // HALVES
    everyone = [(a, z, c) for a in range(groups) for z in range(chips) for c in range(2)]

    def move(value, target):
        pairs = []
        for a, z, c in everyone:
            to = target(a, z, c)
            if to is not None:
                pairs.append((a * shards + 2 * z + c, to[0] * shards + 2 * to[1] + to[2]))
        return lax.ppermute(value, ("grp", "seq"), pairs)

    def to_core(value):
        return move(value, lambda a, z, c: (a, z, 1 - c))

    def to_chip(value, step):
        return move(value, lambda a, z, c: (a, z ^ step, c)) if step else value

    def to_earlier(value, step):
        return move(value, lambda a, z, c: (a - step, z, c) if a >= step else None)

    def to_later(value, step):
        def target(a, z, c):
            to = a + step if c == 1 else a - step
            return (to, z, c) if 0 <= to < groups else None

        return move(value, target)

    maps = (inputs, out_grad, input_map, output_map)
    send, keep, decay, *shared = summary(chips, 0, *maps, log_decay, None)
    first = [to_core(send)]
    kept, decays = [keep], [decay]
    send, keep, decay = summary(chips, 1, *maps, log_decay, shared)
    first.append(to_core(send))
    kept.append(keep)
    decays.append(decay)

    levels = chips.bit_length() - 1
    held = [[], []]
    waiting = [None, None]

    def advance(half, step):
        fixed = (chips, half, strips, head_size)
        if step == 0:
            mine, send = combine(
                chips, first[half], kept[half], decays[half], shared[0]
            )
        elif step < levels:
            held[half][-1] += (waiting[half],)
            mine, send = up(step - 1, *fixed, *held[half][-1])
        elif step == levels:
            held[half][-1] += (waiting[half],)
            (send,) = up(step - 1, *fixed, *held[half][-1])
            waiting[half] = [to_later(send, far) for far in range(1, groups)]
            return send
        elif step <= 2 * levels:
            level = 2 * levels - step
            if level < levels - 1:
                waiting[half] = (held[half][level + 1], waiting[half])
            mine, send = down(level, *fixed, *held[half][level], waiting[half])
            held[half][level] = mine
            waiting[half] = to_chip(send, 1 << level)
            return send
        else:
            held[half] = order(held[half][0], waiting[half])
            waiting[half] = [to_core(value) for value in held[half]]
            return held[half][0]
        held[half].append((mine, send))
        waiting[half] = to_chip(send, 1 << step)
        return send

    chunks = inputs.shape[1] // LANES
    rounds = 2 * levels + 2
    block, ready = (), 0
    for step in range(rounds):
        token = advance(0, step)
        if step:
            advance(1, step - 1)
        if step < 3:
            more = pl.cdiv(chunks - ready, 3 - step)
            block = intra(ready, more, token, *maps, log_decay, shared, block)
            ready += more
            if step == 0:
                first[1], block = lax.optimization_barrier((first[1], block))
            elif step == 1:
                waiting[0], block = lax.optimization_barrier((waiting[0], block))
            else:
                waiting[1], block = lax.optimization_barrier((waiting[1], block))
        elif levels + 1 < step < rounds - 1:
            waiting[0], waiting[1] = lax.optimization_barrier((waiting[0], waiting[1]))
    dx, state_own, back_own, change, db, dc = block
    own_b = held[1][0]
    far_b = to_core(own_b)
    state, back, counted = assemble(
        heads, chips, 0, True, change, first[0], state_own, back_own, held[0], waiting[0]
    )
    grad, *sums, counted = finish(
        heads, 0, STEPS, counted, *maps, shared, dx, (db, dc, change), state, back, None
    )
    got, far_b, counted = lax.optimization_barrier((waiting[1], far_b, counted))
    own_b, far_b = (own_b, got), (far_b, to_core(got))
    state, back, counted = assemble(
        heads, chips, 1, False, counted, first[1], state_own, back_own, own_b, far_b
    )

    later, counted = tiles(core_kernel, "core_sum", counted, to_core(counted))
    got = [to_chip(counted, step) for step in range(1, chips)]
    grad, *sums, token = finish(
        heads, STEPS, 1, counted, *maps, shared, dx, sums, state, back, grad
    )
    later, counted = tiles(count_kernel, "chip_sum", token, later, counted, *got)
    got = [to_earlier(counted, step) for step in range(1, groups)]
    grad, *sums, _ = finish(
        heads, STEPS + 1, 1, counted, *maps, shared, dx, sums, state, back, grad
    )
    return (grad, sums[0], sums[1], add_later(sums[2], later, *got))


def solution(mesh):
    tokens = P(("grp", "seq"), None)
    in_specs = (tokens, tokens, tokens, tokens, P(None, ("grp", "seq")))
    out_specs = (tokens, tokens, tokens, P(None, ("grp", "seq")))
    return jax.shard_map(
        per_device, mesh=mesh, in_specs=in_specs, out_specs=out_specs, check_vma=False
    )
```

```python
import jax
import jax.numpy as jnp
from jax import lax
from jax.experimental import pallas as pl
from jax.experimental.pallas import tpu as pltpu
from jax.sharding import PartitionSpec as P

STATE = 128
STRETCH = 256
LANES = 512
HALVES = 2
STRIP = 128
META = 8
PAD = 2 * META
BIG_VMEM = 56 << 20
SMALL_VMEM = 24 << 20
F32 = jnp.float32
BF16 = jnp.bfloat16
HIGHEST = lax.Precision.HIGHEST


def dot(left, right, left_dim, right_dim, precision=None):
    return lax.dot_general(
        left,
        right,
        (((left_dim,), (right_dim,)), ((), ())),
        precision=precision,
        preferred_element_type=F32,
    )


def iota(shape, dim):
    return lax.broadcasted_iota(jnp.int32, shape, dim)


def lower(length):
    return (iota((length, length), 0) >= iota((length, length), 1)).astype(F32)


def thrice(rates):
    heads, length = rates.shape
    spare = jnp.zeros((STATE - 3 * heads, length), F32)
    return jnp.concatenate([rates, rates, rates, spare], axis=0)


def three_terms(value, heads):
    lane = iota(value.shape, 1)
    first = value.astype(BF16)
    rest = value - first.astype(F32)
    second = rest.astype(BF16)
    third = (rest - second.astype(F32)).astype(BF16)
    return jnp.where(lane < heads, first, jnp.where(lane < 2 * heads, second, third))


def spreader(chunk, heads, head_size, lanes):
    row = iota((STATE, lanes), 0)
    head = (iota((STATE, lanes), 1) + chunk * lanes) // head_size
    hit = (row == head) | (row == head + heads) | (row == head + 2 * heads)
    return hit.astype(F32).astype(BF16)


def head_adder(chunk, head_size, lanes):
    head = (iota((lanes, STATE), 0) + chunk * lanes) // head_size
    return (iota((lanes, STATE), 1) == head).astype(F32).astype(BF16)


def head_sums(value, adder):
    first = value.astype(BF16)
    second = (value - first.astype(F32)).astype(BF16)
    return dot(first, adder, 1, 0) + dot(second, adder, 1, 0)


def decay_terms(rates, heads):
    length = rates.shape[1]
    running = dot(lower(length), thrice(rates), 1, 1, HIGHEST)
    last = running[length - 1 : length, :]
    return (
        running,
        three_terms(jnp.exp(last - running), heads),
        three_terms(jnp.exp(running), heads),
    )


def term_pair(value):
    first = value.astype(BF16)
    return first, (value - first.astype(F32)).astype(BF16)


def lane_spread(per_strip, head_size):
    head = iota((STRIP, STRIP), 0) % per_strip
    return (iota((STRIP, STRIP), 1) // head_size == head).astype(F32)


def spread_rows(rows, offset, strips, head_size):
    per_strip = STRIP // head_size
    lane = iota((strips, STRIP), 1)
    row = iota((strips, STRIP), 0) + offset
    picked = [jnp.where(lane // per_strip == row, value, 0.0) for value in rows]
    stacked = jnp.concatenate(picked, axis=0) if len(picked) > 1 else picked[0]
    wide = dot(stacked, lane_spread(per_strip, head_size), 1, 0, HIGHEST)
    return [wide[i * strips : (i + 1) * strips, :] for i in range(len(rows))]


def whole(*shape):
    return pl.BlockSpec(shape, lambda *_: (0,) * len(shape))


def lanes_of(rows):
    return pl.BlockSpec((rows, LANES), lambda c: (0, c))


def half_lanes(rows, lanes, half, steps):
    return pl.BlockSpec((rows, lanes), lambda c: (0, half * steps + c))


LITTLE = pl.CostEstimate(flops=1, bytes_accessed=1, transcendentals=0)


def position():
    shard = lax.axis_index("seq")
    return shard & 1, shard >> 1


STEPS = 2


def summary_kernel(heads, chips, half, x_ref, g_ref, write_ref, read_ref, *refs):
    place = position()
    chunk = pl.program_id(0)
    lanes = x_ref.shape[1]
    strips = lanes // STRIP
    half_strips = strips * STEPS
    head_size = lanes * STEPS * HALVES // heads
    part = STATE // chips
    if half == 0:
        rates_ref, send_ref, keep_ref, decay_ref, log_ref, run_ref, tail_ref, lead_ref = refs[:8]
    else:
        log_ref, tail_ref, lead_ref, send_ref, keep_ref, decay_ref = refs[:6]
    write_t, read_t = refs[-2:]

    @pl.when(chunk == 0)
    def _():
        if half == 0:
            running, tail, lead = decay_terms(rates_ref[...], heads)
            run_ref[...] = running
            tail_ref[...] = tail
            lead_ref[...] = lead
            log_ref[...] = jnp.broadcast_to(running[STRETCH - 1 :, :], (META, STRIP))
        send_ref[pl.ds(half_strips * STATE, META), :] = log_ref[...]
        write_t[...] = write_ref[...].astype(F32).T.astype(BF16)
        read_t[...] = read_ref[...].astype(F32).T.astype(BF16)

    spread = spreader(half * STEPS + chunk, heads, head_size, lanes)
    tail = dot(tail_ref[...], spread, 1, 0)
    lead = dot(lead_ref[...], spread, 1, 0)
    inputs_tail = (x_ref[...].astype(F32) * tail).astype(BF16)
    grads_lead = (g_ref[...].astype(F32) * lead).astype(BF16)
    state = dot(write_t[...], inputs_tail, 1, 0)
    back = dot(read_t[...], grads_lead, 1, 0)
    first = place[0] == 0
    send = jnp.where(first, state, back)
    keep = jnp.where(first, back, state)
    for strip in range(strips):
        at = chunk * strips + strip
        wide = slice(strip * STRIP, (strip + 1) * STRIP)
        decay_ref[pl.ds(at, 1), :] = lead[STRETCH - 1 :, wide]
        for quarter in range(chips):
            rows = pl.ds(pl.multiple_of((quarter * half_strips + at) * part, part), part)
            mine = slice(quarter * part, (quarter + 1) * part)
            send_ref[rows, :] = send[mine, wide]
            keep_ref[rows, :] = keep[mine, wide]


def summary(chips, half, x, g, write_map, read_map, rates, shared):
    tokens, wide = x.shape
    heads = rates.shape[0]
    lanes = wide // (STEPS * HALVES)
    strips = wide // STRIP // HALVES
    terms = [
        jax.ShapeDtypeStruct((META, STRIP), F32),
        jax.ShapeDtypeStruct((tokens, STRIP), F32),
        jax.ShapeDtypeStruct((tokens, STRIP), BF16),
        jax.ShapeDtypeStruct((tokens, STRIP), BF16),
    ]
    out_shape = [
        jax.ShapeDtypeStruct((strips * STATE + META, STRIP), F32),
        jax.ShapeDtypeStruct((strips * STATE, STRIP), F32),
        jax.ShapeDtypeStruct((strips, STRIP), F32),
    ]
    if half == 0:
        extra = [rates]
        out_shape = out_shape + terms
    else:
        extra = [shared[0], shared[2], shared[3]]
    return pl.pallas_call(
        lambda *refs: summary_kernel(heads, chips, half, *refs),
        grid=(STEPS,),
        in_specs=[
            half_lanes(tokens, lanes, half, STEPS),
            half_lanes(tokens, lanes, half, STEPS),
            whole(tokens, STATE),
            whole(tokens, STATE),
        ]
        + [whole(*value.shape) for value in extra],
        out_specs=[whole(*out.shape) for out in out_shape],
        out_shape=out_shape,
        scratch_shapes=[
            pltpu.VMEM((STATE, tokens), BF16),
            pltpu.VMEM((STATE, tokens), BF16),
        ],
        compiler_params=pltpu.CompilerParams(vmem_limit_bytes=BIG_VMEM),
        cost_estimate=LITTLE,
        name="summary",
    )(x, g, write_map, read_map, *extra)


def combine_kernel(chips, first_ref, keep_ref, decay_ref, log_ref, mine_ref, send_ref):
    place = position()
    strips = decay_ref.shape[0]
    part = STATE // chips
    size = mine_ref.shape[0]
    bit = place[1] & 1
    for base, out_ref in ((bit * size, mine_ref), ((1 - bit) * size, send_ref)):
        for strip in range(strips):
            decay = decay_ref[strip : strip + 1, :]
            for at in range(strip * part, size, strips * part):
                rows = pl.ds(pl.multiple_of(base + at, part), part)
                out_ref[at : at + part, :] = first_ref[rows, :] * decay + keep_ref[rows, :]
    meta = first_ref[2 * size :, :] + log_ref[...]
    send_ref[size : size + META, :] = meta
    send_ref[size + META :, :] = meta


def halves(size):
    return (
        [whole(size, STRIP), whole(size + PAD, STRIP)],
        [
            jax.ShapeDtypeStruct((size, STRIP), F32),
            jax.ShapeDtypeStruct((size + PAD, STRIP), F32),
        ],
    )


def combine(chips, first, keep, decay, log):
    out_specs, out_shape = halves(keep.shape[0] // 2)
    return pl.pallas_call(
        lambda *refs: combine_kernel(chips, *refs),
        in_specs=[whole(*value.shape) for value in (first, keep, decay, log)],
        out_specs=out_specs,
        out_shape=out_shape,
        compiler_params=pltpu.CompilerParams(vmem_limit_bytes=SMALL_VMEM),
        cost_estimate=LITTLE,
        name="combine",
    )(first, keep, decay, log)


def is_ahead(place, level):
    return ((place[1] >> level) & 1) == place[0]


def up_kernel(level, last, part, offset, strips, head_size, mine_ref, log_ref, got_ref, *outs):
    place = position()
    size = mine_ref.shape[0]
    ahead = is_ahead(place, level)
    mine_log, got_log = log_ref[size : size + 1, :], got_ref[size : size + 1, :]
    mine_wide, got_wide = spread_rows(
        [jnp.where(ahead, 1.0, jnp.exp(got_log)), jnp.where(ahead, jnp.exp(mine_log), 1.0)],
        offset,
        strips,
        head_size,
    )
    bit = (place[1] >> (level + 1)) & 1
    half = size if last else size // 2
    targets = ((0, outs[0]),) if last else ((bit * half, outs[0]), ((1 - bit) * half, outs[1]))
    for base, out_ref in targets:
        for strip in range(strips):
            one = slice(strip, strip + 1)
            for at in range(strip * part, half, strips * part):
                rows = slice(at, at + part)
                if not last:
                    rows = pl.ds(pl.multiple_of(base + at, part), part)
                out_ref[at : at + part, :] = (
                    mine_ref[rows, :] * mine_wide[one, :] + got_ref[rows, :] * got_wide[one, :]
                )
    outs[-1][half:, :] = jnp.broadcast_to(mine_log + got_log, (META if last else PAD, STRIP))


def up(level, chips, half, strips, head_size, mine, send, got):
    size = mine.shape[0]
    last = 2 << level == chips
    out_specs, out_shape = halves(size if last else size // 2)
    if last:
        out_specs = [whole(size + META, STRIP)]
        out_shape = [jax.ShapeDtypeStruct((size + META, STRIP), F32)]
    return pl.pallas_call(
        lambda *refs: up_kernel(
            level, last, STATE // chips, half * strips, strips, head_size, *refs
        ),
        in_specs=[whole(size, STRIP), whole(*send.shape), whole(size + PAD, STRIP)],
        out_specs=out_specs,
        out_shape=out_shape,
        compiler_params=pltpu.CompilerParams(vmem_limit_bytes=SMALL_VMEM),
        cost_estimate=LITTLE,
        name="up",
    )(mine, send, got)


def down_kernel(level, top, part, offset, strips, head_size, mine_ref, log_ref, got_ref, *refs):
    place = position()
    sources, (here_ref, there_ref) = refs[:-2], refs[-2:]
    size = mine_ref.shape[0]
    ahead = is_ahead(place, level)
    rows_of = [
        jnp.where(ahead, jnp.exp(got_ref[size : size + 1, :]), 1.0),
        jnp.where(ahead, 1.0, jnp.exp(log_ref[size : size + 1, :])),
    ]
    if top:
        passed = jnp.zeros_like(rows_of[0])
        for ref in sources:
            rows_of.append(jnp.exp(passed))
            passed = passed + ref[size : size + 1, :]
        bases, length = (0,), size
    else:
        length = size // 2
        bit = (place[1] >> (level + 1)) & 1
        bases = (bit * length, (1 - bit) * length)
    here_wide, there_wide, *group_wide = spread_rows(rows_of, offset, strips, head_size)
    for index, base in enumerate(bases):
        for strip in range(strips):
            one = slice(strip, strip + 1)
            for at in range(strip * part, length, strips * part):
                rows = slice(at, at + part)
                if top:
                    entering = sources[0][rows, :] * group_wide[0][one, :]
                    for ref, wide in zip(sources[1:], group_wide[1:]):
                        entering = entering + ref[rows, :] * wide[one, :]
                else:
                    entering = sources[index][rows, :]
                    rows = pl.ds(pl.multiple_of(base + at, part), part)
                got = jnp.where(ahead, got_ref[rows, :], 0.0)
                mine = jnp.where(ahead, 0.0, mine_ref[rows, :])
                here_ref[rows, :] = entering * here_wide[one, :] + got
                there_ref[rows, :] = entering * there_wide[one, :] + mine
    there_ref[size:, :] = jnp.zeros((PAD, STRIP), F32)


def down(level, chips, half, strips, head_size, mine, send, got, sources):
    size = mine.shape[0]
    top = 2 << level == chips
    return pl.pallas_call(
        lambda *refs: down_kernel(
            level, top, STATE // chips, half * strips, strips, head_size, *refs
        ),
        in_specs=[whole(size, STRIP), whole(*send.shape), whole(size + PAD, STRIP)]
        + [whole(*value.shape) for value in sources],
        out_specs=[whole(size, STRIP), whole(size + PAD, STRIP)],
        out_shape=[
            jax.ShapeDtypeStruct((size, STRIP), F32),
            jax.ShapeDtypeStruct((size + PAD, STRIP), F32),
        ],
        compiler_params=pltpu.CompilerParams(vmem_limit_bytes=SMALL_VMEM),
        cost_estimate=LITTLE,
        name="down",
    )(mine, send, got, *sources)


def intra_kernel(
    heads, head_size, start, last,
    after_ref, x_ref, g_ref, write_ref, read_ref, rates_ref, column_ref, tail_ref, lead_ref, *refs,
):
    dx_ref, state_ref, back_ref, change_ref, *sums, row_ref, scores_ref, mask_ref, pairs_ref, \
        write_t, read_t = refs[5 if start else 0 :]
    step = pl.program_id(0)
    chunk = start + step
    lanes = x_ref.shape[1]
    per_chunk = lanes // head_size

    @pl.when(step == 0)
    def _():
        rates = rates_ref[...]
        triangle = lower(STRETCH)
        row_ref[...] = dot(rates, triangle, 1, 1, HIGHEST)
        mask_ref[...] = triangle
        scores_ref[...] = dot(read_ref[...], write_ref[...], 1, 1)
        pairs_ref[...] = refs[4][...] if start else jnp.zeros_like(pairs_ref)
        change_ref[...] = refs[3][...] if start else jnp.zeros_like(change_ref)
        write_t[...] = write_ref[...].astype(F32).T.astype(BF16)
        read_t[...] = read_ref[...].astype(F32).T.astype(BF16)

    columns = pltpu.roll(column_ref[...], STATE - chunk * per_chunk, 1)
    rows = row_ref[pl.ds(pl.multiple_of(chunk * per_chunk, per_chunk), per_chunk), :]
    causal = mask_ref[...] > 0.5
    scores = scores_ref[...]
    pairs = pairs_ref[...]
    low_half = iota((STRETCH, 2 * head_size), 1) < head_size
    adder = head_adder(chunk, head_size, lanes)
    spread = spreader(chunk, heads, head_size, lanes)
    high, low = term_pair(x_ref[...].astype(F32) * dot(tail_ref[...], spread, 1, 0))
    state_ref[...] = dot(write_t[...], high, 1, 0) + dot(write_t[...], low, 1, 0)
    high, low = term_pair(g_ref[...].astype(F32) * dot(lead_ref[...], spread, 1, 0))
    back_ref[...] = dot(read_t[...], high, 1, 0) + dot(read_t[...], low, 1, 0)
    for pair in range(per_chunk // 2):
        strip = slice(pair * 2 * head_size, (pair + 1) * 2 * head_size)
        x = x_ref[:, strip]
        g = g_ref[:, strip]
        ys, dxs = [], []
        for half in range(2):
            head = 2 * pair + half
            gap = columns[:, head : head + 1] - rows[head : head + 1, :]
            decay = jnp.where(causal, jnp.exp(gap), 0.0)
            mixing = (scores * decay).astype(BF16)
            ys.append(dot(mixing, x, 1, 0))
            dxs.append(dot(mixing, g, 0, 0))
            mine = low_half if half == 0 else jnp.logical_not(low_half)
            pairs = pairs + dot(jnp.where(mine, g, jnp.zeros_like(g)), x, 1, 1) * decay
        y = jnp.where(low_half, ys[0], ys[1])
        dx = jnp.where(low_half, dxs[0], dxs[1])
        dx_ref[:, strip] = dx
        change_ref[...] += head_sums(
            g.astype(F32) * y - x.astype(F32) * dx, adder[strip, :]
        )
    pairs_ref[...] = pairs

    @pl.when(step == pl.num_programs(0) - 1)
    def _():
        if last:
            summed = pairs_ref[...].astype(BF16)
            sums[0][...] = dot(summed, read_ref[...], 0, 0)
            sums[1][...] = dot(summed, write_ref[...], 1, 0)
        else:
            sums[0][...] = pairs_ref[...]


def intra(start, steps, after, x, g, write_map, read_map, rates, shared, earlier):
    tokens, wide = x.shape
    heads = rates.shape[0]
    last = (start + steps) * LANES == wide
    lanes = lambda rows: pl.BlockSpec((rows, LANES), lambda c: (0, start + c))
    anywhere = pl.BlockSpec(memory_space=pl.ANY)
    sums = [(tokens, STATE)] * 2 if last else [(tokens, tokens)]
    return pl.pallas_call(
        lambda *refs: intra_kernel(heads, wide // heads, start, last, *refs),
        grid=(steps,),
        in_specs=[
            whole(META, STRIP),
            lanes(tokens),
            lanes(tokens),
            whole(tokens, STATE),
            whole(tokens, STATE),
            whole(heads, tokens),
        ]
        + [whole(tokens, STRIP)] * 3
        + ([anywhere] * 3 + [whole(tokens, STATE), whole(tokens, tokens)] if earlier else []),
        out_specs=[lanes(tokens), lanes(STATE), lanes(STATE), whole(tokens, STATE)]
        + [whole(*shape) for shape in sums],
        out_shape=[
            jax.ShapeDtypeStruct((tokens, wide), F32),
            jax.ShapeDtypeStruct((STATE, wide), F32),
            jax.ShapeDtypeStruct((STATE, wide), F32),
            jax.ShapeDtypeStruct((tokens, STATE), F32),
        ]
        + [jax.ShapeDtypeStruct(shape, F32) for shape in sums],
        scratch_shapes=[
            pltpu.VMEM((heads, tokens), F32),
            pltpu.VMEM((tokens, tokens), F32),
            pltpu.VMEM((tokens, tokens), F32),
            pltpu.VMEM((tokens, tokens), F32),
            pltpu.VMEM((STATE, tokens), BF16),
            pltpu.VMEM((STATE, tokens), BF16),
        ],
        input_output_aliases={9: 0, 10: 1, 11: 2} if earlier else {},
        compiler_params=pltpu.CompilerParams(vmem_limit_bytes=SMALL_VMEM),
        cost_estimate=LITTLE,
        name="intra",
    )(after, x, g, write_map, read_map, rates, *shared[1:], *earlier)


def order_kernel(here_ref, got_ref, low_ref, high_ref):
    place = position()
    bit = place[1] & 1
    here, got = here_ref[...], got_ref[: here_ref.shape[0], :]
    low_ref[...] = jnp.where(bit == 0, here, got)
    high_ref[...] = jnp.where(bit == 0, got, here)


def order(here, got):
    return pl.pallas_call(
        order_kernel,
        in_specs=[whole(*here.shape), whole(*got.shape)],
        out_specs=[whole(*here.shape)] * 2,
        out_shape=[jax.ShapeDtypeStruct(here.shape, F32)] * 2,
        compiler_params=pltpu.CompilerParams(vmem_limit_bytes=SMALL_VMEM),
        cost_estimate=LITTLE,
        name="order",
    )(here, got)


def assemble_kernel(
    heads, chips, half, head_size, ordered,
    after_ref, first_ref, state_own, back_own, *refs,
):
    place = position()
    own_refs, far_refs, (state_ref, back_ref, total_ref) = refs[:2], refs[2:4], refs[4:]
    bit = 0 if ordered else place[1] & 1
    lanes = state_ref.shape[1]
    strips = lanes // STRIP
    part = STATE // chips
    size = strips * part
    log = first_ref[chips * size : chips * size + 1, :]
    decay = spread_rows([jnp.exp(log)], half * strips, strips, head_size)[0]
    is_first = place[0] == 0
    sums = [None] * strips
    for quarter in range(chips):
        rows = slice(quarter * part, (quarter + 1) * part)
        for strip in range(strips):
            wide = slice(strip * STRIP, (strip + 1) * STRIP)
            here = slice(quarter * size + strip * part, quarter * size + (strip + 1) * part)
            piece, at = divmod(here.start, chips // 2 * size)
            there = slice(at, at + part)
            own, far = own_refs[piece][there, :], far_refs[piece][there, :]
            if not ordered:
                own = jnp.where(bit == 0, own, own_refs[1 - piece][there, :])
                far = jnp.where(bit == 0, far, far_refs[1 - piece][there, :])
            own = own * decay[strip : strip + 1, :] + first_ref[here, :]
            state = jnp.where(is_first, far, own).astype(BF16)
            back = jnp.where(is_first, own, far).astype(BF16)
            state_ref[rows, wide] = state
            back_ref[rows, wide] = back
            gain = state.astype(F32) * back_own[rows, wide]
            gain = gain - back.astype(F32) * state_own[rows, wide]
            sums[strip] = gain if sums[strip] is None else sums[strip] + gain
    row_sum = [
        jnp.broadcast_to(jnp.sum(value, axis=0, keepdims=True), (META, STRIP)) for value in sums
    ]
    total = head_sums(jnp.concatenate(row_sum, axis=1), head_adder(half, head_size, lanes))
    total_ref[...] = total + after_ref[...] if half else total


def assemble(heads, chips, half, ordered, after, first, state_own, back_own, own, far):
    wide = state_own.shape[1]
    lanes = wide // HALVES
    mine = pl.BlockSpec((STATE, lanes), lambda c: (0, half))
    return pl.pallas_call(
        lambda *refs: assemble_kernel(heads, chips, half, wide // heads, ordered, *refs),
        grid=(1,),
        in_specs=[whole(META, STRIP), whole(*first.shape), mine, mine]
        + [whole(*value.shape) for value in (*own, *far)],
        out_specs=[whole(STATE, lanes), whole(STATE, lanes), whole(META, STRIP)],
        out_shape=[
            jax.ShapeDtypeStruct((STATE, lanes), BF16),
            jax.ShapeDtypeStruct((STATE, lanes), BF16),
            jax.ShapeDtypeStruct((META, STRIP), F32),
        ],
        compiler_params=pltpu.CompilerParams(vmem_limit_bytes=SMALL_VMEM),
        cost_estimate=LITTLE,
        name="assemble",
    )(after, first, state_own, back_own, *own, *far)


def finish_kernel(
    heads, start, steps, last, x_ref, g_ref, write_ref, read_ref, tail_ref, lead_ref,
    dx_ref, db_ref, dc_ref, change_ref, state_ref, back_ref, *refs,
):
    grad_ref, db_out, dc_out, change_out, token_ref, db_sum, dc_sum, sum_out = refs[-8:]
    chunk = pl.program_id(0)
    lanes = x_ref.shape[1]
    head_size = lanes * STEPS * HALVES // heads
    wide = start + chunk

    @pl.when(chunk == 0)
    def _():
        sum_out[...] = change_ref[...]
        db_sum[...] = db_ref[...]
        dc_sum[...] = dc_ref[...]

    state = state_ref[...]
    back = back_ref[...]
    spread = spreader(wide, heads, head_size, lanes)
    tail = dot(tail_ref[...], spread, 1, 0)
    lead = dot(lead_ref[...], spread, 1, 0)
    x = x_ref[...].astype(F32)
    g = g_ref[...].astype(F32)
    y = dot(read_ref[...], state, 1, 0) * lead
    dx = dot(write_ref[...], back, 1, 0) * tail
    grad_ref[...] = (dx_ref[...] + dx).astype(BF16)
    adder = head_adder(wide, head_size, lanes)
    sum_out[...] += head_sums(g * y - x * dx, adder)
    db_sum[...] += dot((x * tail).astype(BF16), back, 1, 1)
    dc_sum[...] += dot((g * lead).astype(BF16), state, 1, 1)

    @pl.when(chunk == steps - 1)
    def _():
        token_ref[...] = refs[-9][...]
        db_out[...] = db_sum[...].astype(db_out.dtype)
        dc_out[...] = dc_sum[...].astype(dc_out.dtype)
        if last:
            change_out[...] = dot(sum_out[...], lower(STRETCH), 0, 0, HIGHEST)[:heads, :]
        else:
            change_out[...] = sum_out[...]


def finish(heads, start, steps, after, x, g, write_map, read_map, shared, dx, sums, state, back, grad):
    tokens, wide = x.shape
    lanes = wide // (STEPS * HALVES)
    strip = pl.BlockSpec((tokens, lanes), lambda c: (0, start + c))
    own = pl.BlockSpec((STATE, lanes), lambda c: (0, start % STEPS + c))
    last = start + steps == STEPS * HALVES
    kind = BF16 if last else F32
    change = (heads, tokens) if last else (tokens, STATE)
    earlier = [] if grad is None else [grad]
    return pl.pallas_call(
        lambda *refs: finish_kernel(heads, start, steps, last, *refs),
        grid=(steps,),
        in_specs=[strip, strip]
        + [whole(tokens, STATE)] * 4
        + [strip]
        + [whole(tokens, STATE)] * 3
        + [own, own]
        + [pl.BlockSpec(memory_space=pl.ANY)] * len(earlier)
        + [whole(META, STRIP)],
        out_specs=[strip] + [whole(tokens, STATE)] * 2 + [whole(*change), whole(META, STRIP)],
        out_shape=[
            jax.ShapeDtypeStruct((tokens, wide), BF16),
            jax.ShapeDtypeStruct((tokens, STATE), kind),
            jax.ShapeDtypeStruct((tokens, STATE), kind),
            jax.ShapeDtypeStruct(change, F32),
            jax.ShapeDtypeStruct((META, STRIP), F32),
        ],
        scratch_shapes=[pltpu.VMEM((tokens, STATE), F32)] * 3,
        input_output_aliases={12: 0} if earlier else {},
        compiler_params=pltpu.CompilerParams(vmem_limit_bytes=SMALL_VMEM),
        cost_estimate=LITTLE,
        name="finish",
    )(x, g, write_map, read_map, *shared[2:], dx, *sums, state, back, *earlier, after)


def count_kernel(after_ref, later_ref, total_ref, *refs):
    place = position()
    got_refs, (later_out, total_out) = refs[:-2], refs[-2:]
    later, total = later_ref[...], total_ref[...]
    for step, ref in enumerate(got_refs, 1):
        later = later + jnp.where((place[1] ^ step) > place[1], ref[...], 0.0)
        total = total + ref[...]
    later_out[...] = later
    total_out[...] = total


def core_kernel(total_ref, got_ref, later_out, total_out):
    place = position()
    later_out[...] = jnp.where(place[0] == 0, got_ref[...], 0.0)
    total_out[...] = total_ref[...] + got_ref[...]


def tiles(kernel, name, *values):
    return pl.pallas_call(
        kernel,
        in_specs=[whole(META, STRIP)] * len(values),
        out_specs=[whole(META, STRIP)] * 2,
        out_shape=[jax.ShapeDtypeStruct((META, STRIP), F32)] * 2,
        compiler_params=pltpu.CompilerParams(vmem_limit_bytes=SMALL_VMEM),
        cost_estimate=LITTLE,
        name=name,
    )(*values)


def add_later_kernel(suffix_ref, *refs):
    out_ref = refs[-1]
    heads = out_ref.shape[0]
    later = refs[0][...]
    for ref in refs[1:-1]:
        later = later + ref[...]
    out_ref[...] = suffix_ref[...] + later.T[:heads, 0:1]


def add_later(suffix, *parts):
    return pl.pallas_call(
        add_later_kernel,
        in_specs=[whole(*value.shape) for value in (suffix, *parts)],
        out_specs=whole(*suffix.shape),
        out_shape=jax.ShapeDtypeStruct(suffix.shape, F32),
        compiler_params=pltpu.CompilerParams(vmem_limit_bytes=SMALL_VMEM),
        cost_estimate=LITTLE,
        name="add_later",
    )(suffix, *parts)


def per_device(inputs, out_grad, input_map, output_map, log_decay):
    heads = log_decay.shape[0]
    head_size = inputs.shape[1] // heads
    groups, shards = lax.axis_size("grp"), lax.axis_size("seq")
    chips = shards // 2
    strips = inputs.shape[1] // STRIP // HALVES
    everyone = [(a, z, c) for a in range(groups) for z in range(chips) for c in range(2)]

    def move(value, target):
        pairs = []
        for a, z, c in everyone:
            to = target(a, z, c)
            if to is not None:
                pairs.append((a * shards + 2 * z + c, to[0] * shards + 2 * to[1] + to[2]))
        return lax.ppermute(value, ("grp", "seq"), pairs)

    def to_core(value):
        return move(value, lambda a, z, c: (a, z, 1 - c))

    def to_chip(value, step):
        return move(value, lambda a, z, c: (a, z ^ step, c)) if step else value

    def to_earlier(value, step):
        return move(value, lambda a, z, c: (a - step, z, c) if a >= step else None)

    def to_later(value, step):
        def target(a, z, c):
            to = a + step if c == 1 else a - step
            return (to, z, c) if 0 <= to < groups else None

        return move(value, target)

    maps = (inputs, out_grad, input_map, output_map)
    send, keep, decay, *shared = summary(chips, 0, *maps, log_decay, None)
    first = [to_core(send)]
    kept, decays = [keep], [decay]
    send, keep, decay = summary(chips, 1, *maps, log_decay, shared)
    first.append(to_core(send))
    kept.append(keep)
    decays.append(decay)

    levels = chips.bit_length() - 1
    held = [[], []]
    waiting = [None, None]

    def advance(half, step):
        fixed = (chips, half, strips, head_size)
        if step == 0:
            mine, send = combine(
                chips, first[half], kept[half], decays[half], shared[0]
            )
        elif step < levels:
            held[half][-1] += (waiting[half],)
            mine, send = up(step - 1, *fixed, *held[half][-1])
        elif step == levels:
            held[half][-1] += (waiting[half],)
            (send,) = up(step - 1, *fixed, *held[half][-1])
            waiting[half] = [to_later(send, far) for far in range(1, groups)]
            return send
        elif step <= 2 * levels:
            level = 2 * levels - step
            if level < levels - 1:
                waiting[half] = (held[half][level + 1], waiting[half])
            mine, send = down(level, *fixed, *held[half][level], waiting[half])
            held[half][level] = mine
            waiting[half] = to_chip(send, 1 << level)
            return send
        else:
            held[half] = order(held[half][0], waiting[half])
            waiting[half] = [to_core(value) for value in held[half]]
            return held[half][0]
        held[half].append((mine, send))
        waiting[half] = to_chip(send, 1 << step)
        return send

    chunks = inputs.shape[1] // LANES
    rounds = 2 * levels + 2
    block, ready = (), 0
    for step in range(rounds):
        token = advance(0, step)
        if step:
            advance(1, step - 1)
        if step < 3:
            more = pl.cdiv(chunks - ready, 3 - step)
            block = intra(ready, more, token, *maps, log_decay, shared, block)
            ready += more
            if step == 0:
                first[1], block = lax.optimization_barrier((first[1], block))
            else:
                waiting[0], waiting[1], block = lax.optimization_barrier(
                    (waiting[0], waiting[1], block)
                )
        elif levels + 1 < step < rounds - 1:
            waiting[0], waiting[1] = lax.optimization_barrier((waiting[0], waiting[1]))
    dx, state_own, back_own, change, db, dc = block
    own_b = held[1][0]
    far_b = to_core(own_b)
    state, back, counted = assemble(
        heads, chips, 0, True, change, first[0], state_own, back_own, held[0], waiting[0]
    )
    grad, *sums, counted = finish(
        heads, 0, STEPS, counted, *maps, shared, dx, (db, dc, change), state, back, None
    )
    got, far_b, counted = lax.optimization_barrier((waiting[1], far_b, counted))
    own_b, far_b = (own_b, got), (far_b, to_core(got))
    state, back, counted = assemble(
        heads, chips, 1, False, counted, first[1], state_own, back_own, own_b, far_b
    )

    later, counted = tiles(core_kernel, "core_sum", counted, to_core(counted))
    got = [to_chip(counted, step) for step in range(1, chips)]
    grad, *sums, token = finish(
        heads, STEPS, 1, counted, *maps, shared, dx, sums, state, back, grad
    )
    later, counted = tiles(count_kernel, "chip_sum", token, later, counted, *got)
    got = [to_earlier(counted, step) for step in range(1, groups)]
    grad, *sums, _ = finish(
        heads, STEPS + 1, 1, counted, *maps, shared, dx, sums, state, back, grad
    )
    return (grad, sums[0], sums[1], add_later(sums[2], later, *got))


def solution(mesh):
    tokens = P(("grp", "seq"), None)
    in_specs = (tokens, tokens, tokens, tokens, P(None, ("grp", "seq")))
    out_specs = (tokens, tokens, tokens, P(None, ("grp", "seq")))
    return jax.shard_map(
        per_device, mesh=mesh, in_specs=in_specs, out_specs=out_specs, check_vma=False
    )
```

```python
import jax
import jax.numpy as jnp
from jax import lax
from jax.experimental import pallas as pl
from jax.experimental.pallas import tpu as pltpu
from jax.sharding import PartitionSpec as P

STATE = 128
STRETCH = 256
LANES = 512
HALVES = 2
STRIP = 128
META = 8
PAD = 2 * META
BIG_VMEM = 56 << 20
SMALL_VMEM = 24 << 20
F32 = jnp.float32
BF16 = jnp.bfloat16
HIGHEST = lax.Precision.HIGHEST


def dot(left, right, left_dim, right_dim, precision=None):
    return lax.dot_general(
        left,
        right,
        (((left_dim,), (right_dim,)), ((), ())),
        precision=precision,
        preferred_element_type=F32,
    )


def iota(shape, dim):
    return lax.broadcasted_iota(jnp.int32, shape, dim)


def lower(length):
    return (iota((length, length), 0) >= iota((length, length), 1)).astype(F32)


def thrice(rates):
    heads, length = rates.shape
    spare = jnp.zeros((STATE - 3 * heads, length), F32)
    return jnp.concatenate([rates, rates, rates, spare], axis=0)


def three_terms(value, heads):
    lane = iota(value.shape, 1)
    first = value.astype(BF16)
    rest = value - first.astype(F32)
    second = rest.astype(BF16)
    third = (rest - second.astype(F32)).astype(BF16)
    return jnp.where(lane < heads, first, jnp.where(lane < 2 * heads, second, third))


def spreader(chunk, heads, head_size, lanes):
    row = iota((STATE, lanes), 0)
    head = (iota((STATE, lanes), 1) + chunk * lanes) // head_size
    hit = (row == head) | (row == head + heads) | (row == head + 2 * heads)
    return hit.astype(F32).astype(BF16)


def head_adder(chunk, head_size, lanes):
    head = (iota((lanes, STATE), 0) + chunk * lanes) // head_size
    return (iota((lanes, STATE), 1) == head).astype(F32).astype(BF16)


def head_sums(value, adder):
    first = value.astype(BF16)
    second = (value - first.astype(F32)).astype(BF16)
    return dot(first, adder, 1, 0) + dot(second, adder, 1, 0)


def decay_terms(rates, heads):
    length = rates.shape[1]
    running = dot(lower(length), thrice(rates), 1, 1, HIGHEST)
    last = running[length - 1 : length, :]
    return (
        running,
        three_terms(jnp.exp(last - running), heads),
        three_terms(jnp.exp(running), heads),
    )


def term_pair(value):
    first = value.astype(BF16)
    return first, (value - first.astype(F32)).astype(BF16)


def lane_spread(per_strip, head_size):
    head = iota((STRIP, STRIP), 0) % per_strip
    return (iota((STRIP, STRIP), 1) // head_size == head).astype(F32)


def spread_rows(rows, offset, strips, head_size):
    per_strip = STRIP // head_size
    lane = iota((strips, STRIP), 1)
    row = iota((strips, STRIP), 0) + offset
    picked = [jnp.where(lane // per_strip == row, value, 0.0) for value in rows]
    stacked = jnp.concatenate(picked, axis=0) if len(picked) > 1 else picked[0]
    wide = dot(stacked, lane_spread(per_strip, head_size), 1, 0, HIGHEST)
    return [wide[i * strips : (i + 1) * strips, :] for i in range(len(rows))]


def whole(*shape):
    return pl.BlockSpec(shape, lambda *_: (0,) * len(shape))


def lanes_of(rows):
    return pl.BlockSpec((rows, LANES), lambda c: (0, c))


def half_lanes(rows, lanes, half, steps):
    return pl.BlockSpec((rows, lanes), lambda c: (0, half * steps + c))


LITTLE = pl.CostEstimate(flops=1, bytes_accessed=1, transcendentals=0)


def position():
    shard = lax.axis_index("seq")
    return shard & 1, shard >> 1


STEPS = 2
SUMMARY_STEPS = 5


def summary_kernel(heads, chips, half, x_ref, g_ref, write_ref, read_ref, *refs):
    place = position()
    chunk = pl.program_id(0)
    lanes = x_ref.shape[1]
    strips = lanes // STRIP
    half_strips = strips * SUMMARY_STEPS
    head_size = lanes * SUMMARY_STEPS * HALVES // heads
    part = STATE // chips
    if half == 0:
        rates_ref, send_ref, keep_ref, decay_ref, log_ref, run_ref, tail_ref, lead_ref = refs[:8]
    else:
        log_ref, tail_ref, lead_ref, send_ref, keep_ref, decay_ref = refs[:6]
    write_t, read_t = refs[-2:]

    @pl.when(chunk == 0)
    def _():
        if half == 0:
            running, tail, lead = decay_terms(rates_ref[...], heads)
            run_ref[...] = running
            tail_ref[...] = tail
            lead_ref[...] = lead
            log_ref[...] = jnp.broadcast_to(running[STRETCH - 1 :, :], (META, STRIP))
        send_ref[pl.ds(half_strips * STATE, META), :] = log_ref[...]
        write_t[...] = write_ref[...].astype(F32).T.astype(BF16)
        read_t[...] = read_ref[...].astype(F32).T.astype(BF16)

    spread = spreader(half * SUMMARY_STEPS + chunk, heads, head_size, lanes)
    tail = dot(tail_ref[...], spread, 1, 0)
    lead = dot(lead_ref[...], spread, 1, 0)
    inputs_tail = (x_ref[...].astype(F32) * tail).astype(BF16)
    grads_lead = (g_ref[...].astype(F32) * lead).astype(BF16)
    state = dot(write_t[...], inputs_tail, 1, 0)
    back = dot(read_t[...], grads_lead, 1, 0)
    first = place[0] == 0
    send = jnp.where(first, state, back)
    keep = jnp.where(first, back, state)
    for strip in range(strips):
        at = chunk * strips + strip
        wide = slice(strip * STRIP, (strip + 1) * STRIP)
        decay_ref[pl.ds(at, 1), :] = lead[STRETCH - 1 :, wide]
        for quarter in range(chips):
            rows = pl.ds(pl.multiple_of((quarter * half_strips + at) * part, part), part)
            mine = slice(quarter * part, (quarter + 1) * part)
            send_ref[rows, :] = send[mine, wide]
            keep_ref[rows, :] = keep[mine, wide]


def summary(chips, half, x, g, write_map, read_map, rates, shared):
    tokens, wide = x.shape
    heads = rates.shape[0]
    lanes = wide // (SUMMARY_STEPS * HALVES)
    strips = wide // STRIP // HALVES
    terms = [
        jax.ShapeDtypeStruct((META, STRIP), F32),
        jax.ShapeDtypeStruct((tokens, STRIP), F32),
        jax.ShapeDtypeStruct((tokens, STRIP), BF16),
        jax.ShapeDtypeStruct((tokens, STRIP), BF16),
    ]
    out_shape = [
        jax.ShapeDtypeStruct((strips * STATE + META, STRIP), F32),
        jax.ShapeDtypeStruct((strips * STATE, STRIP), F32),
        jax.ShapeDtypeStruct((strips, STRIP), F32),
    ]
    if half == 0:
        extra = [rates]
        out_shape = out_shape + terms
    else:
        extra = [shared[0], shared[2], shared[3]]
    return pl.pallas_call(
        lambda *refs: summary_kernel(heads, chips, half, *refs),
        grid=(SUMMARY_STEPS,),
        in_specs=[
            half_lanes(tokens, lanes, half, SUMMARY_STEPS),
            half_lanes(tokens, lanes, half, SUMMARY_STEPS),
            whole(tokens, STATE),
            whole(tokens, STATE),
        ]
        + [whole(*value.shape) for value in extra],
        out_specs=[whole(*out.shape) for out in out_shape],
        out_shape=out_shape,
        scratch_shapes=[
            pltpu.VMEM((STATE, tokens), BF16),
            pltpu.VMEM((STATE, tokens), BF16),
        ],
        compiler_params=pltpu.CompilerParams(vmem_limit_bytes=BIG_VMEM),
        cost_estimate=LITTLE,
        name="summary",
    )(x, g, write_map, read_map, *extra)


def combine_kernel(chips, first_ref, keep_ref, decay_ref, log_ref, mine_ref, send_ref):
    place = position()
    strips = decay_ref.shape[0]
    part = STATE // chips
    size = mine_ref.shape[0]
    bit = place[1] & 1
    for base, out_ref in ((bit * size, mine_ref), ((1 - bit) * size, send_ref)):
        for strip in range(strips):
            decay = decay_ref[strip : strip + 1, :]
            for at in range(strip * part, size, strips * part):
                rows = pl.ds(pl.multiple_of(base + at, part), part)
                out_ref[at : at + part, :] = first_ref[rows, :] * decay + keep_ref[rows, :]
    meta = first_ref[2 * size :, :] + log_ref[...]
    send_ref[size : size + META, :] = meta
    send_ref[size + META :, :] = meta


def halves(size):
    return (
        [whole(size, STRIP), whole(size + PAD, STRIP)],
        [
            jax.ShapeDtypeStruct((size, STRIP), F32),
            jax.ShapeDtypeStruct((size + PAD, STRIP), F32),
        ],
    )


def combine(chips, first, keep, decay, log):
    out_specs, out_shape = halves(keep.shape[0] // 2)
    return pl.pallas_call(
        lambda *refs: combine_kernel(chips, *refs),
        in_specs=[whole(*value.shape) for value in (first, keep, decay, log)],
        out_specs=out_specs,
        out_shape=out_shape,
        compiler_params=pltpu.CompilerParams(vmem_limit_bytes=SMALL_VMEM),
        cost_estimate=LITTLE,
        name="combine",
    )(first, keep, decay, log)


def is_ahead(place, level):
    return ((place[1] >> level) & 1) == place[0]


def up_kernel(level, last, part, offset, strips, head_size, mine_ref, log_ref, got_ref, *outs):
    place = position()
    size = mine_ref.shape[0]
    ahead = is_ahead(place, level)
    mine_log, got_log = log_ref[size : size + 1, :], got_ref[size : size + 1, :]
    mine_wide, got_wide = spread_rows(
        [jnp.where(ahead, 1.0, jnp.exp(got_log)), jnp.where(ahead, jnp.exp(mine_log), 1.0)],
        offset,
        strips,
        head_size,
    )
    bit = (place[1] >> (level + 1)) & 1
    half = size if last else size // 2
    targets = ((0, outs[0]),) if last else ((bit * half, outs[0]), ((1 - bit) * half, outs[1]))
    for base, out_ref in targets:
        for strip in range(strips):
            one = slice(strip, strip + 1)
            for at in range(strip * part, half, strips * part):
                rows = slice(at, at + part)
                if not last:
                    rows = pl.ds(pl.multiple_of(base + at, part), part)
                out_ref[at : at + part, :] = (
                    mine_ref[rows, :] * mine_wide[one, :] + got_ref[rows, :] * got_wide[one, :]
                )
    outs[-1][half:, :] = jnp.broadcast_to(mine_log + got_log, (META if last else PAD, STRIP))


def up(level, chips, half, strips, head_size, mine, send, got):
    size = mine.shape[0]
    last = 2 << level == chips
    out_specs, out_shape = halves(size if last else size // 2)
    if last:
        out_specs = [whole(size + META, STRIP)]
        out_shape = [jax.ShapeDtypeStruct((size + META, STRIP), F32)]
    return pl.pallas_call(
        lambda *refs: up_kernel(
            level, last, STATE // chips, half * strips, strips, head_size, *refs
        ),
        in_specs=[whole(size, STRIP), whole(*send.shape), whole(size + PAD, STRIP)],
        out_specs=out_specs,
        out_shape=out_shape,
        compiler_params=pltpu.CompilerParams(vmem_limit_bytes=SMALL_VMEM),
        cost_estimate=LITTLE,
        name="up",
    )(mine, send, got)


def down_kernel(level, top, part, offset, strips, head_size, mine_ref, log_ref, got_ref, *refs):
    place = position()
    sources, (here_ref, there_ref) = refs[:-2], refs[-2:]
    size = mine_ref.shape[0]
    ahead = is_ahead(place, level)
    rows_of = [
        jnp.where(ahead, jnp.exp(got_ref[size : size + 1, :]), 1.0),
        jnp.where(ahead, 1.0, jnp.exp(log_ref[size : size + 1, :])),
    ]
    if top:
        passed = jnp.zeros_like(rows_of[0])
        for ref in sources:
            rows_of.append(jnp.exp(passed))
            passed = passed + ref[size : size + 1, :]
        bases, length = (0,), size
    else:
        length = size // 2
        bit = (place[1] >> (level + 1)) & 1
        bases = (bit * length, (1 - bit) * length)
    here_wide, there_wide, *group_wide = spread_rows(rows_of, offset, strips, head_size)
    for index, base in enumerate(bases):
        for strip in range(strips):
            one = slice(strip, strip + 1)
            for at in range(strip * part, length, strips * part):
                rows = slice(at, at + part)
                if top:
                    entering = sources[0][rows, :] * group_wide[0][one, :]
                    for ref, wide in zip(sources[1:], group_wide[1:]):
                        entering = entering + ref[rows, :] * wide[one, :]
                else:
                    entering = sources[index][rows, :]
                    rows = pl.ds(pl.multiple_of(base + at, part), part)
                got = jnp.where(ahead, got_ref[rows, :], 0.0)
                mine = jnp.where(ahead, 0.0, mine_ref[rows, :])
                here_ref[rows, :] = entering * here_wide[one, :] + got
                there_ref[rows, :] = entering * there_wide[one, :] + mine
    there_ref[size:, :] = jnp.zeros((PAD, STRIP), F32)


def down(level, chips, half, strips, head_size, mine, send, got, sources):
    size = mine.shape[0]
    top = 2 << level == chips
    return pl.pallas_call(
        lambda *refs: down_kernel(
            level, top, STATE // chips, half * strips, strips, head_size, *refs
        ),
        in_specs=[whole(size, STRIP), whole(*send.shape), whole(size + PAD, STRIP)]
        + [whole(*value.shape) for value in sources],
        out_specs=[whole(size, STRIP), whole(size + PAD, STRIP)],
        out_shape=[
            jax.ShapeDtypeStruct((size, STRIP), F32),
            jax.ShapeDtypeStruct((size + PAD, STRIP), F32),
        ],
        compiler_params=pltpu.CompilerParams(vmem_limit_bytes=SMALL_VMEM),
        cost_estimate=LITTLE,
        name="down",
    )(mine, send, got, *sources)


def intra_kernel(
    heads, head_size, start, last,
    after_ref, x_ref, g_ref, write_ref, read_ref, rates_ref, column_ref, tail_ref, lead_ref, *refs,
):
    dx_ref, state_ref, back_ref, change_ref, *sums, row_ref, scores_ref, mask_ref, pairs_ref, \
        write_t, read_t = refs[5 if start else 0 :]
    step = pl.program_id(0)
    chunk = start + step
    lanes = x_ref.shape[1]
    per_chunk = lanes // head_size

    @pl.when(step == 0)
    def _():
        rates = rates_ref[...]
        triangle = lower(STRETCH)
        row_ref[...] = dot(rates, triangle, 1, 1, HIGHEST)
        mask_ref[...] = triangle
        scores_ref[...] = dot(read_ref[...], write_ref[...], 1, 1)
        pairs_ref[...] = refs[4][...] if start else jnp.zeros_like(pairs_ref)
        change_ref[...] = refs[3][...] if start else jnp.zeros_like(change_ref)
        write_t[...] = write_ref[...].astype(F32).T.astype(BF16)
        read_t[...] = read_ref[...].astype(F32).T.astype(BF16)

    columns = pltpu.roll(column_ref[...], STATE - chunk * per_chunk, 1)
    rows = row_ref[pl.ds(pl.multiple_of(chunk * per_chunk, per_chunk), per_chunk), :]
    causal = mask_ref[...] > 0.5
    scores = scores_ref[...]
    pairs = pairs_ref[...]
    low_half = iota((STRETCH, 2 * head_size), 1) < head_size
    adder = head_adder(chunk, head_size, lanes)
    spread = spreader(chunk, heads, head_size, lanes)
    high, low = term_pair(x_ref[...].astype(F32) * dot(tail_ref[...], spread, 1, 0))
    state_ref[...] = dot(write_t[...], high, 1, 0) + dot(write_t[...], low, 1, 0)
    high, low = term_pair(g_ref[...].astype(F32) * dot(lead_ref[...], spread, 1, 0))
    back_ref[...] = dot(read_t[...], high, 1, 0) + dot(read_t[...], low, 1, 0)
    for pair in range(per_chunk // 2):
        strip = slice(pair * 2 * head_size, (pair + 1) * 2 * head_size)
        x = x_ref[:, strip]
        g = g_ref[:, strip]
        ys, dxs = [], []
        for half in range(2):
            head = 2 * pair + half
            gap = columns[:, head : head + 1] - rows[head : head + 1, :]
            decay = jnp.where(causal, jnp.exp(gap), 0.0)
            mixing = (scores * decay).astype(BF16)
            ys.append(dot(mixing, x, 1, 0))
            dxs.append(dot(mixing, g, 0, 0))
            mine = low_half if half == 0 else jnp.logical_not(low_half)
            pairs = pairs + dot(jnp.where(mine, g, jnp.zeros_like(g)), x, 1, 1) * decay
        y = jnp.where(low_half, ys[0], ys[1])
        dx = jnp.where(low_half, dxs[0], dxs[1])
        dx_ref[:, strip] = dx
        change_ref[...] += head_sums(
            g.astype(F32) * y - x.astype(F32) * dx, adder[strip, :]
        )
    pairs_ref[...] = pairs

    @pl.when(step == pl.num_programs(0) - 1)
    def _():
        if last:
            summed = pairs_ref[...].astype(BF16)
            sums[0][...] = dot(summed, read_ref[...], 0, 0)
            sums[1][...] = dot(summed, write_ref[...], 1, 0)
        else:
            sums[0][...] = pairs_ref[...]


def intra(start, steps, after, x, g, write_map, read_map, rates, shared, earlier):
    tokens, wide = x.shape
    heads = rates.shape[0]
    last = (start + steps) * LANES == wide
    lanes = lambda rows: pl.BlockSpec((rows, LANES), lambda c: (0, start + c))
    anywhere = pl.BlockSpec(memory_space=pl.ANY)
    sums = [(tokens, STATE)] * 2 if last else [(tokens, tokens)]
    return pl.pallas_call(
        lambda *refs: intra_kernel(heads, wide // heads, start, last, *refs),
        grid=(steps,),
        in_specs=[
            whole(META, STRIP),
            lanes(tokens),
            lanes(tokens),
            whole(tokens, STATE),
            whole(tokens, STATE),
            whole(heads, tokens),
        ]
        + [whole(tokens, STRIP)] * 3
        + ([anywhere] * 3 + [whole(tokens, STATE), whole(tokens, tokens)] if earlier else []),
        out_specs=[lanes(tokens), lanes(STATE), lanes(STATE), whole(tokens, STATE)]
        + [whole(*shape) for shape in sums],
        out_shape=[
            jax.ShapeDtypeStruct((tokens, wide), F32),
            jax.ShapeDtypeStruct((STATE, wide), F32),
            jax.ShapeDtypeStruct((STATE, wide), F32),
            jax.ShapeDtypeStruct((tokens, STATE), F32),
        ]
        + [jax.ShapeDtypeStruct(shape, F32) for shape in sums],
        scratch_shapes=[
            pltpu.VMEM((heads, tokens), F32),
            pltpu.VMEM((tokens, tokens), F32),
            pltpu.VMEM((tokens, tokens), F32),
            pltpu.VMEM((tokens, tokens), F32),
            pltpu.VMEM((STATE, tokens), BF16),
            pltpu.VMEM((STATE, tokens), BF16),
        ],
        input_output_aliases={9: 0, 10: 1, 11: 2} if earlier else {},
        compiler_params=pltpu.CompilerParams(vmem_limit_bytes=SMALL_VMEM),
        cost_estimate=LITTLE,
        name="intra",
    )(after, x, g, write_map, read_map, rates, *shared[1:], *earlier)


def order_kernel(here_ref, got_ref, low_ref, high_ref):
    place = position()
    bit = place[1] & 1
    here, got = here_ref[...], got_ref[: here_ref.shape[0], :]
    low_ref[...] = jnp.where(bit == 0, here, got)
    high_ref[...] = jnp.where(bit == 0, got, here)


def order(here, got):
    return pl.pallas_call(
        order_kernel,
        in_specs=[whole(*here.shape), whole(*got.shape)],
        out_specs=[whole(*here.shape)] * 2,
        out_shape=[jax.ShapeDtypeStruct(here.shape, F32)] * 2,
        compiler_params=pltpu.CompilerParams(vmem_limit_bytes=SMALL_VMEM),
        cost_estimate=LITTLE,
        name="order",
    )(here, got)


def assemble_kernel(
    heads, chips, half, head_size, ordered,
    after_ref, first_ref, state_own, back_own, *refs,
):
    place = position()
    own_refs, far_refs, (state_ref, back_ref, total_ref) = refs[:2], refs[2:4], refs[4:]
    bit = 0 if ordered else place[1] & 1
    lanes = state_ref.shape[1]
    strips = lanes // STRIP
    part = STATE // chips
    size = strips * part
    log = first_ref[chips * size : chips * size + 1, :]
    decay = spread_rows([jnp.exp(log)], half * strips, strips, head_size)[0]
    is_first = place[0] == 0
    sums = [None] * strips
    for quarter in range(chips):
        rows = slice(quarter * part, (quarter + 1) * part)
        for strip in range(strips):
            wide = slice(strip * STRIP, (strip + 1) * STRIP)
            here = slice(quarter * size + strip * part, quarter * size + (strip + 1) * part)
            piece, at = divmod(here.start, chips // 2 * size)
            there = slice(at, at + part)
            own, far = own_refs[piece][there, :], far_refs[piece][there, :]
            if not ordered:
                own = jnp.where(bit == 0, own, own_refs[1 - piece][there, :])
                far = jnp.where(bit == 0, far, far_refs[1 - piece][there, :])
            own = own * decay[strip : strip + 1, :] + first_ref[here, :]
            state = jnp.where(is_first, far, own).astype(BF16)
            back = jnp.where(is_first, own, far).astype(BF16)
            state_ref[rows, wide] = state
            back_ref[rows, wide] = back
            gain = state.astype(F32) * back_own[rows, wide]
            gain = gain - back.astype(F32) * state_own[rows, wide]
            sums[strip] = gain if sums[strip] is None else sums[strip] + gain
    row_sum = [
        jnp.broadcast_to(jnp.sum(value, axis=0, keepdims=True), (META, STRIP)) for value in sums
    ]
    total = head_sums(jnp.concatenate(row_sum, axis=1), head_adder(half, head_size, lanes))
    total_ref[...] = total + after_ref[...] if half else total


def assemble(heads, chips, half, ordered, after, first, state_own, back_own, own, far):
    wide = state_own.shape[1]
    lanes = wide // HALVES
    mine = pl.BlockSpec((STATE, lanes), lambda c: (0, half))
    return pl.pallas_call(
        lambda *refs: assemble_kernel(heads, chips, half, wide // heads, ordered, *refs),
        grid=(1,),
        in_specs=[whole(META, STRIP), whole(*first.shape), mine, mine]
        + [whole(*value.shape) for value in (*own, *far)],
        out_specs=[whole(STATE, lanes), whole(STATE, lanes), whole(META, STRIP)],
        out_shape=[
            jax.ShapeDtypeStruct((STATE, lanes), BF16),
            jax.ShapeDtypeStruct((STATE, lanes), BF16),
            jax.ShapeDtypeStruct((META, STRIP), F32),
        ],
        compiler_params=pltpu.CompilerParams(vmem_limit_bytes=SMALL_VMEM),
        cost_estimate=LITTLE,
        name="assemble",
    )(after, first, state_own, back_own, *own, *far)


def finish_kernel(
    heads, start, steps, last, x_ref, g_ref, write_ref, read_ref, tail_ref, lead_ref,
    dx_ref, db_ref, dc_ref, change_ref, state_ref, back_ref, *refs,
):
    grad_ref, db_out, dc_out, change_out, token_ref, db_sum, dc_sum, sum_out = refs[-8:]
    chunk = pl.program_id(0)
    lanes = x_ref.shape[1]
    head_size = lanes * STEPS * HALVES // heads
    wide = start + chunk

    @pl.when(chunk == 0)
    def _():
        sum_out[...] = change_ref[...]
        db_sum[...] = db_ref[...]
        dc_sum[...] = dc_ref[...]

    state = state_ref[...]
    back = back_ref[...]
    spread = spreader(wide, heads, head_size, lanes)
    tail = dot(tail_ref[...], spread, 1, 0)
    lead = dot(lead_ref[...], spread, 1, 0)
    x = x_ref[...].astype(F32)
    g = g_ref[...].astype(F32)
    y = dot(read_ref[...], state, 1, 0) * lead
    dx = dot(write_ref[...], back, 1, 0) * tail
    grad_ref[...] = (dx_ref[...] + dx).astype(BF16)
    adder = head_adder(wide, head_size, lanes)
    sum_out[...] += head_sums(g * y - x * dx, adder)
    db_sum[...] += dot((x * tail).astype(BF16), back, 1, 1)
    dc_sum[...] += dot((g * lead).astype(BF16), state, 1, 1)

    @pl.when(chunk == steps - 1)
    def _():
        token_ref[...] = refs[-9][...]
        db_out[...] = db_sum[...].astype(db_out.dtype)
        dc_out[...] = dc_sum[...].astype(dc_out.dtype)
        if last:
            change_out[...] = dot(sum_out[...], lower(STRETCH), 0, 0, HIGHEST)[:heads, :]
        else:
            change_out[...] = sum_out[...]


def finish(heads, start, steps, after, x, g, write_map, read_map, shared, dx, sums, state, back, grad):
    tokens, wide = x.shape
    lanes = wide // (STEPS * HALVES)
    strip = pl.BlockSpec((tokens, lanes), lambda c: (0, start + c))
    own = pl.BlockSpec((STATE, lanes), lambda c: (0, start % STEPS + c))
    last = start + steps == STEPS * HALVES
    kind = BF16 if last else F32
    change = (heads, tokens) if last else (tokens, STATE)
    earlier = [] if grad is None else [grad]
    return pl.pallas_call(
        lambda *refs: finish_kernel(heads, start, steps, last, *refs),
        grid=(steps,),
        in_specs=[strip, strip]
        + [whole(tokens, STATE)] * 4
        + [strip]
        + [whole(tokens, STATE)] * 3
        + [own, own]
        + [pl.BlockSpec(memory_space=pl.ANY)] * len(earlier)
        + [whole(META, STRIP)],
        out_specs=[strip] + [whole(tokens, STATE)] * 2 + [whole(*change), whole(META, STRIP)],
        out_shape=[
            jax.ShapeDtypeStruct((tokens, wide), BF16),
            jax.ShapeDtypeStruct((tokens, STATE), kind),
            jax.ShapeDtypeStruct((tokens, STATE), kind),
            jax.ShapeDtypeStruct(change, F32),
            jax.ShapeDtypeStruct((META, STRIP), F32),
        ],
        scratch_shapes=[pltpu.VMEM((tokens, STATE), F32)] * 3,
        input_output_aliases={12: 0} if earlier else {},
        compiler_params=pltpu.CompilerParams(vmem_limit_bytes=SMALL_VMEM),
        cost_estimate=LITTLE,
        name="finish",
    )(x, g, write_map, read_map, *shared[2:], dx, *sums, state, back, *earlier, after)


def count_kernel(after_ref, later_ref, total_ref, *refs):
    place = position()
    got_refs, (later_out, total_out) = refs[:-2], refs[-2:]
    later, total = later_ref[...], total_ref[...]
    for step, ref in enumerate(got_refs, 1):
        later = later + jnp.where((place[1] ^ step) > place[1], ref[...], 0.0)
        total = total + ref[...]
    later_out[...] = later
    total_out[...] = total


def core_kernel(total_ref, got_ref, later_out, total_out):
    place = position()
    later_out[...] = jnp.where(place[0] == 0, got_ref[...], 0.0)
    total_out[...] = total_ref[...] + got_ref[...]


def tiles(kernel, name, *values):
    return pl.pallas_call(
        kernel,
        in_specs=[whole(META, STRIP)] * len(values),
        out_specs=[whole(META, STRIP)] * 2,
        out_shape=[jax.ShapeDtypeStruct((META, STRIP), F32)] * 2,
        compiler_params=pltpu.CompilerParams(vmem_limit_bytes=SMALL_VMEM),
        cost_estimate=LITTLE,
        name=name,
    )(*values)


def add_later_kernel(suffix_ref, *refs):
    out_ref = refs[-1]
    heads = out_ref.shape[0]
    later = refs[0][...]
    for ref in refs[1:-1]:
        later = later + ref[...]
    out_ref[...] = suffix_ref[...] + later.T[:heads, 0:1]


def add_later(suffix, *parts):
    return pl.pallas_call(
        add_later_kernel,
        in_specs=[whole(*value.shape) for value in (suffix, *parts)],
        out_specs=whole(*suffix.shape),
        out_shape=jax.ShapeDtypeStruct(suffix.shape, F32),
        compiler_params=pltpu.CompilerParams(vmem_limit_bytes=SMALL_VMEM),
        cost_estimate=LITTLE,
        name="add_later",
    )(suffix, *parts)


def per_device(inputs, out_grad, input_map, output_map, log_decay):
    heads = log_decay.shape[0]
    head_size = inputs.shape[1] // heads
    groups, shards = lax.axis_size("grp"), lax.axis_size("seq")
    chips = shards // 2
    strips = inputs.shape[1] // STRIP // HALVES
    everyone = [(a, z, c) for a in range(groups) for z in range(chips) for c in range(2)]

    def move(value, target):
        pairs = []
        for a, z, c in everyone:
            to = target(a, z, c)
            if to is not None:
                pairs.append((a * shards + 2 * z + c, to[0] * shards + 2 * to[1] + to[2]))
        return lax.ppermute(value, ("grp", "seq"), pairs)

    def to_core(value):
        return move(value, lambda a, z, c: (a, z, 1 - c))

    def to_chip(value, step):
        return move(value, lambda a, z, c: (a, z ^ step, c)) if step else value

    def to_earlier(value, step):
        return move(value, lambda a, z, c: (a - step, z, c) if a >= step else None)

    def to_later(value, step):
        def target(a, z, c):
            to = a + step if c == 1 else a - step
            return (to, z, c) if 0 <= to < groups else None

        return move(value, target)

    maps = (inputs, out_grad, input_map, output_map)
    send, keep, decay, *shared = summary(chips, 0, *maps, log_decay, None)
    first = [to_core(send)]
    kept, decays = [keep], [decay]
    send, keep, decay = summary(chips, 1, *maps, log_decay, shared)
    first.append(to_core(send))
    kept.append(keep)
    decays.append(decay)

    levels = chips.bit_length() - 1
    held = [[], []]
    waiting = [None, None]

    def advance(half, step):
        fixed = (chips, half, strips, head_size)
        if step == 0:
            mine, send = combine(
                chips, first[half], kept[half], decays[half], shared[0]
            )
        elif step < levels:
            held[half][-1] += (waiting[half],)
            mine, send = up(step - 1, *fixed, *held[half][-1])
        elif step == levels:
            held[half][-1] += (waiting[half],)
            (send,) = up(step - 1, *fixed, *held[half][-1])
            waiting[half] = [to_later(send, far) for far in range(1, groups)]
            return send
        elif step <= 2 * levels:
            level = 2 * levels - step
            if level < levels - 1:
                waiting[half] = (held[half][level + 1], waiting[half])
            mine, send = down(level, *fixed, *held[half][level], waiting[half])
            held[half][level] = mine
            waiting[half] = to_chip(send, 1 << level)
            return send
        else:
            held[half] = order(held[half][0], waiting[half])
            waiting[half] = [to_core(value) for value in held[half]]
            return held[half][0]
        held[half].append((mine, send))
        waiting[half] = to_chip(send, 1 << step)
        return send

    chunks = inputs.shape[1] // LANES
    rounds = 2 * levels + 2
    block, ready = (), 0
    for step in range(rounds):
        token = advance(0, step)
        if step:
            advance(1, step - 1)
        if step < 3:
            more = pl.cdiv(chunks - ready, 3 - step)
            block = intra(ready, more, token, *maps, log_decay, shared, block)
            ready += more
            waiting[0], waiting[1], first[1], block = lax.optimization_barrier(
                (waiting[0], waiting[1], first[1], block)
            )
        elif levels + 1 < step < rounds - 1:
            waiting[0], waiting[1] = lax.optimization_barrier((waiting[0], waiting[1]))
    dx, state_own, back_own, change, db, dc = block
    own_b = held[1][0]
    far_b = to_core(own_b)
    state, back, counted = assemble(
        heads, chips, 0, True, change, first[0], state_own, back_own, held[0], waiting[0]
    )
    grad, *sums, counted = finish(
        heads, 0, STEPS, counted, *maps, shared, dx, (db, dc, change), state, back, None
    )
    got, far_b, counted = lax.optimization_barrier((waiting[1], far_b, counted))
    own_b, far_b = (own_b, got), (far_b, to_core(got))
    state, back, counted = assemble(
        heads, chips, 1, False, counted, first[1], state_own, back_own, own_b, far_b
    )

    later, counted = tiles(core_kernel, "core_sum", counted, to_core(counted))
    got = [to_chip(counted, step) for step in range(1, chips)]
    grad, *sums, token = finish(
        heads, STEPS, 1, counted, *maps, shared, dx, sums, state, back, grad
    )
    later, counted = tiles(count_kernel, "chip_sum", token, later, counted, *got)
    got = [to_earlier(counted, step) for step in range(1, groups)]
    grad, *sums, _ = finish(
        heads, STEPS + 1, 1, counted, *maps, shared, dx, sums, state, back, grad
    )
    return (grad, sums[0], sums[1], add_later(sums[2], later, *got))


def solution(mesh):
    tokens = P(("grp", "seq"), None)
    in_specs = (tokens, tokens, tokens, tokens, P(None, ("grp", "seq")))
    out_specs = (tokens, tokens, tokens, P(None, ("grp", "seq")))
    return jax.shard_map(
        per_device, mesh=mesh, in_specs=in_specs, out_specs=out_specs, check_vma=False
    )
```

```python
import jax
import jax.numpy as jnp
from jax import lax
from jax.experimental import pallas as pl
from jax.experimental.pallas import tpu as pltpu
from jax.sharding import PartitionSpec as P

STATE = 128
STRETCH = 256
LANES = 512
HALVES = 2
STRIP = 128
META = 8
PAD = 2 * META
BIG_VMEM = 56 << 20
SMALL_VMEM = 24 << 20
F32 = jnp.float32
BF16 = jnp.bfloat16
HIGHEST = lax.Precision.HIGHEST


def dot(left, right, left_dim, right_dim, precision=None):
    return lax.dot_general(
        left,
        right,
        (((left_dim,), (right_dim,)), ((), ())),
        precision=precision,
        preferred_element_type=F32,
    )


def iota(shape, dim):
    return lax.broadcasted_iota(jnp.int32, shape, dim)


def lower(length):
    return (iota((length, length), 0) >= iota((length, length), 1)).astype(F32)


def thrice(rates):
    heads, length = rates.shape
    spare = jnp.zeros((STATE - 3 * heads, length), F32)
    return jnp.concatenate([rates, rates, rates, spare], axis=0)


def three_terms(value, heads):
    lane = iota(value.shape, 1)
    first = value.astype(BF16)
    rest = value - first.astype(F32)
    second = rest.astype(BF16)
    third = (rest - second.astype(F32)).astype(BF16)
    return jnp.where(lane < heads, first, jnp.where(lane < 2 * heads, second, third))


def spreader(chunk, heads, head_size, lanes):
    row = iota((STATE, lanes), 0)
    head = (iota((STATE, lanes), 1) + chunk * lanes) // head_size
    hit = (row == head) | (row == head + heads) | (row == head + 2 * heads)
    return hit.astype(F32).astype(BF16)


def head_adder(chunk, head_size, lanes):
    head = (iota((lanes, STATE), 0) + chunk * lanes) // head_size
    return (iota((lanes, STATE), 1) == head).astype(F32).astype(BF16)


def head_sums(value, adder):
    first = value.astype(BF16)
    second = (value - first.astype(F32)).astype(BF16)
    return dot(first, adder, 1, 0) + dot(second, adder, 1, 0)


def decay_terms(rates, heads):
    length = rates.shape[1]
    running = dot(lower(length), thrice(rates), 1, 1, HIGHEST)
    last = running[length - 1 : length, :]
    return (
        running,
        three_terms(jnp.exp(last - running), heads),
        three_terms(jnp.exp(running), heads),
    )


def term_pair(value):
    first = value.astype(BF16)
    return first, (value - first.astype(F32)).astype(BF16)


def lane_spread(per_strip, head_size):
    head = iota((STRIP, STRIP), 0) % per_strip
    return (iota((STRIP, STRIP), 1) // head_size == head).astype(F32)


def spread_rows(rows, offset, strips, head_size):
    per_strip = STRIP // head_size
    lane = iota((strips, STRIP), 1)
    row = iota((strips, STRIP), 0) + offset
    picked = [jnp.where(lane // per_strip == row, value, 0.0) for value in rows]
    stacked = jnp.concatenate(picked, axis=0) if len(picked) > 1 else picked[0]
    wide = dot(stacked, lane_spread(per_strip, head_size), 1, 0, HIGHEST)
    return [wide[i * strips : (i + 1) * strips, :] for i in range(len(rows))]


def whole(*shape):
    return pl.BlockSpec(shape, lambda *_: (0,) * len(shape))


def lanes_of(rows):
    return pl.BlockSpec((rows, LANES), lambda c: (0, c))


def half_lanes(rows, lanes, half, steps):
    return pl.BlockSpec((rows, lanes), lambda c: (0, half * steps + c))


LITTLE = pl.CostEstimate(flops=1, bytes_accessed=1, transcendentals=0)


def position():
    shard = lax.axis_index("seq")
    return shard & 1, shard >> 1


STEPS = 2
SUMMARY_STEPS = 1


def summary_kernel(heads, chips, half, x_ref, g_ref, write_ref, read_ref, *refs):
    place = position()
    chunk = pl.program_id(0)
    lanes = x_ref.shape[1]
    strips = lanes // STRIP
    half_strips = strips * SUMMARY_STEPS
    head_size = lanes * SUMMARY_STEPS * HALVES // heads
    part = STATE // chips
    if half == 0:
        rates_ref, send_ref, keep_ref, decay_ref, log_ref, run_ref, tail_ref, lead_ref = refs[:8]
    else:
        log_ref, tail_ref, lead_ref, send_ref, keep_ref, decay_ref = refs[:6]
    write_t, read_t = refs[-2:]

    @pl.when(chunk == 0)
    def _():
        if half == 0:
            running, tail, lead = decay_terms(rates_ref[...], heads)
            run_ref[...] = running
            tail_ref[...] = tail
            lead_ref[...] = lead
            log_ref[...] = jnp.broadcast_to(running[STRETCH - 1 :, :], (META, STRIP))
        send_ref[pl.ds(half_strips * STATE, META), :] = log_ref[...]
        write_t[...] = write_ref[...].astype(F32).T.astype(BF16)
        read_t[...] = read_ref[...].astype(F32).T.astype(BF16)

    spread = spreader(half * SUMMARY_STEPS + chunk, heads, head_size, lanes)
    tail = dot(tail_ref[...], spread, 1, 0)
    lead = dot(lead_ref[...], spread, 1, 0)
    inputs_tail = (x_ref[...].astype(F32) * tail).astype(BF16)
    grads_lead = (g_ref[...].astype(F32) * lead).astype(BF16)
    state = dot(write_t[...], inputs_tail, 1, 0)
    back = dot(read_t[...], grads_lead, 1, 0)
    first = place[0] == 0
    send = jnp.where(first, state, back)
    keep = jnp.where(first, back, state)
    for strip in range(strips):
        at = chunk * strips + strip
        wide = slice(strip * STRIP, (strip + 1) * STRIP)
        decay_ref[pl.ds(at, 1), :] = lead[STRETCH - 1 :, wide]
        for quarter in range(chips):
            rows = pl.ds(pl.multiple_of((quarter * half_strips + at) * part, part), part)
            mine = slice(quarter * part, (quarter + 1) * part)
            send_ref[rows, :] = send[mine, wide]
            keep_ref[rows, :] = keep[mine, wide]


def summary(chips, half, x, g, write_map, read_map, rates, shared):
    tokens, wide = x.shape
    heads = rates.shape[0]
    lanes = wide // (SUMMARY_STEPS * HALVES)
    strips = wide // STRIP // HALVES
    terms = [
        jax.ShapeDtypeStruct((META, STRIP), F32),
        jax.ShapeDtypeStruct((tokens, STRIP), F32),
        jax.ShapeDtypeStruct((tokens, STRIP), BF16),
        jax.ShapeDtypeStruct((tokens, STRIP), BF16),
    ]
    out_shape = [
        jax.ShapeDtypeStruct((strips * STATE + META, STRIP), F32),
        jax.ShapeDtypeStruct((strips * STATE, STRIP), F32),
        jax.ShapeDtypeStruct((strips, STRIP), F32),
    ]
    if half == 0:
        extra = [rates]
        out_shape = out_shape + terms
    else:
        extra = [shared[0], shared[2], shared[3]]
    return pl.pallas_call(
        lambda *refs: summary_kernel(heads, chips, half, *refs),
        grid=(SUMMARY_STEPS,),
        in_specs=[
            half_lanes(tokens, lanes, half, SUMMARY_STEPS),
            half_lanes(tokens, lanes, half, SUMMARY_STEPS),
            whole(tokens, STATE),
            whole(tokens, STATE),
        ]
        + [whole(*value.shape) for value in extra],
        out_specs=[whole(*out.shape) for out in out_shape],
        out_shape=out_shape,
        scratch_shapes=[
            pltpu.VMEM((STATE, tokens), BF16),
            pltpu.VMEM((STATE, tokens), BF16),
        ],
        compiler_params=pltpu.CompilerParams(vmem_limit_bytes=BIG_VMEM),
        cost_estimate=LITTLE,
        name="summary",
    )(x, g, write_map, read_map, *extra)


def combine_kernel(chips, first_ref, keep_ref, decay_ref, log_ref, mine_ref, send_ref):
    place = position()
    strips = decay_ref.shape[0]
    part = STATE // chips
    size = mine_ref.shape[0]
    bit = place[1] & 1
    for base, out_ref in ((bit * size, mine_ref), ((1 - bit) * size, send_ref)):
        for strip in range(strips):
            decay = decay_ref[strip : strip + 1, :]
            for at in range(strip * part, size, strips * part):
                rows = pl.ds(pl.multiple_of(base + at, part), part)
                out_ref[at : at + part, :] = first_ref[rows, :] * decay + keep_ref[rows, :]
    meta = first_ref[2 * size :, :] + log_ref[...]
    send_ref[size : size + META, :] = meta
    send_ref[size + META :, :] = meta


def halves(size):
    return (
        [whole(size, STRIP), whole(size + PAD, STRIP)],
        [
            jax.ShapeDtypeStruct((size, STRIP), F32),
            jax.ShapeDtypeStruct((size + PAD, STRIP), F32),
        ],
    )


def combine(chips, first, keep, decay, log):
    out_specs, out_shape = halves(keep.shape[0] // 2)
    return pl.pallas_call(
        lambda *refs: combine_kernel(chips, *refs),
        in_specs=[whole(*value.shape) for value in (first, keep, decay, log)],
        out_specs=out_specs,
        out_shape=out_shape,
        compiler_params=pltpu.CompilerParams(vmem_limit_bytes=SMALL_VMEM),
        cost_estimate=LITTLE,
        name="combine",
    )(first, keep, decay, log)


def is_ahead(place, level):
    return ((place[1] >> level) & 1) == place[0]


def up_kernel(level, last, part, offset, strips, head_size, mine_ref, log_ref, got_ref, *outs):
    place = position()
    size = mine_ref.shape[0]
    ahead = is_ahead(place, level)
    mine_log, got_log = log_ref[size : size + 1, :], got_ref[size : size + 1, :]
    mine_wide, got_wide = spread_rows(
        [jnp.where(ahead, 1.0, jnp.exp(got_log)), jnp.where(ahead, jnp.exp(mine_log), 1.0)],
        offset,
        strips,
        head_size,
    )
    bit = (place[1] >> (level + 1)) & 1
    half = size if last else size // 2
    targets = ((0, outs[0]),) if last else ((bit * half, outs[0]), ((1 - bit) * half, outs[1]))
    for base, out_ref in targets:
        for strip in range(strips):
            one = slice(strip, strip + 1)
            for at in range(strip * part, half, strips * part):
                rows = slice(at, at + part)
                if not last:
                    rows = pl.ds(pl.multiple_of(base + at, part), part)
                out_ref[at : at + part, :] = (
                    mine_ref[rows, :] * mine_wide[one, :] + got_ref[rows, :] * got_wide[one, :]
                )
    outs[-1][half:, :] = jnp.broadcast_to(mine_log + got_log, (META if last else PAD, STRIP))


def up(level, chips, half, strips, head_size, mine, send, got):
    size = mine.shape[0]
    last = 2 << level == chips
    out_specs, out_shape = halves(size if last else size // 2)
    if last:
        out_specs = [whole(size + META, STRIP)]
        out_shape = [jax.ShapeDtypeStruct((size + META, STRIP), F32)]
    return pl.pallas_call(
        lambda *refs: up_kernel(
            level, last, STATE // chips, half * strips, strips, head_size, *refs
        ),
        in_specs=[whole(size, STRIP), whole(*send.shape), whole(size + PAD, STRIP)],
        out_specs=out_specs,
        out_shape=out_shape,
        compiler_params=pltpu.CompilerParams(vmem_limit_bytes=SMALL_VMEM),
        cost_estimate=LITTLE,
        name="up",
    )(mine, send, got)


def down_kernel(level, top, part, offset, strips, head_size, mine_ref, log_ref, got_ref, *refs):
    place = position()
    sources, (here_ref, there_ref) = refs[:-2], refs[-2:]
    size = mine_ref.shape[0]
    ahead = is_ahead(place, level)
    rows_of = [
        jnp.where(ahead, jnp.exp(got_ref[size : size + 1, :]), 1.0),
        jnp.where(ahead, 1.0, jnp.exp(log_ref[size : size + 1, :])),
    ]
    if top:
        passed = jnp.zeros_like(rows_of[0])
        for ref in sources:
            rows_of.append(jnp.exp(passed))
            passed = passed + ref[size : size + 1, :]
        bases, length = (0,), size
    else:
        length = size // 2
        bit = (place[1] >> (level + 1)) & 1
        bases = (bit * length, (1 - bit) * length)
    here_wide, there_wide, *group_wide = spread_rows(rows_of, offset, strips, head_size)
    for index, base in enumerate(bases):
        for strip in range(strips):
            one = slice(strip, strip + 1)
            for at in range(strip * part, length, strips * part):
                rows = slice(at, at + part)
                if top:
                    entering = sources[0][rows, :] * group_wide[0][one, :]
                    for ref, wide in zip(sources[1:], group_wide[1:]):
                        entering = entering + ref[rows, :] * wide[one, :]
                else:
                    entering = sources[index][rows, :]
                    rows = pl.ds(pl.multiple_of(base + at, part), part)
                got = jnp.where(ahead, got_ref[rows, :], 0.0)
                mine = jnp.where(ahead, 0.0, mine_ref[rows, :])
                here_ref[rows, :] = entering * here_wide[one, :] + got
                there_ref[rows, :] = entering * there_wide[one, :] + mine
    there_ref[size:, :] = jnp.zeros((PAD, STRIP), F32)


def down(level, chips, half, strips, head_size, mine, send, got, sources):
    size = mine.shape[0]
    top = 2 << level == chips
    return pl.pallas_call(
        lambda *refs: down_kernel(
            level, top, STATE // chips, half * strips, strips, head_size, *refs
        ),
        in_specs=[whole(size, STRIP), whole(*send.shape), whole(size + PAD, STRIP)]
        + [whole(*value.shape) for value in sources],
        out_specs=[whole(size, STRIP), whole(size + PAD, STRIP)],
        out_shape=[
            jax.ShapeDtypeStruct((size, STRIP), F32),
            jax.ShapeDtypeStruct((size + PAD, STRIP), F32),
        ],
        compiler_params=pltpu.CompilerParams(vmem_limit_bytes=SMALL_VMEM),
        cost_estimate=LITTLE,
        name="down",
    )(mine, send, got, *sources)


def intra_kernel(
    heads, head_size, start, last,
    after_ref, x_ref, g_ref, write_ref, read_ref, rates_ref, column_ref, tail_ref, lead_ref, *refs,
):
    dx_ref, state_ref, back_ref, change_ref, *sums, row_ref, scores_ref, mask_ref, pairs_ref, \
        write_t, read_t = refs[5 if start else 0 :]
    step = pl.program_id(0)
    chunk = start + step
    lanes = x_ref.shape[1]
    per_chunk = lanes // head_size

    @pl.when(step == 0)
    def _():
        rates = rates_ref[...]
        triangle = lower(STRETCH)
        row_ref[...] = dot(rates, triangle, 1, 1, HIGHEST)
        mask_ref[...] = triangle
        scores_ref[...] = dot(read_ref[...], write_ref[...], 1, 1)
        pairs_ref[...] = refs[4][...] if start else jnp.zeros_like(pairs_ref)
        change_ref[...] = refs[3][...] if start else jnp.zeros_like(change_ref)
        write_t[...] = write_ref[...].astype(F32).T.astype(BF16)
        read_t[...] = read_ref[...].astype(F32).T.astype(BF16)

    columns = pltpu.roll(column_ref[...], STATE - chunk * per_chunk, 1)
    rows = row_ref[pl.ds(pl.multiple_of(chunk * per_chunk, per_chunk), per_chunk), :]
    causal = mask_ref[...] > 0.5
    scores = scores_ref[...]
    pairs = pairs_ref[...]
    low_half = iota((STRETCH, 2 * head_size), 1) < head_size
    adder = head_adder(chunk, head_size, lanes)
    spread = spreader(chunk, heads, head_size, lanes)
    high, low = term_pair(x_ref[...].astype(F32) * dot(tail_ref[...], spread, 1, 0))
    state_ref[...] = dot(write_t[...], high, 1, 0) + dot(write_t[...], low, 1, 0)
    high, low = term_pair(g_ref[...].astype(F32) * dot(lead_ref[...], spread, 1, 0))
    back_ref[...] = dot(read_t[...], high, 1, 0) + dot(read_t[...], low, 1, 0)
    for pair in range(per_chunk // 2):
        strip = slice(pair * 2 * head_size, (pair + 1) * 2 * head_size)
        x = x_ref[:, strip]
        g = g_ref[:, strip]
        ys, dxs = [], []
        for half in range(2):
            head = 2 * pair + half
            gap = columns[:, head : head + 1] - rows[head : head + 1, :]
            decay = jnp.where(causal, jnp.exp(gap), 0.0)
            mixing = (scores * decay).astype(BF16)
            ys.append(dot(mixing, x, 1, 0))
            dxs.append(dot(mixing, g, 0, 0))
            mine = low_half if half == 0 else jnp.logical_not(low_half)
            pairs = pairs + dot(jnp.where(mine, g, jnp.zeros_like(g)), x, 1, 1) * decay
        y = jnp.where(low_half, ys[0], ys[1])
        dx = jnp.where(low_half, dxs[0], dxs[1])
        dx_ref[:, strip] = dx
        change_ref[...] += head_sums(
            g.astype(F32) * y - x.astype(F32) * dx, adder[strip, :]
        )
    pairs_ref[...] = pairs

    @pl.when(step == pl.num_programs(0) - 1)
    def _():
        if last:
            summed = pairs_ref[...].astype(BF16)
            sums[0][...] = dot(summed, read_ref[...], 0, 0)
            sums[1][...] = dot(summed, write_ref[...], 1, 0)
        else:
            sums[0][...] = pairs_ref[...]


def intra(start, steps, after, x, g, write_map, read_map, rates, shared, earlier):
    tokens, wide = x.shape
    heads = rates.shape[0]
    last = (start + steps) * LANES == wide
    lanes = lambda rows: pl.BlockSpec((rows, LANES), lambda c: (0, start + c))
    anywhere = pl.BlockSpec(memory_space=pl.ANY)
    sums = [(tokens, STATE)] * 2 if last else [(tokens, tokens)]
    return pl.pallas_call(
        lambda *refs: intra_kernel(heads, wide // heads, start, last, *refs),
        grid=(steps,),
        in_specs=[
            whole(META, STRIP),
            lanes(tokens),
            lanes(tokens),
            whole(tokens, STATE),
            whole(tokens, STATE),
            whole(heads, tokens),
        ]
        + [whole(tokens, STRIP)] * 3
        + ([anywhere] * 3 + [whole(tokens, STATE), whole(tokens, tokens)] if earlier else []),
        out_specs=[lanes(tokens), lanes(STATE), lanes(STATE), whole(tokens, STATE)]
        + [whole(*shape) for shape in sums],
        out_shape=[
            jax.ShapeDtypeStruct((tokens, wide), F32),
            jax.ShapeDtypeStruct((STATE, wide), F32),
            jax.ShapeDtypeStruct((STATE, wide), F32),
            jax.ShapeDtypeStruct((tokens, STATE), F32),
        ]
        + [jax.ShapeDtypeStruct(shape, F32) for shape in sums],
        scratch_shapes=[
            pltpu.VMEM((heads, tokens), F32),
            pltpu.VMEM((tokens, tokens), F32),
            pltpu.VMEM((tokens, tokens), F32),
            pltpu.VMEM((tokens, tokens), F32),
            pltpu.VMEM((STATE, tokens), BF16),
            pltpu.VMEM((STATE, tokens), BF16),
        ],
        input_output_aliases={9: 0, 10: 1, 11: 2} if earlier else {},
        compiler_params=pltpu.CompilerParams(vmem_limit_bytes=SMALL_VMEM),
        cost_estimate=LITTLE,
        name="intra",
    )(after, x, g, write_map, read_map, rates, *shared[1:], *earlier)


def order_kernel(here_ref, got_ref, low_ref, high_ref):
    place = position()
    bit = place[1] & 1
    here, got = here_ref[...], got_ref[: here_ref.shape[0], :]
    low_ref[...] = jnp.where(bit == 0, here, got)
    high_ref[...] = jnp.where(bit == 0, got, here)


def order(here, got):
    return pl.pallas_call(
        order_kernel,
        in_specs=[whole(*here.shape), whole(*got.shape)],
        out_specs=[whole(*here.shape)] * 2,
        out_shape=[jax.ShapeDtypeStruct(here.shape, F32)] * 2,
        compiler_params=pltpu.CompilerParams(vmem_limit_bytes=SMALL_VMEM),
        cost_estimate=LITTLE,
        name="order",
    )(here, got)


def assemble_kernel(
    heads, chips, half, head_size, ordered,
    after_ref, first_ref, state_own, back_own, *refs,
):
    place = position()
    own_refs, far_refs, (state_ref, back_ref, total_ref) = refs[:2], refs[2:4], refs[4:]
    bit = 0 if ordered else place[1] & 1
    lanes = state_ref.shape[1]
    strips = lanes // STRIP
    part = STATE // chips
    size = strips * part
    log = first_ref[chips * size : chips * size + 1, :]
    decay = spread_rows([jnp.exp(log)], half * strips, strips, head_size)[0]
    is_first = place[0] == 0
    sums = [None] * strips
    for quarter in range(chips):
        rows = slice(quarter * part, (quarter + 1) * part)
        for strip in range(strips):
            wide = slice(strip * STRIP, (strip + 1) * STRIP)
            here = slice(quarter * size + strip * part, quarter * size + (strip + 1) * part)
            piece, at = divmod(here.start, chips // 2 * size)
            there = slice(at, at + part)
            own, far = own_refs[piece][there, :], far_refs[piece][there, :]
            if not ordered:
                own = jnp.where(bit == 0, own, own_refs[1 - piece][there, :])
                far = jnp.where(bit == 0, far, far_refs[1 - piece][there, :])
            own = own * decay[strip : strip + 1, :] + first_ref[here, :]
            state = jnp.where(is_first, far, own).astype(BF16)
            back = jnp.where(is_first, own, far).astype(BF16)
            state_ref[rows, wide] = state
            back_ref[rows, wide] = back
            gain = state.astype(F32) * back_own[rows, wide]
            gain = gain - back.astype(F32) * state_own[rows, wide]
            sums[strip] = gain if sums[strip] is None else sums[strip] + gain
    row_sum = [
        jnp.broadcast_to(jnp.sum(value, axis=0, keepdims=True), (META, STRIP)) for value in sums
    ]
    total = head_sums(jnp.concatenate(row_sum, axis=1), head_adder(half, head_size, lanes))
    total_ref[...] = total + after_ref[...] if half else total


def assemble(heads, chips, half, ordered, after, first, state_own, back_own, own, far):
    wide = state_own.shape[1]
    lanes = wide // HALVES
    mine = pl.BlockSpec((STATE, lanes), lambda c: (0, half))
    return pl.pallas_call(
        lambda *refs: assemble_kernel(heads, chips, half, wide // heads, ordered, *refs),
        grid=(1,),
        in_specs=[whole(META, STRIP), whole(*first.shape), mine, mine]
        + [whole(*value.shape) for value in (*own, *far)],
        out_specs=[whole(STATE, lanes), whole(STATE, lanes), whole(META, STRIP)],
        out_shape=[
            jax.ShapeDtypeStruct((STATE, lanes), BF16),
            jax.ShapeDtypeStruct((STATE, lanes), BF16),
            jax.ShapeDtypeStruct((META, STRIP), F32),
        ],
        compiler_params=pltpu.CompilerParams(vmem_limit_bytes=SMALL_VMEM),
        cost_estimate=LITTLE,
        name="assemble",
    )(after, first, state_own, back_own, *own, *far)


def finish_kernel(
    heads, head_size, start, steps, last, x_ref, g_ref, write_ref, read_ref, tail_ref, lead_ref,
    dx_ref, db_ref, dc_ref, change_ref, state_ref, back_ref, *refs,
):
    grad_ref, db_out, dc_out, change_out, token_ref, db_sum, dc_sum, sum_out = refs[-8:]
    chunk = pl.program_id(0)
    lanes = x_ref.shape[1]
    wide = start + chunk

    @pl.when(chunk == 0)
    def _():
        sum_out[...] = change_ref[...]
        db_sum[...] = db_ref[...]
        dc_sum[...] = dc_ref[...]

    state = state_ref[...]
    back = back_ref[...]
    spread = spreader(wide, heads, head_size, lanes)
    tail = dot(tail_ref[...], spread, 1, 0)
    lead = dot(lead_ref[...], spread, 1, 0)
    x = x_ref[...].astype(F32)
    g = g_ref[...].astype(F32)
    y = dot(read_ref[...], state, 1, 0) * lead
    dx = dot(write_ref[...], back, 1, 0) * tail
    grad_ref[...] = (dx_ref[...] + dx).astype(BF16)
    adder = head_adder(wide, head_size, lanes)
    sum_out[...] += head_sums(g * y - x * dx, adder)
    db_sum[...] += dot((x * tail).astype(BF16), back, 1, 1)
    dc_sum[...] += dot((g * lead).astype(BF16), state, 1, 1)

    @pl.when(chunk == steps - 1)
    def _():
        token_ref[...] = refs[-9][...]
        db_out[...] = db_sum[...].astype(db_out.dtype)
        dc_out[...] = dc_sum[...].astype(dc_out.dtype)
        if last:
            change_out[...] = dot(sum_out[...], lower(STRETCH), 0, 0, HIGHEST)[:heads, :]
        else:
            change_out[...] = sum_out[...]


def finish(heads, lanes, start, steps, after, x, g, write_map, read_map, shared, dx, sums, state, back, grad):
    tokens, wide = x.shape
    strip = pl.BlockSpec((tokens, lanes), lambda c: (0, start + c))
    first = start % (wide // HALVES // lanes)
    own = pl.BlockSpec((STATE, lanes), lambda c: (0, first + c))
    last = (start + steps) * lanes == wide
    kind = BF16 if last else F32
    change = (heads, tokens) if last else (tokens, STATE)
    earlier = [] if grad is None else [grad]
    return pl.pallas_call(
        lambda *refs: finish_kernel(heads, wide // heads, start, steps, last, *refs),
        grid=(steps,),
        in_specs=[strip, strip]
        + [whole(tokens, STATE)] * 4
        + [strip]
        + [whole(tokens, STATE)] * 3
        + [own, own]
        + [pl.BlockSpec(memory_space=pl.ANY)] * len(earlier)
        + [whole(META, STRIP)],
        out_specs=[strip] + [whole(tokens, STATE)] * 2 + [whole(*change), whole(META, STRIP)],
        out_shape=[
            jax.ShapeDtypeStruct((tokens, wide), BF16),
            jax.ShapeDtypeStruct((tokens, STATE), kind),
            jax.ShapeDtypeStruct((tokens, STATE), kind),
            jax.ShapeDtypeStruct(change, F32),
            jax.ShapeDtypeStruct((META, STRIP), F32),
        ],
        scratch_shapes=[pltpu.VMEM((tokens, STATE), F32)] * 3,
        input_output_aliases={12: 0} if earlier else {},
        compiler_params=pltpu.CompilerParams(vmem_limit_bytes=SMALL_VMEM),
        cost_estimate=LITTLE,
        name="finish",
    )(x, g, write_map, read_map, *shared[2:], dx, *sums, state, back, *earlier, after)


def count_kernel(after_ref, later_ref, total_ref, *refs):
    place = position()
    got_refs, (later_out, total_out) = refs[:-2], refs[-2:]
    later, total = later_ref[...], total_ref[...]
    for step, ref in enumerate(got_refs, 1):
        later = later + jnp.where((place[1] ^ step) > place[1], ref[...], 0.0)
        total = total + ref[...]
    later_out[...] = later
    total_out[...] = total


def core_kernel(total_ref, got_ref, later_out, total_out):
    place = position()
    later_out[...] = jnp.where(place[0] == 0, got_ref[...], 0.0)
    total_out[...] = total_ref[...] + got_ref[...]


def tiles(kernel, name, *values):
    return pl.pallas_call(
        kernel,
        in_specs=[whole(META, STRIP)] * len(values),
        out_specs=[whole(META, STRIP)] * 2,
        out_shape=[jax.ShapeDtypeStruct((META, STRIP), F32)] * 2,
        compiler_params=pltpu.CompilerParams(vmem_limit_bytes=SMALL_VMEM),
        cost_estimate=LITTLE,
        name=name,
    )(*values)


def add_later_kernel(suffix_ref, *refs):
    out_ref = refs[-1]
    heads = out_ref.shape[0]
    later = refs[0][...]
    for ref in refs[1:-1]:
        later = later + ref[...]
    out_ref[...] = suffix_ref[...] + later.T[:heads, 0:1]


def add_later(suffix, *parts):
    return pl.pallas_call(
        add_later_kernel,
        in_specs=[whole(*value.shape) for value in (suffix, *parts)],
        out_specs=whole(*suffix.shape),
        out_shape=jax.ShapeDtypeStruct(suffix.shape, F32),
        compiler_params=pltpu.CompilerParams(vmem_limit_bytes=SMALL_VMEM),
        cost_estimate=LITTLE,
        name="add_later",
    )(suffix, *parts)


def per_device(inputs, out_grad, input_map, output_map, log_decay):
    heads = log_decay.shape[0]
    head_size = inputs.shape[1] // heads
    groups, shards = lax.axis_size("grp"), lax.axis_size("seq")
    chips = shards // 2
    strips = inputs.shape[1] // STRIP // HALVES
    everyone = [(a, z, c) for a in range(groups) for z in range(chips) for c in range(2)]

    def move(value, target):
        pairs = []
        for a, z, c in everyone:
            to = target(a, z, c)
            if to is not None:
                pairs.append((a * shards + 2 * z + c, to[0] * shards + 2 * to[1] + to[2]))
        return lax.ppermute(value, ("grp", "seq"), pairs)

    def to_core(value):
        return move(value, lambda a, z, c: (a, z, 1 - c))

    def to_chip(value, step):
        return move(value, lambda a, z, c: (a, z ^ step, c)) if step else value

    def to_earlier(value, step):
        return move(value, lambda a, z, c: (a - step, z, c) if a >= step else None)

    def to_later(value, step):
        def target(a, z, c):
            to = a + step if c == 1 else a - step
            return (to, z, c) if 0 <= to < groups else None

        return move(value, target)

    maps = (inputs, out_grad, input_map, output_map)
    send, keep, decay, *shared = summary(chips, 0, *maps, log_decay, None)
    first = [to_core(send)]
    kept, decays = [keep], [decay]
    send, keep, decay = summary(chips, 1, *maps, log_decay, shared)
    first.append(to_core(send))
    kept.append(keep)
    decays.append(decay)

    levels = chips.bit_length() - 1
    held = [[], []]
    waiting = [None, None]

    def advance(half, step):
        fixed = (chips, half, strips, head_size)
        if step == 0:
            mine, send = combine(
                chips, first[half], kept[half], decays[half], shared[0]
            )
        elif step < levels:
            held[half][-1] += (waiting[half],)
            mine, send = up(step - 1, *fixed, *held[half][-1])
        elif step == levels:
            held[half][-1] += (waiting[half],)
            (send,) = up(step - 1, *fixed, *held[half][-1])
            waiting[half] = [to_later(send, far) for far in range(1, groups)]
            return send
        elif step <= 2 * levels:
            level = 2 * levels - step
            if level < levels - 1:
                waiting[half] = (held[half][level + 1], waiting[half])
            mine, send = down(level, *fixed, *held[half][level], waiting[half])
            held[half][level] = mine
            waiting[half] = to_chip(send, 1 << level)
            return send
        else:
            held[half] = order(held[half][0], waiting[half])
            waiting[half] = [to_core(value) for value in held[half]]
            return held[half][0]
        held[half].append((mine, send))
        waiting[half] = to_chip(send, 1 << step)
        return send

    chunks = inputs.shape[1] // LANES
    rounds = 2 * levels + 2
    block, ready = (), 0
    for step in range(rounds):
        token = advance(0, step)
        if step:
            advance(1, step - 1)
        if step < 3:
            more = pl.cdiv(chunks - ready, 3 - step)
            block = intra(ready, more, token, *maps, log_decay, shared, block)
            ready += more
            waiting[0], waiting[1], first[1], block = lax.optimization_barrier(
                (waiting[0], waiting[1], first[1], block)
            )
        elif levels + 1 < step < rounds - 1:
            waiting[0], waiting[1] = lax.optimization_barrier((waiting[0], waiting[1]))
    dx, state_own, back_own, change, db, dc = block
    lanes = inputs.shape[1] // HALVES // STEPS
    own_b = held[1][0]
    far_b = to_core(own_b)
    state, back, counted = assemble(
        heads, chips, 0, True, change, first[0], state_own, back_own, held[0], waiting[0]
    )
    grad, *sums, counted = finish(
        heads, lanes * STEPS, 0, 1, counted, *maps, shared, dx, (db, dc, change), state, back, None
    )
    got, far_b, counted = lax.optimization_barrier((waiting[1], far_b, counted))
    own_b, far_b = (own_b, got), (far_b, to_core(got))
    state, back, counted = assemble(
        heads, chips, 1, False, counted, first[1], state_own, back_own, own_b, far_b
    )

    later, counted = tiles(core_kernel, "core_sum", counted, to_core(counted))
    got = [to_chip(counted, step) for step in range(1, chips)]
    grad, *sums, token = finish(
        heads, lanes, STEPS, 1, counted, *maps, shared, dx, sums, state, back, grad
    )
    later, counted = tiles(count_kernel, "chip_sum", token, later, counted, *got)
    got = [to_earlier(counted, step) for step in range(1, groups)]
    grad, *sums, _ = finish(
        heads, lanes, STEPS + 1, 1, counted, *maps, shared, dx, sums, state, back, grad
    )
    return (grad, sums[0], sums[1], add_later(sums[2], later, *got))


def solution(mesh):
    tokens = P(("grp", "seq"), None)
    in_specs = (tokens, tokens, tokens, tokens, P(None, ("grp", "seq")))
    out_specs = (tokens, tokens, tokens, P(None, ("grp", "seq")))
    return jax.shard_map(
        per_device, mesh=mesh, in_specs=in_specs, out_specs=out_specs, check_vma=False
    )
```

```python
import jax
import jax.numpy as jnp
from jax import lax
from jax.experimental import pallas as pl
from jax.experimental.pallas import tpu as pltpu
from jax.sharding import PartitionSpec as P

STATE = 128
STRETCH = 256
LANES = 512
HALVES = 2
STRIP = 128
META = 8
PAD = 2 * META
BIG_VMEM = 56 << 20
SMALL_VMEM = 24 << 20
F32 = jnp.float32
BF16 = jnp.bfloat16
HIGHEST = lax.Precision.HIGHEST


def dot(left, right, left_dim, right_dim, precision=None):
    return lax.dot_general(
        left,
        right,
        (((left_dim,), (right_dim,)), ((), ())),
        precision=precision,
        preferred_element_type=F32,
    )


def iota(shape, dim):
    return lax.broadcasted_iota(jnp.int32, shape, dim)


def lower(length):
    return (iota((length, length), 0) >= iota((length, length), 1)).astype(F32)


def thrice(rates):
    heads, length = rates.shape
    spare = jnp.zeros((STATE - 3 * heads, length), F32)
    return jnp.concatenate([rates, rates, rates, spare], axis=0)


def three_terms(value, heads):
    lane = iota(value.shape, 1)
    first = value.astype(BF16)
    rest = value - first.astype(F32)
    second = rest.astype(BF16)
    third = (rest - second.astype(F32)).astype(BF16)
    return jnp.where(lane < heads, first, jnp.where(lane < 2 * heads, second, third))


def spreader(chunk, heads, head_size, lanes):
    row = iota((STATE, lanes), 0)
    head = (iota((STATE, lanes), 1) + chunk * lanes) // head_size
    hit = (row == head) | (row == head + heads) | (row == head + 2 * heads)
    return hit.astype(F32).astype(BF16)


def head_adder(chunk, head_size, lanes):
    head = (iota((lanes, STATE), 0) + chunk * lanes) // head_size
    return (iota((lanes, STATE), 1) == head).astype(F32).astype(BF16)


def head_sums(value, adder):
    first = value.astype(BF16)
    second = (value - first.astype(F32)).astype(BF16)
    return dot(first, adder, 1, 0) + dot(second, adder, 1, 0)


def decay_terms(rates, heads):
    length = rates.shape[1]
    running = dot(lower(length), thrice(rates), 1, 1, HIGHEST)
    last = running[length - 1 : length, :]
    return (
        running,
        three_terms(jnp.exp(last - running), heads),
        three_terms(jnp.exp(running), heads),
    )


def term_pair(value):
    first = value.astype(BF16)
    return first, (value - first.astype(F32)).astype(BF16)


def lane_spread(per_strip, head_size):
    head = iota((STRIP, STRIP), 0) % per_strip
    return (iota((STRIP, STRIP), 1) // head_size == head).astype(F32)


def spread_rows(rows, offset, strips, head_size):
    per_strip = STRIP // head_size
    lane = iota((strips, STRIP), 1)
    row = iota((strips, STRIP), 0) + offset
    picked = [jnp.where(lane // per_strip == row, value, 0.0) for value in rows]
    stacked = jnp.concatenate(picked, axis=0) if len(picked) > 1 else picked[0]
    wide = dot(stacked, lane_spread(per_strip, head_size), 1, 0, HIGHEST)
    return [wide[i * strips : (i + 1) * strips, :] for i in range(len(rows))]


def whole(*shape):
    return pl.BlockSpec(shape, lambda *_: (0,) * len(shape))


def lanes_of(rows):
    return pl.BlockSpec((rows, LANES), lambda c: (0, c))


def half_lanes(rows, lanes, half, steps):
    return pl.BlockSpec((rows, lanes), lambda c: (0, half * steps + c))


LITTLE = pl.CostEstimate(flops=1, bytes_accessed=1, transcendentals=0)


def position():
    shard = lax.axis_index("seq")
    return shard & 1, shard >> 1


STEPS = 2
SUMMARY_STEPS = 1


def summary_kernel(heads, chips, half, x_ref, g_ref, write_ref, read_ref, *refs):
    place = position()
    chunk = pl.program_id(0)
    lanes = x_ref.shape[1]
    strips = lanes // STRIP
    half_strips = strips * SUMMARY_STEPS
    head_size = lanes * SUMMARY_STEPS * HALVES // heads
    part = STATE // chips
    if half == 0:
        rates_ref, send_ref, keep_ref, decay_ref, log_ref, run_ref, tail_ref, lead_ref = refs[:8]
    else:
        log_ref, tail_ref, lead_ref, send_ref, keep_ref, decay_ref = refs[:6]
    write_t, read_t = refs[-2:]

    @pl.when(chunk == 0)
    def _():
        if half == 0:
            running, tail, lead = decay_terms(rates_ref[...], heads)
            run_ref[...] = running
            tail_ref[...] = tail
            lead_ref[...] = lead
            log_ref[...] = jnp.broadcast_to(running[STRETCH - 1 :, :], (META, STRIP))
        send_ref[pl.ds(half_strips * STATE, META), :] = log_ref[...]
        write_t[...] = write_ref[...].astype(F32).T.astype(BF16)
        read_t[...] = read_ref[...].astype(F32).T.astype(BF16)

    spread = spreader(half * SUMMARY_STEPS + chunk, heads, head_size, lanes)
    tail = dot(tail_ref[...], spread, 1, 0)
    lead = dot(lead_ref[...], spread, 1, 0)
    inputs_tail = (x_ref[...].astype(F32) * tail).astype(BF16)
    grads_lead = (g_ref[...].astype(F32) * lead).astype(BF16)
    state = dot(write_t[...], inputs_tail, 1, 0)
    back = dot(read_t[...], grads_lead, 1, 0)
    first = place[0] == 0
    send = jnp.where(first, state, back)
    keep = jnp.where(first, back, state)
    for strip in range(strips):
        at = chunk * strips + strip
        wide = slice(strip * STRIP, (strip + 1) * STRIP)
        decay_ref[pl.ds(at, 1), :] = lead[STRETCH - 1 :, wide]
        for quarter in range(chips):
            rows = pl.ds(pl.multiple_of((quarter * half_strips + at) * part, part), part)
            mine = slice(quarter * part, (quarter + 1) * part)
            send_ref[rows, :] = send[mine, wide]
            keep_ref[rows, :] = keep[mine, wide]


def summary(chips, half, x, g, write_map, read_map, rates, shared):
    tokens, wide = x.shape
    heads = rates.shape[0]
    lanes = wide // (SUMMARY_STEPS * HALVES)
    strips = wide // STRIP // HALVES
    terms = [
        jax.ShapeDtypeStruct((META, STRIP), F32),
        jax.ShapeDtypeStruct((tokens, STRIP), F32),
        jax.ShapeDtypeStruct((tokens, STRIP), BF16),
        jax.ShapeDtypeStruct((tokens, STRIP), BF16),
    ]
    out_shape = [
        jax.ShapeDtypeStruct((strips * STATE + META, STRIP), F32),
        jax.ShapeDtypeStruct((strips * STATE, STRIP), F32),
        jax.ShapeDtypeStruct((strips, STRIP), F32),
    ]
    if half == 0:
        extra = [rates]
        out_shape = out_shape + terms
    else:
        extra = [shared[0], shared[2], shared[3]]
    return pl.pallas_call(
        lambda *refs: summary_kernel(heads, chips, half, *refs),
        grid=(SUMMARY_STEPS,),
        in_specs=[
            half_lanes(tokens, lanes, half, SUMMARY_STEPS),
            half_lanes(tokens, lanes, half, SUMMARY_STEPS),
            whole(tokens, STATE),
            whole(tokens, STATE),
        ]
        + [whole(*value.shape) for value in extra],
        out_specs=[whole(*out.shape) for out in out_shape],
        out_shape=out_shape,
        scratch_shapes=[
            pltpu.VMEM((STATE, tokens), BF16),
            pltpu.VMEM((STATE, tokens), BF16),
        ],
        compiler_params=pltpu.CompilerParams(vmem_limit_bytes=BIG_VMEM),
        cost_estimate=LITTLE,
        name="summary",
    )(x, g, write_map, read_map, *extra)


def combine_kernel(chips, first_ref, keep_ref, decay_ref, log_ref, mine_ref, send_ref):
    place = position()
    strips = decay_ref.shape[0]
    part = STATE // chips
    size = mine_ref.shape[0]
    bit = place[1] & 1
    for base, out_ref in ((bit * size, mine_ref), ((1 - bit) * size, send_ref)):
        for strip in range(strips):
            decay = decay_ref[strip : strip + 1, :]
            for at in range(strip * part, size, strips * part):
                rows = pl.ds(pl.multiple_of(base + at, part), part)
                out_ref[at : at + part, :] = first_ref[rows, :] * decay + keep_ref[rows, :]
    meta = first_ref[2 * size :, :] + log_ref[...]
    send_ref[size : size + META, :] = meta
    send_ref[size + META :, :] = meta


def halves(size):
    return (
        [whole(size, STRIP), whole(size + PAD, STRIP)],
        [
            jax.ShapeDtypeStruct((size, STRIP), F32),
            jax.ShapeDtypeStruct((size + PAD, STRIP), F32),
        ],
    )


def combine(chips, first, keep, decay, log):
    out_specs, out_shape = halves(keep.shape[0] // 2)
    return pl.pallas_call(
        lambda *refs: combine_kernel(chips, *refs),
        in_specs=[whole(*value.shape) for value in (first, keep, decay, log)],
        out_specs=out_specs,
        out_shape=out_shape,
        compiler_params=pltpu.CompilerParams(vmem_limit_bytes=SMALL_VMEM),
        cost_estimate=LITTLE,
        name="combine",
    )(first, keep, decay, log)


def is_ahead(place, level):
    return ((place[1] >> level) & 1) == place[0]


def up_kernel(level, last, part, offset, strips, head_size, mine_ref, log_ref, got_ref, *outs):
    place = position()
    size = mine_ref.shape[0]
    ahead = is_ahead(place, level)
    mine_log, got_log = log_ref[size : size + 1, :], got_ref[size : size + 1, :]
    mine_wide, got_wide = spread_rows(
        [jnp.where(ahead, 1.0, jnp.exp(got_log)), jnp.where(ahead, jnp.exp(mine_log), 1.0)],
        offset,
        strips,
        head_size,
    )
    bit = (place[1] >> (level + 1)) & 1
    half = size if last else size // 2
    targets = ((0, outs[0]),) if last else ((bit * half, outs[0]), ((1 - bit) * half, outs[1]))
    for base, out_ref in targets:
        for strip in range(strips):
            one = slice(strip, strip + 1)
            for at in range(strip * part, half, strips * part):
                rows = slice(at, at + part)
                if not last:
                    rows = pl.ds(pl.multiple_of(base + at, part), part)
                out_ref[at : at + part, :] = (
                    mine_ref[rows, :] * mine_wide[one, :] + got_ref[rows, :] * got_wide[one, :]
                )
    outs[-1][half:, :] = jnp.broadcast_to(mine_log + got_log, (META if last else PAD, STRIP))


def up(level, chips, half, strips, head_size, mine, send, got):
    size = mine.shape[0]
    last = 2 << level == chips
    out_specs, out_shape = halves(size if last else size // 2)
    if last:
        out_specs = [whole(size + META, STRIP)]
        out_shape = [jax.ShapeDtypeStruct((size + META, STRIP), F32)]
    return pl.pallas_call(
        lambda *refs: up_kernel(
            level, last, STATE // chips, half * strips, strips, head_size, *refs
        ),
        in_specs=[whole(size, STRIP), whole(*send.shape), whole(size + PAD, STRIP)],
        out_specs=out_specs,
        out_shape=out_shape,
        compiler_params=pltpu.CompilerParams(vmem_limit_bytes=SMALL_VMEM),
        cost_estimate=LITTLE,
        name="up",
    )(mine, send, got)


def down_kernel(level, top, part, offset, strips, head_size, mine_ref, log_ref, got_ref, *refs):
    place = position()
    sources, (here_ref, there_ref) = refs[:-2], refs[-2:]
    size = mine_ref.shape[0]
    ahead = is_ahead(place, level)
    rows_of = [
        jnp.where(ahead, jnp.exp(got_ref[size : size + 1, :]), 1.0),
        jnp.where(ahead, 1.0, jnp.exp(log_ref[size : size + 1, :])),
    ]
    if top:
        passed = jnp.zeros_like(rows_of[0])
        for ref in sources:
            rows_of.append(jnp.exp(passed))
            passed = passed + ref[size : size + 1, :]
        bases, length = (0,), size
    else:
        length = size // 2
        bit = (place[1] >> (level + 1)) & 1
        bases = (bit * length, (1 - bit) * length)
    here_wide, there_wide, *group_wide = spread_rows(rows_of, offset, strips, head_size)
    for index, base in enumerate(bases):
        for strip in range(strips):
            one = slice(strip, strip + 1)
            for at in range(strip * part, length, strips * part):
                rows = slice(at, at + part)
                if top:
                    entering = sources[0][rows, :] * group_wide[0][one, :]
                    for ref, wide in zip(sources[1:], group_wide[1:]):
                        entering = entering + ref[rows, :] * wide[one, :]
                else:
                    entering = sources[index][rows, :]
                    rows = pl.ds(pl.multiple_of(base + at, part), part)
                got = jnp.where(ahead, got_ref[rows, :], 0.0)
                mine = jnp.where(ahead, 0.0, mine_ref[rows, :])
                here_ref[rows, :] = entering * here_wide[one, :] + got
                there_ref[rows, :] = entering * there_wide[one, :] + mine
    there_ref[size:, :] = jnp.zeros((PAD, STRIP), F32)


def down(level, chips, half, strips, head_size, mine, send, got, sources):
    size = mine.shape[0]
    top = 2 << level == chips
    return pl.pallas_call(
        lambda *refs: down_kernel(
            level, top, STATE // chips, half * strips, strips, head_size, *refs
        ),
        in_specs=[whole(size, STRIP), whole(*send.shape), whole(size + PAD, STRIP)]
        + [whole(*value.shape) for value in sources],
        out_specs=[whole(size, STRIP), whole(size + PAD, STRIP)],
        out_shape=[
            jax.ShapeDtypeStruct((size, STRIP), F32),
            jax.ShapeDtypeStruct((size + PAD, STRIP), F32),
        ],
        compiler_params=pltpu.CompilerParams(vmem_limit_bytes=SMALL_VMEM),
        cost_estimate=LITTLE,
        name="down",
    )(mine, send, got, *sources)


def intra_kernel(
    heads, head_size, start, last,
    after_ref, x_ref, g_ref, write_ref, read_ref, rates_ref, column_ref, tail_ref, lead_ref, *refs,
):
    dx_ref, state_ref, back_ref, change_ref, *sums, row_ref, scores_ref, mask_ref, pairs_ref, \
        write_t, read_t = refs[5 if start else 0 :]
    step = pl.program_id(0)
    chunk = start + step
    lanes = x_ref.shape[1]
    per_chunk = lanes // head_size

    @pl.when(step == 0)
    def _():
        rates = rates_ref[...]
        triangle = lower(STRETCH)
        row_ref[...] = dot(rates, triangle, 1, 1, HIGHEST)
        mask_ref[...] = triangle
        scores_ref[...] = dot(read_ref[...], write_ref[...], 1, 1)
        pairs_ref[...] = refs[4][...] if start else jnp.zeros_like(pairs_ref)
        change_ref[...] = refs[3][...] if start else jnp.zeros_like(change_ref)
        write_t[...] = write_ref[...].astype(F32).T.astype(BF16)
        read_t[...] = read_ref[...].astype(F32).T.astype(BF16)

    columns = pltpu.roll(column_ref[...], STATE - chunk * per_chunk, 1)
    rows = row_ref[pl.ds(pl.multiple_of(chunk * per_chunk, per_chunk), per_chunk), :]
    causal = mask_ref[...] > 0.5
    scores = scores_ref[...]
    pairs = pairs_ref[...]
    low_half = iota((STRETCH, 2 * head_size), 1) < head_size
    adder = head_adder(chunk, head_size, lanes)
    spread = spreader(chunk, heads, head_size, lanes)
    high, low = term_pair(x_ref[...].astype(F32) * dot(tail_ref[...], spread, 1, 0))
    state_ref[...] = dot(write_t[...], high, 1, 0) + dot(write_t[...], low, 1, 0)
    high, low = term_pair(g_ref[...].astype(F32) * dot(lead_ref[...], spread, 1, 0))
    back_ref[...] = dot(read_t[...], high, 1, 0) + dot(read_t[...], low, 1, 0)
    for pair in range(per_chunk // 2):
        strip = slice(pair * 2 * head_size, (pair + 1) * 2 * head_size)
        x = x_ref[:, strip]
        g = g_ref[:, strip]
        ys, dxs = [], []
        for half in range(2):
            head = 2 * pair + half
            gap = columns[:, head : head + 1] - rows[head : head + 1, :]
            decay = jnp.where(causal, jnp.exp(gap), 0.0)
            mixing = (scores * decay).astype(BF16)
            ys.append(dot(mixing, x, 1, 0))
            dxs.append(dot(mixing, g, 0, 0))
            mine = low_half if half == 0 else jnp.logical_not(low_half)
            pairs = pairs + dot(jnp.where(mine, g, jnp.zeros_like(g)), x, 1, 1) * decay
        y = jnp.where(low_half, ys[0], ys[1])
        dx = jnp.where(low_half, dxs[0], dxs[1])
        dx_ref[:, strip] = dx
        change_ref[...] += head_sums(
            g.astype(F32) * y - x.astype(F32) * dx, adder[strip, :]
        )
    pairs_ref[...] = pairs

    @pl.when(step == pl.num_programs(0) - 1)
    def _():
        if last:
            summed = pairs_ref[...].astype(BF16)
            sums[0][...] = dot(summed, read_ref[...], 0, 0)
            sums[1][...] = dot(summed, write_ref[...], 1, 0)
        else:
            sums[0][...] = pairs_ref[...]


def intra(start, steps, after, x, g, write_map, read_map, rates, shared, earlier):
    tokens, wide = x.shape
    heads = rates.shape[0]
    last = (start + steps) * LANES == wide
    lanes = lambda rows: pl.BlockSpec((rows, LANES), lambda c: (0, start + c))
    anywhere = pl.BlockSpec(memory_space=pl.ANY)
    sums = [(tokens, STATE)] * 2 if last else [(tokens, tokens)]
    return pl.pallas_call(
        lambda *refs: intra_kernel(heads, wide // heads, start, last, *refs),
        grid=(steps,),
        in_specs=[
            whole(META, STRIP),
            lanes(tokens),
            lanes(tokens),
            whole(tokens, STATE),
            whole(tokens, STATE),
            whole(heads, tokens),
        ]
        + [whole(tokens, STRIP)] * 3
        + ([anywhere] * 3 + [whole(tokens, STATE), whole(tokens, tokens)] if earlier else []),
        out_specs=[lanes(tokens), lanes(STATE), lanes(STATE), whole(tokens, STATE)]
        + [whole(*shape) for shape in sums],
        out_shape=[
            jax.ShapeDtypeStruct((tokens, wide), F32),
            jax.ShapeDtypeStruct((STATE, wide), F32),
            jax.ShapeDtypeStruct((STATE, wide), F32),
            jax.ShapeDtypeStruct((tokens, STATE), F32),
        ]
        + [jax.ShapeDtypeStruct(shape, F32) for shape in sums],
        scratch_shapes=[
            pltpu.VMEM((heads, tokens), F32),
            pltpu.VMEM((tokens, tokens), F32),
            pltpu.VMEM((tokens, tokens), F32),
            pltpu.VMEM((tokens, tokens), F32),
            pltpu.VMEM((STATE, tokens), BF16),
            pltpu.VMEM((STATE, tokens), BF16),
        ],
        input_output_aliases={9: 0, 10: 1, 11: 2} if earlier else {},
        compiler_params=pltpu.CompilerParams(vmem_limit_bytes=SMALL_VMEM),
        cost_estimate=LITTLE,
        name="intra",
    )(after, x, g, write_map, read_map, rates, *shared[1:], *earlier)


def order_kernel(here_ref, got_ref, low_ref, high_ref):
    place = position()
    bit = place[1] & 1
    here, got = here_ref[...], got_ref[: here_ref.shape[0], :]
    low_ref[...] = jnp.where(bit == 0, here, got)
    high_ref[...] = jnp.where(bit == 0, got, here)


def order(here, got):
    return pl.pallas_call(
        order_kernel,
        in_specs=[whole(*here.shape), whole(*got.shape)],
        out_specs=[whole(*here.shape)] * 2,
        out_shape=[jax.ShapeDtypeStruct(here.shape, F32)] * 2,
        compiler_params=pltpu.CompilerParams(vmem_limit_bytes=SMALL_VMEM),
        cost_estimate=LITTLE,
        name="order",
    )(here, got)


def assemble_kernel(
    heads, chips, half, head_size, ordered,
    after_ref, first_ref, state_own, back_own, *refs,
):
    place = position()
    own_refs, far_refs, (state_ref, back_ref, total_ref) = refs[:2], refs[2:4], refs[4:]
    bit = 0 if ordered else place[1] & 1
    lanes = state_ref.shape[1]
    strips = lanes // STRIP
    part = STATE // chips
    size = strips * part
    log = first_ref[chips * size : chips * size + 1, :]
    decay = spread_rows([jnp.exp(log)], half * strips, strips, head_size)[0]
    is_first = place[0] == 0
    sums = [None] * strips
    for quarter in range(chips):
        rows = slice(quarter * part, (quarter + 1) * part)
        for strip in range(strips):
            wide = slice(strip * STRIP, (strip + 1) * STRIP)
            here = slice(quarter * size + strip * part, quarter * size + (strip + 1) * part)
            piece, at = divmod(here.start, chips // 2 * size)
            there = slice(at, at + part)
            own, far = own_refs[piece][there, :], far_refs[piece][there, :]
            if not ordered:
                own = jnp.where(bit == 0, own, own_refs[1 - piece][there, :])
                far = jnp.where(bit == 0, far, far_refs[1 - piece][there, :])
            own = own * decay[strip : strip + 1, :] + first_ref[here, :]
            state = jnp.where(is_first, far, own).astype(BF16)
            back = jnp.where(is_first, own, far).astype(BF16)
            state_ref[rows, wide] = state
            back_ref[rows, wide] = back
            gain = state.astype(F32) * back_own[rows, wide]
            gain = gain - back.astype(F32) * state_own[rows, wide]
            sums[strip] = gain if sums[strip] is None else sums[strip] + gain
    row_sum = [
        jnp.broadcast_to(jnp.sum(value, axis=0, keepdims=True), (META, STRIP)) for value in sums
    ]
    total = head_sums(jnp.concatenate(row_sum, axis=1), head_adder(half, head_size, lanes))
    total_ref[...] = total + after_ref[...] if half else total


def assemble(heads, chips, half, ordered, after, first, state_own, back_own, own, far):
    wide = state_own.shape[1]
    lanes = wide // HALVES
    mine = pl.BlockSpec((STATE, lanes), lambda c: (0, half))
    return pl.pallas_call(
        lambda *refs: assemble_kernel(heads, chips, half, wide // heads, ordered, *refs),
        grid=(1,),
        in_specs=[whole(META, STRIP), whole(*first.shape), mine, mine]
        + [whole(*value.shape) for value in (*own, *far)],
        out_specs=[whole(STATE, lanes), whole(STATE, lanes), whole(META, STRIP)],
        out_shape=[
            jax.ShapeDtypeStruct((STATE, lanes), BF16),
            jax.ShapeDtypeStruct((STATE, lanes), BF16),
            jax.ShapeDtypeStruct((META, STRIP), F32),
        ],
        compiler_params=pltpu.CompilerParams(vmem_limit_bytes=SMALL_VMEM),
        cost_estimate=LITTLE,
        name="assemble",
    )(after, first, state_own, back_own, *own, *far)


def finish_kernel(
    heads, head_size, start, steps, last, x_ref, g_ref, write_ref, read_ref, tail_ref, lead_ref,
    dx_ref, db_ref, dc_ref, change_ref, state_ref, back_ref, *refs,
):
    grad_ref, db_out, dc_out, change_out, token_ref, db_sum, dc_sum, sum_out = refs[-8:]
    chunk = pl.program_id(0)
    lanes = x_ref.shape[1]
    wide = start + chunk

    @pl.when(chunk == 0)
    def _():
        sum_out[...] = change_ref[...]
        db_sum[...] = db_ref[...]
        dc_sum[...] = dc_ref[...]

    state = state_ref[...]
    back = back_ref[...]
    spread = spreader(wide, heads, head_size, lanes)
    tail = dot(tail_ref[...], spread, 1, 0)
    lead = dot(lead_ref[...], spread, 1, 0)
    x = x_ref[...].astype(F32)
    g = g_ref[...].astype(F32)
    y = dot(read_ref[...], state, 1, 0) * lead
    dx = dot(write_ref[...], back, 1, 0) * tail
    grad_ref[...] = (dx_ref[...] + dx).astype(BF16)
    adder = head_adder(wide, head_size, lanes)
    sum_out[...] += head_sums(g * y - x * dx, adder)
    db_sum[...] += dot((x * tail).astype(BF16), back, 1, 1)
    dc_sum[...] += dot((g * lead).astype(BF16), state, 1, 1)

    @pl.when(chunk == steps - 1)
    def _():
        token_ref[...] = refs[-9][...]
        db_out[...] = db_sum[...].astype(db_out.dtype)
        dc_out[...] = dc_sum[...].astype(dc_out.dtype)
        if last:
            change_out[...] = dot(sum_out[...], lower(STRETCH), 0, 0, HIGHEST)[:heads, :]
        else:
            change_out[...] = sum_out[...]


def finish(heads, lanes, start, steps, after, x, g, write_map, read_map, shared, dx, sums, state, back, grad):
    tokens, wide = x.shape
    strip = pl.BlockSpec((tokens, lanes), lambda c: (0, start + c))
    first = start % (wide // HALVES // lanes)
    own = pl.BlockSpec((STATE, lanes), lambda c: (0, first + c))
    last = (start + steps) * lanes == wide
    kind = BF16 if last else F32
    change = (heads, tokens) if last else (tokens, STATE)
    earlier = [] if grad is None else [grad]
    return pl.pallas_call(
        lambda *refs: finish_kernel(heads, wide // heads, start, steps, last, *refs),
        grid=(steps,),
        in_specs=[strip, strip]
        + [whole(tokens, STATE)] * 4
        + [strip]
        + [whole(tokens, STATE)] * 3
        + [own, own]
        + [pl.BlockSpec(memory_space=pl.ANY)] * len(earlier)
        + [whole(META, STRIP)],
        out_specs=[strip] + [whole(tokens, STATE)] * 2 + [whole(*change), whole(META, STRIP)],
        out_shape=[
            jax.ShapeDtypeStruct((tokens, wide), BF16),
            jax.ShapeDtypeStruct((tokens, STATE), kind),
            jax.ShapeDtypeStruct((tokens, STATE), kind),
            jax.ShapeDtypeStruct(change, F32),
            jax.ShapeDtypeStruct((META, STRIP), F32),
        ],
        scratch_shapes=[pltpu.VMEM((tokens, STATE), F32)] * 3,
        input_output_aliases={12: 0} if earlier else {},
        compiler_params=pltpu.CompilerParams(vmem_limit_bytes=SMALL_VMEM),
        cost_estimate=LITTLE,
        name="finish",
    )(x, g, write_map, read_map, *shared[2:], dx, *sums, state, back, *earlier, after)


def count_kernel(after_ref, later_ref, total_ref, *refs):
    place = position()
    got_refs, (later_out, total_out) = refs[:-2], refs[-2:]
    later, total = later_ref[...], total_ref[...]
    for step, ref in enumerate(got_refs, 1):
        later = later + jnp.where((place[1] ^ step) > place[1], ref[...], 0.0)
        total = total + ref[...]
    later_out[...] = later
    total_out[...] = total


def core_kernel(total_ref, got_ref, later_out, total_out):
    place = position()
    later_out[...] = jnp.where(place[0] == 0, got_ref[...], 0.0)
    total_out[...] = total_ref[...] + got_ref[...]


def tiles(kernel, name, *values):
    return pl.pallas_call(
        kernel,
        in_specs=[whole(META, STRIP)] * len(values),
        out_specs=[whole(META, STRIP)] * 2,
        out_shape=[jax.ShapeDtypeStruct((META, STRIP), F32)] * 2,
        compiler_params=pltpu.CompilerParams(vmem_limit_bytes=SMALL_VMEM),
        cost_estimate=LITTLE,
        name=name,
    )(*values)


def add_later_kernel(suffix_ref, *refs):
    out_ref = refs[-1]
    heads = out_ref.shape[0]
    later = refs[0][...]
    for ref in refs[1:-1]:
        later = later + ref[...]
    out_ref[...] = suffix_ref[...] + later.T[:heads, 0:1]


def add_later(suffix, *parts):
    return pl.pallas_call(
        add_later_kernel,
        in_specs=[whole(*value.shape) for value in (suffix, *parts)],
        out_specs=whole(*suffix.shape),
        out_shape=jax.ShapeDtypeStruct(suffix.shape, F32),
        compiler_params=pltpu.CompilerParams(vmem_limit_bytes=SMALL_VMEM),
        cost_estimate=LITTLE,
        name="add_later",
    )(suffix, *parts)


def per_device(inputs, out_grad, input_map, output_map, log_decay):
    heads = log_decay.shape[0]
    head_size = inputs.shape[1] // heads
    groups, shards = lax.axis_size("grp"), lax.axis_size("seq")
    chips = shards // 2
    strips = inputs.shape[1] // STRIP // HALVES
    everyone = [(a, z, c) for a in range(groups) for z in range(chips) for c in range(2)]

    def move(value, target):
        pairs = []
        for a, z, c in everyone:
            to = target(a, z, c)
            if to is not None:
                pairs.append((a * shards + 2 * z + c, to[0] * shards + 2 * to[1] + to[2]))
        return lax.ppermute(value, ("grp", "seq"), pairs)

    def to_core(value):
        return move(value, lambda a, z, c: (a, z, 1 - c))

    def to_chip(value, step):
        return move(value, lambda a, z, c: (a, z ^ step, c)) if step else value

    def to_earlier(value, step):
        return move(value, lambda a, z, c: (a - step, z, c) if a >= step else None)

    def to_later(value, step):
        def target(a, z, c):
            to = a + step if c == 1 else a - step
            return (to, z, c) if 0 <= to < groups else None

        return move(value, target)

    maps = (inputs, out_grad, input_map, output_map)
    send, keep, decay, *shared = summary(chips, 0, *maps, log_decay, None)
    first = [to_core(send)]
    kept, decays = [keep], [decay]
    send, keep, decay = summary(chips, 1, *maps, log_decay, shared)
    first.append(to_core(send))
    kept.append(keep)
    decays.append(decay)

    levels = chips.bit_length() - 1
    held = [[], []]
    waiting = [None, None]

    def advance(half, step):
        fixed = (chips, half, strips, head_size)
        if step == 0:
            mine, send = combine(
                chips, first[half], kept[half], decays[half], shared[0]
            )
        elif step < levels:
            held[half][-1] += (waiting[half],)
            mine, send = up(step - 1, *fixed, *held[half][-1])
        elif step == levels:
            held[half][-1] += (waiting[half],)
            (send,) = up(step - 1, *fixed, *held[half][-1])
            waiting[half] = [to_later(send, far) for far in range(1, groups)]
            return send
        elif step <= 2 * levels:
            level = 2 * levels - step
            if level < levels - 1:
                waiting[half] = (held[half][level + 1], waiting[half])
            mine, send = down(level, *fixed, *held[half][level], waiting[half])
            held[half][level] = mine
            waiting[half] = to_chip(send, 1 << level)
            return send
        else:
            held[half] = order(held[half][0], waiting[half])
            waiting[half] = [to_core(value) for value in held[half]]
            return held[half][0]
        held[half].append((mine, send))
        waiting[half] = to_chip(send, 1 << step)
        return send

    chunks = inputs.shape[1] // LANES
    rounds = 2 * levels + 2
    block, ready = (), 0
    for step in range(rounds):
        token = advance(0, step)
        if step:
            advance(1, step - 1)
        if step < 3:
            more = pl.cdiv(chunks - ready, 3 - step)
            block = intra(ready, more, token, *maps, log_decay, shared, block)
            ready += more
            if step < 2:
                waiting[0], waiting[1], first[1], block = lax.optimization_barrier(
                    (waiting[0], waiting[1], first[1], block)
                )
            else:
                waiting[1], block = lax.optimization_barrier((waiting[1], block))
        elif levels + 1 < step < rounds - 1:
            waiting[0], waiting[1] = lax.optimization_barrier((waiting[0], waiting[1]))
    dx, state_own, back_own, change, db, dc = block
    lanes = inputs.shape[1] // HALVES // STEPS
    own_b = held[1][0]
    far_b = to_core(own_b)
    state, back, counted = assemble(
        heads, chips, 0, True, change, first[0], state_own, back_own, held[0], waiting[0]
    )
    grad, *sums, counted = finish(
        heads, lanes * STEPS, 0, 1, counted, *maps, shared, dx, (db, dc, change), state, back, None
    )
    got, far_b, counted = lax.optimization_barrier((waiting[1], far_b, counted))
    own_b, far_b = (own_b, got), (far_b, to_core(got))
    state, back, counted = assemble(
        heads, chips, 1, False, counted, first[1], state_own, back_own, own_b, far_b
    )

    later, counted = tiles(core_kernel, "core_sum", counted, to_core(counted))
    got = [to_chip(counted, step) for step in range(1, chips)]
    grad, *sums, token = finish(
        heads, lanes, STEPS, 1, counted, *maps, shared, dx, sums, state, back, grad
    )
    later, counted = tiles(count_kernel, "chip_sum", token, later, counted, *got)
    got = [to_earlier(counted, step) for step in range(1, groups)]
    grad, *sums, _ = finish(
        heads, lanes, STEPS + 1, 1, counted, *maps, shared, dx, sums, state, back, grad
    )
    return (grad, sums[0], sums[1], add_later(sums[2], later, *got))


def solution(mesh):
    tokens = P(("grp", "seq"), None)
    in_specs = (tokens, tokens, tokens, tokens, P(None, ("grp", "seq")))
    out_specs = (tokens, tokens, tokens, P(None, ("grp", "seq")))
    return jax.shard_map(
        per_device, mesh=mesh, in_specs=in_specs, out_specs=out_specs, check_vma=False
    )
```

```python
import jax
import jax.numpy as jnp
from jax import lax
from jax.experimental import pallas as pl
from jax.experimental.pallas import tpu as pltpu
from jax.sharding import PartitionSpec as P

STATE = 128
STRETCH = 256
LANES = 512
HALVES = 2
STRIP = 128
META = 8
PAD = 2 * META
BIG_VMEM = 56 << 20
SMALL_VMEM = 24 << 20
F32 = jnp.float32
BF16 = jnp.bfloat16
HIGHEST = lax.Precision.HIGHEST


def dot(left, right, left_dim, right_dim, precision=None):
    return lax.dot_general(
        left,
        right,
        (((left_dim,), (right_dim,)), ((), ())),
        precision=precision,
        preferred_element_type=F32,
    )


def iota(shape, dim):
    return lax.broadcasted_iota(jnp.int32, shape, dim)


def lower(length):
    return (iota((length, length), 0) >= iota((length, length), 1)).astype(F32)


def thrice(rates):
    heads, length = rates.shape
    spare = jnp.zeros((STATE - 3 * heads, length), F32)
    return jnp.concatenate([rates, rates, rates, spare], axis=0)


def three_terms(value, heads):
    lane = iota(value.shape, 1)
    first = value.astype(BF16)
    rest = value - first.astype(F32)
    second = rest.astype(BF16)
    third = (rest - second.astype(F32)).astype(BF16)
    return jnp.where(lane < heads, first, jnp.where(lane < 2 * heads, second, third))


def spreader(chunk, heads, head_size, lanes):
    row = iota((STATE, lanes), 0)
    head = (iota((STATE, lanes), 1) + chunk * lanes) // head_size
    hit = (row == head) | (row == head + heads) | (row == head + 2 * heads)
    return hit.astype(F32).astype(BF16)


def head_adder(chunk, head_size, lanes):
    head = (iota((lanes, STATE), 0) + chunk * lanes) // head_size
    return (iota((lanes, STATE), 1) == head).astype(F32).astype(BF16)


def head_sums(value, adder):
    first = value.astype(BF16)
    second = (value - first.astype(F32)).astype(BF16)
    return dot(first, adder, 1, 0) + dot(second, adder, 1, 0)


def decay_terms(rates, heads):
    length = rates.shape[1]
    running = dot(lower(length), thrice(rates), 1, 1, HIGHEST)
    last = running[length - 1 : length, :]
    return (
        running,
        three_terms(jnp.exp(last - running), heads),
        three_terms(jnp.exp(running), heads),
    )


def term_pair(value):
    first = value.astype(BF16)
    return first, (value - first.astype(F32)).astype(BF16)


def lane_spread(per_strip, head_size):
    head = iota((STRIP, STRIP), 0) % per_strip
    return (iota((STRIP, STRIP), 1) // head_size == head).astype(F32)


def spread_rows(rows, offset, strips, head_size):
    per_strip = STRIP // head_size
    lane = iota((strips, STRIP), 1)
    row = iota((strips, STRIP), 0) + offset
    picked = [jnp.where(lane // per_strip == row, value, 0.0) for value in rows]
    stacked = jnp.concatenate(picked, axis=0) if len(picked) > 1 else picked[0]
    wide = dot(stacked, lane_spread(per_strip, head_size), 1, 0, HIGHEST)
    return [wide[i * strips : (i + 1) * strips, :] for i in range(len(rows))]


def whole(*shape):
    return pl.BlockSpec(shape, lambda *_: (0,) * len(shape))


def lanes_of(rows):
    return pl.BlockSpec((rows, LANES), lambda c: (0, c))


def half_lanes(rows, lanes, half, steps):
    return pl.BlockSpec((rows, lanes), lambda c: (0, half * steps + c))


LITTLE = pl.CostEstimate(flops=1, bytes_accessed=1, transcendentals=0)


def position():
    shard = lax.axis_index("seq")
    return shard & 1, shard >> 1


STEPS = 2
SUMMARY_STEPS = 1


def summary_kernel(heads, chips, half, x_ref, g_ref, write_ref, read_ref, *refs):
    place = position()
    chunk = pl.program_id(0)
    lanes = x_ref.shape[1]
    strips = lanes // STRIP
    half_strips = strips * SUMMARY_STEPS
    head_size = lanes * SUMMARY_STEPS * HALVES // heads
    part = STATE // chips
    if half == 0:
        rates_ref, send_ref, keep_ref, decay_ref, log_ref, run_ref, tail_ref, lead_ref = refs[:8]
    else:
        log_ref, tail_ref, lead_ref, send_ref, keep_ref, decay_ref = refs[:6]
    write_t, read_t = refs[-2:]

    @pl.when(chunk == 0)
    def _():
        if half == 0:
            running, tail, lead = decay_terms(rates_ref[...], heads)
            run_ref[...] = running
            tail_ref[...] = tail
            lead_ref[...] = lead
            log_ref[...] = jnp.broadcast_to(running[STRETCH - 1 :, :], (META, STRIP))
        send_ref[pl.ds(half_strips * STATE, META), :] = log_ref[...]
        write_t[...] = write_ref[...].astype(F32).T.astype(BF16)
        read_t[...] = read_ref[...].astype(F32).T.astype(BF16)

    spread = spreader(half * SUMMARY_STEPS + chunk, heads, head_size, lanes)
    tail = dot(tail_ref[...], spread, 1, 0)
    lead = dot(lead_ref[...], spread, 1, 0)
    inputs_tail = (x_ref[...].astype(F32) * tail).astype(BF16)
    grads_lead = (g_ref[...].astype(F32) * lead).astype(BF16)
    state = dot(write_t[...], inputs_tail, 1, 0)
    back = dot(read_t[...], grads_lead, 1, 0)
    first = place[0] == 0
    send = jnp.where(first, state, back)
    keep = jnp.where(first, back, state)
    for strip in range(strips):
        at = chunk * strips + strip
        wide = slice(strip * STRIP, (strip + 1) * STRIP)
        decay_ref[pl.ds(at, 1), :] = lead[STRETCH - 1 :, wide]
        for quarter in range(chips):
            rows = pl.ds(pl.multiple_of((quarter * half_strips + at) * part, part), part)
            mine = slice(quarter * part, (quarter + 1) * part)
            send_ref[rows, :] = send[mine, wide]
            keep_ref[rows, :] = keep[mine, wide]


def summary(chips, half, x, g, write_map, read_map, rates, shared):
    tokens, wide = x.shape
    heads = rates.shape[0]
    lanes = wide // (SUMMARY_STEPS * HALVES)
    strips = wide // STRIP // HALVES
    terms = [
        jax.ShapeDtypeStruct((META, STRIP), F32),
        jax.ShapeDtypeStruct((tokens, STRIP), F32),
        jax.ShapeDtypeStruct((tokens, STRIP), BF16),
        jax.ShapeDtypeStruct((tokens, STRIP), BF16),
    ]
    out_shape = [
        jax.ShapeDtypeStruct((strips * STATE + META, STRIP), F32),
        jax.ShapeDtypeStruct((strips * STATE, STRIP), F32),
        jax.ShapeDtypeStruct((strips, STRIP), F32),
    ]
    if half == 0:
        extra = [rates]
        out_shape = out_shape + terms
    else:
        extra = [shared[0], shared[2], shared[3]]
    return pl.pallas_call(
        lambda *refs: summary_kernel(heads, chips, half, *refs),
        grid=(SUMMARY_STEPS,),
        in_specs=[
            half_lanes(tokens, lanes, half, SUMMARY_STEPS),
            half_lanes(tokens, lanes, half, SUMMARY_STEPS),
            whole(tokens, STATE),
            whole(tokens, STATE),
        ]
        + [whole(*value.shape) for value in extra],
        out_specs=[whole(*out.shape) for out in out_shape],
        out_shape=out_shape,
        scratch_shapes=[
            pltpu.VMEM((STATE, tokens), BF16),
            pltpu.VMEM((STATE, tokens), BF16),
        ],
        compiler_params=pltpu.CompilerParams(vmem_limit_bytes=BIG_VMEM),
        cost_estimate=LITTLE,
        name="summary",
    )(x, g, write_map, read_map, *extra)


def combine_kernel(chips, first_ref, keep_ref, decay_ref, log_ref, mine_ref, send_ref):
    place = position()
    strips = decay_ref.shape[0]
    part = STATE // chips
    size = mine_ref.shape[0]
    bit = place[1] & 1
    for base, out_ref in ((bit * size, mine_ref), ((1 - bit) * size, send_ref)):
        for strip in range(strips):
            decay = decay_ref[strip : strip + 1, :]
            for at in range(strip * part, size, strips * part):
                rows = pl.ds(pl.multiple_of(base + at, part), part)
                out_ref[at : at + part, :] = first_ref[rows, :] * decay + keep_ref[rows, :]
    meta = first_ref[2 * size :, :] + log_ref[...]
    send_ref[size : size + META, :] = meta
    send_ref[size + META :, :] = meta


def halves(size):
    return (
        [whole(size, STRIP), whole(size + PAD, STRIP)],
        [
            jax.ShapeDtypeStruct((size, STRIP), F32),
            jax.ShapeDtypeStruct((size + PAD, STRIP), F32),
        ],
    )


def combine(chips, first, keep, decay, log):
    out_specs, out_shape = halves(keep.shape[0] // 2)
    return pl.pallas_call(
        lambda *refs: combine_kernel(chips, *refs),
        in_specs=[whole(*value.shape) for value in (first, keep, decay, log)],
        out_specs=out_specs,
        out_shape=out_shape,
        compiler_params=pltpu.CompilerParams(vmem_limit_bytes=SMALL_VMEM),
        cost_estimate=LITTLE,
        name="combine",
    )(first, keep, decay, log)


def is_ahead(place, level):
    return ((place[1] >> level) & 1) == place[0]


def up_kernel(level, last, part, offset, strips, head_size, mine_ref, log_ref, got_ref, *outs):
    place = position()
    size = mine_ref.shape[0]
    ahead = is_ahead(place, level)
    mine_log, got_log = log_ref[size : size + 1, :], got_ref[size : size + 1, :]
    mine_wide, got_wide = spread_rows(
        [jnp.where(ahead, 1.0, jnp.exp(got_log)), jnp.where(ahead, jnp.exp(mine_log), 1.0)],
        offset,
        strips,
        head_size,
    )
    bit = (place[1] >> (level + 1)) & 1
    half = size if last else size // 2
    targets = ((0, outs[0]),) if last else ((bit * half, outs[0]), ((1 - bit) * half, outs[1]))
    for base, out_ref in targets:
        for strip in range(strips):
            one = slice(strip, strip + 1)
            for at in range(strip * part, half, strips * part):
                rows = slice(at, at + part)
                if not last:
                    rows = pl.ds(pl.multiple_of(base + at, part), part)
                out_ref[at : at + part, :] = (
                    mine_ref[rows, :] * mine_wide[one, :] + got_ref[rows, :] * got_wide[one, :]
                )
    outs[-1][half:, :] = jnp.broadcast_to(mine_log + got_log, (META if last else PAD, STRIP))


def up(level, chips, half, strips, head_size, mine, send, got):
    size = mine.shape[0]
    last = 2 << level == chips
    out_specs, out_shape = halves(size if last else size // 2)
    if last:
        out_specs = [whole(size + META, STRIP)]
        out_shape = [jax.ShapeDtypeStruct((size + META, STRIP), F32)]
    return pl.pallas_call(
        lambda *refs: up_kernel(
            level, last, STATE // chips, half * strips, strips, head_size, *refs
        ),
        in_specs=[whole(size, STRIP), whole(*send.shape), whole(size + PAD, STRIP)],
        out_specs=out_specs,
        out_shape=out_shape,
        compiler_params=pltpu.CompilerParams(vmem_limit_bytes=SMALL_VMEM),
        cost_estimate=LITTLE,
        name="up",
    )(mine, send, got)


def down_kernel(level, top, part, offset, strips, head_size, mine_ref, log_ref, got_ref, *refs):
    place = position()
    sources, (here_ref, there_ref) = refs[:-2], refs[-2:]
    size = mine_ref.shape[0]
    ahead = is_ahead(place, level)
    rows_of = [
        jnp.where(ahead, jnp.exp(got_ref[size : size + 1, :]), 1.0),
        jnp.where(ahead, 1.0, jnp.exp(log_ref[size : size + 1, :])),
    ]
    if top:
        passed = jnp.zeros_like(rows_of[0])
        for ref in sources:
            rows_of.append(jnp.exp(passed))
            passed = passed + ref[size : size + 1, :]
        bases, length = (0,), size
    else:
        length = size // 2
        bit = (place[1] >> (level + 1)) & 1
        bases = (bit * length, (1 - bit) * length)
    here_wide, there_wide, *group_wide = spread_rows(rows_of, offset, strips, head_size)
    for index, base in enumerate(bases):
        for strip in range(strips):
            one = slice(strip, strip + 1)
            for at in range(strip * part, length, strips * part):
                rows = slice(at, at + part)
                if top:
                    entering = sources[0][rows, :] * group_wide[0][one, :]
                    for ref, wide in zip(sources[1:], group_wide[1:]):
                        entering = entering + ref[rows, :] * wide[one, :]
                else:
                    entering = sources[index][rows, :]
                    rows = pl.ds(pl.multiple_of(base + at, part), part)
                got = jnp.where(ahead, got_ref[rows, :], 0.0)
                mine = jnp.where(ahead, 0.0, mine_ref[rows, :])
                here_ref[rows, :] = entering * here_wide[one, :] + got
                there_ref[rows, :] = entering * there_wide[one, :] + mine
    there_ref[size:, :] = jnp.zeros((PAD, STRIP), F32)


def down(level, chips, half, strips, head_size, mine, send, got, sources):
    size = mine.shape[0]
    top = 2 << level == chips
    return pl.pallas_call(
        lambda *refs: down_kernel(
            level, top, STATE // chips, half * strips, strips, head_size, *refs
        ),
        in_specs=[whole(size, STRIP), whole(*send.shape), whole(size + PAD, STRIP)]
        + [whole(*value.shape) for value in sources],
        out_specs=[whole(size, STRIP), whole(size + PAD, STRIP)],
        out_shape=[
            jax.ShapeDtypeStruct((size, STRIP), F32),
            jax.ShapeDtypeStruct((size + PAD, STRIP), F32),
        ],
        compiler_params=pltpu.CompilerParams(vmem_limit_bytes=SMALL_VMEM),
        cost_estimate=LITTLE,
        name="down",
    )(mine, send, got, *sources)


def intra_kernel(
    heads, head_size, start, last,
    after_ref, x_ref, g_ref, write_ref, read_ref, rates_ref, column_ref, tail_ref, lead_ref, *refs,
):
    dx_ref, state_ref, back_ref, change_ref, *sums, row_ref, scores_ref, mask_ref, pairs_ref, \
        write_t, read_t = refs[5 if start else 0 :]
    step = pl.program_id(0)
    chunk = start + step
    lanes = x_ref.shape[1]
    per_chunk = lanes // head_size

    @pl.when(step == 0)
    def _():
        rates = rates_ref[...]
        triangle = lower(STRETCH)
        row_ref[...] = dot(rates, triangle, 1, 1, HIGHEST)
        mask_ref[...] = triangle
        scores_ref[...] = dot(read_ref[...], write_ref[...], 1, 1)
        pairs_ref[...] = refs[4][...] if start else jnp.zeros_like(pairs_ref)
        change_ref[...] = refs[3][...] if start else jnp.zeros_like(change_ref)
        write_t[...] = write_ref[...].astype(F32).T.astype(BF16)
        read_t[...] = read_ref[...].astype(F32).T.astype(BF16)

    columns = pltpu.roll(column_ref[...], STATE - chunk * per_chunk, 1)
    rows = row_ref[pl.ds(pl.multiple_of(chunk * per_chunk, per_chunk), per_chunk), :]
    causal = mask_ref[...] > 0.5
    scores = scores_ref[...]
    pairs = pairs_ref[...]
    low_half = iota((STRETCH, 2 * head_size), 1) < head_size
    adder = head_adder(chunk, head_size, lanes)
    spread = spreader(chunk, heads, head_size, lanes)
    high, low = term_pair(x_ref[...].astype(F32) * dot(tail_ref[...], spread, 1, 0))
    state_ref[...] = dot(write_t[...], high, 1, 0) + dot(write_t[...], low, 1, 0)
    high, low = term_pair(g_ref[...].astype(F32) * dot(lead_ref[...], spread, 1, 0))
    back_ref[...] = dot(read_t[...], high, 1, 0) + dot(read_t[...], low, 1, 0)
    for pair in range(per_chunk // 2):
        strip = slice(pair * 2 * head_size, (pair + 1) * 2 * head_size)
        x = x_ref[:, strip]
        g = g_ref[:, strip]
        ys, dxs = [], []
        for half in range(2):
            head = 2 * pair + half
            gap = columns[:, head : head + 1] - rows[head : head + 1, :]
            decay = jnp.where(causal, jnp.exp(gap), 0.0)
            mixing = (scores * decay).astype(BF16)
            ys.append(dot(mixing, x, 1, 0))
            dxs.append(dot(mixing, g, 0, 0))
            mine = low_half if half == 0 else jnp.logical_not(low_half)
            pairs = pairs + dot(jnp.where(mine, g, jnp.zeros_like(g)), x, 1, 1) * decay
        y = jnp.where(low_half, ys[0], ys[1])
        dx = jnp.where(low_half, dxs[0], dxs[1])
        dx_ref[:, strip] = dx
        change_ref[...] += head_sums(
            g.astype(F32) * y - x.astype(F32) * dx, adder[strip, :]
        )
    pairs_ref[...] = pairs

    @pl.when(step == pl.num_programs(0) - 1)
    def _():
        if last:
            summed = pairs_ref[...].astype(BF16)
            sums[0][...] = dot(summed, read_ref[...], 0, 0)
            sums[1][...] = dot(summed, write_ref[...], 1, 0)
        else:
            sums[0][...] = pairs_ref[...]


def intra(start, steps, after, x, g, write_map, read_map, rates, shared, earlier):
    tokens, wide = x.shape
    heads = rates.shape[0]
    last = (start + steps) * LANES == wide
    lanes = lambda rows: pl.BlockSpec((rows, LANES), lambda c: (0, start + c))
    anywhere = pl.BlockSpec(memory_space=pl.ANY)
    sums = [(tokens, STATE)] * 2 if last else [(tokens, tokens)]
    return pl.pallas_call(
        lambda *refs: intra_kernel(heads, wide // heads, start, last, *refs),
        grid=(steps,),
        in_specs=[
            whole(META, STRIP),
            lanes(tokens),
            lanes(tokens),
            whole(tokens, STATE),
            whole(tokens, STATE),
            whole(heads, tokens),
        ]
        + [whole(tokens, STRIP)] * 3
        + ([anywhere] * 3 + [whole(tokens, STATE), whole(tokens, tokens)] if earlier else []),
        out_specs=[lanes(tokens), lanes(STATE), lanes(STATE), whole(tokens, STATE)]
        + [whole(*shape) for shape in sums],
        out_shape=[
            jax.ShapeDtypeStruct((tokens, wide), F32),
            jax.ShapeDtypeStruct((STATE, wide), F32),
            jax.ShapeDtypeStruct((STATE, wide), F32),
            jax.ShapeDtypeStruct((tokens, STATE), F32),
        ]
        + [jax.ShapeDtypeStruct(shape, F32) for shape in sums],
        scratch_shapes=[
            pltpu.VMEM((heads, tokens), F32),
            pltpu.VMEM((tokens, tokens), F32),
            pltpu.VMEM((tokens, tokens), F32),
            pltpu.VMEM((tokens, tokens), F32),
            pltpu.VMEM((STATE, tokens), BF16),
            pltpu.VMEM((STATE, tokens), BF16),
        ],
        input_output_aliases={9: 0, 10: 1, 11: 2} if earlier else {},
        compiler_params=pltpu.CompilerParams(vmem_limit_bytes=SMALL_VMEM),
        cost_estimate=LITTLE,
        name="intra",
    )(after, x, g, write_map, read_map, rates, *shared[1:], *earlier)


def order_kernel(here_ref, got_ref, low_ref, high_ref):
    place = position()
    bit = place[1] & 1
    here, got = here_ref[...], got_ref[: here_ref.shape[0], :]
    low_ref[...] = jnp.where(bit == 0, here, got)
    high_ref[...] = jnp.where(bit == 0, got, here)


def order(here, got):
    return pl.pallas_call(
        order_kernel,
        in_specs=[whole(*here.shape), whole(*got.shape)],
        out_specs=[whole(*here.shape)] * 2,
        out_shape=[jax.ShapeDtypeStruct(here.shape, F32)] * 2,
        compiler_params=pltpu.CompilerParams(vmem_limit_bytes=SMALL_VMEM),
        cost_estimate=LITTLE,
        name="order",
    )(here, got)


def assemble_kernel(
    heads, chips, half, head_size, ordered,
    after_ref, first_ref, state_own, back_own, *refs,
):
    place = position()
    own_refs, far_refs, (state_ref, back_ref, total_ref) = refs[:2], refs[2:4], refs[4:]
    bit = 0 if ordered else place[1] & 1
    lanes = state_ref.shape[1]
    strips = lanes // STRIP
    part = STATE // chips
    size = strips * part
    log = first_ref[chips * size : chips * size + 1, :]
    decay = spread_rows([jnp.exp(log)], half * strips, strips, head_size)[0]
    is_first = place[0] == 0
    sums = [None] * strips
    for quarter in range(chips):
        rows = slice(quarter * part, (quarter + 1) * part)
        for strip in range(strips):
            wide = slice(strip * STRIP, (strip + 1) * STRIP)
            here = slice(quarter * size + strip * part, quarter * size + (strip + 1) * part)
            piece, at = divmod(here.start, chips // 2 * size)
            there = slice(at, at + part)
            own, far = own_refs[piece][there, :], far_refs[piece][there, :]
            if not ordered:
                own = jnp.where(bit == 0, own, own_refs[1 - piece][there, :])
                far = jnp.where(bit == 0, far, far_refs[1 - piece][there, :])
            own = own * decay[strip : strip + 1, :] + first_ref[here, :]
            state = jnp.where(is_first, far, own).astype(BF16)
            back = jnp.where(is_first, own, far).astype(BF16)
            state_ref[rows, wide] = state
            back_ref[rows, wide] = back
            whole_at = slice(half * lanes + wide.start, half * lanes + wide.stop)
            gain = state.astype(F32) * back_own[rows, whole_at]
            gain = gain - back.astype(F32) * state_own[rows, whole_at]
            sums[strip] = gain if sums[strip] is None else sums[strip] + gain
    row_sum = [
        jnp.broadcast_to(jnp.sum(value, axis=0, keepdims=True), (META, STRIP)) for value in sums
    ]
    total = head_sums(jnp.concatenate(row_sum, axis=1), head_adder(half, head_size, lanes))
    total_ref[...] = total + after_ref[...] if half else total


def assemble(heads, chips, half, ordered, after, first, state_own, back_own, own, far):
    wide = state_own.shape[1]
    lanes = wide // HALVES
    return pl.pallas_call(
        lambda *refs: assemble_kernel(heads, chips, half, wide // heads, ordered, *refs),
        in_specs=[
            whole(*value.shape) for value in (after, first, state_own, back_own, *own, *far)
        ],
        out_specs=[whole(STATE, lanes), whole(STATE, lanes), whole(META, STRIP)],
        out_shape=[
            jax.ShapeDtypeStruct((STATE, lanes), BF16),
            jax.ShapeDtypeStruct((STATE, lanes), BF16),
            jax.ShapeDtypeStruct((META, STRIP), F32),
        ],
        compiler_params=pltpu.CompilerParams(vmem_limit_bytes=SMALL_VMEM),
        cost_estimate=LITTLE,
        name="assemble",
    )(after, first, state_own, back_own, *own, *far)


def finish_kernel(
    heads, head_size, start, steps, last, x_ref, g_ref, write_ref, read_ref, tail_ref, lead_ref,
    dx_ref, db_ref, dc_ref, change_ref, state_ref, back_ref, *refs,
):
    grad_ref, db_out, dc_out, change_out, token_ref, db_sum, dc_sum, sum_out = refs[-8:]
    chunk = pl.program_id(0)
    lanes = x_ref.shape[1]
    wide = start + chunk

    @pl.when(chunk == 0)
    def _():
        sum_out[...] = change_ref[...]
        db_sum[...] = db_ref[...]
        dc_sum[...] = dc_ref[...]

    state = state_ref[...]
    back = back_ref[...]
    spread = spreader(wide, heads, head_size, lanes)
    tail = dot(tail_ref[...], spread, 1, 0)
    lead = dot(lead_ref[...], spread, 1, 0)
    x = x_ref[...].astype(F32)
    g = g_ref[...].astype(F32)
    y = dot(read_ref[...], state, 1, 0) * lead
    dx = dot(write_ref[...], back, 1, 0) * tail
    grad_ref[...] = (dx_ref[...] + dx).astype(BF16)
    adder = head_adder(wide, head_size, lanes)
    sum_out[...] += head_sums(g * y - x * dx, adder)
    db_sum[...] += dot((x * tail).astype(BF16), back, 1, 1)
    dc_sum[...] += dot((g * lead).astype(BF16), state, 1, 1)

    @pl.when(chunk == steps - 1)
    def _():
        token_ref[...] = refs[-9][...]
        db_out[...] = db_sum[...].astype(db_out.dtype)
        dc_out[...] = dc_sum[...].astype(dc_out.dtype)
        if last:
            change_out[...] = dot(sum_out[...], lower(STRETCH), 0, 0, HIGHEST)[:heads, :]
        else:
            change_out[...] = sum_out[...]


def finish(heads, lanes, start, steps, after, x, g, write_map, read_map, shared, dx, sums, state, back, grad):
    tokens, wide = x.shape
    strip = pl.BlockSpec((tokens, lanes), lambda c: (0, start + c))
    first = start % (wide // HALVES // lanes)
    own = pl.BlockSpec((STATE, lanes), lambda c: (0, first + c))
    last = (start + steps) * lanes == wide
    kind = BF16 if last else F32
    change = (heads, tokens) if last else (tokens, STATE)
    earlier = [] if grad is None else [grad]
    return pl.pallas_call(
        lambda *refs: finish_kernel(heads, wide // heads, start, steps, last, *refs),
        grid=(steps,),
        in_specs=[strip, strip]
        + [whole(tokens, STATE)] * 4
        + [strip]
        + [whole(tokens, STATE)] * 3
        + [own, own]
        + [pl.BlockSpec(memory_space=pl.ANY)] * len(earlier)
        + [whole(META, STRIP)],
        out_specs=[strip] + [whole(tokens, STATE)] * 2 + [whole(*change), whole(META, STRIP)],
        out_shape=[
            jax.ShapeDtypeStruct((tokens, wide), BF16),
            jax.ShapeDtypeStruct((tokens, STATE), kind),
            jax.ShapeDtypeStruct((tokens, STATE), kind),
            jax.ShapeDtypeStruct(change, F32),
            jax.ShapeDtypeStruct((META, STRIP), F32),
        ],
        scratch_shapes=[pltpu.VMEM((tokens, STATE), F32)] * 3,
        input_output_aliases={12: 0} if earlier else {},
        compiler_params=pltpu.CompilerParams(vmem_limit_bytes=SMALL_VMEM),
        cost_estimate=LITTLE,
        name="finish",
    )(x, g, write_map, read_map, *shared[2:], dx, *sums, state, back, *earlier, after)


def count_kernel(after_ref, later_ref, total_ref, *refs):
    place = position()
    got_refs, (later_out, total_out) = refs[:-2], refs[-2:]
    later, total = later_ref[...], total_ref[...]
    for step, ref in enumerate(got_refs, 1):
        later = later + jnp.where((place[1] ^ step) > place[1], ref[...], 0.0)
        total = total + ref[...]
    later_out[...] = later
    total_out[...] = total


def core_kernel(total_ref, got_ref, later_out, total_out):
    place = position()
    later_out[...] = jnp.where(place[0] == 0, got_ref[...], 0.0)
    total_out[...] = total_ref[...] + got_ref[...]


def tiles(kernel, name, *values):
    return pl.pallas_call(
        kernel,
        in_specs=[whole(META, STRIP)] * len(values),
        out_specs=[whole(META, STRIP)] * 2,
        out_shape=[jax.ShapeDtypeStruct((META, STRIP), F32)] * 2,
        compiler_params=pltpu.CompilerParams(vmem_limit_bytes=SMALL_VMEM),
        cost_estimate=LITTLE,
        name=name,
    )(*values)


def add_later_kernel(suffix_ref, *refs):
    out_ref = refs[-1]
    heads = out_ref.shape[0]
    later = refs[0][...]
    for ref in refs[1:-1]:
        later = later + ref[...]
    out_ref[...] = suffix_ref[...] + later.T[:heads, 0:1]


def add_later(suffix, *parts):
    return pl.pallas_call(
        add_later_kernel,
        in_specs=[whole(*value.shape) for value in (suffix, *parts)],
        out_specs=whole(*suffix.shape),
        out_shape=jax.ShapeDtypeStruct(suffix.shape, F32),
        compiler_params=pltpu.CompilerParams(vmem_limit_bytes=SMALL_VMEM),
        cost_estimate=LITTLE,
        name="add_later",
    )(suffix, *parts)


def per_device(inputs, out_grad, input_map, output_map, log_decay):
    heads = log_decay.shape[0]
    head_size = inputs.shape[1] // heads
    groups, shards = lax.axis_size("grp"), lax.axis_size("seq")
    chips = shards // 2
    strips = inputs.shape[1] // STRIP // HALVES
    everyone = [(a, z, c) for a in range(groups) for z in range(chips) for c in range(2)]

    def move(value, target):
        pairs = []
        for a, z, c in everyone:
            to = target(a, z, c)
            if to is not None:
                pairs.append((a * shards + 2 * z + c, to[0] * shards + 2 * to[1] + to[2]))
        return lax.ppermute(value, ("grp", "seq"), pairs)

    def to_core(value):
        return move(value, lambda a, z, c: (a, z, 1 - c))

    def to_chip(value, step):
        return move(value, lambda a, z, c: (a, z ^ step, c)) if step else value

    def to_earlier(value, step):
        return move(value, lambda a, z, c: (a - step, z, c) if a >= step else None)

    def to_later(value, step):
        def target(a, z, c):
            to = a + step if c == 1 else a - step
            return (to, z, c) if 0 <= to < groups else None

        return move(value, target)

    maps = (inputs, out_grad, input_map, output_map)
    send, keep, decay, *shared = summary(chips, 0, *maps, log_decay, None)
    first = [to_core(send)]
    kept, decays = [keep], [decay]
    send, keep, decay = summary(chips, 1, *maps, log_decay, shared)
    first.append(to_core(send))
    kept.append(keep)
    decays.append(decay)

    levels = chips.bit_length() - 1
    held = [[], []]
    waiting = [None, None]

    def advance(half, step):
        fixed = (chips, half, strips, head_size)
        if step == 0:
            mine, send = combine(
                chips, first[half], kept[half], decays[half], shared[0]
            )
        elif step < levels:
            held[half][-1] += (waiting[half],)
            mine, send = up(step - 1, *fixed, *held[half][-1])
        elif step == levels:
            held[half][-1] += (waiting[half],)
            (send,) = up(step - 1, *fixed, *held[half][-1])
            waiting[half] = [to_later(send, far) for far in range(1, groups)]
            return send
        elif step <= 2 * levels:
            level = 2 * levels - step
            if level < levels - 1:
                waiting[half] = (held[half][level + 1], waiting[half])
            mine, send = down(level, *fixed, *held[half][level], waiting[half])
            held[half][level] = mine
            waiting[half] = to_chip(send, 1 << level)
            return send
        else:
            held[half] = order(held[half][0], waiting[half])
            waiting[half] = [to_core(value) for value in held[half]]
            return held[half][0]
        held[half].append((mine, send))
        waiting[half] = to_chip(send, 1 << step)
        return send

    chunks = inputs.shape[1] // LANES
    rounds = 2 * levels + 2
    block, ready = (), 0
    for step in range(rounds):
        token = advance(0, step)
        if step:
            advance(1, step - 1)
        if step < 3:
            more = pl.cdiv(chunks - ready, 3 - step)
            block = intra(ready, more, token, *maps, log_decay, shared, block)
            ready += more
            waiting[0], waiting[1], first[1], block = lax.optimization_barrier(
                (waiting[0], waiting[1], first[1], block)
            )
        elif levels + 1 < step < rounds - 1:
            waiting[0], waiting[1] = lax.optimization_barrier((waiting[0], waiting[1]))
    dx, state_own, back_own, change, db, dc = block
    lanes = inputs.shape[1] // HALVES // STEPS
    own_b = held[1][0]
    far_b = to_core(own_b)
    state, back, counted = assemble(
        heads, chips, 0, True, shared[0], first[0], state_own, back_own, held[0], waiting[0]
    )
    grad, *sums, counted = finish(
        heads, lanes * STEPS, 0, 1, counted, *maps, shared, dx, (db, dc, change), state, back, None
    )
    got, far_b, counted = lax.optimization_barrier((waiting[1], far_b, counted))
    own_b, far_b = (own_b, got), (far_b, to_core(got))
    state, back, counted = assemble(
        heads, chips, 1, False, counted, first[1], state_own, back_own, own_b, far_b
    )

    later, counted = tiles(core_kernel, "core_sum", counted, to_core(counted))
    got = [to_chip(counted, step) for step in range(1, chips)]
    grad, *sums, token = finish(
        heads, lanes, STEPS, 1, counted, *maps, shared, dx, sums, state, back, grad
    )
    later, counted = tiles(count_kernel, "chip_sum", token, later, counted, *got)
    got = [to_earlier(counted, step) for step in range(1, groups)]
    grad, *sums, _ = finish(
        heads, lanes, STEPS + 1, 1, counted, *maps, shared, dx, sums, state, back, grad
    )
    return (grad, sums[0], sums[1], add_later(sums[2], later, *got))


def solution(mesh):
    tokens = P(("grp", "seq"), None)
    in_specs = (tokens, tokens, tokens, tokens, P(None, ("grp", "seq")))
    out_specs = (tokens, tokens, tokens, P(None, ("grp", "seq")))
    return jax.shard_map(
        per_device, mesh=mesh, in_specs=in_specs, out_specs=out_specs, check_vma=False
    )
```

```python
import jax
import jax.numpy as jnp
from jax import lax
from jax.experimental import pallas as pl
from jax.experimental.pallas import tpu as pltpu
from jax.sharding import PartitionSpec as P

STATE = 128
STRETCH = 256
LANES = 512
HALVES = 2
STRIP = 128
META = 8
PAD = 2 * META
BIG_VMEM = 56 << 20
SMALL_VMEM = 24 << 20
F32 = jnp.float32
BF16 = jnp.bfloat16
HIGHEST = lax.Precision.HIGHEST


def dot(left, right, left_dim, right_dim, precision=None):
    return lax.dot_general(
        left,
        right,
        (((left_dim,), (right_dim,)), ((), ())),
        precision=precision,
        preferred_element_type=F32,
    )


def iota(shape, dim):
    return lax.broadcasted_iota(jnp.int32, shape, dim)


def lower(length):
    return (iota((length, length), 0) >= iota((length, length), 1)).astype(F32)


def thrice(rates):
    heads, length = rates.shape
    spare = jnp.zeros((STATE - 3 * heads, length), F32)
    return jnp.concatenate([rates, rates, rates, spare], axis=0)


def three_terms(value, heads):
    lane = iota(value.shape, 1)
    first = value.astype(BF16)
    rest = value - first.astype(F32)
    second = rest.astype(BF16)
    third = (rest - second.astype(F32)).astype(BF16)
    return jnp.where(lane < heads, first, jnp.where(lane < 2 * heads, second, third))


def spreader(chunk, heads, head_size, lanes):
    row = iota((STATE, lanes), 0)
    head = (iota((STATE, lanes), 1) + chunk * lanes) // head_size
    hit = (row == head) | (row == head + heads) | (row == head + 2 * heads)
    return hit.astype(F32).astype(BF16)


def head_adder(chunk, head_size, lanes):
    head = (iota((lanes, STATE), 0) + chunk * lanes) // head_size
    return (iota((lanes, STATE), 1) == head).astype(F32).astype(BF16)


def head_sums(value, adder):
    first = value.astype(BF16)
    second = (value - first.astype(F32)).astype(BF16)
    return dot(first, adder, 1, 0) + dot(second, adder, 1, 0)


def decay_terms(rates, heads):
    length = rates.shape[1]
    running = dot(lower(length), thrice(rates), 1, 1, HIGHEST)
    last = running[length - 1 : length, :]
    return (
        running,
        three_terms(jnp.exp(last - running), heads),
        three_terms(jnp.exp(running), heads),
    )


def term_pair(value):
    first = value.astype(BF16)
    return first, (value - first.astype(F32)).astype(BF16)


def lane_spread(per_strip, head_size):
    head = iota((STRIP, STRIP), 0) % per_strip
    return (iota((STRIP, STRIP), 1) // head_size == head).astype(F32)


def spread_rows(rows, offset, strips, head_size):
    per_strip = STRIP // head_size
    lane = iota((strips, STRIP), 1)
    row = iota((strips, STRIP), 0) + offset
    picked = [jnp.where(lane // per_strip == row, value, 0.0) for value in rows]
    stacked = jnp.concatenate(picked, axis=0) if len(picked) > 1 else picked[0]
    wide = dot(stacked, lane_spread(per_strip, head_size), 1, 0, HIGHEST)
    return [wide[i * strips : (i + 1) * strips, :] for i in range(len(rows))]


def whole(*shape):
    return pl.BlockSpec(shape, lambda *_: (0,) * len(shape))


def lanes_of(rows):
    return pl.BlockSpec((rows, LANES), lambda c: (0, c))


def half_lanes(rows, lanes, half, steps):
    return pl.BlockSpec((rows, lanes), lambda c: (0, half * steps + c))


LITTLE = pl.CostEstimate(flops=1, bytes_accessed=1, transcendentals=0)


def position():
    shard = lax.axis_index("seq")
    return shard & 1, shard >> 1


SUMMARY_STEPS = 1


def summary_kernel(heads, chips, half, x_ref, g_ref, write_ref, read_ref, *refs):
    place = position()
    chunk = pl.program_id(0)
    lanes = x_ref.shape[1]
    strips = lanes // STRIP
    half_strips = strips * SUMMARY_STEPS
    head_size = lanes * SUMMARY_STEPS * HALVES // heads
    part = STATE // chips
    if half == 0:
        rates_ref, send_ref, keep_ref, decay_ref, log_ref, run_ref, tail_ref, lead_ref = refs[:8]
    else:
        log_ref, tail_ref, lead_ref, send_ref, keep_ref, decay_ref = refs[:6]
    write_t, read_t = refs[-2:]

    @pl.when(chunk == 0)
    def _():
        if half == 0:
            running, tail, lead = decay_terms(rates_ref[...], heads)
            run_ref[...] = running
            tail_ref[...] = tail
            lead_ref[...] = lead
            log_ref[...] = jnp.broadcast_to(running[STRETCH - 1 :, :], (META, STRIP))
        send_ref[pl.ds(half_strips * STATE, META), :] = log_ref[...]
        write_t[...] = write_ref[...].astype(F32).T.astype(BF16)
        read_t[...] = read_ref[...].astype(F32).T.astype(BF16)

    spread = spreader(half * SUMMARY_STEPS + chunk, heads, head_size, lanes)
    tail = dot(tail_ref[...], spread, 1, 0)
    lead = dot(lead_ref[...], spread, 1, 0)
    inputs_tail = (x_ref[...].astype(F32) * tail).astype(BF16)
    grads_lead = (g_ref[...].astype(F32) * lead).astype(BF16)
    state = dot(write_t[...], inputs_tail, 1, 0)
    back = dot(read_t[...], grads_lead, 1, 0)
    first = place[0] == 0
    send = jnp.where(first, state, back)
    keep = jnp.where(first, back, state)
    for strip in range(strips):
        at = chunk * strips + strip
        wide = slice(strip * STRIP, (strip + 1) * STRIP)
        decay_ref[pl.ds(at, 1), :] = lead[STRETCH - 1 :, wide]
        for quarter in range(chips):
            rows = pl.ds(pl.multiple_of((quarter * half_strips + at) * part, part), part)
            mine = slice(quarter * part, (quarter + 1) * part)
            send_ref[rows, :] = send[mine, wide]
            keep_ref[rows, :] = keep[mine, wide]


def summary(chips, half, x, g, write_map, read_map, rates, shared):
    tokens, wide = x.shape
    heads = rates.shape[0]
    lanes = wide // (SUMMARY_STEPS * HALVES)
    strips = wide // STRIP // HALVES
    terms = [
        jax.ShapeDtypeStruct((META, STRIP), F32),
        jax.ShapeDtypeStruct((tokens, STRIP), F32),
        jax.ShapeDtypeStruct((tokens, STRIP), BF16),
        jax.ShapeDtypeStruct((tokens, STRIP), BF16),
    ]
    out_shape = [
        jax.ShapeDtypeStruct((strips * STATE + META, STRIP), F32),
        jax.ShapeDtypeStruct((strips * STATE, STRIP), F32),
        jax.ShapeDtypeStruct((strips, STRIP), F32),
    ]
    if half == 0:
        extra = [rates]
        out_shape = out_shape + terms
    else:
        extra = [shared[0], shared[2], shared[3]]
    return pl.pallas_call(
        lambda *refs: summary_kernel(heads, chips, half, *refs),
        grid=(SUMMARY_STEPS,),
        in_specs=[
            half_lanes(tokens, lanes, half, SUMMARY_STEPS),
            half_lanes(tokens, lanes, half, SUMMARY_STEPS),
            whole(tokens, STATE),
            whole(tokens, STATE),
        ]
        + [whole(*value.shape) for value in extra],
        out_specs=[whole(*out.shape) for out in out_shape],
        out_shape=out_shape,
        scratch_shapes=[
            pltpu.VMEM((STATE, tokens), BF16),
            pltpu.VMEM((STATE, tokens), BF16),
        ],
        compiler_params=pltpu.CompilerParams(vmem_limit_bytes=BIG_VMEM),
        cost_estimate=LITTLE,
        name="summary",
    )(x, g, write_map, read_map, *extra)


def combine_kernel(chips, first_ref, keep_ref, decay_ref, log_ref, mine_ref, send_ref):
    place = position()
    strips = decay_ref.shape[0]
    part = STATE // chips
    size = mine_ref.shape[0]
    bit = place[1] & 1
    for base, out_ref in ((bit * size, mine_ref), ((1 - bit) * size, send_ref)):
        for strip in range(strips):
            decay = decay_ref[strip : strip + 1, :]
            for at in range(strip * part, size, strips * part):
                rows = pl.ds(pl.multiple_of(base + at, part), part)
                out_ref[at : at + part, :] = first_ref[rows, :] * decay + keep_ref[rows, :]
    meta = first_ref[2 * size :, :] + log_ref[...]
    send_ref[size : size + META, :] = meta
    send_ref[size + META :, :] = meta


def halves(size):
    return (
        [whole(size, STRIP), whole(size + PAD, STRIP)],
        [
            jax.ShapeDtypeStruct((size, STRIP), F32),
            jax.ShapeDtypeStruct((size + PAD, STRIP), F32),
        ],
    )


def combine(chips, first, keep, decay, log):
    out_specs, out_shape = halves(keep.shape[0] // 2)
    return pl.pallas_call(
        lambda *refs: combine_kernel(chips, *refs),
        in_specs=[whole(*value.shape) for value in (first, keep, decay, log)],
        out_specs=out_specs,
        out_shape=out_shape,
        compiler_params=pltpu.CompilerParams(vmem_limit_bytes=SMALL_VMEM),
        cost_estimate=LITTLE,
        name="combine",
    )(first, keep, decay, log)


def is_ahead(place, level):
    return ((place[1] >> level) & 1) == place[0]


def up_kernel(level, last, part, offset, strips, head_size, mine_ref, log_ref, got_ref, *outs):
    place = position()
    size = mine_ref.shape[0]
    ahead = is_ahead(place, level)
    mine_log, got_log = log_ref[size : size + 1, :], got_ref[size : size + 1, :]
    mine_wide, got_wide = spread_rows(
        [jnp.where(ahead, 1.0, jnp.exp(got_log)), jnp.where(ahead, jnp.exp(mine_log), 1.0)],
        offset,
        strips,
        head_size,
    )
    bit = (place[1] >> (level + 1)) & 1
    half = size if last else size // 2
    targets = ((0, outs[0]),) if last else ((bit * half, outs[0]), ((1 - bit) * half, outs[1]))
    for base, out_ref in targets:
        for strip in range(strips):
            one = slice(strip, strip + 1)
            for at in range(strip * part, half, strips * part):
                rows = slice(at, at + part)
                if not last:
                    rows = pl.ds(pl.multiple_of(base + at, part), part)
                out_ref[at : at + part, :] = (
                    mine_ref[rows, :] * mine_wide[one, :] + got_ref[rows, :] * got_wide[one, :]
                )
    outs[-1][half:, :] = jnp.broadcast_to(mine_log + got_log, (META if last else PAD, STRIP))


def up(level, chips, half, strips, head_size, mine, send, got):
    size = mine.shape[0]
    last = 2 << level == chips
    out_specs, out_shape = halves(size if last else size // 2)
    if last:
        out_specs = [whole(size + META, STRIP)]
        out_shape = [jax.ShapeDtypeStruct((size + META, STRIP), F32)]
    return pl.pallas_call(
        lambda *refs: up_kernel(
            level, last, STATE // chips, half * strips, strips, head_size, *refs
        ),
        in_specs=[whole(size, STRIP), whole(*send.shape), whole(size + PAD, STRIP)],
        out_specs=out_specs,
        out_shape=out_shape,
        compiler_params=pltpu.CompilerParams(vmem_limit_bytes=SMALL_VMEM),
        cost_estimate=LITTLE,
        name="up",
    )(mine, send, got)


def down_kernel(level, top, part, offset, strips, head_size, mine_ref, log_ref, got_ref, *refs):
    place = position()
    sources, (here_ref, there_ref) = refs[:-2], refs[-2:]
    size = mine_ref.shape[0]
    ahead = is_ahead(place, level)
    rows_of = [
        jnp.where(ahead, jnp.exp(got_ref[size : size + 1, :]), 1.0),
        jnp.where(ahead, 1.0, jnp.exp(log_ref[size : size + 1, :])),
    ]
    if top:
        passed = jnp.zeros_like(rows_of[0])
        for ref in sources:
            rows_of.append(jnp.exp(passed))
            passed = passed + ref[size : size + 1, :]
        bases, length = (0,), size
    else:
        length = size // 2
        bit = (place[1] >> (level + 1)) & 1
        bases = (bit * length, (1 - bit) * length)
    here_wide, there_wide, *group_wide = spread_rows(rows_of, offset, strips, head_size)
    for index, base in enumerate(bases):
        for strip in range(strips):
            one = slice(strip, strip + 1)
            for at in range(strip * part, length, strips * part):
                rows = slice(at, at + part)
                if top:
                    entering = sources[0][rows, :] * group_wide[0][one, :]
                    for ref, wide in zip(sources[1:], group_wide[1:]):
                        entering = entering + ref[rows, :] * wide[one, :]
                else:
                    entering = sources[index][rows, :]
                    rows = pl.ds(pl.multiple_of(base + at, part), part)
                got = jnp.where(ahead, got_ref[rows, :], 0.0)
                mine = jnp.where(ahead, 0.0, mine_ref[rows, :])
                here_ref[rows, :] = entering * here_wide[one, :] + got
                there_ref[rows, :] = entering * there_wide[one, :] + mine
    there_ref[size:, :] = jnp.zeros((PAD, STRIP), F32)


def down(level, chips, half, strips, head_size, mine, send, got, sources):
    size = mine.shape[0]
    top = 2 << level == chips
    return pl.pallas_call(
        lambda *refs: down_kernel(
            level, top, STATE // chips, half * strips, strips, head_size, *refs
        ),
        in_specs=[whole(size, STRIP), whole(*send.shape), whole(size + PAD, STRIP)]
        + [whole(*value.shape) for value in sources],
        out_specs=[whole(size, STRIP), whole(size + PAD, STRIP)],
        out_shape=[
            jax.ShapeDtypeStruct((size, STRIP), F32),
            jax.ShapeDtypeStruct((size + PAD, STRIP), F32),
        ],
        compiler_params=pltpu.CompilerParams(vmem_limit_bytes=SMALL_VMEM),
        cost_estimate=LITTLE,
        name="down",
    )(mine, send, got, *sources)


def intra_kernel(
    heads, head_size, start, last,
    after_ref, x_ref, g_ref, write_ref, read_ref, rates_ref, column_ref, tail_ref, lead_ref, *refs,
):
    dx_ref, state_ref, back_ref, change_ref, *sums, row_ref, scores_ref, mask_ref, pairs_ref, \
        write_t, read_t = refs[5 if start else 0 :]
    step = pl.program_id(0)
    chunk = start + step
    lanes = x_ref.shape[1]
    per_chunk = lanes // head_size

    @pl.when(step == 0)
    def _():
        rates = rates_ref[...]
        triangle = lower(STRETCH)
        row_ref[...] = dot(rates, triangle, 1, 1, HIGHEST)
        mask_ref[...] = triangle
        scores_ref[...] = dot(read_ref[...], write_ref[...], 1, 1)
        pairs_ref[...] = refs[4][...] if start else jnp.zeros_like(pairs_ref)
        change_ref[...] = refs[3][...] if start else jnp.zeros_like(change_ref)
        write_t[...] = write_ref[...].astype(F32).T.astype(BF16)
        read_t[...] = read_ref[...].astype(F32).T.astype(BF16)

    columns = pltpu.roll(column_ref[...], STATE - chunk * per_chunk, 1)
    rows = row_ref[pl.ds(pl.multiple_of(chunk * per_chunk, per_chunk), per_chunk), :]
    causal = mask_ref[...] > 0.5
    scores = scores_ref[...]
    pairs = pairs_ref[...]
    low_half = iota((STRETCH, 2 * head_size), 1) < head_size
    adder = head_adder(chunk, head_size, lanes)
    spread = spreader(chunk, heads, head_size, lanes)
    high, low = term_pair(x_ref[...].astype(F32) * dot(tail_ref[...], spread, 1, 0))
    state_ref[...] = dot(write_t[...], high, 1, 0) + dot(write_t[...], low, 1, 0)
    high, low = term_pair(g_ref[...].astype(F32) * dot(lead_ref[...], spread, 1, 0))
    back_ref[...] = dot(read_t[...], high, 1, 0) + dot(read_t[...], low, 1, 0)
    for pair in range(per_chunk // 2):
        strip = slice(pair * 2 * head_size, (pair + 1) * 2 * head_size)
        x = x_ref[:, strip]
        g = g_ref[:, strip]
        ys, dxs = [], []
        for half in range(2):
            head = 2 * pair + half
            gap = columns[:, head : head + 1] - rows[head : head + 1, :]
            decay = jnp.where(causal, jnp.exp(gap), 0.0)
            mixing = (scores * decay).astype(BF16)
            ys.append(dot(mixing, x, 1, 0))
            dxs.append(dot(mixing, g, 0, 0))
            mine = low_half if half == 0 else jnp.logical_not(low_half)
            pairs = pairs + dot(jnp.where(mine, g, jnp.zeros_like(g)), x, 1, 1) * decay
        y = jnp.where(low_half, ys[0], ys[1])
        dx = jnp.where(low_half, dxs[0], dxs[1])
        dx_ref[:, strip] = dx
        change_ref[...] += head_sums(
            g.astype(F32) * y - x.astype(F32) * dx, adder[strip, :]
        )
    pairs_ref[...] = pairs

    @pl.when(step == pl.num_programs(0) - 1)
    def _():
        if last:
            summed = pairs_ref[...].astype(BF16)
            sums[0][...] = dot(summed, read_ref[...], 0, 0)
            sums[1][...] = dot(summed, write_ref[...], 1, 0)
        else:
            sums[0][...] = pairs_ref[...]


def intra(start, steps, after, x, g, write_map, read_map, rates, shared, earlier):
    tokens, wide = x.shape
    heads = rates.shape[0]
    last = (start + steps) * LANES == wide
    lanes = lambda rows: pl.BlockSpec((rows, LANES), lambda c: (0, start + c))
    anywhere = pl.BlockSpec(memory_space=pl.ANY)
    sums = [(tokens, STATE)] * 2 if last else [(tokens, tokens)]
    return pl.pallas_call(
        lambda *refs: intra_kernel(heads, wide // heads, start, last, *refs),
        grid=(steps,),
        in_specs=[
            whole(META, STRIP),
            lanes(tokens),
            lanes(tokens),
            whole(tokens, STATE),
            whole(tokens, STATE),
            whole(heads, tokens),
        ]
        + [whole(tokens, STRIP)] * 3
        + ([anywhere] * 3 + [whole(tokens, STATE), whole(tokens, tokens)] if earlier else []),
        out_specs=[lanes(tokens), lanes(STATE), lanes(STATE), whole(tokens, STATE)]
        + [whole(*shape) for shape in sums],
        out_shape=[
            jax.ShapeDtypeStruct((tokens, wide), F32),
            jax.ShapeDtypeStruct((STATE, wide), F32),
            jax.ShapeDtypeStruct((STATE, wide), F32),
            jax.ShapeDtypeStruct((tokens, STATE), F32),
        ]
        + [jax.ShapeDtypeStruct(shape, F32) for shape in sums],
        scratch_shapes=[
            pltpu.VMEM((heads, tokens), F32),
            pltpu.VMEM((tokens, tokens), F32),
            pltpu.VMEM((tokens, tokens), F32),
            pltpu.VMEM((tokens, tokens), F32),
            pltpu.VMEM((STATE, tokens), BF16),
            pltpu.VMEM((STATE, tokens), BF16),
        ],
        input_output_aliases={9: 0, 10: 1, 11: 2} if earlier else {},
        compiler_params=pltpu.CompilerParams(vmem_limit_bytes=SMALL_VMEM),
        cost_estimate=LITTLE,
        name="intra",
    )(after, x, g, write_map, read_map, rates, *shared[1:], *earlier)


def order_kernel(here_ref, got_ref, low_ref, high_ref):
    place = position()
    bit = place[1] & 1
    here, got = here_ref[...], got_ref[: here_ref.shape[0], :]
    low_ref[...] = jnp.where(bit == 0, here, got)
    high_ref[...] = jnp.where(bit == 0, got, here)


def order(here, got):
    return pl.pallas_call(
        order_kernel,
        in_specs=[whole(*here.shape), whole(*got.shape)],
        out_specs=[whole(*here.shape)] * 2,
        out_shape=[jax.ShapeDtypeStruct(here.shape, F32)] * 2,
        compiler_params=pltpu.CompilerParams(vmem_limit_bytes=SMALL_VMEM),
        cost_estimate=LITTLE,
        name="order",
    )(here, got)


def assemble_kernel(
    heads, chips, half, head_size, ordered,
    after_ref, first_ref, state_own, back_own, *refs,
):
    place = position()
    own_refs, far_refs, (state_ref, back_ref, total_ref) = refs[:2], refs[2:4], refs[4:]
    bit = 0 if ordered else place[1] & 1
    lanes = state_ref.shape[1]
    strips = lanes // STRIP
    part = STATE // chips
    size = strips * part
    log = first_ref[chips * size : chips * size + 1, :]
    decay = spread_rows([jnp.exp(log)], half * strips, strips, head_size)[0]
    is_first = place[0] == 0
    sums = [None] * strips
    for quarter in range(chips):
        rows = slice(quarter * part, (quarter + 1) * part)
        for strip in range(strips):
            wide = slice(strip * STRIP, (strip + 1) * STRIP)
            here = slice(quarter * size + strip * part, quarter * size + (strip + 1) * part)
            piece, at = divmod(here.start, chips // 2 * size)
            there = slice(at, at + part)
            own, far = own_refs[piece][there, :], far_refs[piece][there, :]
            if not ordered:
                own = jnp.where(bit == 0, own, own_refs[1 - piece][there, :])
                far = jnp.where(bit == 0, far, far_refs[1 - piece][there, :])
            own = own * decay[strip : strip + 1, :] + first_ref[here, :]
            state = jnp.where(is_first, far, own).astype(BF16)
            back = jnp.where(is_first, own, far).astype(BF16)
            state_ref[rows, wide] = state
            back_ref[rows, wide] = back
            whole_at = slice(half * lanes + wide.start, half * lanes + wide.stop)
            gain = state.astype(F32) * back_own[rows, whole_at]
            gain = gain - back.astype(F32) * state_own[rows, whole_at]
            sums[strip] = gain if sums[strip] is None else sums[strip] + gain
    row_sum = [
        jnp.broadcast_to(jnp.sum(value, axis=0, keepdims=True), (META, STRIP)) for value in sums
    ]
    total = head_sums(jnp.concatenate(row_sum, axis=1), head_adder(half, head_size, lanes))
    total_ref[...] = total + after_ref[...] if half else total


def assemble(heads, chips, half, ordered, after, first, state_own, back_own, own, far):
    wide = state_own.shape[1]
    lanes = wide // HALVES
    return pl.pallas_call(
        lambda *refs: assemble_kernel(heads, chips, half, wide // heads, ordered, *refs),
        in_specs=[
            whole(*value.shape) for value in (after, first, state_own, back_own, *own, *far)
        ],
        out_specs=[whole(STATE, lanes), whole(STATE, lanes), whole(META, STRIP)],
        out_shape=[
            jax.ShapeDtypeStruct((STATE, lanes), BF16),
            jax.ShapeDtypeStruct((STATE, lanes), BF16),
            jax.ShapeDtypeStruct((META, STRIP), F32),
        ],
        compiler_params=pltpu.CompilerParams(vmem_limit_bytes=SMALL_VMEM),
        cost_estimate=LITTLE,
        name="assemble",
    )(after, first, state_own, back_own, *own, *far)


def finish_kernel(
    heads, head_size, start, steps, last, x_ref, g_ref, write_ref, read_ref, tail_ref, lead_ref,
    dx_ref, db_ref, dc_ref, change_ref, state_ref, back_ref, *refs,
):
    grad_ref, db_out, dc_out, change_out, token_ref, db_sum, dc_sum, sum_out = refs[-8:]
    chunk = pl.program_id(0)
    lanes = x_ref.shape[1]
    wide = start + chunk

    @pl.when(chunk == 0)
    def _():
        sum_out[...] = change_ref[...]
        db_sum[...] = db_ref[...]
        dc_sum[...] = dc_ref[...]

    state = state_ref[...]
    back = back_ref[...]
    spread = spreader(wide, heads, head_size, lanes)
    tail = dot(tail_ref[...], spread, 1, 0)
    lead = dot(lead_ref[...], spread, 1, 0)
    x = x_ref[...].astype(F32)
    g = g_ref[...].astype(F32)
    y = dot(read_ref[...], state, 1, 0) * lead
    dx = dot(write_ref[...], back, 1, 0) * tail
    grad_ref[...] = (dx_ref[...] + dx).astype(BF16)
    adder = head_adder(wide, head_size, lanes)
    sum_out[...] += head_sums(g * y - x * dx, adder)
    db_sum[...] += dot((x * tail).astype(BF16), back, 1, 1)
    dc_sum[...] += dot((g * lead).astype(BF16), state, 1, 1)

    @pl.when(chunk == steps - 1)
    def _():
        token_ref[...] = refs[-9][...]
        db_out[...] = db_sum[...].astype(db_out.dtype)
        dc_out[...] = dc_sum[...].astype(dc_out.dtype)
        if last:
            change_out[...] = dot(sum_out[...], lower(STRETCH), 0, 0, HIGHEST)[:heads, :]
        else:
            change_out[...] = sum_out[...]


def finish(heads, lanes, start, steps, after, x, g, write_map, read_map, shared, dx, sums, state, back, grad):
    tokens, wide = x.shape
    strip = pl.BlockSpec((tokens, lanes), lambda c: (0, start + c))
    first = start % (wide // HALVES // lanes)
    own = pl.BlockSpec((STATE, lanes), lambda c: (0, first + c))
    last = (start + steps) * lanes == wide
    kind = BF16 if last else F32
    change = (heads, tokens) if last else (tokens, STATE)
    earlier = [] if grad is None else [grad]
    return pl.pallas_call(
        lambda *refs: finish_kernel(heads, wide // heads, start, steps, last, *refs),
        grid=(steps,),
        in_specs=[strip, strip]
        + [whole(tokens, STATE)] * 4
        + [strip]
        + [whole(tokens, STATE)] * 3
        + [own, own]
        + [pl.BlockSpec(memory_space=pl.ANY)] * len(earlier)
        + [whole(META, STRIP)],
        out_specs=[strip] + [whole(tokens, STATE)] * 2 + [whole(*change), whole(META, STRIP)],
        out_shape=[
            jax.ShapeDtypeStruct((tokens, wide), BF16),
            jax.ShapeDtypeStruct((tokens, STATE), kind),
            jax.ShapeDtypeStruct((tokens, STATE), kind),
            jax.ShapeDtypeStruct(change, F32),
            jax.ShapeDtypeStruct((META, STRIP), F32),
        ],
        scratch_shapes=[pltpu.VMEM((tokens, STATE), F32)] * 3,
        input_output_aliases={12: 0} if earlier else {},
        compiler_params=pltpu.CompilerParams(vmem_limit_bytes=SMALL_VMEM),
        cost_estimate=LITTLE,
        name="finish",
    )(x, g, write_map, read_map, *shared[2:], dx, *sums, state, back, *earlier, after)


def count_kernel(after_ref, later_ref, total_ref, *refs):
    place = position()
    got_refs, (later_out, total_out) = refs[:-2], refs[-2:]
    later, total = later_ref[...], total_ref[...]
    for step, ref in enumerate(got_refs, 1):
        later = later + jnp.where((place[1] ^ step) > place[1], ref[...], 0.0)
        total = total + ref[...]
    later_out[...] = later
    total_out[...] = total


def core_kernel(total_ref, got_ref, later_out, total_out):
    place = position()
    later_out[...] = jnp.where(place[0] == 0, got_ref[...], 0.0)
    total_out[...] = total_ref[...] + got_ref[...]


def tiles(kernel, name, *values):
    return pl.pallas_call(
        kernel,
        in_specs=[whole(META, STRIP)] * len(values),
        out_specs=[whole(META, STRIP)] * 2,
        out_shape=[jax.ShapeDtypeStruct((META, STRIP), F32)] * 2,
        compiler_params=pltpu.CompilerParams(vmem_limit_bytes=SMALL_VMEM),
        cost_estimate=LITTLE,
        name=name,
    )(*values)


def add_later_kernel(suffix_ref, *refs):
    out_ref = refs[-1]
    heads = out_ref.shape[0]
    later = refs[0][...]
    for ref in refs[1:-1]:
        later = later + ref[...]
    out_ref[...] = suffix_ref[...] + later.T[:heads, 0:1]


def add_later(suffix, *parts):
    return pl.pallas_call(
        add_later_kernel,
        in_specs=[whole(*value.shape) for value in (suffix, *parts)],
        out_specs=whole(*suffix.shape),
        out_shape=jax.ShapeDtypeStruct(suffix.shape, F32),
        compiler_params=pltpu.CompilerParams(vmem_limit_bytes=SMALL_VMEM),
        cost_estimate=LITTLE,
        name="add_later",
    )(suffix, *parts)


def per_device(inputs, out_grad, input_map, output_map, log_decay):
    heads = log_decay.shape[0]
    head_size = inputs.shape[1] // heads
    groups, shards = lax.axis_size("grp"), lax.axis_size("seq")
    chips = shards // 2
    strips = inputs.shape[1] // STRIP // HALVES
    everyone = [(a, z, c) for a in range(groups) for z in range(chips) for c in range(2)]

    def move(value, target):
        pairs = []
        for a, z, c in everyone:
            to = target(a, z, c)
            if to is not None:
                pairs.append((a * shards + 2 * z + c, to[0] * shards + 2 * to[1] + to[2]))
        return lax.ppermute(value, ("grp", "seq"), pairs)

    def to_core(value):
        return move(value, lambda a, z, c: (a, z, 1 - c))

    def to_chip(value, step):
        return move(value, lambda a, z, c: (a, z ^ step, c)) if step else value

    def to_earlier(value, step):
        return move(value, lambda a, z, c: (a - step, z, c) if a >= step else None)

    def to_later(value, step):
        def target(a, z, c):
            to = a + step if c == 1 else a - step
            return (to, z, c) if 0 <= to < groups else None

        return move(value, target)

    maps = (inputs, out_grad, input_map, output_map)
    send, keep, decay, *shared = summary(chips, 0, *maps, log_decay, None)
    first = [to_core(send)]
    kept, decays = [keep], [decay]
    send, keep, decay = summary(chips, 1, *maps, log_decay, shared)
    first.append(to_core(send))
    kept.append(keep)
    decays.append(decay)

    levels = chips.bit_length() - 1
    held = [[], []]
    waiting = [None, None]

    def advance(half, step):
        fixed = (chips, half, strips, head_size)
        if step == 0:
            mine, send = combine(
                chips, first[half], kept[half], decays[half], shared[0]
            )
        elif step < levels:
            held[half][-1] += (waiting[half],)
            mine, send = up(step - 1, *fixed, *held[half][-1])
        elif step == levels:
            held[half][-1] += (waiting[half],)
            (send,) = up(step - 1, *fixed, *held[half][-1])
            waiting[half] = [to_later(send, far) for far in range(1, groups)]
            return send
        elif step <= 2 * levels:
            level = 2 * levels - step
            if level < levels - 1:
                waiting[half] = (held[half][level + 1], waiting[half])
            mine, send = down(level, *fixed, *held[half][level], waiting[half])
            held[half][level] = mine
            waiting[half] = to_chip(send, 1 << level)
            return send
        else:
            held[half] = order(held[half][0], waiting[half])
            waiting[half] = [to_core(value) for value in held[half]]
            return held[half][0]
        held[half].append((mine, send))
        waiting[half] = to_chip(send, 1 << step)
        return send

    chunks = inputs.shape[1] // LANES
    rounds = 2 * levels + 2
    block, ready = (), 0
    for step in range(rounds):
        token = advance(0, step)
        if step:
            advance(1, step - 1)
        if step < 3:
            more = pl.cdiv(chunks - ready, 3 - step)
            block = intra(ready, more, token, *maps, log_decay, shared, block)
            ready += more
            waiting[0], waiting[1], first[1], block = lax.optimization_barrier(
                (waiting[0], waiting[1], first[1], block)
            )
        elif levels + 1 < step < rounds - 1:
            waiting[0], waiting[1] = lax.optimization_barrier((waiting[0], waiting[1]))
    dx, state_own, back_own, change, db, dc = block
    lanes = inputs.shape[1] // HALVES
    own_b = held[1][0]
    far_b = to_core(own_b)
    state, back, counted = assemble(
        heads, chips, 0, True, shared[0], first[0], state_own, back_own, held[0], waiting[0]
    )
    grad, *sums, counted = finish(
        heads, lanes, 0, 1, counted, *maps, shared, dx, (db, dc, change), state, back, None
    )
    got, far_b, counted = lax.optimization_barrier((waiting[1], far_b, counted))
    own_b, far_b = (own_b, got), (far_b, to_core(got))
    state, back, counted = assemble(
        heads, chips, 1, False, counted, first[1], state_own, back_own, own_b, far_b
    )

    later, counted = tiles(core_kernel, "core_sum", counted, to_core(counted))
    got = [to_chip(counted, step) for step in range(1, chips)]
    later, counted = tiles(count_kernel, "chip_sum", counted, later, counted, *got)
    got = [to_earlier(counted, step) for step in range(1, groups)]
    grad, *sums, _ = finish(
        heads, lanes, 1, 1, counted, *maps, shared, dx, sums, state, back, grad
    )
    return (grad, sums[0], sums[1], add_later(sums[2], later, *got))


def solution(mesh):
    tokens = P(("grp", "seq"), None)
    in_specs = (tokens, tokens, tokens, tokens, P(None, ("grp", "seq")))
    out_specs = (tokens, tokens, tokens, P(None, ("grp", "seq")))
    return jax.shard_map(
        per_device, mesh=mesh, in_specs=in_specs, out_specs=out_specs, check_vma=False
    )
```
